32 devices in a mesh: row: 8 (over z, y), col: 4 (over x, core).
Axes of the slice: x: 2, y: 2, z: 4, core: 2. Of those that a mesh axis runs over, the one named last changes fastest.
Arguments:
- features: bfloat16 [8192, 256], P(('row', 'col')), may hold values from -6 to 6
- weight: bfloat16 [256, 256], replicated, may hold values from -0.375 to 0.375
- adj_tiles: bfloat16 [8, 4, 256, 128, 128], P('row', 'col'), may hold values from -0.078125 to 0.078125
- tile_rows: int32 [8, 4, 256], P('row', 'col'), may hold values from 0 to 7, as said below
- tile_cols: int32 [8, 4, 256], P('row', 'col'), may hold values from 0 to 15
- tile_counts: int32 [8, 4], P('row', 'col'), may hold values from 21 to 256, as said below
- out_grad: bfloat16 [8192, 256], P(('row', 'col')), may hold values from -6 to 6
Outputs:
- activations: bfloat16 [8192, 256], P(('row', 'col'))
- grad_features: bfloat16 [8192, 256], P(('row', 'col'))
- grad_weight: float32 [256, 256], replicated
The draws below stay inside these ranges and needn't reach their ends.
Inputs may be any that keep to these rules, and one draw needn't show every extreme that they name: `tile_counts`: some device holds exactly 256 live slots in every draw. `tile_rows`: slots may name the same block pair; their values then add.
All inputs are finite; a program needn't handle non-finite values.
Results may differ from the reference program's by a relative error of at most 0.025.
Values may be sent and summed in bfloat16 or wider, within the bound.
No kernel may reach another device: no remote copies, remote signals or barrier semaphores. Data moves between devices by JAX's collectives and lax.ppermute only.
A program may use at most 128 MiB of HBM per device.

```python
import math
import jax
import jax.numpy as jnp
from jax import lax

HIDDEN_SIZE = 256
BLOCK = 128
TILE_CAP = 256
BPD = 2
RBG = 8
CB = 16
NODES = 8192
N_ROW = 8
N_COL = 4


def draw_tile_rows(key, part):
    return jax.random.randint(jax.random.fold_in(key, 101), (N_ROW, N_COL, TILE_CAP), 0, RBG, dtype=jnp.int32)


def draw_tile_cols(key, part):
    return jax.random.randint(jax.random.fold_in(key, 202), (N_ROW, N_COL, TILE_CAP), 0, CB, dtype=jnp.int32)


def draw_tile_counts(key, part):
    first = jax.random.fold_in(key, 303)
    second = jax.random.fold_in(key, 404)
    base = TILE_CAP // 12 + jax.random.randint(first, (N_ROW * N_COL,), 0, TILE_CAP // 2, dtype=jnp.int32)
    heavy = jax.random.randint(second, (3,), 0, N_ROW * N_COL, dtype=jnp.int32)
    base = base.at[heavy].set(TILE_CAP)
    return base.reshape(N_ROW, N_COL)


def block_levels(stream_key, shape, shards, low, largest):
    gain = 1.0
    for dim, shards_of in shards:
        steps = jax.random.uniform(jax.random.fold_in(jax.random.fold_in(stream_key, 6), dim), (shards_of,), jnp.float32, low / len(shards), largest / len(shards))
        gain = gain * jnp.repeat(jnp.exp(steps), shape[dim] // shards_of).reshape((-1,) + (1,) * (len(shape) - 1 - dim))
    return gain


def noise(stream_key, shape, deviation, limit, pieces=(), kind=jnp.bfloat16):
    values = deviation * jax.random.normal(stream_key, shape, jnp.float32)
    if pieces:
        values = values * block_levels(stream_key, shape, pieces, -0.22, 0.18)
    return jnp.clip(values, -limit, limit).astype(kind)


def setup_inputs(seed: int = 0) -> dict:
    key_list = jax.random.split(jax.random.key(seed), 8)
    features = noise(key_list[0], (NODES, HIDDEN_SIZE), 1.0, 6.0, ((0, 32),))
    weight = noise(key_list[1], (HIDDEN_SIZE, HIDDEN_SIZE), HIDDEN_SIZE ** -0.5, 0.375)
    adj_tiles = noise(key_list[2], (N_ROW, N_COL, TILE_CAP, BLOCK, BLOCK), (TILE_CAP * BLOCK // (3 * BPD)) ** -0.5, 0.078125, ((0, 8), (1, 4)))
    tile_rows = draw_tile_rows(jax.random.fold_in(key_list[7], 71), 0)
    tile_cols = draw_tile_cols(jax.random.fold_in(key_list[7], 71), 0)
    tile_counts = draw_tile_counts(jax.random.fold_in(key_list[7], 71), 0)
    out_grad = noise(key_list[6], (NODES, HIDDEN_SIZE), 1.0, 6.0, ((0, 32),))
    return {"features": features, "weight": weight, "adj_tiles": adj_tiles, "tile_rows": tile_rows, "tile_cols": tile_cols, "tile_counts": tile_counts, "out_grad": out_grad}


def reference(features, weight, adj_tiles, tile_rows, tile_cols, tile_counts, out_grad):
    nblocks = NODES // BLOCK
    projected = jnp.dot(features, weight, preferred_element_type=jnp.float32).astype(jnp.bfloat16)
    proj_blocks = projected.reshape(nblocks, BLOCK, HIDDEN_SIZE).astype(jnp.float32)
    cells = N_ROW * N_COL
    tiles_flat = adj_tiles.reshape(cells, TILE_CAP, BLOCK, BLOCK)
    rows_flat = tile_rows.reshape(cells, TILE_CAP)
    cols_flat = tile_cols.reshape(cells, TILE_CAP)
    counts_flat = tile_counts.reshape(cells)
    cell_ids = jnp.arange(cells, dtype=jnp.int32)
    slot_ids = jnp.arange(TILE_CAP, dtype=jnp.int32)
    local_cols = jnp.arange(CB, dtype=jnp.int32)

    def column_map(c_idx, cid):
        return ((cid // BPD * N_COL + c_idx) * BPD + cid % BPD).astype(jnp.int32)

    def rounded(partial_value):
        low = lax.optimization_barrier(partial_value.astype(jnp.bfloat16))
        return low.astype(jnp.float32)

    def forward_cell(total, xs):
        tiles, rid, cid, count, cell = xs
        r_idx = (cell // N_COL).astype(jnp.int32)
        c_idx = (cell % N_COL).astype(jnp.int32)
        gcol = column_map(c_idx, cid)
        live = (slot_ids < count).astype(jnp.float32)
        prod = jnp.einsum('sij,sjf->sif', tiles.astype(jnp.float32), proj_blocks[gcol])
        partial_value = jnp.zeros((RBG, BLOCK, HIDDEN_SIZE), jnp.float32).at[rid].add(prod * live[:, None, None])
        first = (r_idx * RBG).astype(jnp.int32)
        zero = jnp.zeros((), jnp.int32)
        current = lax.dynamic_slice(total, (first, zero, zero), (RBG, BLOCK, HIDDEN_SIZE))
        return (lax.dynamic_update_slice(total, current + rounded(partial_value), (first, zero, zero)), None)
    start = jnp.zeros((nblocks, BLOCK, HIDDEN_SIZE), jnp.float32)
    xs = (tiles_flat, rows_flat, cols_flat, counts_flat, cell_ids)
    pre_blocks, _ = lax.scan(forward_cell, start, xs)
    pre = pre_blocks.reshape(NODES, HIDDEN_SIZE)
    sig = jax.nn.sigmoid(pre)
    activations = (pre * sig).astype(jnp.bfloat16)
    grad_pre = (out_grad.astype(jnp.float32) * sig * (1.0 + pre * (1.0 - sig))).astype(jnp.bfloat16)
    grad_blocks = grad_pre.reshape(nblocks, BLOCK, HIDDEN_SIZE).astype(jnp.float32)

    def backward_cell(total, xs):
        tiles, rid, cid, count, cell = xs
        r_idx = (cell // N_COL).astype(jnp.int32)
        c_idx = (cell % N_COL).astype(jnp.int32)
        grow = (r_idx * RBG + rid).astype(jnp.int32)
        live = (slot_ids < count).astype(jnp.float32)
        prod = jnp.einsum('sji,sjf->sif', tiles.astype(jnp.float32), grad_blocks[grow])
        partial_value = jnp.zeros((CB, BLOCK, HIDDEN_SIZE), jnp.float32).at[cid].add(prod * live[:, None, None])
        return (total.at[column_map(c_idx, local_cols)].add(rounded(partial_value)), None)
    back_blocks, _ = lax.scan(backward_cell, start, xs)
    grad_proj = back_blocks.reshape(NODES, HIDDEN_SIZE).astype(jnp.bfloat16)
    grad_features = lax.dot_general(grad_proj, weight, (((1,), (1,)), ((), ())), preferred_element_type=jnp.float32).astype(jnp.bfloat16)
    grad_weight = lax.dot_general(features, grad_proj, (((0,), (0,)), ((), ())), preferred_element_type=jnp.float32) * (1.0 / math.sqrt(NODES))
    return (activations, grad_features, grad_weight)
```

```python
import functools
import math

import jax
import jax.numpy as jnp
from jax import lax
from jax.experimental import pallas as pl
from jax.experimental.pallas import tpu as pltpu
from jax.sharding import PartitionSpec as P

chunk_tiles = 16
chunk_slots = 4
strips_per_step = 8
strip_slots = 8
vmem_bytes = 56 * 1024 * 1024


def build_kernel(rows_ref, cols_ref, count_ref, tiles_ref, dense_ref, total, held, sems, *, per_strip, strips, steps):
    side = tiles_ref.shape[1]
    first_strip = pl.program_id(0) * strips
    count = count_ref[0]
    chunks = (count + chunk_tiles - 1) // chunk_tiles

    def fetch(index):
        slot = lax.rem(index, chunk_slots)
        return pltpu.make_async_copy(
            tiles_ref.at[pl.ds(index * chunk_tiles, chunk_tiles)], held.at[slot], sems.at[slot]
        )

    for ahead in range(chunk_slots - 1):
        @pl.when(ahead < chunks)
        def _():
            fetch(ahead).start()

    def clear(strip, carry):
        total[strip] = jnp.zeros(total.shape[1:], jnp.float32)
        return carry

    lax.fori_loop(0, strips, clear, 0)

    def chunk_step(index, carry):
        @pl.when(index + chunk_slots - 1 < chunks)
        def _():
            fetch(index + chunk_slots - 1).start()

        fetch(index).wait()
        slot = lax.rem(index, chunk_slots)
        for lane in range(chunk_tiles):
            place = index * chunk_tiles + lane
            col = cols_ref[place]
            strip = col // per_strip - first_strip
            live = place < count
            if steps > 1:
                live = live & (strip >= 0) & (strip < strips)
            strip = jnp.where(live, strip, strips)
            down = pl.ds(pl.multiple_of(rows_ref[place] * side, side), side)
            along = pl.ds(pl.multiple_of(lax.rem(col, per_strip) * side, side), side)
            total[strip, down, along] += held[slot, lane].astype(jnp.float32)
        return carry

    lax.fori_loop(0, chunks, chunk_step, 0)

    def round_strip(strip, carry):
        dense_ref[strip] = total[strip].astype(jnp.bfloat16)
        return carry

    lax.fori_loop(0, strips, round_strip, 0)


def build_dense(rows, cols, count, tiles, row_blocks, col_strips, per_strip):
    capacity, side, _ = tiles.shape
    strips = min(strips_per_step, col_strips)
    steps = col_strips // strips
    high, wide = row_blocks * side, per_strip * side
    return pl.pallas_call(
        functools.partial(build_kernel, per_strip=per_strip, strips=strips, steps=steps),
        out_shape=jax.ShapeDtypeStruct((col_strips, high, wide), jnp.bfloat16),
        grid_spec=pltpu.PrefetchScalarGridSpec(
            num_scalar_prefetch=3,
            grid=(steps,),
            in_specs=[pl.BlockSpec(memory_space=pl.ANY)],
            out_specs=pl.BlockSpec((strips, high, wide), lambda i, *_: (i, 0, 0)),
            scratch_shapes=[
                pltpu.VMEM((strips + 1, high, wide), jnp.float32),
                pltpu.VMEM((chunk_slots, chunk_tiles, side, side), jnp.bfloat16),
                pltpu.SemaphoreType.DMA((chunk_slots,)),
            ],
        ),
        compiler_params=pltpu.CompilerParams(vmem_limit_bytes=vmem_bytes),
        cost_estimate=pl.CostEstimate(
            flops=capacity * side * side,
            bytes_accessed=2 * (capacity * side * side + col_strips * high * wide),
            transcendentals=0,
        ),
        name="build_dense",
    )(rows, cols, count, tiles)


def forward_kernel(source_ref, dense_ref, *refs):
    shards, (out_ref, held, total, sems) = refs[:-4], refs[-4:]
    slots = held.shape[0]

    def fetch(index):
        slot = index % slots
        return pltpu.make_async_copy(dense_ref.at[source_ref[index]], held.at[slot], sems.at[slot])

    for index in range(slots):
        fetch(index).start()
    for index, shard in enumerate(shards):
        fetch(index).wait()
        part = jnp.dot(held[index % slots], shard[...], preferred_element_type=jnp.float32)
        if index + slots < len(shards):
            fetch(index + slots).start()
        if index == 0:
            total[...] = part
        elif index < len(shards) - 1:
            total[...] += part
        else:
            out_ref[...] = (total[...] + part).astype(jnp.bfloat16)


def forward_product(source, dense, shards):
    strips, high, wide = dense.shape
    slots = min(strips, strip_slots)
    width = shards[0].shape[1]
    return pl.pallas_call(
        forward_kernel,
        out_shape=jax.ShapeDtypeStruct((high, width), jnp.bfloat16),
        in_specs=[pl.BlockSpec(memory_space=pltpu.SMEM), pl.BlockSpec(memory_space=pl.ANY)]
        + [pl.BlockSpec(memory_space=pltpu.VMEM)] * len(shards),
        out_specs=pl.BlockSpec(memory_space=pltpu.VMEM),
        scratch_shapes=[
            pltpu.VMEM((slots, high, wide), jnp.bfloat16),
            pltpu.VMEM((high, width), jnp.float32),
            pltpu.SemaphoreType.DMA((slots,)),
        ],
        compiler_params=pltpu.CompilerParams(vmem_limit_bytes=vmem_bytes),
        cost_estimate=pl.CostEstimate(
            flops=2 * strips * high * wide * width,
            bytes_accessed=2 * (strips * high * wide + strips * wide * width + high * width),
            transcendentals=0,
        ),
        name="forward_product",
    )(source, dense, *shards)


def middle_kernel(place_ref, parts_ref, weight_ref, cotangent_ref, act_ref, back_ref, *refs, scale):
    chunk_refs, product = refs[:-1], refs[-1]
    width = weight_ref.shape[0]
    aggregate = parts_ref[0].astype(jnp.float32)
    for index in range(1, parts_ref.shape[0]):
        aggregate += parts_ref[index].astype(jnp.float32)
    high = aggregate.astype(jnp.bfloat16)
    low = (aggregate - high.astype(jnp.float32)).astype(jnp.bfloat16)
    weight = weight_ref[...]
    pre = jnp.dot(high, weight, preferred_element_type=jnp.float32)
    pre += jnp.dot(low, weight, preferred_element_type=jnp.float32)
    sig = jax.nn.sigmoid(pre)
    act_ref[...] = (pre * sig).astype(jnp.bfloat16)
    grad = (cotangent_ref[...].astype(jnp.float32) * sig * (1.0 + pre * (1.0 - sig))).astype(jnp.bfloat16)
    back_ref[...] = lax.dot_general(
        grad, weight, (((1,), (1,)), ((), ())), preferred_element_type=jnp.float32
    ).astype(jnp.bfloat16)
    over_nodes = (((0,), (0,)), ((), ()))
    terms = lax.dot_general(high, grad, over_nodes, preferred_element_type=jnp.float32)
    terms += lax.dot_general(low, grad, over_nodes, preferred_element_type=jnp.float32)
    product[...] = terms * scale
    count = len(chunk_refs)
    rows = width // count
    for index, chunk_ref in enumerate(chunk_refs):
        first = lax.rem(place_ref[0] + index, count) * rows
        chunk_ref[...] = product[pl.ds(pl.multiple_of(first, rows), rows), :]


def middle(place, parts, weight, cotangent, total_nodes):
    count, rows, width = parts.shape
    return pl.pallas_call(
        functools.partial(middle_kernel, scale=1.0 / math.sqrt(total_nodes)),
        out_shape=[
            jax.ShapeDtypeStruct((rows, width), jnp.bfloat16),
            jax.ShapeDtypeStruct((rows, width), jnp.bfloat16),
        ]
        + [jax.ShapeDtypeStruct((width // count, width), jnp.float32)] * count,
        in_specs=[pl.BlockSpec(memory_space=pltpu.SMEM)] + [pl.BlockSpec(memory_space=pltpu.VMEM)] * 3,
        out_specs=[pl.BlockSpec(memory_space=pltpu.VMEM)] * (2 + count),
        scratch_shapes=[pltpu.VMEM((width, width), jnp.float32)],
        compiler_params=pltpu.CompilerParams(vmem_limit_bytes=vmem_bytes),
        cost_estimate=pl.CostEstimate(
            flops=10 * rows * width * width, bytes_accessed=2 * (count + 5) * rows * width, transcendentals=rows * width
        ),
        name="middle",
    )(place, parts, weight, cotangent)


def backward_kernel(dense_ref, grads_ref, out_ref, held, sems):
    strips, slots = dense_ref.shape[0], held.shape[0]

    def fetch(index):
        slot = index % slots
        return pltpu.make_async_copy(dense_ref.at[index], held.at[slot], sems.at[slot])

    for index in range(slots):
        fetch(index).start()
    grads = grads_ref[...].T
    for index in range(strips):
        fetch(index).wait()
        part = jnp.dot(grads, held[index % slots], preferred_element_type=jnp.float32)
        if index + slots < strips:
            fetch(index + slots).start()
        out_ref[index] = part.T.astype(jnp.bfloat16)


def backward_product(dense, grads):
    strips, high, wide = dense.shape
    slots = min(strips, strip_slots)
    width = grads.shape[1]
    return pl.pallas_call(
        backward_kernel,
        out_shape=jax.ShapeDtypeStruct((strips, wide, width), jnp.bfloat16),
        in_specs=[pl.BlockSpec(memory_space=pl.ANY), pl.BlockSpec(memory_space=pltpu.VMEM)],
        out_specs=pl.BlockSpec(memory_space=pltpu.VMEM),
        scratch_shapes=[
            pltpu.VMEM((slots, high, wide), jnp.bfloat16),
            pltpu.SemaphoreType.DMA((slots,)),
        ],
        compiler_params=pltpu.CompilerParams(vmem_limit_bytes=vmem_bytes),
        cost_estimate=pl.CostEstimate(
            flops=2 * strips * high * wide * width,
            bytes_accessed=2 * (strips * high * wide + strips * wide * width + high * width),
            transcendentals=0,
        ),
        name="backward_product",
    )(dense, grads)


def finish_kernel(place_ref, parts_ref, *refs):
    chunk_refs, (features_ref, weight_ref) = refs[:-2], refs[-2:]
    total = parts_ref[0].astype(jnp.float32)
    for index in range(1, parts_ref.shape[0]):
        total += parts_ref[index].astype(jnp.float32)
    features_ref[...] = total.astype(jnp.bfloat16)
    count = len(chunk_refs)
    rows = chunk_refs[0].shape[0]
    for index, chunk_ref in enumerate(chunk_refs):
        first = lax.rem(place_ref[0] + (count - index), count) * rows
        weight_ref[pl.ds(pl.multiple_of(first, rows), rows), :] = chunk_ref[...]


def finish(place, parts, chunks):
    count, rows, width = parts.shape
    return pl.pallas_call(
        finish_kernel,
        out_shape=[
            jax.ShapeDtypeStruct((rows, width), jnp.bfloat16),
            jax.ShapeDtypeStruct((len(chunks) * chunks[0].shape[0], width), jnp.float32),
        ],
        in_specs=[pl.BlockSpec(memory_space=pltpu.SMEM)] + [pl.BlockSpec(memory_space=pltpu.VMEM)] * (1 + len(chunks)),
        out_specs=[pl.BlockSpec(memory_space=pltpu.VMEM)] * 2,
        compiler_params=pltpu.CompilerParams(vmem_limit_bytes=vmem_bytes),
        cost_estimate=pl.CostEstimate(
            flops=count * rows * width, bytes_accessed=2 * (count + 5) * rows * width, transcendentals=0
        ),
        name="finish",
    )(place, parts, *chunks)


def shifted(value, axis, step):
    size = lax.axis_size(axis)
    return lax.ppermute(value, axis, [(i, (i + step) % size) for i in range(size)])


def per_device(features, weight, adj_tiles, tile_rows, tile_cols, tile_counts, out_grad):
    node_rows, width = features.shape
    capacity, side = adj_tiles.shape[2:4]
    tiles = adj_tiles.reshape(capacity, side, side)
    rows = tile_rows.reshape(capacity)
    cols = tile_cols.reshape(capacity)
    count = tile_counts.reshape(1)
    row_count = lax.axis_size("row")
    col_count = lax.axis_size("col")
    per_strip = node_rows // side
    row_place = lax.axis_index("row")
    col_place = lax.axis_index("col").astype(jnp.int32).reshape(1)

    shards = [features] + [shifted(features, "row", step) for step in range(1, row_count)]
    source = lax.rem(row_place + row_count - jnp.arange(row_count, dtype=jnp.int32), row_count)
    dense = build_dense(rows, cols, count, tiles, col_count * per_strip, row_count, per_strip)

    cell = forward_product(source, dense, shards)
    parts = lax.all_to_all(cell, "col", 0, 0, tiled=True).reshape(col_count, node_rows, width)
    activations, back, *terms = middle(col_place, parts, weight, out_grad, node_rows * row_count * col_count)
    grads = lax.all_gather(back, "col", axis=0, tiled=True)

    owned = terms[0]
    for step in range(1, col_count):
        owned = owned + shifted(terms[step], "col", step)
    low = owned.astype(jnp.bfloat16)
    row_terms = jnp.stack([low] + [shifted(low, "row", step) for step in range(1, row_count)])
    ordered = jnp.take(row_terms, lax.rem(row_place + row_count - jnp.arange(row_count), row_count), axis=0)
    owned = jnp.sum(ordered.astype(jnp.float32), axis=0)
    chunks = [owned] + [shifted(owned, "col", step) for step in range(1, col_count)]

    cell_back = backward_product(dense, grads)
    back_parts = lax.all_to_all(cell_back, "row", 0, 0, tiled=True)
    grad_features, grad_weight = finish(col_place, back_parts, chunks)
    return (activations, grad_features, grad_weight)


def solution(mesh):
    placed = (
        P(("row", "col"), None),
        P(),
        P("row", "col", None, None, None),
        P("row", "col", None),
        P("row", "col", None),
        P("row", "col"),
        P(("row", "col"), None),
    )
    return jax.shard_map(
        per_device,
        mesh=mesh,
        in_specs=placed,
        out_specs=(P(("row", "col"), None), P(("row", "col"), None), P()),
        check_vma=False,
    )
```

```python
import functools
import math

import jax
import jax.numpy as jnp
from jax import lax
from jax.experimental import pallas as pl
from jax.experimental.pallas import tpu as pltpu
from jax.sharding import PartitionSpec as P

chunk_tiles = 16
chunk_slots = 4
strips_per_step = 8
part_slots = 4
mib = 1024 * 1024


def scratch_bytes(*shapes):
    return sum(math.prod(shape) * jnp.dtype(kind).itemsize for shape, kind in shapes)


def build_kernel(rows_ref, cols_ref, count_ref, tiles_ref, dense_ref, total, held, sems, *, blocks, steps):
    side = tiles_ref.shape[1]
    first_block = pl.program_id(0) * blocks
    count = count_ref[0]
    chunks = (count + chunk_tiles - 1) // chunk_tiles

    def fetch(index):
        slot = lax.rem(index, chunk_slots)
        return pltpu.make_async_copy(
            tiles_ref.at[pl.ds(index * chunk_tiles, chunk_tiles)], held.at[slot], sems.at[slot]
        )

    for ahead in range(chunk_slots - 1):
        @pl.when(ahead < chunks)
        def _():
            fetch(ahead).start()

    row_blocks = dense_ref.shape[0] // side

    def clear(block, carry):
        down = pl.ds(pl.multiple_of(block * side, side), side)
        total[down, :] = jnp.zeros((side, total.shape[1]), jnp.float32)
        return carry

    lax.fori_loop(0, row_blocks, clear, 0)

    def chunk_step(index, carry):
        @pl.when(index + chunk_slots - 1 < chunks)
        def _():
            fetch(index + chunk_slots - 1).start()

        fetch(index).wait()
        slot = lax.rem(index, chunk_slots)
        for lane in range(chunk_tiles):
            place = index * chunk_tiles + lane
            col = cols_ref[place] - first_block
            live = place < count
            if steps > 1:
                live = live & (col >= 0) & (col < blocks)
                col = jnp.where(live, col, 0)
            row = jnp.where(live, rows_ref[place], row_blocks)
            down = pl.ds(pl.multiple_of(row * side, side), side)
            along = pl.ds(pl.multiple_of(col * side, side), side)
            total[down, along] += held[slot, lane].astype(jnp.float32)
        return carry

    lax.fori_loop(0, chunks, chunk_step, 0)

    def round_block(block, carry):
        down = pl.ds(pl.multiple_of(block * side, side), side)
        dense_ref[down, :] = total[down, :].astype(jnp.bfloat16)
        return carry

    lax.fori_loop(0, row_blocks, round_block, 0)


def build_dense(rows, cols, count, tiles, row_blocks, col_blocks, per_strip):
    capacity, side, _ = tiles.shape
    blocks = min(strips_per_step * per_strip, col_blocks)
    steps = col_blocks // blocks
    high, wide = row_blocks * side, blocks * side
    total = ((high + side, wide), jnp.float32)
    held = ((chunk_slots, chunk_tiles, side, side), jnp.bfloat16)
    block = ((high, wide), jnp.bfloat16)
    return pl.pallas_call(
        functools.partial(build_kernel, blocks=blocks, steps=steps),
        out_shape=jax.ShapeDtypeStruct((high, col_blocks * side), jnp.bfloat16),
        grid_spec=pltpu.PrefetchScalarGridSpec(
            num_scalar_prefetch=3,
            grid=(steps,),
            in_specs=[pl.BlockSpec(memory_space=pl.ANY)],
            out_specs=pl.BlockSpec((high, wide), lambda i, *_: (0, i)),
            scratch_shapes=[
                pltpu.VMEM(*total),
                pltpu.VMEM(*held),
                pltpu.SemaphoreType.DMA((chunk_slots,)),
            ],
        ),
        compiler_params=pltpu.CompilerParams(vmem_limit_bytes=scratch_bytes(total, held, block, block) + 4 * mib),
        cost_estimate=pl.CostEstimate(
            flops=capacity * side * side,
            bytes_accessed=2 * (capacity * side * side + high * col_blocks * side),
            transcendentals=0,
        ),
        name="build_dense",
    )(rows, cols, count, tiles)


def forward_kernel(place_ref, dense_ref, *refs, halves):
    half_refs, refs = refs[:halves], refs[halves:]
    *out_refs, held, depth, sems, depth_sems = refs
    count = len(out_refs)
    rows = held.shape[1]
    slots = held.shape[0]
    wide = depth.shape[1] // halves

    def fetch(order):
        first = lax.rem(place_ref[0] + 1 + order, count) * rows
        slot = order % slots
        return pltpu.make_async_copy(
            dense_ref.at[pl.ds(pl.multiple_of(first, rows), rows)], held.at[slot], sems.at[slot]
        )

    copies = []
    for index, half in enumerate(half_refs):
        copy = pltpu.make_async_copy(half, depth.at[:, pl.ds(index * wide, wide)], depth_sems.at[index])
        copy.start()
        copies.append(copy)
    for order in range(slots):
        fetch(order).start()
    for copy in copies:
        copy.wait()
    for order in range(count):
        fetch(order).wait()
        part = jnp.dot(held[order % slots], depth[...], preferred_element_type=jnp.float32)
        if order + slots < count:
            fetch(order + slots).start()
        out_refs[(order + 1) % count][...] = part.astype(jnp.bfloat16)


def forward_product(place, dense, halves, count):
    high, deep = dense.shape
    width = sum(half.shape[1] for half in halves)
    rows = high // count
    slots = min(count, part_slots)
    held = ((slots, rows, deep), jnp.bfloat16)
    depth = ((deep, width), jnp.bfloat16)
    out = ((high, width), jnp.float32)
    return pl.pallas_call(
        functools.partial(forward_kernel, halves=len(halves)),
        out_shape=[jax.ShapeDtypeStruct((rows, width), jnp.bfloat16)] * count,
        in_specs=[pl.BlockSpec(memory_space=pltpu.SMEM)] + [pl.BlockSpec(memory_space=pl.ANY)] * (1 + len(halves)),
        out_specs=[pl.BlockSpec(memory_space=pltpu.VMEM)] * count,
        scratch_shapes=[
            pltpu.VMEM(*held),
            pltpu.VMEM(*depth),
            pltpu.SemaphoreType.DMA((slots,)),
            pltpu.SemaphoreType.DMA((len(halves),)),
        ],
        compiler_params=pltpu.CompilerParams(vmem_limit_bytes=scratch_bytes(held, depth, out) + 6 * mib),
        cost_estimate=pl.CostEstimate(
            flops=2 * high * deep * width,
            bytes_accessed=2 * (high * deep + deep * width + high * width),
            transcendentals=0,
        ),
        name="forward_product",
    )(place, dense, *halves)


def middle_kernel(*refs, count, scale):
    parts = refs[:count]
    weight_ref, cotangent_ref, act_ref, back_ref, terms_ref = refs[count:]
    aggregate = parts[0][...].astype(jnp.float32)
    for part in parts[1:]:
        aggregate += part[...].astype(jnp.float32)
    high = aggregate.astype(jnp.bfloat16)
    low = (aggregate - high.astype(jnp.float32)).astype(jnp.bfloat16)
    weight = weight_ref[...]
    pre = jnp.dot(high, weight, preferred_element_type=jnp.float32)
    pre += jnp.dot(low, weight, preferred_element_type=jnp.float32)
    sig = jax.nn.sigmoid(pre)
    grad = (cotangent_ref[...].astype(jnp.float32) * sig * (1.0 + pre * (1.0 - sig))).astype(jnp.bfloat16)
    back_ref[...] = lax.dot_general(
        grad, weight, (((1,), (1,)), ((), ())), preferred_element_type=jnp.float32
    ).astype(jnp.bfloat16)
    act_ref[...] = (pre * sig).astype(jnp.bfloat16)
    over_nodes = (((0,), (0,)), ((), ()))
    terms = lax.dot_general(high, grad, over_nodes, preferred_element_type=jnp.float32)
    terms += lax.dot_general(low, grad, over_nodes, preferred_element_type=jnp.float32)
    terms_ref[...] = terms * scale


def middle(parts, weight, cotangent, total_nodes):
    rows, width = cotangent.shape
    count = len(parts)
    return pl.pallas_call(
        functools.partial(middle_kernel, count=count, scale=1.0 / math.sqrt(total_nodes)),
        out_shape=[
            jax.ShapeDtypeStruct((rows, width), jnp.bfloat16),
            jax.ShapeDtypeStruct((rows, width), jnp.bfloat16),
            jax.ShapeDtypeStruct((width, width), jnp.float32),
        ],
        in_specs=[pl.BlockSpec(memory_space=pltpu.VMEM)] * (count + 2),
        out_specs=[pl.BlockSpec(memory_space=pltpu.VMEM)] * 3,
        compiler_params=pltpu.CompilerParams(vmem_limit_bytes=12 * mib),
        cost_estimate=pl.CostEstimate(
            flops=10 * rows * width * width, bytes_accessed=2 * (count + 6) * rows * width, transcendentals=rows * width
        ),
        name="middle",
    )(*parts, weight, cotangent)


def backward_kernel(dense_ref, grads_ref, out_ref, held, results, sems, out_sems):
    strips, wide, _ = out_ref.shape
    slots = held.shape[0]
    per_part = held.shape[2] // wide

    def fetch(part):
        along = pl.ds(part * per_part * wide, per_part * wide)
        slot = part % slots
        return pltpu.make_async_copy(dense_ref.at[:, along], held.at[slot], sems.at[slot])

    def store(part):
        strips_of = pl.ds(part * per_part, per_part)
        return pltpu.make_async_copy(results.at[strips_of], out_ref.at[strips_of], out_sems.at[part])

    parts = strips // per_part
    for part in range(slots):
        fetch(part).start()
    grads = grads_ref[...].T
    for part in range(parts):
        fetch(part).wait()
        for index in range(per_part):
            product = jnp.dot(
                grads, held[part % slots, :, index * wide : (index + 1) * wide], preferred_element_type=jnp.float32
            )
            results[part * per_part + index] = product.astype(jnp.bfloat16).T
        store(part).start()
        if part + slots < parts:
            fetch(part + slots).start()
    for part in range(parts):
        store(part).wait()


def backward_product(dense, grads, strips):
    high, deep = dense.shape
    width = grads.shape[1]
    wide = deep // strips
    per_part = 2 if strips % 2 == 0 else 1
    parts = strips // per_part
    slots = min(parts, part_slots)
    held = ((slots, high, per_part * wide), jnp.bfloat16)
    results = ((strips, wide, width), jnp.bfloat16)
    return pl.pallas_call(
        backward_kernel,
        out_shape=jax.ShapeDtypeStruct((strips, wide, width), jnp.bfloat16),
        in_specs=[pl.BlockSpec(memory_space=pl.ANY), pl.BlockSpec(memory_space=pltpu.VMEM)],
        out_specs=pl.BlockSpec(memory_space=pl.ANY),
        scratch_shapes=[
            pltpu.VMEM(*held),
            pltpu.VMEM(*results),
            pltpu.SemaphoreType.DMA((slots,)),
            pltpu.SemaphoreType.DMA((parts,)),
        ],
        compiler_params=pltpu.CompilerParams(vmem_limit_bytes=scratch_bytes(held, results, results) + 8 * mib),
        cost_estimate=pl.CostEstimate(
            flops=2 * high * deep * width,
            bytes_accessed=2 * (high * deep + deep * width + high * width),
            transcendentals=0,
        ),
        name="backward_product",
    )(dense, grads)


def shifted(value, axis, step):
    size = lax.axis_size(axis)
    return lax.ppermute(value, axis, [(i, (i + step) % size) for i in range(size)])


def summed_everywhere(terms):
    devices = lax.axis_size("row") * lax.axis_size("col")
    height, width = terms.shape
    rows = height // devices
    if rows < 8:
        return lax.psum(terms, ("row", "col"))
    sent = lax.all_to_all(terms.reshape(devices, rows, width), ("row", "col"), 0, 0, tiled=True)
    owned = jnp.sum(sent, axis=0)
    copies = jnp.broadcast_to(owned[None], (devices, rows, width))
    return lax.all_to_all(copies, ("row", "col"), 0, 0, tiled=True).reshape(height, width)


def per_device(features, weight, adj_tiles, tile_rows, tile_cols, tile_counts, out_grad):
    node_rows, width = features.shape
    capacity, side = adj_tiles.shape[2:4]
    tiles = adj_tiles.reshape(capacity, side, side)
    rows = tile_rows.reshape(capacity)
    cols = tile_cols.reshape(capacity)
    count = tile_counts.reshape(1)
    row_count = lax.axis_size("row")
    col_count = lax.axis_size("col")
    per_strip = node_rows // side
    col_place = lax.axis_index("col").astype(jnp.int32).reshape(1)

    half = width // 2
    halves = [lax.all_gather(features[:, at : at + half], "row", axis=0, tiled=True) for at in (0, half)]
    dense = build_dense(rows, cols, count, tiles, col_count * per_strip, row_count * per_strip, per_strip)

    cells = forward_product(col_place, dense, halves, col_count)
    parts = [cells[0]] + [shifted(cells[step], "col", step) for step in range(1, col_count)]
    activations, back, terms = middle(parts, weight, out_grad, node_rows * row_count * col_count)
    grad_weight = summed_everywhere(terms)
    grads = lax.all_gather(back, "col", axis=0, tiled=True)

    cell_back = backward_product(dense, grads, row_count)
    back_parts = lax.all_to_all(cell_back, "row", 0, 0, tiled=True)
    grad_features = jnp.sum(back_parts.astype(jnp.float32), axis=0).astype(jnp.bfloat16)
    return (activations, grad_features, grad_weight)


def solution(mesh):
    placed = (
        P(("row", "col"), None),
        P(),
        P("row", "col", None, None, None),
        P("row", "col", None),
        P("row", "col", None),
        P("row", "col"),
        P(("row", "col"), None),
    )
    return jax.shard_map(
        per_device,
        mesh=mesh,
        in_specs=placed,
        out_specs=(P(("row", "col"), None), P(("row", "col"), None), P()),
        check_vma=False,
    )
```

```python
import functools
import math

import jax
import jax.numpy as jnp
from jax import lax
from jax.experimental import pallas as pl
from jax.experimental.pallas import tpu as pltpu
from jax.sharding import PartitionSpec as P

chunk_tiles = 16
chunk_slots = 4
strips_per_step = 8
mib = 1024 * 1024


def scratch_bytes(*shapes):
    return sum(math.prod(shape) * jnp.dtype(kind).itemsize for shape, kind in shapes)


def build_kernel(rows_ref, cols_ref, count_ref, tiles_ref, dense_ref, total, held, sems, *, blocks, steps):
    side = tiles_ref.shape[1]
    first_block = pl.program_id(0) * blocks
    count = count_ref[0]
    chunks = (count + chunk_tiles - 1) // chunk_tiles

    def fetch(index):
        slot = lax.rem(index, chunk_slots)
        return pltpu.make_async_copy(
            tiles_ref.at[pl.ds(index * chunk_tiles, chunk_tiles)], held.at[slot], sems.at[slot]
        )

    for ahead in range(chunk_slots - 1):
        @pl.when(ahead < chunks)
        def _():
            fetch(ahead).start()

    row_blocks = dense_ref.shape[0] // side

    def clear(block, carry):
        down = pl.ds(pl.multiple_of(block * side, side), side)
        total[down, :] = jnp.zeros((side, total.shape[1]), jnp.float32)
        return carry

    lax.fori_loop(0, row_blocks, clear, 0)

    def chunk_step(index, carry):
        @pl.when(index + chunk_slots - 1 < chunks)
        def _():
            fetch(index + chunk_slots - 1).start()

        fetch(index).wait()
        slot = lax.rem(index, chunk_slots)
        for lane in range(chunk_tiles):
            place = index * chunk_tiles + lane
            col = cols_ref[place] - first_block
            live = place < count
            if steps > 1:
                live = live & (col >= 0) & (col < blocks)
                col = jnp.where(live, col, 0)
            row = jnp.where(live, rows_ref[place], row_blocks)
            down = pl.ds(pl.multiple_of(row * side, side), side)
            along = pl.ds(pl.multiple_of(col * side, side), side)
            total[down, along] += held[slot, lane].astype(jnp.float32)
        return carry

    lax.fori_loop(0, chunks, chunk_step, 0)

    def round_block(block, carry):
        down = pl.ds(pl.multiple_of(block * side, side), side)
        dense_ref[down, :] = total[down, :].astype(jnp.bfloat16)
        return carry

    lax.fori_loop(0, row_blocks, round_block, 0)


def build_dense(rows, cols, count, tiles, row_blocks, col_blocks, per_strip):
    capacity, side, _ = tiles.shape
    blocks = min(strips_per_step * per_strip, col_blocks)
    steps = col_blocks // blocks
    high, wide = row_blocks * side, blocks * side
    total = ((high + side, wide), jnp.float32)
    held = ((chunk_slots, chunk_tiles, side, side), jnp.bfloat16)
    block = ((high, wide), jnp.bfloat16)
    return pl.pallas_call(
        functools.partial(build_kernel, blocks=blocks, steps=steps),
        out_shape=jax.ShapeDtypeStruct((high, col_blocks * side), jnp.bfloat16),
        grid_spec=pltpu.PrefetchScalarGridSpec(
            num_scalar_prefetch=3,
            grid=(steps,),
            in_specs=[pl.BlockSpec(memory_space=pltpu.HBM)],
            out_specs=pl.BlockSpec((high, wide), lambda i, *_: (0, i)),
            scratch_shapes=[
                pltpu.VMEM(*total),
                pltpu.VMEM(*held),
                pltpu.SemaphoreType.DMA((chunk_slots,)),
            ],
        ),
        compiler_params=pltpu.CompilerParams(vmem_limit_bytes=46 * mib),
        cost_estimate=pl.CostEstimate(
            flops=capacity * side * side,
            bytes_accessed=2 * (capacity * side * side + high * col_blocks * side),
            transcendentals=0,
        ),
        name="build_dense",
    )(rows, cols, count, tiles)


def ring_place(row, count):
    return jnp.where(lax.rem(row, 2) == 0, row // 2, count - 1 - row // 2)


def ring_row(place, count):
    place = lax.rem(place + 2 * count, count)
    return jnp.where(place < count // 2, 2 * place, 2 * (count - 1 - place) + 1)


def forward_kernel(row_ref, col_ref, dense_ref, *refs, offsets, partners, row_count):
    piece_refs, refs = refs[: len(offsets)], refs[len(offsets) :]
    out_refs, (depth, sems) = refs[:-2], refs[-2:]
    rows = out_refs[0].shape[0]
    place = ring_place(row_ref[0], row_count)
    copies = []
    for index, (offset, piece) in enumerate(zip(offsets, piece_refs)):
        high = piece.shape[0]
        down = pl.ds(pl.multiple_of(ring_row(place + offset, row_count) * high, high), high)
        copy = pltpu.make_async_copy(piece, depth.at[down], sems.at[index])
        copy.start()
        copies.append(copy)
    for copy in copies:
        copy.wait()
    for partner, out_ref in zip(partners, out_refs):
        down = pl.ds(pl.multiple_of((col_ref[0] ^ partner) * rows, rows), rows)
        part = jnp.dot(dense_ref[down, :], depth[...], preferred_element_type=jnp.float32)
        out_ref[...] = part.astype(jnp.bfloat16)


def forward_product(row_place, col_place, dense, shards, partners, row_count, col_count):
    offsets = tuple(offset for offset, _ in shards)
    arrays = [array for _, array in shards]
    high, deep = dense.shape
    width = arrays[0].shape[1]
    rows = high // col_count
    cell = ((high, deep), jnp.bfloat16)
    depth = ((deep, width), jnp.bfloat16)
    out = ((high, width), jnp.float32)
    return pl.pallas_call(
        functools.partial(forward_kernel, offsets=offsets, partners=partners, row_count=row_count),
        out_shape=[jax.ShapeDtypeStruct((rows, width), jnp.bfloat16)] * len(partners),
        in_specs=[pl.BlockSpec(memory_space=pltpu.SMEM)] * 2
        + [pl.BlockSpec(memory_space=pltpu.VMEM)]
        + [pl.BlockSpec(memory_space=pl.ANY)] * len(arrays),
        out_specs=[pl.BlockSpec(memory_space=pltpu.VMEM)] * len(partners),
        scratch_shapes=[pltpu.VMEM(*depth), pltpu.SemaphoreType.DMA((len(arrays),))],
        compiler_params=pltpu.CompilerParams(vmem_limit_bytes=scratch_bytes(cell, depth, out) + 6 * mib),
        cost_estimate=pl.CostEstimate(
            flops=2 * rows * len(partners) * deep * width,
            bytes_accessed=2 * (rows * len(partners) * deep + deep * width + rows * len(partners) * width),
            transcendentals=0,
        ),
        name="forward_product",
    )(row_place, col_place, dense, *arrays)


def middle_kernel(*refs, count, scale):
    parts = refs[:count]
    weight_ref, cotangent_ref, act_ref, back_ref, terms_ref = refs[count:]
    aggregate = parts[0][...].astype(jnp.float32)
    for part in parts[1:]:
        aggregate += part[...].astype(jnp.float32)
    high = aggregate.astype(jnp.bfloat16)
    low = (aggregate - high.astype(jnp.float32)).astype(jnp.bfloat16)
    weight = weight_ref[...]
    pre = jnp.dot(high, weight, preferred_element_type=jnp.float32)
    pre += jnp.dot(low, weight, preferred_element_type=jnp.float32)
    sig = jax.nn.sigmoid(pre)
    grad = (cotangent_ref[...].astype(jnp.float32) * sig * (1.0 + pre * (1.0 - sig))).astype(jnp.bfloat16)
    back_ref[...] = lax.dot_general(
        weight, grad, (((1,), (1,)), ((), ())), preferred_element_type=jnp.float32
    ).astype(jnp.bfloat16)
    act_ref[...] = (pre * sig).astype(jnp.bfloat16)
    over_nodes = (((0,), (0,)), ((), ()))
    terms = lax.dot_general(high, grad, over_nodes, preferred_element_type=jnp.float32)
    terms += lax.dot_general(low, grad, over_nodes, preferred_element_type=jnp.float32)
    terms_ref[...] = terms * scale


def middle(parts, weight, cotangent, total_nodes):
    rows, width = cotangent.shape
    count = len(parts)
    return pl.pallas_call(
        functools.partial(middle_kernel, count=count, scale=1.0 / math.sqrt(total_nodes)),
        out_shape=[
            jax.ShapeDtypeStruct((rows, width), jnp.bfloat16),
            jax.ShapeDtypeStruct((width, rows), jnp.bfloat16),
            jax.ShapeDtypeStruct((width, width), jnp.float32),
        ],
        in_specs=[pl.BlockSpec(memory_space=pltpu.VMEM)] * (count + 2),
        out_specs=[pl.BlockSpec(memory_space=pltpu.VMEM)] * 3,
        compiler_params=pltpu.CompilerParams(vmem_limit_bytes=12 * mib),
        cost_estimate=pl.CostEstimate(
            flops=10 * rows * width * width, bytes_accessed=2 * (count + 6) * rows * width, transcendentals=rows * width
        ),
        name="middle",
    )(*parts, weight, cotangent)


def backward_kernel(row_ref, col_ref, dense_ref, *refs, count, offsets, row_count):
    grad_refs, refs = refs[:count], refs[count:]
    out_refs, (depth, sems) = refs[:-2], refs[-2:]
    width, rows = grad_refs[0].shape
    wide = dense_ref.shape[1] // row_count
    copies = []
    for partner, grad in enumerate(grad_refs):
        along = pl.ds(pl.multiple_of((col_ref[0] ^ partner) * rows, rows), rows)
        copy = pltpu.make_async_copy(grad, depth.at[:, along], sems.at[partner])
        copy.start()
        copies.append(copy)
    for copy in copies:
        copy.wait()
    place = ring_place(row_ref[0], row_count)
    for index, offset in enumerate(offsets):
        along = pl.ds(pl.multiple_of(ring_row(place + offset, row_count) * wide, wide), wide)
        part = jnp.dot(depth[...], dense_ref[:, along], preferred_element_type=jnp.float32)
        out_refs[index][...] = part.astype(jnp.bfloat16)


def backward_product(row_place, col_place, dense, grads, offsets, row_count):
    high, deep = dense.shape
    width = grads[0].shape[0]
    wide = deep // row_count
    cell = ((high, deep), jnp.bfloat16)
    depth = ((width, high), jnp.bfloat16)
    out = ((len(offsets), width, wide), jnp.float32)
    return pl.pallas_call(
        functools.partial(backward_kernel, count=len(grads), offsets=offsets, row_count=row_count),
        out_shape=[jax.ShapeDtypeStruct((width, wide), jnp.bfloat16)] * len(offsets),
        in_specs=[pl.BlockSpec(memory_space=pltpu.SMEM)] * 2
        + [pl.BlockSpec(memory_space=pltpu.VMEM)]
        + [pl.BlockSpec(memory_space=pl.ANY)] * len(grads),
        out_specs=[pl.BlockSpec(memory_space=pltpu.VMEM)] * len(offsets),
        scratch_shapes=[pltpu.VMEM(*depth), pltpu.SemaphoreType.DMA((len(grads),))],
        compiler_params=pltpu.CompilerParams(vmem_limit_bytes=scratch_bytes(cell, depth, out) + 6 * mib),
        cost_estimate=pl.CostEstimate(
            flops=2 * high * wide * width, bytes_accessed=2 * wide * len(offsets) * width, transcendentals=0
        ),
        name="backward_product",
    )(row_place, col_place, dense, *grads)


def finish_kernel(first_ref, second_ref, third_ref, out_ref):
    total = first_ref[...].astype(jnp.float32) + second_ref[...].astype(jnp.float32) + third_ref[...].astype(jnp.float32)
    out_ref[...] = total.astype(jnp.bfloat16).T


def finish(first, second, third):
    width, rows = first.shape
    return pl.pallas_call(
        finish_kernel,
        out_shape=jax.ShapeDtypeStruct((rows, width), jnp.bfloat16),
        in_specs=[pl.BlockSpec(memory_space=pltpu.VMEM)] * 3,
        out_specs=pl.BlockSpec(memory_space=pltpu.VMEM),
        compiler_params=pltpu.CompilerParams(vmem_limit_bytes=8 * mib),
        cost_estimate=pl.CostEstimate(flops=3 * rows * width, bytes_accessed=8 * rows * width, transcendentals=0),
        name="finish",
    )(first, second, third)


def around(value, step):
    count = lax.axis_size("row")
    order = list(range(0, count, 2)) + list(range(count - 1, 0, -2))
    return lax.ppermute(value, "row", [(order[i], order[(i + step) % count]) for i in range(count)])


def swapped(value, axis, partner):
    return lax.ppermute(value, axis, [(i, i ^ partner) for i in range(lax.axis_size(axis))])


def gathered_shards(own, beside):
    reach = lax.axis_size("row") // 2
    shards = [(0, own)]
    up = down = own
    for step in range(1, reach + 1):
        up = around(up, 1)
        shards.append((-step, up))
        if step < reach:
            down = around(down, -1)
            shards.append((step, down))
        if step == 1:
            up, down, beside = lax.optimization_barrier((up, down, beside))
    return shards, beside


def added(first, second):
    return (first.astype(jnp.float32) + second.astype(jnp.float32)).astype(jnp.bfloat16)


def summed_everywhere(terms):
    place = lax.axis_index("col")
    bits = [1 << bit for bit in range((lax.axis_size("col") - 1).bit_length())]
    for bit in bits:
        half = terms.shape[0] // 2
        upper = (place & bit) != 0
        kept = jnp.where(upper, terms[half:], terms[:half])
        sent = jnp.where(upper, terms[:half], terms[half:])
        terms = kept + swapped(sent, "col", bit)
    for bit in [1 << bit for bit in range((lax.axis_size("row") - 1).bit_length())]:
        terms = terms + swapped(terms, "row", bit)
    for bit in reversed(bits):
        other = swapped(terms, "col", bit)
        upper = (place & bit) != 0
        terms = jnp.concatenate([jnp.where(upper, other, terms), jnp.where(upper, terms, other)])
    return terms


def per_device(features, weight, adj_tiles, tile_rows, tile_cols, tile_counts, out_grad):
    node_rows, width = features.shape
    capacity, side = adj_tiles.shape[2:4]
    tiles = adj_tiles.reshape(capacity, side, side)
    rows = tile_rows.reshape(capacity)
    cols = tile_cols.reshape(capacity)
    count = tile_counts.reshape(1)
    row_count = lax.axis_size("row")
    col_count = lax.axis_size("col")
    per_strip = node_rows // side
    row_place = lax.axis_index("row").astype(jnp.int32).reshape(1)
    col_place = lax.axis_index("col").astype(jnp.int32).reshape(1)

    dense = build_dense(rows, cols, count, tiles, col_count * per_strip, row_count * per_strip, per_strip)
    shards, dense = gathered_shards(features, dense)

    far = tuple(range(col_count // 2, col_count))
    near = tuple(range(col_count // 2))
    sent = forward_product(row_place, col_place, dense, shards, far, row_count, col_count)
    parts = [swapped(part, "col", partner) for partner, part in zip(far, sent)]
    own, *sent = forward_product(row_place, col_place, dense, shards, near, row_count, col_count)
    parts += [own] + [swapped(part, "col", partner) for partner, part in zip(near[1:], sent)]

    activations, back, terms = middle(parts, weight, out_grad, node_rows * row_count * col_count)
    grads = [back] + [swapped(back, "col", partner) for partner in range(1, col_count)]
    grad_weight = summed_everywhere(terms)

    reach = row_count // 2
    (opposite,) = backward_product(row_place, col_place, dense, grads, (reach,), row_count)
    opposite, cell = lax.optimization_barrier((opposite, dense))
    up, down = around(opposite, 1), None
    offsets = tuple(sign * step for step in range(reach - 1, 0, -1) for sign in (1, -1)) + (0,)
    *strips, own = backward_product(row_place, col_place, cell, grads, offsets, row_count)
    for step in range(reach - 1):
        above, below = strips[2 * step : 2 * step + 2]
        up = around(added(above, up), 1)
        down = around(below if down is None else added(below, down), -1)
    grad_features = finish(own, up, down)
    return (activations, grad_features, grad_weight)


def solution(mesh):
    placed = (
        P(("row", "col"), None),
        P(),
        P("row", "col", None, None, None),
        P("row", "col", None),
        P("row", "col", None),
        P("row", "col"),
        P(("row", "col"), None),
    )
    return jax.shard_map(
        per_device,
        mesh=mesh,
        in_specs=placed,
        out_specs=(P(("row", "col"), None), P(("row", "col"), None), P()),
        check_vma=False,
    )
```

```python
import functools
import math

import jax
import jax.numpy as jnp
from jax import lax
from jax.experimental import pallas as pl
from jax.experimental.pallas import tpu as pltpu
from jax.sharding import PartitionSpec as P

chunk_tiles = 16
chunk_slots = 4
strips_per_step = 8
mib = 1024 * 1024


def scratch_bytes(*shapes):
    return sum(math.prod(shape) * jnp.dtype(kind).itemsize for shape, kind in shapes)


def build_kernel(rows_ref, cols_ref, count_ref, tiles_ref, dense_ref, total, held, sems, *, blocks, steps):
    side = tiles_ref.shape[1]
    first_block = pl.program_id(0) * blocks
    count = count_ref[0]
    chunks = (count + chunk_tiles - 1) // chunk_tiles

    def fetch(index):
        slot = lax.rem(index, chunk_slots)
        return pltpu.make_async_copy(
            tiles_ref.at[pl.ds(index * chunk_tiles, chunk_tiles)], held.at[slot], sems.at[slot]
        )

    for ahead in range(chunk_slots - 1):
        @pl.when(ahead < chunks)
        def _():
            fetch(ahead).start()

    row_blocks = dense_ref.shape[0] // side

    def clear(block, carry):
        down = pl.ds(pl.multiple_of(block * side, side), side)
        total[down, :] = jnp.zeros((side, total.shape[1]), jnp.float32)
        return carry

    lax.fori_loop(0, row_blocks, clear, 0)

    def chunk_step(index, carry):
        @pl.when(index + chunk_slots - 1 < chunks)
        def _():
            fetch(index + chunk_slots - 1).start()

        fetch(index).wait()
        slot = lax.rem(index, chunk_slots)
        for lane in range(chunk_tiles):
            place = index * chunk_tiles + lane
            col = cols_ref[place] - first_block
            live = place < count
            if steps > 1:
                live = live & (col >= 0) & (col < blocks)
                col = jnp.where(live, col, 0)
            row = jnp.where(live, rows_ref[place], row_blocks)
            down = pl.ds(pl.multiple_of(row * side, side), side)
            along = pl.ds(pl.multiple_of(col * side, side), side)
            total[down, along] += held[slot, lane].astype(jnp.float32)
        return carry

    lax.fori_loop(0, chunks, chunk_step, 0)

    def round_block(block, carry):
        down = pl.ds(pl.multiple_of(block * side, side), side)
        dense_ref[down, :] = total[down, :].astype(jnp.bfloat16)
        return carry

    lax.fori_loop(0, row_blocks, round_block, 0)


def build_dense(rows, cols, count, tiles, row_blocks, col_blocks, per_strip):
    capacity, side, _ = tiles.shape
    blocks = min(strips_per_step * per_strip, col_blocks)
    steps = col_blocks // blocks
    high, wide = row_blocks * side, blocks * side
    total = ((high + side, wide), jnp.float32)
    held = ((chunk_slots, chunk_tiles, side, side), jnp.bfloat16)
    block = ((high, wide), jnp.bfloat16)
    return pl.pallas_call(
        functools.partial(build_kernel, blocks=blocks, steps=steps),
        out_shape=jax.ShapeDtypeStruct((high, col_blocks * side), jnp.bfloat16),
        grid_spec=pltpu.PrefetchScalarGridSpec(
            num_scalar_prefetch=3,
            grid=(steps,),
            in_specs=[pl.BlockSpec(memory_space=pltpu.HBM)],
            out_specs=pl.BlockSpec((high, wide), lambda i, *_: (0, i)),
            scratch_shapes=[
                pltpu.VMEM(*total),
                pltpu.VMEM(*held),
                pltpu.SemaphoreType.DMA((chunk_slots,)),
            ],
        ),
        compiler_params=pltpu.CompilerParams(vmem_limit_bytes=46 * mib),
        cost_estimate=pl.CostEstimate(
            flops=capacity * side * side,
            bytes_accessed=2 * (capacity * side * side + high * col_blocks * side),
            transcendentals=0,
        ),
        name="build_dense",
    )(rows, cols, count, tiles)


def ring_place(row, count):
    return jnp.where(lax.rem(row, 2) == 0, row // 2, count - 1 - row // 2)


def ring_row(place, count):
    place = lax.rem(place + 2 * count, count)
    return jnp.where(place < count // 2, 2 * place, 2 * (count - 1 - place) + 1)


def forward_kernel(dense_ref, *refs, offsets, partners, row_count):
    piece_refs, out_refs = refs[: len(offsets)], refs[len(offsets) :]
    rows = out_refs[0].shape[0]
    place = ring_place(lax.axis_index("row"), row_count)
    col = lax.axis_index("col")
    starts = []
    for offset, piece in zip(offsets, piece_refs):
        high = piece.shape[0]
        starts.append(pl.multiple_of(ring_row(place + offset, row_count) * high, high))
    for partner, out_ref in zip(partners, out_refs):
        down = pl.ds(pl.multiple_of((col ^ partner) * rows, rows), rows)
        total = None
        for start, piece in zip(starts, piece_refs):
            part = jnp.dot(
                dense_ref[down, pl.ds(start, piece.shape[0])], piece[...], preferred_element_type=jnp.float32
            )
            total = part if total is None else total + part
        out_ref[...] = total.astype(jnp.bfloat16)


def forward_product(dense, shards, partners, row_count, col_count):
    offsets = tuple(offset for offset, _ in shards)
    arrays = [array for _, array in shards]
    high, deep = dense.shape
    width = arrays[0].shape[1]
    rows = high // col_count
    cell = ((high, deep), jnp.bfloat16)
    depth = ((deep, width), jnp.bfloat16)
    out = ((high, width), jnp.float32)
    return pl.pallas_call(
        functools.partial(forward_kernel, offsets=offsets, partners=partners, row_count=row_count),
        out_shape=[jax.ShapeDtypeStruct((rows, width), jnp.bfloat16)] * len(partners),
        in_specs=[pl.BlockSpec(memory_space=pltpu.VMEM)] * (1 + len(arrays)),
        out_specs=[pl.BlockSpec(memory_space=pltpu.VMEM)] * len(partners),
        compiler_params=pltpu.CompilerParams(vmem_limit_bytes=scratch_bytes(cell, depth, out) + 6 * mib),
        cost_estimate=pl.CostEstimate(
            flops=2 * rows * len(partners) * deep * width,
            bytes_accessed=2 * (rows * len(partners) * deep + deep * width + rows * len(partners) * width),
            transcendentals=0,
        ),
        name="forward_product",
    )(dense, *arrays)


def middle_kernel(*refs, count, scale):
    parts = refs[:count]
    weight_ref, cotangent_ref, act_ref, back_ref, *chunk_refs, product = refs[count:]
    aggregate = parts[0][...].astype(jnp.float32)
    for part in parts[1:]:
        aggregate += part[...].astype(jnp.float32)
    high = aggregate.astype(jnp.bfloat16)
    low = (aggregate - high.astype(jnp.float32)).astype(jnp.bfloat16)
    weight = weight_ref[...]
    pre = jnp.dot(high, weight, preferred_element_type=jnp.float32)
    pre += jnp.dot(low, weight, preferred_element_type=jnp.float32)
    sig = jax.nn.sigmoid(pre)
    grad = (cotangent_ref[...].astype(jnp.float32) * sig * (1.0 + pre * (1.0 - sig))).astype(jnp.bfloat16)
    back_ref[...] = lax.dot_general(
        weight, grad, (((1,), (1,)), ((), ())), preferred_element_type=jnp.float32
    ).astype(jnp.bfloat16)
    act_ref[...] = (pre * sig).astype(jnp.bfloat16)
    over_nodes = (((0,), (0,)), ((), ()))
    terms = lax.dot_general(high, grad, over_nodes, preferred_element_type=jnp.float32)
    terms += lax.dot_general(low, grad, over_nodes, preferred_element_type=jnp.float32)
    product[...] = terms * scale
    rows = product.shape[0] // count
    col = lax.axis_index("col")
    for partner, chunk_ref in enumerate(chunk_refs):
        chunk_ref[...] = product[pl.ds(pl.multiple_of((col ^ partner) * rows, rows), rows), :]


def middle(parts, weight, cotangent, total_nodes):
    rows, width = cotangent.shape
    count = len(parts)
    return pl.pallas_call(
        functools.partial(middle_kernel, count=count, scale=1.0 / math.sqrt(total_nodes)),
        out_shape=[
            jax.ShapeDtypeStruct((rows, width), jnp.bfloat16),
            jax.ShapeDtypeStruct((width, rows), jnp.bfloat16),
        ]
        + [jax.ShapeDtypeStruct((width // count, width), jnp.float32)] * count,
        in_specs=[pl.BlockSpec(memory_space=pltpu.VMEM)] * (count + 2),
        out_specs=[pl.BlockSpec(memory_space=pltpu.VMEM)] * (2 + count),
        scratch_shapes=[pltpu.VMEM((width, width), jnp.float32)],
        compiler_params=pltpu.CompilerParams(vmem_limit_bytes=12 * mib),
        cost_estimate=pl.CostEstimate(
            flops=10 * rows * width * width, bytes_accessed=2 * (count + 6) * rows * width, transcendentals=rows * width
        ),
        name="middle",
    )(*parts, weight, cotangent)


def backward_kernel(dense_ref, *refs, count, offsets, row_count):
    grad_refs, refs = refs[:count], refs[count:]
    out_refs, (depth, sems) = refs[:-2], refs[-2:]
    width, rows = grad_refs[0].shape
    wide = dense_ref.shape[1] // row_count
    col = lax.axis_index("col")
    copies = []
    for partner, grad in enumerate(grad_refs):
        along = pl.ds(pl.multiple_of((col ^ partner) * rows, rows), rows)
        copy = pltpu.make_async_copy(grad, depth.at[:, along], sems.at[partner])
        copy.start()
        copies.append(copy)
    for copy in copies:
        copy.wait()
    place = ring_place(lax.axis_index("row"), row_count)
    for index, offset in enumerate(offsets):
        along = pl.ds(pl.multiple_of(ring_row(place + offset, row_count) * wide, wide), wide)
        part = jnp.dot(depth[...], dense_ref[:, along], preferred_element_type=jnp.float32)
        out_refs[index][...] = part.astype(jnp.bfloat16)


def backward_product(dense, grads, offsets, row_count):
    high, deep = dense.shape
    width = grads[0].shape[0]
    wide = deep // row_count
    cell = ((high, deep), jnp.bfloat16)
    depth = ((width, high), jnp.bfloat16)
    out = ((len(offsets), width, wide), jnp.float32)
    return pl.pallas_call(
        functools.partial(backward_kernel, count=len(grads), offsets=offsets, row_count=row_count),
        out_shape=[jax.ShapeDtypeStruct((width, wide), jnp.bfloat16)] * len(offsets),
        in_specs=[pl.BlockSpec(memory_space=pltpu.VMEM)] + [pl.BlockSpec(memory_space=pl.ANY)] * len(grads),
        out_specs=[pl.BlockSpec(memory_space=pltpu.VMEM)] * len(offsets),
        scratch_shapes=[pltpu.VMEM(*depth), pltpu.SemaphoreType.DMA((len(grads),))],
        compiler_params=pltpu.CompilerParams(vmem_limit_bytes=scratch_bytes(cell, depth, out) + 6 * mib),
        cost_estimate=pl.CostEstimate(
            flops=2 * high * wide * width, bytes_accessed=2 * wide * len(offsets) * width, transcendentals=0
        ),
        name="backward_product",
    )(dense, *grads)


def finish_kernel(first_ref, second_ref, third_ref, *refs):
    chunk_refs, (features_ref, weight_ref) = refs[:-2], refs[-2:]
    total = first_ref[...].astype(jnp.float32) + second_ref[...].astype(jnp.float32) + third_ref[...].astype(jnp.float32)
    features_ref[...] = total.astype(jnp.bfloat16).T
    rows = chunk_refs[0].shape[0]
    col = lax.axis_index("col")
    for partner, chunk_ref in enumerate(chunk_refs):
        weight_ref[pl.ds(pl.multiple_of((col ^ partner) * rows, rows), rows), :] = chunk_ref[...]


def finish(first, second, third, chunks):
    width, rows = first.shape
    return pl.pallas_call(
        finish_kernel,
        out_shape=[
            jax.ShapeDtypeStruct((rows, width), jnp.bfloat16),
            jax.ShapeDtypeStruct((width, width), jnp.float32),
        ],
        in_specs=[pl.BlockSpec(memory_space=pltpu.VMEM)] * (3 + len(chunks)),
        out_specs=[pl.BlockSpec(memory_space=pltpu.VMEM)] * 2,
        compiler_params=pltpu.CompilerParams(vmem_limit_bytes=8 * mib),
        cost_estimate=pl.CostEstimate(flops=3 * rows * width, bytes_accessed=16 * rows * width, transcendentals=0),
        name="finish",
    )(first, second, third, *chunks)


def around(value, step):
    count = lax.axis_size("row")
    order = list(range(0, count, 2)) + list(range(count - 1, 0, -2))
    return lax.ppermute(value, "row", [(order[i], order[(i + step) % count]) for i in range(count)])


def swapped(value, axis, partner):
    return lax.ppermute(value, axis, [(i, i ^ partner) for i in range(lax.axis_size(axis))])


def gathered_shards(own, beside):
    reach = lax.axis_size("row") // 2
    shards = [(0, own)]
    up = down = own
    for step in range(1, reach + 1):
        up = around(up, 1)
        shards.append((-step, up))
        if step < reach:
            down = around(down, -1)
            shards.append((step, down))
        if step == 1:
            up, down, beside = lax.optimization_barrier((up, down, beside))
    return shards, beside


def added(first, second):
    return (first.astype(jnp.float32) + second.astype(jnp.float32)).astype(jnp.bfloat16)


def partners_sum(values):
    while len(values) > 1:
        values = [values[i] + values[i + 1] for i in range(0, len(values), 2)]
    return values[0]


def per_device(features, weight, adj_tiles, tile_rows, tile_cols, tile_counts, out_grad):
    node_rows, width = features.shape
    capacity, side = adj_tiles.shape[2:4]
    tiles = adj_tiles.reshape(capacity, side, side)
    rows = tile_rows.reshape(capacity)
    cols = tile_cols.reshape(capacity)
    count = tile_counts.reshape(1)
    row_count = lax.axis_size("row")
    col_count = lax.axis_size("col")
    per_strip = node_rows // side
    dense = build_dense(rows, cols, count, tiles, col_count * per_strip, row_count * per_strip, per_strip)
    shards, dense = gathered_shards(features, dense)

    far = tuple(range(col_count // 2, col_count))
    near = tuple(range(col_count // 2))
    sent = forward_product(dense, shards, far, row_count, col_count)
    parts = [swapped(part, "col", partner) for partner, part in zip(far, sent)]
    own, *sent = forward_product(dense, shards, near, row_count, col_count)
    parts += [own] + [swapped(part, "col", partner) for partner, part in zip(near[1:], sent)]

    activations, back, *terms = middle(parts, weight, out_grad, node_rows * row_count * col_count)
    grads = [back] + [swapped(back, "col", partner) for partner in range(1, col_count)]
    terms = terms[:1] + [swapped(terms[partner], "col", partner) for partner in range(1, col_count)]
    grads, terms = lax.optimization_barrier((grads, terms))

    reach = row_count // 2
    chunk = partners_sum(terms)
    doublings = [1 << bit for bit in range((row_count - 1).bit_length())]
    chunks = None
    (opposite,) = backward_product(dense, grads, (reach,), row_count)
    opposite, cell = lax.optimization_barrier((opposite, dense))
    up, down = around(opposite, 1), None
    offsets = tuple(sign * step for step in range(reach - 1, 0, -1) for sign in (1, -1)) + (0,)
    *strips, own = backward_product(cell, grads, offsets, row_count)
    for step in range(reach):
        if doublings:
            other = swapped(chunk, "row", doublings.pop(0))
        elif chunks is None:
            chunks = [chunk] + [swapped(chunk, "col", partner) for partner in range(1, col_count)]
        if step == 0:
            up, other = lax.optimization_barrier((up, other))
        elif chunks is None:
            up, down, other = lax.optimization_barrier((up, down, other))
        if chunks is None:
            chunk = chunk + other
        if step < reach - 1:
            above, below = strips[2 * step : 2 * step + 2]
            up = around(added(above, up), 1)
            down = around(below if down is None else added(below, down), -1)
    while doublings:
        chunk = chunk + swapped(chunk, "row", doublings.pop(0))
    if chunks is None:
        chunks = [chunk] + [swapped(chunk, "col", partner) for partner in range(1, col_count)]
    grad_features, grad_weight = finish(own, up, down, chunks)
    return (activations, grad_features, grad_weight)


def solution(mesh):
    placed = (
        P(("row", "col"), None),
        P(),
        P("row", "col", None, None, None),
        P("row", "col", None),
        P("row", "col", None),
        P("row", "col"),
        P(("row", "col"), None),
    )
    return jax.shard_map(
        per_device,
        mesh=mesh,
        in_specs=placed,
        out_specs=(P(("row", "col"), None), P(("row", "col"), None), P()),
        check_vma=False,
    )
```

```python
import functools
import math

import jax
import jax.numpy as jnp
from jax import lax
from jax.experimental import pallas as pl
from jax.experimental.pallas import tpu as pltpu
from jax.sharding import PartitionSpec as P

chunk_tiles = 16
chunk_slots = 4
strips_per_step = 8
mib = 1024 * 1024


def scratch_bytes(*shapes):
    return sum(math.prod(shape) * jnp.dtype(kind).itemsize for shape, kind in shapes)


def build_kernel(rows_ref, cols_ref, count_ref, tiles_ref, dense_ref, total, held, sems, *, blocks, steps):
    side = tiles_ref.shape[1]
    first_block = pl.program_id(0) * blocks
    count = count_ref[0]
    chunks = (count + chunk_tiles - 1) // chunk_tiles

    def fetch(index):
        slot = lax.rem(index, chunk_slots)
        return pltpu.make_async_copy(
            tiles_ref.at[pl.ds(index * chunk_tiles, chunk_tiles)], held.at[slot], sems.at[slot]
        )

    for ahead in range(chunk_slots - 1):
        @pl.when(ahead < chunks)
        def _():
            fetch(ahead).start()

    row_blocks = dense_ref.shape[0] // side

    def clear(block, carry):
        down = pl.ds(pl.multiple_of(block * side, side), side)
        total[down, :] = jnp.zeros((side, total.shape[1]), jnp.float32)
        return carry

    lax.fori_loop(0, row_blocks, clear, 0)

    def chunk_step(index, carry):
        @pl.when(index + chunk_slots - 1 < chunks)
        def _():
            fetch(index + chunk_slots - 1).start()

        fetch(index).wait()
        slot = lax.rem(index, chunk_slots)
        for lane in range(chunk_tiles):
            place = index * chunk_tiles + lane
            col = cols_ref[place] - first_block
            live = place < count
            if steps > 1:
                live = live & (col >= 0) & (col < blocks)
                col = jnp.where(live, col, 0)
            row = jnp.where(live, rows_ref[place], row_blocks)
            down = pl.ds(pl.multiple_of(row * side, side), side)
            along = pl.ds(pl.multiple_of(col * side, side), side)
            total[down, along] += held[slot, lane].astype(jnp.float32)
        return carry

    lax.fori_loop(0, chunks, chunk_step, 0)

    def round_block(block, carry):
        down = pl.ds(pl.multiple_of(block * side, side), side)
        dense_ref[down, :] = total[down, :].astype(jnp.bfloat16)
        return carry

    lax.fori_loop(0, row_blocks, round_block, 0)


def build_dense(rows, cols, count, tiles, row_blocks, col_blocks, per_strip):
    capacity, side, _ = tiles.shape
    blocks = min(strips_per_step * per_strip, col_blocks)
    steps = col_blocks // blocks
    high, wide = row_blocks * side, blocks * side
    total = ((high + side, wide), jnp.float32)
    held = ((chunk_slots, chunk_tiles, side, side), jnp.bfloat16)
    block = ((high, wide), jnp.bfloat16)
    return pl.pallas_call(
        functools.partial(build_kernel, blocks=blocks, steps=steps),
        out_shape=jax.ShapeDtypeStruct((high, col_blocks * side), jnp.bfloat16),
        grid_spec=pltpu.PrefetchScalarGridSpec(
            num_scalar_prefetch=3,
            grid=(steps,),
            in_specs=[pl.BlockSpec(memory_space=pltpu.HBM)],
            out_specs=pl.BlockSpec((high, wide), lambda i, *_: (0, i)),
            scratch_shapes=[
                pltpu.VMEM(*total),
                pltpu.VMEM(*held),
                pltpu.SemaphoreType.DMA((chunk_slots,)),
            ],
        ),
        compiler_params=pltpu.CompilerParams(vmem_limit_bytes=46 * mib),
        cost_estimate=pl.CostEstimate(
            flops=capacity * side * side,
            bytes_accessed=2 * (capacity * side * side + high * col_blocks * side),
            transcendentals=0,
        ),
        name="build_dense",
    )(rows, cols, count, tiles)


def ring_place(row, count):
    return jnp.where(lax.rem(row, 2) == 0, row // 2, count - 1 - row // 2)


def ring_row(place, count):
    place = lax.rem(place + 2 * count, count)
    return jnp.where(place < count // 2, 2 * place, 2 * (count - 1 - place) + 1)


def forward_kernel(dense_ref, *refs, pieces, sibling, row_count):
    piece_refs, out_ref = refs[: len(pieces)], refs[len(pieces)]
    count = lax.axis_size("col")
    rows = dense_ref.shape[0] // count
    block = dense_ref.shape[1] // row_count
    place = ring_place(lax.axis_index("row"), row_count)
    col = lax.axis_index("col") ^ sibling
    operands = []
    for piece, ref in zip(pieces, piece_refs):
        for offset, first, start, high in piece:
            along = pl.ds(pl.multiple_of(ring_row(place + offset, row_count) * block + first, 128), high)
            operands.append((along, ref, pl.ds(start, high)))
    for index in range(count // 2):
        down = pl.ds(pl.multiple_of((col ^ (2 * index)) * rows, rows), rows)
        total = None
        for along, ref, part in operands:
            product = jnp.dot(dense_ref[down, along], ref[part, :], preferred_element_type=jnp.float32)
            total = product if total is None else total + product
        out_ref[pl.ds(index * rows, rows), :] = total.astype(jnp.bfloat16)


def forward_product(dense, shards, sibling, row_count, col_count):
    pieces = tuple(piece for piece, _ in shards)
    arrays = [array for _, array in shards]
    high, deep = dense.shape
    width = arrays[0].shape[1]
    half = high // 2
    cell = ((high, deep), jnp.bfloat16)
    depth = ((deep, width), jnp.bfloat16)
    out = ((high, width), jnp.float32)
    return pl.pallas_call(
        functools.partial(forward_kernel, pieces=pieces, sibling=sibling, row_count=row_count),
        out_shape=jax.ShapeDtypeStruct((half, width), jnp.bfloat16),
        in_specs=[pl.BlockSpec(memory_space=pltpu.VMEM)] * (1 + len(arrays)),
        out_specs=pl.BlockSpec(memory_space=pltpu.VMEM),
        compiler_params=pltpu.CompilerParams(vmem_limit_bytes=scratch_bytes(cell, depth, out) + 6 * mib),
        cost_estimate=pl.CostEstimate(
            flops=2 * half * deep * width,
            bytes_accessed=2 * (half * deep + deep * width + half * width),
            transcendentals=0,
        ),
        name="forward_product",
    )(dense, *arrays)


def middle_kernel(*refs, blocks, scale):
    sums, refs = refs[:blocks], refs[blocks:]
    weight_ref, refs = refs[0], refs[1:]
    cotangent_refs, (act_ref, message_ref, chunk_ref, sent_ref, product) = refs[:blocks], refs[blocks:]
    weight = weight_ref[...]
    rows, width = act_ref.shape
    over_nodes = (((0,), (0,)), ((), ()))
    terms = None
    for index in range(blocks):
        aggregate = sums[0][pl.ds(index * rows, rows), :].astype(jnp.float32)
        for other in range(1, blocks):
            aggregate += sums[other][pl.ds((index ^ other) * rows, rows), :].astype(jnp.float32)
        high = aggregate.astype(jnp.bfloat16)
        low = (aggregate - high.astype(jnp.float32)).astype(jnp.bfloat16)
        pre = jnp.dot(high, weight, preferred_element_type=jnp.float32)
        pre += jnp.dot(low, weight, preferred_element_type=jnp.float32)
        sig = jax.nn.sigmoid(pre)
        cotangent = cotangent_refs[index][...].astype(jnp.float32)
        grad = (cotangent * sig * (1.0 + pre * (1.0 - sig))).astype(jnp.bfloat16)
        message_ref[pl.ds(index * width, width), :] = lax.dot_general(
            weight, grad, (((1,), (1,)), ((), ())), preferred_element_type=jnp.float32
        ).astype(jnp.bfloat16)
        if index == 0:
            act_ref[...] = (pre * sig).astype(jnp.bfloat16)
        part = lax.dot_general(high, grad, over_nodes, preferred_element_type=jnp.float32)
        part += lax.dot_general(low, grad, over_nodes, preferred_element_type=jnp.float32)
        terms = part if terms is None else terms + part
    product[...] = terms * scale
    col = lax.axis_index("col")
    size = chunk_ref.shape[0]
    chunk_ref[...] = product[pl.ds(pl.multiple_of(col * size, size), size), :]
    sent = product[pl.ds(pl.multiple_of((col ^ 1) * size, size), size), :]
    high = sent.astype(jnp.bfloat16)
    low = (sent - high.astype(jnp.float32)).astype(jnp.bfloat16)
    message_ref[pl.ds(blocks * width, size), :] = high
    message_ref[pl.ds(blocks * width + size, size), :] = low
    sent_ref[...] = high.astype(jnp.float32) + low.astype(jnp.float32)


def middle(sums, weight, cotangents, total_nodes):
    rows, width = cotangents[0].shape
    blocks = len(cotangents)
    size = width // (2 * blocks)
    return pl.pallas_call(
        functools.partial(middle_kernel, blocks=blocks, scale=1.0 / math.sqrt(total_nodes)),
        out_shape=[
            jax.ShapeDtypeStruct((rows, width), jnp.bfloat16),
            jax.ShapeDtypeStruct((blocks * width + 2 * size, rows), jnp.bfloat16),
            jax.ShapeDtypeStruct((size, width), jnp.float32),
            jax.ShapeDtypeStruct((size, width), jnp.float32),
        ],
        in_specs=[pl.BlockSpec(memory_space=pltpu.VMEM)] * (2 * blocks + 1),
        out_specs=[pl.BlockSpec(memory_space=pltpu.VMEM)] * 4,
        scratch_shapes=[pltpu.VMEM((width, width), jnp.float32)],
        compiler_params=pltpu.CompilerParams(vmem_limit_bytes=12 * mib),
        cost_estimate=pl.CostEstimate(
            flops=10 * blocks * rows * width * width,
            bytes_accessed=2 * (blocks * blocks + 2 * blocks + 4) * rows * width,
            transcendentals=blocks * rows * width,
        ),
        name="middle",
    )(*sums, weight, *cotangents)


def backward_kernel(dense_ref, own_ref, sibling_ref, *refs, outputs, row_count):
    out_refs, (depth, sems) = refs[:-2], refs[-2:]
    count = lax.axis_size("col")
    width, rows = depth.shape[0], own_ref.shape[1]
    wide = dense_ref.shape[1] // row_count
    col = lax.axis_index("col")
    copies = []
    for index in range(count):
        block = pl.ds(index // 2 * width, width)
        along = pl.ds(pl.multiple_of((col ^ index) * rows, rows), rows)
        source = sibling_ref if index % 2 else own_ref
        copy = pltpu.make_async_copy(source.at[block], depth.at[:, along], sems.at[index])
        copy.start()
        copies.append(copy)
    for copy in copies:
        copy.wait()
    place = ring_place(lax.axis_index("row"), row_count)
    for offset in sorted({offset for output in outputs for offset, _, _ in output}):
        along = pl.ds(pl.multiple_of(ring_row(place + offset, row_count) * wide, wide), wide)
        part = jnp.dot(depth[...], dense_ref[:, along], preferred_element_type=jnp.float32).astype(jnp.bfloat16)
        for output, out_ref in zip(outputs, out_refs):
            start = 0
            for other, first, high in output:
                if other == offset:
                    out_ref[start : start + high, :] = part[first : first + high, :]
                start += high


def backward_product(dense, own, sibling, width, outputs, row_count, col_count):
    high, deep = dense.shape
    wide = deep // row_count
    offsets = {offset for output in outputs for offset, _, _ in output}
    cell = ((high, deep), jnp.bfloat16)
    depth = ((width, high), jnp.bfloat16)
    out = ((len(offsets), width, wide), jnp.float32)
    return pl.pallas_call(
        functools.partial(backward_kernel, outputs=outputs, row_count=row_count),
        out_shape=[
            jax.ShapeDtypeStruct((sum(rows for _, _, rows in output), wide), jnp.bfloat16) for output in outputs
        ],
        in_specs=[pl.BlockSpec(memory_space=pltpu.VMEM)] + [pl.BlockSpec(memory_space=pl.ANY)] * 2,
        out_specs=[pl.BlockSpec(memory_space=pltpu.VMEM)] * len(outputs),
        scratch_shapes=[pltpu.VMEM(*depth), pltpu.SemaphoreType.DMA((col_count,))],
        compiler_params=pltpu.CompilerParams(vmem_limit_bytes=scratch_bytes(cell, depth, out) + 6 * mib),
        cost_estimate=pl.CostEstimate(
            flops=2 * high * wide * width, bytes_accessed=2 * wide * len(offsets) * width, transcendentals=0
        ),
        name="backward_product",
    )(dense, own, sibling)


def finish_kernel(*refs, parts):
    part_refs, chunk_refs, (features_ref, weight_ref) = refs[:parts], refs[parts:-2], refs[-2:]
    total = part_refs[0][...].astype(jnp.float32)
    for part_ref in part_refs[1:]:
        total += part_ref[...].astype(jnp.float32)
    features_ref[...] = total.astype(jnp.bfloat16).T
    rows = chunk_refs[0].shape[0]
    col = lax.axis_index("col")
    for partner, chunk_ref in enumerate(chunk_refs):
        weight_ref[pl.ds(pl.multiple_of((col ^ partner) * rows, rows), rows), :] = chunk_ref[...]


def finish(parts, chunks):
    width, rows = parts[0].shape
    return pl.pallas_call(
        functools.partial(finish_kernel, parts=len(parts)),
        out_shape=[
            jax.ShapeDtypeStruct((rows, width), jnp.bfloat16),
            jax.ShapeDtypeStruct((width, width), jnp.float32),
        ],
        in_specs=[pl.BlockSpec(memory_space=pltpu.VMEM)] * (len(parts) + len(chunks)),
        out_specs=[pl.BlockSpec(memory_space=pltpu.VMEM)] * 2,
        compiler_params=pltpu.CompilerParams(vmem_limit_bytes=8 * mib),
        cost_estimate=pl.CostEstimate(
            flops=len(parts) * rows * width, bytes_accessed=2 * (len(parts) + 5) * rows * width, transcendentals=0
        ),
        name="finish",
    )(*parts, *chunks)


def around(value, step):
    count = lax.axis_size("row")
    order = list(range(0, count, 2)) + list(range(count - 1, 0, -2))
    return lax.ppermute(value, "row", [(order[i], order[(i + step) % count]) for i in range(count)])


def swapped(value, axis, partner):
    return lax.ppermute(value, axis, [(i, i ^ partner) for i in range(lax.axis_size(axis))])


def gathered_shards(own, beside):
    count = lax.axis_size("row")
    rows = own.shape[0]
    half = rows // 2
    shards = [(((0, 0, 0, rows),), own)]
    if count == 8:
        far_up, far_down, up, down = (around(own, step) for step in (2, -2, 1, -1))
        for offset, array in ((-2, far_up), (2, far_down), (-1, up), (1, down)):
            shards.append((((offset, 0, 0, rows),), array))
        far_up, far_down, up, down, beside = lax.optimization_barrier((far_up, far_down, up, down, beside))
        up = around(jnp.concatenate([up, far_up[:half]]), 2)
        down = around(jnp.concatenate([down, far_down[half:]]), -2)
        shards.append((((-3, 0, 0, rows), (-4, 0, rows, half)), up))
        shards.append((((3, 0, 0, rows), (4, half, rows, half)), down))
        return shards, beside
    up = down = own
    for step in range(1, count // 2 + 1):
        up = around(up, 1)
        shards.append((((-step, 0, 0, rows),), up))
        if step < count // 2:
            down = around(down, -1)
            shards.append((((step, 0, 0, rows),), down))
        if step == 1:
            up, down, beside = lax.optimization_barrier((up, down, beside))
    return shards, beside


def added(first, second, at=0):
    spare = first.shape[0] - at - second.shape[0]
    second = jnp.pad(second.astype(jnp.float32), ((at, spare), (0, 0)))
    return (first.astype(jnp.float32) + second).astype(jnp.bfloat16)


def partners_sum(values):
    while len(values) > 1:
        values = [values[i] + values[i + 1] for i in range(0, len(values), 2)]
    return values[0]


def scattered_sums(dense, own, sibling, chunk):
    row_count, col_count = lax.axis_size("row"), lax.axis_size("col")
    width = chunk.shape[1]
    half = width // 2
    reach = row_count // 2

    def strips(cell, outputs):
        return backward_product(cell, own, sibling, width, outputs, row_count, col_count)

    def given_to_column(chunk):
        return [chunk] + [swapped(chunk, "col", partner) for partner in range(1, col_count)]

    if row_count == 8:
        far = strips(dense, (((3, 0, width), (4, 0, half)), ((-3, 0, width), (4, half, half))))
        far, cell = lax.optimization_barrier((far, dense))
        up, down = around(far[0], 2), around(far[1], -2)
        others = [swapped(chunk, "row", partner) for partner in (2, 4, 6)]
        up, down, others = lax.optimization_barrier((up, down, others))
        above, below, above_far, below_far, mine = strips(
            cell, tuple(((offset, 0, width),) for offset in (1, -1, 2, -2, 0))
        )
        above_far, below_far = added(above_far, up[width:]), added(below_far, down[width:], half)
        above, below = added(above, up[:width]), added(below, down[:width])
        parts = [mine, around(above_far, 2), around(below_far, -2), around(above, 1), around(below, -1)]
        return parts, given_to_column(partners_sum([chunk] + others))
    (far,) = strips(dense, (((reach, 0, width),),))
    far, cell = lax.optimization_barrier((far, dense))
    up, down = around(far, 1), None
    offsets = tuple(sign * step for step in range(reach - 1, 0, -1) for sign in (1, -1)) + (0,)
    *rest, mine = strips(cell, tuple(((offset, 0, width),) for offset in offsets))
    for step in range(reach - 1):
        above, below = rest[2 * step : 2 * step + 2]
        up = around(added(above, up), 1)
        down = around(below if down is None else added(below, down), -1)
    for bit in range(1, (row_count - 1).bit_length()):
        chunk = chunk + swapped(chunk, "row", 1 << bit)
    return [mine, up, down], given_to_column(chunk)


def per_device(features, weight, adj_tiles, tile_rows, tile_cols, tile_counts, out_grad):
    node_rows, width = features.shape
    capacity, side = adj_tiles.shape[2:4]
    tiles = adj_tiles.reshape(capacity, side, side)
    rows = tile_rows.reshape(capacity)
    cols = tile_cols.reshape(capacity)
    count = tile_counts.reshape(1)
    row_count = lax.axis_size("row")
    col_count = lax.axis_size("col")
    per_strip = node_rows // side
    dense = build_dense(rows, cols, count, tiles, col_count * per_strip, row_count * per_strip, per_strip)
    cotangents = [out_grad] + [swapped(out_grad, "col", partner) for partner in range(2, col_count, 2)]
    shards, (dense, cotangents) = gathered_shards(features, (dense, cotangents))

    for_sibling = forward_product(dense, shards, 1, row_count, col_count)
    for_sibling, cell = lax.optimization_barrier((for_sibling, dense))
    sums = added(forward_product(cell, shards, 0, row_count, col_count), swapped(for_sibling, "col", 1))
    sums = [sums] + [swapped(sums, "col", partner) for partner in range(2, col_count, 2)]
    activations, message, chunk, sent = middle(sums, weight, cotangents, node_rows * row_count * col_count)

    sibling = swapped(message, "col", 1)
    across = swapped(chunk, "row", 1)
    across_sibling = lax.ppermute(
        sent,
        ("row", "col"),
        [(r * col_count + c, (r ^ 1) * col_count + (c ^ 1)) for r in range(row_count) for c in range(col_count)],
    )
    message, sibling, across, across_sibling = lax.optimization_barrier((message, sibling, across, across_sibling))
    size = chunk.shape[0]
    high, low = sibling[-2 * size : -size], sibling[-size:]
    chunk = (chunk + (high.astype(jnp.float32) + low.astype(jnp.float32))) + (across + across_sibling)

    parts, chunks = scattered_sums(dense, message, sibling, chunk)
    grad_features, grad_weight = finish(parts, chunks)
    return (activations, grad_features, grad_weight)


def solution(mesh):
    placed = (
        P(("row", "col"), None),
        P(),
        P("row", "col", None, None, None),
        P("row", "col", None),
        P("row", "col", None),
        P("row", "col"),
        P(("row", "col"), None),
    )
    return jax.shard_map(
        per_device,
        mesh=mesh,
        in_specs=placed,
        out_specs=(P(("row", "col"), None), P(("row", "col"), None), P()),
        check_vma=False,
    )
```

```python
import functools
import math

import jax
import jax.numpy as jnp
from jax import lax
from jax.experimental import pallas as pl
from jax.experimental.pallas import tpu as pltpu
from jax.sharding import PartitionSpec as P

chunk_tiles = 16
chunk_slots = 4
strips_per_step = 8
mib = 1024 * 1024


def scratch_bytes(*shapes):
    return sum(math.prod(shape) * jnp.dtype(kind).itemsize for shape, kind in shapes)


def build_kernel(list_ref, tiles_ref, dense_ref, total, held, sems, *, blocks, steps):
    side = tiles_ref.shape[1]
    first_block = pl.program_id(0) * blocks
    count = list_ref[0] >> 16
    chunks = (count + chunk_tiles - 1) // chunk_tiles

    def fetch(index):
        slot = lax.rem(index, chunk_slots)
        return pltpu.make_async_copy(
            tiles_ref.at[pl.ds(index * chunk_tiles, chunk_tiles)], held.at[slot], sems.at[slot]
        )

    for ahead in range(chunk_slots - 1):
        @pl.when(ahead < chunks)
        def _():
            fetch(ahead).start()

    row_blocks = dense_ref.shape[0] // side

    def clear(block, carry):
        down = pl.ds(pl.multiple_of(block * side, side), side)
        total[down, :] = jnp.zeros((side, total.shape[1]), jnp.float32)
        return carry

    lax.fori_loop(0, row_blocks, clear, 0)

    def target(place):
        code = list_ref[place]
        col = (code & 255) - first_block
        live = place < count
        if steps > 1:
            live = live & (col >= 0) & (col < blocks)
            col = jnp.where(live, col, 0)
        row = jnp.where(live, (code >> 8) & 255, row_blocks)
        return row, col

    def chunk_step(index, carry):
        @pl.when(index + chunk_slots - 1 < chunks)
        def _():
            fetch(index + chunk_slots - 1).start()

        fetch(index).wait()
        slot = lax.rem(index, chunk_slots)
        for lane in range(0, chunk_tiles, 2):
            spots, olds, news = [], [], []
            for place in (index * chunk_tiles + lane, index * chunk_tiles + lane + 1):
                row, col = target(place)
                spots.append((row, col))
                olds.append(
                    (pl.ds(pl.multiple_of(row * side, side), side), pl.ds(pl.multiple_of(col * side, side), side))
                )
            sums = [total[at] for at in olds]
            tiles = [held[slot, lane + turn].astype(jnp.float32) for turn in range(2)]
            same = (spots[0][0] == spots[1][0]) & (spots[0][1] == spots[1][1])
            news = [sums[0] + tiles[0], sums[1] + tiles[1] + jnp.where(same, tiles[0], 0.0)]
            for at, new in zip(olds, news):
                total[at] = new
        return carry

    lax.fori_loop(0, chunks, chunk_step, 0)

    def round_block(block, carry):
        down = pl.ds(pl.multiple_of(block * side, side), side)
        dense_ref[down, :] = total[down, :].astype(jnp.bfloat16)
        return carry

    lax.fori_loop(0, row_blocks, round_block, 0)


def build_dense(packed, tiles, row_blocks, col_blocks, per_strip):
    capacity, side, _ = tiles.shape
    blocks = min(strips_per_step * per_strip, col_blocks)
    steps = col_blocks // blocks
    high, wide = row_blocks * side, blocks * side
    total = ((high + side, wide), jnp.float32)
    held = ((chunk_slots, chunk_tiles, side, side), jnp.bfloat16)
    block = ((high, wide), jnp.bfloat16)
    return pl.pallas_call(
        functools.partial(build_kernel, blocks=blocks, steps=steps),
        out_shape=jax.ShapeDtypeStruct((high, col_blocks * side), jnp.bfloat16),
        grid_spec=pltpu.PrefetchScalarGridSpec(
            num_scalar_prefetch=1,
            grid=(steps,),
            in_specs=[pl.BlockSpec(memory_space=pltpu.HBM)],
            out_specs=pl.BlockSpec((high, wide), lambda i, *_: (0, i)),
            scratch_shapes=[
                pltpu.VMEM(*total),
                pltpu.VMEM(*held),
                pltpu.SemaphoreType.DMA((chunk_slots,)),
            ],
        ),
        compiler_params=pltpu.CompilerParams(vmem_limit_bytes=46 * mib),
        cost_estimate=pl.CostEstimate(
            flops=capacity * side * side,
            bytes_accessed=2 * (capacity * side * side + high * col_blocks * side),
            transcendentals=0,
        ),
        name="build_dense",
    )(packed, tiles)


def ring_place(row, count):
    return jnp.where(lax.rem(row, 2) == 0, row // 2, count - 1 - row // 2)


def ring_row(place, count):
    place = lax.rem(place + 2 * count, count)
    return jnp.where(place < count // 2, 2 * place, 2 * (count - 1 - place) + 1)


def forward_kernel(dense_ref, *refs, pieces, sibling, row_count):
    piece_refs, out_ref = refs[: len(pieces)], refs[len(pieces)]
    count = lax.axis_size("col")
    rows = dense_ref.shape[0] // count
    block = dense_ref.shape[1] // row_count
    place = ring_place(lax.axis_index("row"), row_count)
    col = lax.axis_index("col") ^ sibling
    operands = []
    for piece, ref in zip(pieces, piece_refs):
        for offset, first, start, high in piece:
            along = pl.ds(pl.multiple_of(ring_row(place + offset, row_count) * block + first, 128), high)
            operands.append((along, ref, pl.ds(start, high)))
    for index in range(count // 2):
        down = pl.ds(pl.multiple_of((col ^ (2 * index)) * rows, rows), rows)
        total = None
        for along, ref, part in operands:
            product = jnp.dot(dense_ref[down, along], ref[part, :], preferred_element_type=jnp.float32)
            total = product if total is None else total + product
        out_ref[pl.ds(index * rows, rows), :] = total.astype(jnp.bfloat16)


def forward_product(dense, shards, sibling, row_count, col_count):
    pieces = tuple(piece for piece, _ in shards)
    arrays = [array for _, array in shards]
    high, deep = dense.shape
    width = arrays[0].shape[1]
    half = high // 2
    cell = ((high, deep), jnp.bfloat16)
    depth = ((deep, width), jnp.bfloat16)
    out = ((high, width), jnp.float32)
    return pl.pallas_call(
        functools.partial(forward_kernel, pieces=pieces, sibling=sibling, row_count=row_count),
        out_shape=jax.ShapeDtypeStruct((half, width), jnp.bfloat16),
        in_specs=[pl.BlockSpec(memory_space=pltpu.VMEM)] * (1 + len(arrays)),
        out_specs=pl.BlockSpec(memory_space=pltpu.VMEM),
        compiler_params=pltpu.CompilerParams(vmem_limit_bytes=scratch_bytes(cell, depth, out) + 6 * mib),
        cost_estimate=pl.CostEstimate(
            flops=2 * half * deep * width,
            bytes_accessed=2 * (half * deep + deep * width + half * width),
            transcendentals=0,
        ),
        name="forward_product",
    )(dense, *arrays)


def middle_kernel(*refs, blocks, scale):
    sums, refs = refs[:blocks], refs[blocks:]
    weight_ref, refs = refs[0], refs[1:]
    cotangent_refs, (act_ref, message_ref, chunk_ref, product) = refs[:blocks], refs[blocks:]
    weight = weight_ref[...]
    rows, width = act_ref.shape
    over_nodes = (((0,), (0,)), ((), ()))
    terms = None
    for index in range(blocks):
        aggregate = sums[0][pl.ds(index * rows, rows), :].astype(jnp.float32)
        for other in range(1, blocks):
            aggregate += sums[other][pl.ds((index ^ other) * rows, rows), :].astype(jnp.float32)
        high = aggregate.astype(jnp.bfloat16)
        low = (aggregate - high.astype(jnp.float32)).astype(jnp.bfloat16)
        pre = jnp.dot(high, weight, preferred_element_type=jnp.float32)
        pre += jnp.dot(low, weight, preferred_element_type=jnp.float32)
        sig = jax.nn.sigmoid(pre)
        cotangent = cotangent_refs[index][...].astype(jnp.float32)
        grad = (cotangent * sig * (1.0 + pre * (1.0 - sig))).astype(jnp.bfloat16)
        message_ref[pl.ds(index * width, width), :] = lax.dot_general(
            weight, grad, (((1,), (1,)), ((), ())), preferred_element_type=jnp.float32
        ).astype(jnp.bfloat16)
        if index == 0:
            act_ref[...] = (pre * sig).astype(jnp.bfloat16)
        part = lax.dot_general(high, grad, over_nodes, preferred_element_type=jnp.float32)
        part += lax.dot_general(low, grad, over_nodes, preferred_element_type=jnp.float32)
        terms = part if terms is None else terms + part
    product[...] = terms * scale
    col = lax.axis_index("col")
    size = chunk_ref.shape[0]
    chunk_ref[...] = product[pl.ds(pl.multiple_of(col * size, size), size), :]
    sent = product[pl.ds(pl.multiple_of((col ^ 1) * size, size), size), :]
    high = sent.astype(jnp.bfloat16)
    low = (sent - high.astype(jnp.float32)).astype(jnp.bfloat16)
    message_ref[pl.ds(blocks * width, size), :] = high
    message_ref[pl.ds(blocks * width + size, size), :] = low


def middle(sums, weight, cotangents, total_nodes):
    rows, width = cotangents[0].shape
    blocks = len(cotangents)
    size = width // (2 * blocks)
    return pl.pallas_call(
        functools.partial(middle_kernel, blocks=blocks, scale=1.0 / math.sqrt(total_nodes)),
        out_shape=[
            jax.ShapeDtypeStruct((rows, width), jnp.bfloat16),
            jax.ShapeDtypeStruct((blocks * width + 2 * size, rows), jnp.bfloat16),
            jax.ShapeDtypeStruct((size, width), jnp.float32),
        ],
        in_specs=[pl.BlockSpec(memory_space=pltpu.VMEM)] * (2 * blocks + 1),
        out_specs=[pl.BlockSpec(memory_space=pltpu.VMEM)] * 3,
        scratch_shapes=[pltpu.VMEM((width, width), jnp.float32)],
        compiler_params=pltpu.CompilerParams(vmem_limit_bytes=12 * mib),
        cost_estimate=pl.CostEstimate(
            flops=10 * blocks * rows * width * width,
            bytes_accessed=2 * (blocks * blocks + 2 * blocks + 4) * rows * width,
            transcendentals=blocks * rows * width,
        ),
        name="middle",
    )(*sums, weight, *cotangents)


def backward_kernel(dense_ref, own_ref, sibling_ref, chunk_ref, *refs, outputs, row_count):
    out_refs, (depth, sems) = refs[:-2], refs[-2:]
    count = lax.axis_size("col")
    width, rows = depth.shape[0], own_ref.shape[1]
    wide = dense_ref.shape[1] // row_count
    col = lax.axis_index("col")
    copies = []
    for index in range(count):
        block = pl.ds(index // 2 * width, width)
        along = pl.ds(pl.multiple_of((col ^ index) * rows, rows), rows)
        source = sibling_ref if index % 2 else own_ref
        copy = pltpu.make_async_copy(source.at[block], depth.at[:, along], sems.at[index])
        copy.start()
        copies.append(copy)
    size = chunk_ref.shape[0]
    from_sibling = count // 2 * width
    high, low = (sibling_ref[pl.ds(from_sibling + turn * size, size), :].astype(jnp.float32) for turn in range(2))
    terms = (chunk_ref[...] + (high + low)).astype(jnp.bfloat16)
    for copy in copies:
        copy.wait()
    place = ring_place(lax.axis_index("row"), row_count)
    for (offset, tail), out_ref in zip(outputs, out_refs):
        if tail != "terms alone":
            along = pl.ds(pl.multiple_of(ring_row(place + offset, row_count) * wide, wide), wide)
            part = jnp.dot(depth[...], dense_ref[:, along], preferred_element_type=jnp.float32)
            out_ref[pl.ds(0, width), :] = part.astype(jnp.bfloat16)
        if tail == "terms alone":
            out_ref[...] = terms
        elif tail == "terms":
            out_ref[pl.ds(width, size), :] = terms
        elif tail == "zeros":
            out_ref[pl.ds(width, size), :] = jnp.zeros_like(terms)


def backward_product(dense, own, sibling, chunk, outputs, row_count, col_count):
    high, deep = dense.shape
    size, width = chunk.shape
    wide = deep // row_count
    heights = {"": width, "terms alone": size, "terms": width + size, "zeros": width + size}
    cell = ((high, deep), jnp.bfloat16)
    depth = ((width, high), jnp.bfloat16)
    out = ((len(outputs), width + size, wide), jnp.float32)
    return pl.pallas_call(
        functools.partial(backward_kernel, outputs=outputs, row_count=row_count),
        out_shape=[jax.ShapeDtypeStruct((heights[tail], wide), jnp.bfloat16) for _, tail in outputs],
        in_specs=[pl.BlockSpec(memory_space=pltpu.VMEM)] * 4,
        out_specs=[pl.BlockSpec(memory_space=pltpu.VMEM)] * len(outputs),
        scratch_shapes=[pltpu.VMEM(*depth), pltpu.SemaphoreType.DMA((col_count,))],
        compiler_params=pltpu.CompilerParams(vmem_limit_bytes=scratch_bytes(cell, depth, out) + 6 * mib),
        cost_estimate=pl.CostEstimate(
            flops=2 * high * wide * width, bytes_accessed=2 * wide * len(outputs) * width, transcendentals=0
        ),
        name="backward_product",
    )(dense, own, sibling, chunk)


def terms_kernel(*refs, offsets, first_rows):
    term_refs, out_ref, places = refs[:-2], refs[-2], refs[-1]
    row_count, size, _ = places.shape
    place = ring_place(lax.axis_index("row"), row_count)
    for offset, first, ref in zip(offsets, first_rows, term_refs):
        places[ring_row(place + offset, row_count)] = ref[pl.ds(first, size), :].astype(jnp.float32)
    total = places[0]
    for index in range(1, row_count):
        total += places[index]
    out_ref[...] = total


def summed_terms(terms, size):
    offsets = tuple(offset for offset, _, _ in terms)
    first_rows = tuple(first for _, first, _ in terms)
    arrays = [array for _, _, array in terms]
    width = arrays[0].shape[1]
    return pl.pallas_call(
        functools.partial(terms_kernel, offsets=offsets, first_rows=first_rows),
        out_shape=jax.ShapeDtypeStruct((size, width), jnp.float32),
        in_specs=[pl.BlockSpec(memory_space=pltpu.VMEM)] * len(arrays),
        out_specs=pl.BlockSpec(memory_space=pltpu.VMEM),
        scratch_shapes=[pltpu.VMEM((len(arrays), size, width), jnp.float32)],
        compiler_params=pltpu.CompilerParams(
            vmem_limit_bytes=scratch_bytes(*((array.shape, array.dtype) for array in arrays)) + 8 * mib
        ),
        cost_estimate=pl.CostEstimate(
            flops=len(arrays) * size * width, bytes_accessed=2 * len(arrays) * size * width, transcendentals=0
        ),
        name="summed_terms",
    )(*arrays)


def finish_kernel(*refs, parts):
    part_refs, chunk_refs, (features_ref, weight_ref) = refs[:parts], refs[parts:-2], refs[-2:]
    width = features_ref.shape[1]
    total = part_refs[0][pl.ds(0, width), :].astype(jnp.float32)
    for part_ref in part_refs[1:]:
        total += part_ref[pl.ds(0, width), :].astype(jnp.float32)
    features_ref[...] = total.astype(jnp.bfloat16).T
    rows = chunk_refs[0].shape[0]
    col = lax.axis_index("col")
    for partner, chunk_ref in enumerate(chunk_refs):
        weight_ref[pl.ds(pl.multiple_of((col ^ partner) * rows, rows), rows), :] = chunk_ref[...]


def finish(parts, chunks):
    width, rows = parts[0].shape
    return pl.pallas_call(
        functools.partial(finish_kernel, parts=len(parts)),
        out_shape=[
            jax.ShapeDtypeStruct((rows, width), jnp.bfloat16),
            jax.ShapeDtypeStruct((width, width), jnp.float32),
        ],
        in_specs=[pl.BlockSpec(memory_space=pltpu.VMEM)] * (len(parts) + len(chunks)),
        out_specs=[pl.BlockSpec(memory_space=pltpu.VMEM)] * 2,
        compiler_params=pltpu.CompilerParams(vmem_limit_bytes=8 * mib),
        cost_estimate=pl.CostEstimate(
            flops=len(parts) * rows * width, bytes_accessed=2 * (len(parts) + 5) * rows * width, transcendentals=0
        ),
        name="finish",
    )(*parts, *chunks)


def around(value, step):
    count = lax.axis_size("row")
    order = list(range(0, count, 2)) + list(range(count - 1, 0, -2))
    return lax.ppermute(value, "row", [(order[i], order[(i + step) % count]) for i in range(count)])


def swapped(value, axis, partner):
    return lax.ppermute(value, axis, [(i, i ^ partner) for i in range(lax.axis_size(axis))])


def gathered_shards(own, beside):
    reach = lax.axis_size("row") // 2
    rows = own.shape[0]
    shards = [(((0, 0, 0, rows),), own)]
    up = down = own
    for step in range(1, reach + 1):
        up = around(up, 1)
        shards.append((((-step, 0, 0, rows),), up))
        if step < reach:
            down = around(down, -1)
            shards.append((((step, 0, 0, rows),), down))
        if step == 1:
            up, down, beside = lax.optimization_barrier((up, down, beside))
    return shards, beside


def added(first, second):
    return (first.astype(jnp.float32) + second[: first.shape[0]].astype(jnp.float32)).astype(jnp.bfloat16)


def scattered_sums(dense, own, sibling, chunk):
    row_count, col_count = lax.axis_size("row"), lax.axis_size("col")
    size, width = chunk.shape
    reach = row_count // 2
    first = ((reach, "terms"), (1 - reach, "terms"), (0, "terms alone"))
    above, below, terms = backward_product(dense, own, sibling, chunk, first, row_count, col_count)
    above, below, terms, cell = lax.optimization_barrier((above, below, terms, dense))
    up, down = around(above, 1), around(below, -1)
    up, down, opposite = lax.optimization_barrier((up, down, around(terms, reach)))
    all_terms = [(0, 0, terms), (reach, 0, opposite)]

    ups = tuple((offset, "zeros" if offset > 1 else "") for offset in range(reach - 1, 0, -1))
    downs = tuple((-offset, "zeros") for offset in range(reach - 2, 0, -1))
    strips = backward_product(cell, own, sibling, chunk, ups + downs + ((0, ""),), row_count, col_count)
    ups, downs, mine = strips[: reach - 1], strips[reach - 1 : -1], strips[-1]
    for step in range(1, reach):
        all_terms += [(-step, width, up), (step, width, down)]
        up = around(added(ups[step - 1], up), 1)
        if step < reach - 1:
            down = around(added(downs[step - 1], down), -1)
    chunk = summed_terms(all_terms, size)
    chunks = [chunk] + [swapped(chunk, "col", partner) for partner in range(1, col_count)]
    return [mine, up, down], chunks


def per_device(features, weight, adj_tiles, tile_rows, tile_cols, tile_counts, out_grad):
    node_rows, width = features.shape
    capacity, side = adj_tiles.shape[2:4]
    tiles = adj_tiles.reshape(capacity, side, side)
    packed = ((tile_counts[:, :, None] << 16) | (tile_rows << 8) | tile_cols).reshape(capacity)
    row_count = lax.axis_size("row")
    col_count = lax.axis_size("col")
    per_strip = node_rows // side
    dense = build_dense(packed, tiles, col_count * per_strip, row_count * per_strip, per_strip)
    cotangents = [out_grad] + [swapped(out_grad, "col", partner) for partner in range(2, col_count, 2)]
    shards, (dense, cotangents) = gathered_shards(features, (dense, cotangents))

    for_sibling = forward_product(dense, shards, 1, row_count, col_count)
    for_sibling, cell = lax.optimization_barrier((for_sibling, dense))
    sums = added(forward_product(cell, shards, 0, row_count, col_count), swapped(for_sibling, "col", 1))
    sums = [sums] + [swapped(sums, "col", partner) for partner in range(2, col_count, 2)]
    activations, message, chunk = middle(sums, weight, cotangents, node_rows * row_count * col_count)
    sibling = swapped(message, "col", 1)
    parts, chunks = scattered_sums(dense, message, sibling, chunk)
    grad_features, grad_weight = finish(parts, chunks)
    return (activations, grad_features, grad_weight)


def solution(mesh):
    placed = (
        P(("row", "col"), None),
        P(),
        P("row", "col", None, None, None),
        P("row", "col", None),
        P("row", "col", None),
        P("row", "col"),
        P(("row", "col"), None),
    )
    return jax.shard_map(
        per_device,
        mesh=mesh,
        in_specs=placed,
        out_specs=(P(("row", "col"), None), P(("row", "col"), None), P()),
        check_vma=False,
    )
```

```python
import functools
import math

import jax
import jax.numpy as jnp
from jax import lax
from jax.experimental import pallas as pl
from jax.experimental.pallas import tpu as pltpu
from jax.sharding import PartitionSpec as P

chunk_tiles = 16
chunk_slots = 8
build_grant = 44
strips_per_step = 8
mib = 1024 * 1024


def scratch_bytes(*shapes):
    return sum(math.prod(shape) * jnp.dtype(kind).itemsize for shape, kind in shapes)


def add_tiles(list_ref, tiles_ref, total, held, sems, begin, end, *, first_block, blocks, steps):
    side = tiles_ref.shape[1]
    capacity = tiles_ref.shape[0]
    count = list_ref[2 * capacity]
    slots = held.shape[0]
    row_blocks = total.shape[0] // side - 1

    def fetch(index):
        slot = lax.rem(index - begin, slots)
        return pltpu.make_async_copy(
            tiles_ref.at[pl.ds(index * chunk_tiles, chunk_tiles)], held.at[slot], sems.at[slot]
        )

    def start(index, carry):
        fetch(index).start()
        return carry

    lax.fori_loop(begin, jnp.minimum(end, begin + slots), start, 0)

    def target(place):
        col = list_ref[capacity + place] - first_block
        live = place < count
        if steps > 1:
            live = live & (col >= 0) & (col < blocks)
            col = jnp.where(live, col, 0)
        row = jnp.where(live, list_ref[place], row_blocks)
        return row, col

    def chunk_step(index, carry):
        fetch(index).wait()
        slot = lax.rem(index - begin, slots)
        for lane in range(0, chunk_tiles, 2):
            spots = [target(index * chunk_tiles + lane + turn) for turn in range(2)]
            at = [
                (pl.ds(pl.multiple_of(row * side, side), side), pl.ds(pl.multiple_of(col * side, side), side))
                for row, col in spots
            ]
            first, second = total[at[0]], total[at[1]]
            tiles = [held[slot, lane + turn].astype(jnp.float32) for turn in range(2)]
            same = (spots[0][0] == spots[1][0]) & (spots[0][1] == spots[1][1])
            total[at[0]] = first + tiles[0]
            total[at[1]] = second + tiles[1] + jnp.where(same, tiles[0], 0.0)

        @pl.when(index + slots < end)
        def _():
            fetch(index + slots).start()

        return carry

    return lambda: lax.fori_loop(begin, end, chunk_step, 0)


def each_row_block(total, side, action):
    def step(block, carry):
        action(pl.ds(pl.multiple_of(block * side, side), side))
        return carry

    lax.fori_loop(0, total.shape[0] // side - 1, step, 0)


def live_chunks(list_ref, tiles_ref):
    return (list_ref[2 * tiles_ref.shape[0]] + chunk_tiles - 1) // chunk_tiles


def build_first_kernel(list_ref, tiles_ref, dense_ref, total, held, sems, *, blocks):
    half = (live_chunks(list_ref, tiles_ref) + 1) // 2
    run = add_tiles(list_ref, tiles_ref, total, held, sems, 0, half, first_block=0, blocks=blocks, steps=1)

    def clear(down):
        total[down, :] = jnp.zeros((down.size, total.shape[1]), jnp.float32)

    def rounded(down):
        dense_ref[down, :] = total[down, :].astype(jnp.bfloat16)

    each_row_block(total, tiles_ref.shape[1], clear)
    run()
    each_row_block(total, tiles_ref.shape[1], rounded)


def build_rest_kernel(list_ref, tiles_ref, half_ref, dense_ref, total, held, sems, *, blocks):
    chunks = live_chunks(list_ref, tiles_ref)
    run = add_tiles(
        list_ref, tiles_ref, total, held, sems, (chunks + 1) // 2, chunks, first_block=0, blocks=blocks, steps=1
    )

    def widened(down):
        total[down, :] = half_ref[down, :].astype(jnp.float32)

    def rounded(down):
        dense_ref[down, :] = total[down, :].astype(jnp.bfloat16)

    each_row_block(total, tiles_ref.shape[1], widened)
    run()
    each_row_block(total, tiles_ref.shape[1], rounded)


def build_whole_kernel(list_ref, tiles_ref, dense_ref, total, held, sems, *, blocks, steps):
    chunks = live_chunks(list_ref, tiles_ref)
    first_block = pl.program_id(0) * blocks
    run = add_tiles(
        list_ref, tiles_ref, total, held, sems, 0, chunks, first_block=first_block, blocks=blocks, steps=steps
    )

    def clear(down):
        total[down, :] = jnp.zeros((down.size, total.shape[1]), jnp.float32)

    def rounded(down):
        dense_ref[down, :] = total[down, :].astype(jnp.bfloat16)

    each_row_block(total, tiles_ref.shape[1], clear)
    run()
    each_row_block(total, tiles_ref.shape[1], rounded)


def build_stages(packed, tiles, row_blocks, col_blocks, per_strip):
    capacity, side, _ = tiles.shape
    blocks = min(strips_per_step * per_strip, col_blocks)
    steps = col_blocks // blocks
    high, wide = row_blocks * side, blocks * side
    total = ((high + side, wide), jnp.float32)
    held = ((min(chunk_slots, capacity // chunk_tiles), chunk_tiles, side, side), jnp.bfloat16)
    cost = pl.CostEstimate(
        flops=capacity * side * side, bytes_accessed=capacity * side * side + high * wide, transcendentals=0
    )
    held_scratch = [pltpu.VMEM(*held), pltpu.SemaphoreType.DMA((held[0][0],))]
    dense_shape = jax.ShapeDtypeStruct((high, col_blocks * side), jnp.bfloat16)
    whole = pl.BlockSpec(memory_space=pltpu.VMEM)
    apart = pl.BlockSpec(memory_space=pl.ANY)
    listed = pl.BlockSpec(memory_space=pltpu.SMEM)
    if steps > 1:
        block = ((high, wide), jnp.bfloat16)
        return [
            lambda _: pl.pallas_call(
                functools.partial(build_whole_kernel, blocks=blocks, steps=steps),
                out_shape=dense_shape,
                grid_spec=pltpu.PrefetchScalarGridSpec(
                    num_scalar_prefetch=1,
                    grid=(steps,),
                    in_specs=[apart],
                    out_specs=pl.BlockSpec((high, wide), lambda i, *_: (0, i)),
                    scratch_shapes=[pltpu.VMEM(*total)] + held_scratch,
                ),
                compiler_params=pltpu.CompilerParams(
                    vmem_limit_bytes=scratch_bytes(total, held, block, block) + 4 * mib
                ),
                cost_estimate=cost,
                name="build_whole",
            )(packed, tiles)
        ]
    params = pltpu.CompilerParams(vmem_limit_bytes=build_grant * mib)
    scratch = [pltpu.VMEM(*total)] + held_scratch
    return [
        lambda _: pl.pallas_call(
            functools.partial(build_first_kernel, blocks=blocks),
            out_shape=dense_shape,
            in_specs=[listed, apart],
            out_specs=whole,
            scratch_shapes=scratch,
            compiler_params=params,
            cost_estimate=cost,
            name="build_first",
        )(packed, tiles),
        lambda half: pl.pallas_call(
            functools.partial(build_rest_kernel, blocks=blocks),
            out_shape=dense_shape,
            in_specs=[listed, apart, whole],
            out_specs=whole,
            scratch_shapes=scratch,
            compiler_params=params,
            cost_estimate=cost,
            name="build_rest",
        )(packed, tiles, half),
    ]


def ring_place(row, count):
    return jnp.where(lax.rem(row, 2) == 0, row // 2, count - 1 - row // 2)


def ring_row(place, count):
    place = lax.rem(place + 2 * count, count)
    return jnp.where(place < count // 2, 2 * place, 2 * (count - 1 - place) + 1)


def forward_kernel(dense_ref, *refs, pieces, sibling, row_count):
    piece_refs, out_ref = refs[: len(pieces)], refs[len(pieces)]
    count = lax.axis_size("col")
    rows = dense_ref.shape[0] // count
    block = dense_ref.shape[1] // row_count
    place = ring_place(lax.axis_index("row"), row_count)
    col = lax.axis_index("col") ^ sibling
    operands = []
    for piece, ref in zip(pieces, piece_refs):
        for offset, first, start, high in piece:
            along = pl.ds(pl.multiple_of(ring_row(place + offset, row_count) * block + first, 128), high)
            operands.append((along, ref, pl.ds(start, high)))
    for index in range(count // 2):
        down = pl.ds(pl.multiple_of((col ^ (2 * index)) * rows, rows), rows)
        total = None
        for along, ref, part in operands:
            product = jnp.dot(dense_ref[down, along], ref[part, :], preferred_element_type=jnp.float32)
            total = product if total is None else total + product
        out_ref[pl.ds(index * rows, rows), :] = total.astype(jnp.bfloat16)


def forward_product(dense, shards, sibling, row_count, col_count):
    pieces = tuple(piece for piece, _ in shards)
    arrays = [array for _, array in shards]
    high, deep = dense.shape
    width = arrays[0].shape[1]
    half = high // 2
    cell = ((high, deep), jnp.bfloat16)
    depth = ((deep, width), jnp.bfloat16)
    out = ((high, width), jnp.float32)
    return pl.pallas_call(
        functools.partial(forward_kernel, pieces=pieces, sibling=sibling, row_count=row_count),
        out_shape=jax.ShapeDtypeStruct((half, width), jnp.bfloat16),
        in_specs=[pl.BlockSpec(memory_space=pltpu.VMEM)] * (1 + len(arrays)),
        out_specs=pl.BlockSpec(memory_space=pltpu.VMEM),
        compiler_params=pltpu.CompilerParams(vmem_limit_bytes=scratch_bytes(cell, depth, out) + 6 * mib),
        cost_estimate=pl.CostEstimate(
            flops=2 * half * deep * width,
            bytes_accessed=2 * (half * deep + deep * width + half * width),
            transcendentals=0,
        ),
        name="forward_product",
    )(dense, *arrays)


def middle_kernel(*refs, blocks, scale):
    sums, refs = refs[:blocks], refs[blocks:]
    weight_ref, refs = refs[0], refs[1:]
    cotangent_refs, (act_ref, message_ref, chunk_ref, product) = refs[:blocks], refs[blocks:]
    weight = weight_ref[...]
    rows, width = act_ref.shape
    over_nodes = (((0,), (0,)), ((), ()))
    terms = None
    for index in range(blocks):
        aggregate = sums[0][pl.ds(index * rows, rows), :].astype(jnp.float32)
        for other in range(1, blocks):
            aggregate += sums[other][pl.ds((index ^ other) * rows, rows), :].astype(jnp.float32)
        high = aggregate.astype(jnp.bfloat16)
        low = (aggregate - high.astype(jnp.float32)).astype(jnp.bfloat16)
        pre = jnp.dot(high, weight, preferred_element_type=jnp.float32)
        pre += jnp.dot(low, weight, preferred_element_type=jnp.float32)
        sig = jax.nn.sigmoid(pre)
        cotangent = cotangent_refs[index][...].astype(jnp.float32)
        grad = (cotangent * sig * (1.0 + pre * (1.0 - sig))).astype(jnp.bfloat16)
        message_ref[pl.ds(index * width, width), :] = lax.dot_general(
            weight, grad, (((1,), (1,)), ((), ())), preferred_element_type=jnp.float32
        ).astype(jnp.bfloat16)
        if index == 0:
            act_ref[...] = (pre * sig).astype(jnp.bfloat16)
        part = lax.dot_general(high, grad, over_nodes, preferred_element_type=jnp.float32)
        part += lax.dot_general(low, grad, over_nodes, preferred_element_type=jnp.float32)
        terms = part if terms is None else terms + part
    product[...] = terms * scale
    col = lax.axis_index("col")
    size = chunk_ref.shape[0]
    chunk_ref[...] = product[pl.ds(pl.multiple_of(col * size, size), size), :]
    sent = product[pl.ds(pl.multiple_of((col ^ 1) * size, size), size), :]
    high = sent.astype(jnp.bfloat16)
    low = (sent - high.astype(jnp.float32)).astype(jnp.bfloat16)
    message_ref[pl.ds(blocks * width, size), :] = high
    message_ref[pl.ds(blocks * width + size, size), :] = low


def middle(sums, weight, cotangents, total_nodes):
    rows, width = cotangents[0].shape
    blocks = len(cotangents)
    size = width // (2 * blocks)
    return pl.pallas_call(
        functools.partial(middle_kernel, blocks=blocks, scale=1.0 / math.sqrt(total_nodes)),
        out_shape=[
            jax.ShapeDtypeStruct((rows, width), jnp.bfloat16),
            jax.ShapeDtypeStruct((blocks * width + 2 * size, rows), jnp.bfloat16),
            jax.ShapeDtypeStruct((size, width), jnp.float32),
        ],
        in_specs=[pl.BlockSpec(memory_space=pltpu.VMEM)] * (2 * blocks + 1),
        out_specs=[pl.BlockSpec(memory_space=pltpu.VMEM)] * 3,
        scratch_shapes=[pltpu.VMEM((width, width), jnp.float32)],
        compiler_params=pltpu.CompilerParams(vmem_limit_bytes=12 * mib),
        cost_estimate=pl.CostEstimate(
            flops=10 * blocks * rows * width * width,
            bytes_accessed=2 * (blocks * blocks + 2 * blocks + 4) * rows * width,
            transcendentals=blocks * rows * width,
        ),
        name="middle",
    )(*sums, weight, *cotangents)


def backward_kernel(dense_ref, own_ref, sibling_ref, chunk_ref, *refs, outputs, row_count):
    out_refs, (depth, sems) = refs[:-2], refs[-2:]
    count = lax.axis_size("col")
    width, rows = depth.shape[0], own_ref.shape[1]
    wide = dense_ref.shape[1] // row_count
    col = lax.axis_index("col")
    copies = []
    for index in range(count):
        block = pl.ds(index // 2 * width, width)
        along = pl.ds(pl.multiple_of((col ^ index) * rows, rows), rows)
        source = sibling_ref if index % 2 else own_ref
        copy = pltpu.make_async_copy(source.at[block], depth.at[:, along], sems.at[index])
        copy.start()
        copies.append(copy)
    size = chunk_ref.shape[0]
    from_sibling = count // 2 * width
    high, low = (sibling_ref[pl.ds(from_sibling + turn * size, size), :].astype(jnp.float32) for turn in range(2))
    terms = (chunk_ref[...] + (high + low)).astype(jnp.bfloat16)
    for copy in copies:
        copy.wait()
    place = ring_place(lax.axis_index("row"), row_count)
    for (offset, tail), out_ref in zip(outputs, out_refs):
        if tail != "terms alone":
            along = pl.ds(pl.multiple_of(ring_row(place + offset, row_count) * wide, wide), wide)
            part = jnp.dot(depth[...], dense_ref[:, along], preferred_element_type=jnp.float32)
            out_ref[pl.ds(0, width), :] = part.astype(jnp.bfloat16)
        if tail == "terms alone":
            out_ref[...] = terms
        elif tail == "terms":
            out_ref[pl.ds(width, size), :] = terms
        elif tail == "zeros":
            out_ref[pl.ds(width, size), :] = jnp.zeros_like(terms)


def backward_product(dense, own, sibling, chunk, outputs, row_count, col_count):
    high, deep = dense.shape
    size, width = chunk.shape
    wide = deep // row_count
    heights = {"": width, "terms alone": size, "terms": width + size, "zeros": width + size}
    cell = ((high, deep), jnp.bfloat16)
    depth = ((width, high), jnp.bfloat16)
    out = ((len(outputs), width + size, wide), jnp.float32)
    return pl.pallas_call(
        functools.partial(backward_kernel, outputs=outputs, row_count=row_count),
        out_shape=[jax.ShapeDtypeStruct((heights[tail], wide), jnp.bfloat16) for _, tail in outputs],
        in_specs=[pl.BlockSpec(memory_space=pltpu.VMEM)] * 4,
        out_specs=[pl.BlockSpec(memory_space=pltpu.VMEM)] * len(outputs),
        scratch_shapes=[pltpu.VMEM(*depth), pltpu.SemaphoreType.DMA((col_count,))],
        compiler_params=pltpu.CompilerParams(vmem_limit_bytes=scratch_bytes(cell, depth, out) + 6 * mib),
        cost_estimate=pl.CostEstimate(
            flops=2 * high * wide * width, bytes_accessed=2 * wide * len(outputs) * width, transcendentals=0
        ),
        name="backward_product",
    )(dense, own, sibling, chunk)


def terms_kernel(*refs, offsets, first_rows):
    term_refs, out_ref, places = refs[:-2], refs[-2], refs[-1]
    row_count, size, _ = places.shape
    place = ring_place(lax.axis_index("row"), row_count)
    for offset, first, ref in zip(offsets, first_rows, term_refs):
        places[ring_row(place + offset, row_count)] = ref[pl.ds(first, size), :].astype(jnp.float32)
    total = places[0]
    for index in range(1, row_count):
        total += places[index]
    out_ref[...] = total


def summed_terms(terms, size):
    offsets = tuple(offset for offset, _, _ in terms)
    first_rows = tuple(first for _, first, _ in terms)
    arrays = [array for _, _, array in terms]
    width = arrays[0].shape[1]
    return pl.pallas_call(
        functools.partial(terms_kernel, offsets=offsets, first_rows=first_rows),
        out_shape=jax.ShapeDtypeStruct((size, width), jnp.float32),
        in_specs=[pl.BlockSpec(memory_space=pltpu.VMEM)] * len(arrays),
        out_specs=pl.BlockSpec(memory_space=pltpu.VMEM),
        scratch_shapes=[pltpu.VMEM((len(arrays), size, width), jnp.float32)],
        compiler_params=pltpu.CompilerParams(
            vmem_limit_bytes=scratch_bytes(*((array.shape, array.dtype) for array in arrays)) + 8 * mib
        ),
        cost_estimate=pl.CostEstimate(
            flops=len(arrays) * size * width, bytes_accessed=2 * len(arrays) * size * width, transcendentals=0
        ),
        name="summed_terms",
    )(*arrays)


def finish_kernel(*refs, parts):
    part_refs, chunk_refs, (features_ref, weight_ref) = refs[:parts], refs[parts:-2], refs[-2:]
    width = features_ref.shape[1]
    total = part_refs[0][pl.ds(0, width), :].astype(jnp.float32)
    for part_ref in part_refs[1:]:
        total += part_ref[pl.ds(0, width), :].astype(jnp.float32)
    features_ref[...] = total.astype(jnp.bfloat16).T
    rows = chunk_refs[0].shape[0]
    col = lax.axis_index("col")
    for partner, chunk_ref in enumerate(chunk_refs):
        weight_ref[pl.ds(pl.multiple_of((col ^ partner) * rows, rows), rows), :] = chunk_ref[...]


def finish(parts, chunks):
    width, rows = parts[0].shape
    return pl.pallas_call(
        functools.partial(finish_kernel, parts=len(parts)),
        out_shape=[
            jax.ShapeDtypeStruct((rows, width), jnp.bfloat16),
            jax.ShapeDtypeStruct((width, width), jnp.float32),
        ],
        in_specs=[pl.BlockSpec(memory_space=pltpu.VMEM)] * (len(parts) + len(chunks)),
        out_specs=[pl.BlockSpec(memory_space=pltpu.VMEM)] * 2,
        compiler_params=pltpu.CompilerParams(vmem_limit_bytes=8 * mib),
        cost_estimate=pl.CostEstimate(
            flops=len(parts) * rows * width, bytes_accessed=2 * (len(parts) + 5) * rows * width, transcendentals=0
        ),
        name="finish",
    )(*parts, *chunks)


def around(value, step):
    count = lax.axis_size("row")
    order = list(range(0, count, 2)) + list(range(count - 1, 0, -2))
    return lax.ppermute(value, "row", [(order[i], order[(i + step) % count]) for i in range(count)])


def swapped(value, axis, partner):
    return lax.ppermute(value, axis, [(i, i ^ partner) for i in range(lax.axis_size(axis))])


def gathered_shards(own, stages, cotangent):
    reach = lax.axis_size("row") // 2
    rows = own.shape[0]
    shards = [(((0, 0, 0, rows),), own)]
    up = down = own
    beside = None
    cotangents = [cotangent]
    for step in range(1, reach + 1):
        up = around(up, 1)
        if step < reach:
            down = around(down, -1)
        if step <= len(stages):
            up, down, beside = lax.optimization_barrier((up, down, stages[step - 1](beside)))
        elif step == len(stages) + 1:
            others = [swapped(cotangent, "col", partner) for partner in range(2, lax.axis_size("col"), 2)]
            up, down, others = lax.optimization_barrier((up, down, others))
            cotangents += others
        shards.append((((-step, 0, 0, rows),), up))
        if step < reach:
            shards.append((((step, 0, 0, rows),), down))
    return shards, beside, cotangents


def added(first, second):
    return (first.astype(jnp.float32) + second[: first.shape[0]].astype(jnp.float32)).astype(jnp.bfloat16)


def scattered_sums(dense, own, sibling, chunk):
    row_count, col_count = lax.axis_size("row"), lax.axis_size("col")
    size, width = chunk.shape
    reach = row_count // 2
    first = ((reach, "terms"), (1 - reach, "terms"), (0, "terms alone"))
    above, below, terms = backward_product(dense, own, sibling, chunk, first, row_count, col_count)
    above, below, terms, cell = lax.optimization_barrier((above, below, terms, dense))
    up, down = around(above, 1), around(below, -1)
    all_terms = [(0, 0, terms)]

    ups = tuple((offset, "zeros" if offset > 1 else "") for offset in range(reach - 1, 0, -1))
    downs = tuple((-offset, "zeros") for offset in range(reach - 2, 0, -1))
    strips = backward_product(cell, own, sibling, chunk, ups + downs + ((0, ""),), row_count, col_count)
    ups, downs, mine = strips[: reach - 1], strips[reach - 1 : -1], strips[-1]
    for step in range(1, reach):
        all_terms += [(-step, width, up), (step, width, down)]
        up = around(added(ups[step - 1], up), 1)
        if step < reach - 1:
            down = around(added(downs[step - 1], down), -1)
        if step == 1:
            up, down, opposite = lax.optimization_barrier((up, down, around(terms, reach)))
            all_terms.append((reach, 0, opposite))
    chunk = summed_terms(all_terms, size)
    chunks = [chunk] + [swapped(chunk, "col", partner) for partner in range(1, col_count)]
    return [mine, up, down], chunks


def per_device(features, weight, adj_tiles, tile_rows, tile_cols, tile_counts, out_grad):
    node_rows, width = features.shape
    capacity, side = adj_tiles.shape[2:4]
    tiles = adj_tiles.reshape(capacity, side, side)
    packed = jnp.concatenate([tile_rows, tile_cols, tile_counts[:, :, None]], axis=2).reshape(2 * capacity + 1)
    row_count = lax.axis_size("row")
    col_count = lax.axis_size("col")
    per_strip = node_rows // side
    stages = build_stages(packed, tiles, col_count * per_strip, row_count * per_strip, per_strip)
    shards, dense, cotangents = gathered_shards(features, stages, out_grad)

    for_sibling = forward_product(dense, shards, 1, row_count, col_count)
    for_sibling, cell = lax.optimization_barrier((for_sibling, dense))
    sums = added(forward_product(cell, shards, 0, row_count, col_count), swapped(for_sibling, "col", 1))
    sums = [sums] + [swapped(sums, "col", partner) for partner in range(2, col_count, 2)]
    activations, message, chunk = middle(sums, weight, cotangents, node_rows * row_count * col_count)
    sibling = swapped(message, "col", 1)
    parts, chunks = scattered_sums(dense, message, sibling, chunk)
    grad_features, grad_weight = finish(parts, chunks)
    return (activations, grad_features, grad_weight)


def solution(mesh):
    placed = (
        P(("row", "col"), None),
        P(),
        P("row", "col", None, None, None),
        P("row", "col", None),
        P("row", "col", None),
        P("row", "col"),
        P(("row", "col"), None),
    )
    return jax.shard_map(
        per_device,
        mesh=mesh,
        in_specs=placed,
        out_specs=(P(("row", "col"), None), P(("row", "col"), None), P()),
        check_vma=False,
    )
```

```python
import functools
import math

import jax
import jax.numpy as jnp
from jax import lax
from jax.experimental import pallas as pl
from jax.experimental.pallas import tpu as pltpu
from jax.sharding import PartitionSpec as P

chunk_tiles = 16
chunk_slots = 8
build_grant = 44
strips_per_step = 8
mib = 1024 * 1024


def scratch_bytes(*shapes):
    return sum(math.prod(shape) * jnp.dtype(kind).itemsize for shape, kind in shapes)


def add_tiles(list_ref, tiles_ref, total, seen, held, sems, begin, end, *, base, first_block, blocks, steps):
    side = tiles_ref.shape[1]
    capacity = tiles_ref.shape[0]
    count = list_ref[2 * capacity]
    slots = held.shape[0]
    row_blocks = total.shape[0] // side - 1

    def fetch(index):
        slot = lax.rem(index - begin, slots)
        return pltpu.make_async_copy(
            tiles_ref.at[pl.ds(index * chunk_tiles, chunk_tiles)], held.at[slot], sems.at[slot]
        )

    def start(index, carry):
        fetch(index).start()
        return carry

    lax.fori_loop(begin, jnp.minimum(end, begin + slots), start, 0)

    def forget(index, carry):
        for turn in range(8):
            seen[index * 8 + turn] = 0
        return carry

    lax.fori_loop(0, seen.shape[0] // 8, forget, 0)

    def target(place):
        col = list_ref[capacity + place] - first_block
        live = place < count
        if steps > 1:
            live = live & (col >= 0) & (col < blocks)
            col = jnp.where(live, col, 0)
        row = jnp.where(live, list_ref[place], row_blocks)
        return row, col

    def chunk_step(index, carry):
        fetch(index).wait()
        slot = lax.rem(index - begin, slots)
        for lane in range(0, chunk_tiles, 2):
            spots = [target(index * chunk_tiles + lane + turn) for turn in range(2)]
            at = [
                (pl.ds(pl.multiple_of(row * side, side), side), pl.ds(pl.multiple_of(col * side, side), side))
                for row, col in spots
            ]
            first, second = (
                jnp.where(seen[row * blocks + col] != 0, total[spot], base(row, col))
                for (row, col), spot in zip(spots, at)
            )
            tiles = [held[slot, lane + turn].astype(jnp.float32) for turn in range(2)]
            same = (spots[0][0] == spots[1][0]) & (spots[0][1] == spots[1][1])
            total[at[0]] = first + tiles[0]
            total[at[1]] = second + tiles[1] + jnp.where(same, tiles[0], 0.0)
            for row, col in spots:
                seen[row * blocks + col] = 1

        @pl.when(index + slots < end)
        def _():
            fetch(index + slots).start()

        return carry

    lax.fori_loop(begin, end, chunk_step, 0)


def round_blocks(dense_ref, total, seen, side, blocks, unseen):
    def step(row, carry):
        down = pl.ds(pl.multiple_of(row * side, side), side)
        for col in range(blocks):
            along = pl.ds(col * side, side)
            touched = seen[row * blocks + col] != 0

            @pl.when(touched)
            def _():
                dense_ref[down, along] = total[down, along].astype(jnp.bfloat16)

            @pl.when(jnp.logical_not(touched))
            def _():
                dense_ref[down, along] = unseen(down, along)

        return carry

    lax.fori_loop(0, total.shape[0] // side - 1, step, 0)


def live_chunks(list_ref, tiles_ref):
    return (list_ref[2 * tiles_ref.shape[0]] + chunk_tiles - 1) // chunk_tiles


def build_first_kernel(list_ref, tiles_ref, dense_ref, total, seen, held, sems, *, blocks):
    side = tiles_ref.shape[1]
    half = (live_chunks(list_ref, tiles_ref) + 1) // 2
    add_tiles(
        list_ref, tiles_ref, total, seen, held, sems, 0, half,
        base=lambda row, col: 0.0, first_block=0, blocks=blocks, steps=1,
    )
    round_blocks(
        dense_ref, total, seen, side, blocks, lambda down, along: jnp.zeros((side, side), jnp.bfloat16)
    )


def build_rest_kernel(list_ref, tiles_ref, half_ref, dense_ref, total, seen, held, sems, *, blocks):
    side = tiles_ref.shape[1]
    chunks = live_chunks(list_ref, tiles_ref)
    last = half_ref.shape[0] // side - 1

    def base(row, col):
        down = pl.ds(pl.multiple_of(jnp.minimum(row, last) * side, side), side)
        return half_ref[down, pl.ds(pl.multiple_of(col * side, side), side)].astype(jnp.float32)

    add_tiles(
        list_ref, tiles_ref, total, seen, held, sems, (chunks + 1) // 2, chunks,
        base=base, first_block=0, blocks=blocks, steps=1,
    )
    round_blocks(dense_ref, total, seen, side, blocks, lambda down, along: half_ref[down, along])


def build_whole_kernel(list_ref, tiles_ref, dense_ref, total, seen, held, sems, *, blocks, steps):
    side = tiles_ref.shape[1]
    add_tiles(
        list_ref, tiles_ref, total, seen, held, sems, 0, live_chunks(list_ref, tiles_ref),
        base=lambda row, col: 0.0, first_block=pl.program_id(0) * blocks, blocks=blocks, steps=steps,
    )
    round_blocks(
        dense_ref, total, seen, side, blocks, lambda down, along: jnp.zeros((side, side), jnp.bfloat16)
    )


def build_stages(packed, tiles, row_blocks, col_blocks, per_strip):
    capacity, side, _ = tiles.shape
    blocks = min(strips_per_step * per_strip, col_blocks)
    steps = col_blocks // blocks
    high, wide = row_blocks * side, blocks * side
    total = ((high + side, wide), jnp.float32)
    held = ((min(chunk_slots, capacity // chunk_tiles), chunk_tiles, side, side), jnp.bfloat16)
    cost = pl.CostEstimate(
        flops=capacity * side * side, bytes_accessed=capacity * side * side + high * wide, transcendentals=0
    )
    scratch = [
        pltpu.VMEM(*total),
        pltpu.SMEM((-(-(row_blocks + 1) * blocks // 8) * 8,), jnp.int32),
        pltpu.VMEM(*held),
        pltpu.SemaphoreType.DMA((held[0][0],)),
    ]
    dense_shape = jax.ShapeDtypeStruct((high, col_blocks * side), jnp.bfloat16)
    whole = pl.BlockSpec(memory_space=pltpu.VMEM)
    apart = pl.BlockSpec(memory_space=pl.ANY)
    listed = pl.BlockSpec(memory_space=pltpu.SMEM)
    if steps > 1:
        block = ((high, wide), jnp.bfloat16)
        return [
            lambda _: pl.pallas_call(
                functools.partial(build_whole_kernel, blocks=blocks, steps=steps),
                out_shape=dense_shape,
                grid_spec=pltpu.PrefetchScalarGridSpec(
                    num_scalar_prefetch=1,
                    grid=(steps,),
                    in_specs=[apart],
                    out_specs=pl.BlockSpec((high, wide), lambda i, *_: (0, i)),
                    scratch_shapes=scratch,
                ),
                compiler_params=pltpu.CompilerParams(
                    vmem_limit_bytes=scratch_bytes(total, held, block, block) + 4 * mib
                ),
                cost_estimate=cost,
                name="build_whole",
            )(packed, tiles)
        ]
    params = pltpu.CompilerParams(vmem_limit_bytes=build_grant * mib)
    return [
        lambda _: pl.pallas_call(
            functools.partial(build_first_kernel, blocks=blocks),
            out_shape=dense_shape,
            in_specs=[listed, apart],
            out_specs=whole,
            scratch_shapes=scratch,
            compiler_params=params,
            cost_estimate=cost,
            name="build_first",
        )(packed, tiles),
        lambda half: pl.pallas_call(
            functools.partial(build_rest_kernel, blocks=blocks),
            out_shape=dense_shape,
            in_specs=[listed, apart, whole],
            out_specs=whole,
            scratch_shapes=scratch,
            compiler_params=params,
            cost_estimate=cost,
            name="build_rest",
        )(packed, tiles, half),
    ]


def ring_place(row, count):
    return jnp.where(lax.rem(row, 2) == 0, row // 2, count - 1 - row // 2)


def ring_row(place, count):
    place = lax.rem(place + 2 * count, count)
    return jnp.where(place < count // 2, 2 * place, 2 * (count - 1 - place) + 1)


def forward_kernel(dense_ref, *refs, pieces, sibling, row_count):
    piece_refs, out_ref = refs[: len(pieces)], refs[len(pieces)]
    count = lax.axis_size("col")
    rows = dense_ref.shape[0] // count
    block = dense_ref.shape[1] // row_count
    place = ring_place(lax.axis_index("row"), row_count)
    col = lax.axis_index("col") ^ sibling
    operands = []
    for piece, ref in zip(pieces, piece_refs):
        for offset, first, start, high in piece:
            along = pl.ds(pl.multiple_of(ring_row(place + offset, row_count) * block + first, 128), high)
            operands.append((along, ref, pl.ds(start, high)))
    for index in range(count // 2):
        down = pl.ds(pl.multiple_of((col ^ (2 * index)) * rows, rows), rows)
        total = None
        for along, ref, part in operands:
            product = jnp.dot(dense_ref[down, along], ref[part, :], preferred_element_type=jnp.float32)
            total = product if total is None else total + product
        out_ref[pl.ds(index * rows, rows), :] = total.astype(jnp.bfloat16)


def forward_product(dense, shards, sibling, row_count, col_count):
    pieces = tuple(piece for piece, _ in shards)
    arrays = [array for _, array in shards]
    high, deep = dense.shape
    width = arrays[0].shape[1]
    half = high // 2
    cell = ((high, deep), jnp.bfloat16)
    depth = ((deep, width), jnp.bfloat16)
    out = ((high, width), jnp.float32)
    return pl.pallas_call(
        functools.partial(forward_kernel, pieces=pieces, sibling=sibling, row_count=row_count),
        out_shape=jax.ShapeDtypeStruct((half, width), jnp.bfloat16),
        in_specs=[pl.BlockSpec(memory_space=pltpu.VMEM)] * (1 + len(arrays)),
        out_specs=pl.BlockSpec(memory_space=pltpu.VMEM),
        compiler_params=pltpu.CompilerParams(vmem_limit_bytes=scratch_bytes(cell, depth, out) + 6 * mib),
        cost_estimate=pl.CostEstimate(
            flops=2 * half * deep * width,
            bytes_accessed=2 * (half * deep + deep * width + half * width),
            transcendentals=0,
        ),
        name="forward_product",
    )(dense, *arrays)


def middle_kernel(*refs, blocks, scale):
    sums, refs = refs[:blocks], refs[blocks:]
    weight_ref, refs = refs[0], refs[1:]
    cotangent_refs, (act_ref, message_ref, chunk_ref, product) = refs[:blocks], refs[blocks:]
    weight = weight_ref[...]
    rows, width = act_ref.shape
    over_nodes = (((0,), (0,)), ((), ()))
    terms = None
    for index in range(blocks):
        aggregate = sums[0][pl.ds(index * rows, rows), :].astype(jnp.float32)
        for other in range(1, blocks):
            aggregate += sums[other][pl.ds((index ^ other) * rows, rows), :].astype(jnp.float32)
        high = aggregate.astype(jnp.bfloat16)
        low = (aggregate - high.astype(jnp.float32)).astype(jnp.bfloat16)
        pre = jnp.dot(high, weight, preferred_element_type=jnp.float32)
        pre += jnp.dot(low, weight, preferred_element_type=jnp.float32)
        sig = jax.nn.sigmoid(pre)
        cotangent = cotangent_refs[index][...].astype(jnp.float32)
        grad = (cotangent * sig * (1.0 + pre * (1.0 - sig))).astype(jnp.bfloat16)
        message_ref[pl.ds(index * width, width), :] = lax.dot_general(
            weight, grad, (((1,), (1,)), ((), ())), preferred_element_type=jnp.float32
        ).astype(jnp.bfloat16)
        if index == 0:
            act_ref[...] = (pre * sig).astype(jnp.bfloat16)
        part = lax.dot_general(high, grad, over_nodes, preferred_element_type=jnp.float32)
        part += lax.dot_general(low, grad, over_nodes, preferred_element_type=jnp.float32)
        terms = part if terms is None else terms + part
    product[...] = terms * scale
    col = lax.axis_index("col")
    size = chunk_ref.shape[0]
    chunk_ref[...] = product[pl.ds(pl.multiple_of(col * size, size), size), :]
    sent = product[pl.ds(pl.multiple_of((col ^ 1) * size, size), size), :]
    high = sent.astype(jnp.bfloat16)
    low = (sent - high.astype(jnp.float32)).astype(jnp.bfloat16)
    message_ref[pl.ds(blocks * width, size), :] = high
    message_ref[pl.ds(blocks * width + size, size), :] = low


def middle(sums, weight, cotangents, total_nodes):
    rows, width = cotangents[0].shape
    blocks = len(cotangents)
    size = width // (2 * blocks)
    return pl.pallas_call(
        functools.partial(middle_kernel, blocks=blocks, scale=1.0 / math.sqrt(total_nodes)),
        out_shape=[
            jax.ShapeDtypeStruct((rows, width), jnp.bfloat16),
            jax.ShapeDtypeStruct((blocks * width + 2 * size, rows), jnp.bfloat16),
            jax.ShapeDtypeStruct((size, width), jnp.float32),
        ],
        in_specs=[pl.BlockSpec(memory_space=pltpu.VMEM)] * (2 * blocks + 1),
        out_specs=[pl.BlockSpec(memory_space=pltpu.VMEM)] * 3,
        scratch_shapes=[pltpu.VMEM((width, width), jnp.float32)],
        compiler_params=pltpu.CompilerParams(vmem_limit_bytes=12 * mib),
        cost_estimate=pl.CostEstimate(
            flops=10 * blocks * rows * width * width,
            bytes_accessed=2 * (blocks * blocks + 2 * blocks + 4) * rows * width,
            transcendentals=blocks * rows * width,
        ),
        name="middle",
    )(*sums, weight, *cotangents)


def backward_kernel(dense_ref, own_ref, sibling_ref, chunk_ref, *refs, outputs, row_count):
    out_refs, (depth, sems) = refs[:-2], refs[-2:]
    count = lax.axis_size("col")
    width, rows = depth.shape[0], own_ref.shape[1]
    wide = dense_ref.shape[1] // row_count
    col = lax.axis_index("col")
    copies = []
    for index in range(count):
        block = pl.ds(index // 2 * width, width)
        along = pl.ds(pl.multiple_of((col ^ index) * rows, rows), rows)
        source = sibling_ref if index % 2 else own_ref
        copy = pltpu.make_async_copy(source.at[block], depth.at[:, along], sems.at[index])
        copy.start()
        copies.append(copy)
    size = chunk_ref.shape[0]
    from_sibling = count // 2 * width
    high, low = (sibling_ref[pl.ds(from_sibling + turn * size, size), :].astype(jnp.float32) for turn in range(2))
    terms = (chunk_ref[...] + (high + low)).astype(jnp.bfloat16)
    for copy in copies:
        copy.wait()
    place = ring_place(lax.axis_index("row"), row_count)
    for (offset, tail), out_ref in zip(outputs, out_refs):
        if tail != "terms alone":
            along = pl.ds(pl.multiple_of(ring_row(place + offset, row_count) * wide, wide), wide)
            part = jnp.dot(depth[...], dense_ref[:, along], preferred_element_type=jnp.float32)
            out_ref[pl.ds(0, width), :] = part.astype(jnp.bfloat16)
        if tail == "terms alone":
            out_ref[...] = terms
        elif tail == "terms":
            out_ref[pl.ds(width, size), :] = terms
        elif tail == "zeros":
            out_ref[pl.ds(width, size), :] = jnp.zeros_like(terms)


def backward_product(dense, own, sibling, chunk, outputs, row_count, col_count):
    high, deep = dense.shape
    size, width = chunk.shape
    wide = deep // row_count
    heights = {"": width, "terms alone": size, "terms": width + size, "zeros": width + size}
    cell = ((high, deep), jnp.bfloat16)
    depth = ((width, high), jnp.bfloat16)
    out = ((len(outputs), width + size, wide), jnp.float32)
    return pl.pallas_call(
        functools.partial(backward_kernel, outputs=outputs, row_count=row_count),
        out_shape=[jax.ShapeDtypeStruct((heights[tail], wide), jnp.bfloat16) for _, tail in outputs],
        in_specs=[pl.BlockSpec(memory_space=pltpu.VMEM)] * 4,
        out_specs=[pl.BlockSpec(memory_space=pltpu.VMEM)] * len(outputs),
        scratch_shapes=[pltpu.VMEM(*depth), pltpu.SemaphoreType.DMA((col_count,))],
        compiler_params=pltpu.CompilerParams(vmem_limit_bytes=scratch_bytes(cell, depth, out) + 6 * mib),
        cost_estimate=pl.CostEstimate(
            flops=2 * high * wide * width, bytes_accessed=2 * wide * len(outputs) * width, transcendentals=0
        ),
        name="backward_product",
    )(dense, own, sibling, chunk)


def terms_kernel(*refs, offsets, first_rows):
    term_refs, out_ref, places = refs[:-2], refs[-2], refs[-1]
    row_count, size, _ = places.shape
    place = ring_place(lax.axis_index("row"), row_count)
    for offset, first, ref in zip(offsets, first_rows, term_refs):
        places[ring_row(place + offset, row_count)] = ref[pl.ds(first, size), :].astype(jnp.float32)
    total = places[0]
    for index in range(1, row_count):
        total += places[index]
    out_ref[...] = total


def summed_terms(terms, size):
    offsets = tuple(offset for offset, _, _ in terms)
    first_rows = tuple(first for _, first, _ in terms)
    arrays = [array for _, _, array in terms]
    width = arrays[0].shape[1]
    return pl.pallas_call(
        functools.partial(terms_kernel, offsets=offsets, first_rows=first_rows),
        out_shape=jax.ShapeDtypeStruct((size, width), jnp.float32),
        in_specs=[pl.BlockSpec(memory_space=pltpu.VMEM)] * len(arrays),
        out_specs=pl.BlockSpec(memory_space=pltpu.VMEM),
        scratch_shapes=[pltpu.VMEM((len(arrays), size, width), jnp.float32)],
        compiler_params=pltpu.CompilerParams(
            vmem_limit_bytes=scratch_bytes(*((array.shape, array.dtype) for array in arrays)) + 8 * mib
        ),
        cost_estimate=pl.CostEstimate(
            flops=len(arrays) * size * width, bytes_accessed=2 * len(arrays) * size * width, transcendentals=0
        ),
        name="summed_terms",
    )(*arrays)


def finish_kernel(*refs, parts):
    part_refs, chunk_refs, (features_ref, weight_ref) = refs[:parts], refs[parts:-2], refs[-2:]
    width = features_ref.shape[1]
    total = part_refs[0][pl.ds(0, width), :].astype(jnp.float32)
    for part_ref in part_refs[1:]:
        total += part_ref[pl.ds(0, width), :].astype(jnp.float32)
    features_ref[...] = total.astype(jnp.bfloat16).T
    rows = chunk_refs[0].shape[0]
    col = lax.axis_index("col")
    for partner, chunk_ref in enumerate(chunk_refs):
        weight_ref[pl.ds(pl.multiple_of((col ^ partner) * rows, rows), rows), :] = chunk_ref[...]


def finish(parts, chunks):
    width, rows = parts[0].shape
    return pl.pallas_call(
        functools.partial(finish_kernel, parts=len(parts)),
        out_shape=[
            jax.ShapeDtypeStruct((rows, width), jnp.bfloat16),
            jax.ShapeDtypeStruct((width, width), jnp.float32),
        ],
        in_specs=[pl.BlockSpec(memory_space=pltpu.VMEM)] * (len(parts) + len(chunks)),
        out_specs=[pl.BlockSpec(memory_space=pltpu.VMEM)] * 2,
        compiler_params=pltpu.CompilerParams(vmem_limit_bytes=8 * mib),
        cost_estimate=pl.CostEstimate(
            flops=len(parts) * rows * width, bytes_accessed=2 * (len(parts) + 5) * rows * width, transcendentals=0
        ),
        name="finish",
    )(*parts, *chunks)


def around(value, step):
    count = lax.axis_size("row")
    order = list(range(0, count, 2)) + list(range(count - 1, 0, -2))
    return lax.ppermute(value, "row", [(order[i], order[(i + step) % count]) for i in range(count)])


def swapped(value, axis, partner):
    return lax.ppermute(value, axis, [(i, i ^ partner) for i in range(lax.axis_size(axis))])


def gathered_shards(own, stages, cotangent):
    reach = lax.axis_size("row") // 2
    rows = own.shape[0]
    shards = [(((0, 0, 0, rows),), own)]
    up = down = own
    beside = None
    cotangents = [cotangent]
    for step in range(1, reach + 1):
        up = around(up, 1)
        if step < reach:
            down = around(down, -1)
        if step <= len(stages):
            up, down, beside = lax.optimization_barrier((up, down, stages[step - 1](beside)))
        elif step == reach:
            others = [swapped(cotangent, "col", partner) for partner in range(2, lax.axis_size("col"), 2)]
            up, others = lax.optimization_barrier((up, others))
            cotangents += others
        shards.append((((-step, 0, 0, rows),), up))
        if step < reach:
            shards.append((((step, 0, 0, rows),), down))
    return shards, beside, cotangents


def added(first, second):
    return (first.astype(jnp.float32) + second[: first.shape[0]].astype(jnp.float32)).astype(jnp.bfloat16)


def scattered_sums(dense, own, sibling, chunk):
    row_count, col_count = lax.axis_size("row"), lax.axis_size("col")
    size, width = chunk.shape
    reach = row_count // 2
    first = ((reach, "terms"), (1 - reach, "terms"), (0, "terms alone"))
    above, below, terms = backward_product(dense, own, sibling, chunk, first, row_count, col_count)
    above, below, terms, cell = lax.optimization_barrier((above, below, terms, dense))
    up, down = around(above, 1), around(below, -1)
    all_terms = [(0, 0, terms)]

    ups = tuple((offset, "zeros" if offset > 1 else "") for offset in range(reach - 1, 0, -1))
    downs = tuple((-offset, "zeros") for offset in range(reach - 2, 0, -1))
    strips = backward_product(cell, own, sibling, chunk, ups + downs + ((0, ""),), row_count, col_count)
    ups, downs, mine = strips[: reach - 1], strips[reach - 1 : -1], strips[-1]
    for step in range(1, reach):
        all_terms += [(-step, width, up), (step, width, down)]
        if step == reach - 1:
            all_terms.append((reach, 0, around(down[width:], -1)))
        up = around(added(ups[step - 1], up), 1)
        if step < reach - 1:
            down = around(added(downs[step - 1], down), -1)
    chunk = summed_terms(all_terms, size)
    chunks = [chunk] + [swapped(chunk, "col", partner) for partner in range(1, col_count)]
    return [mine, up, down], chunks


def per_device(features, weight, adj_tiles, tile_rows, tile_cols, tile_counts, out_grad):
    node_rows, width = features.shape
    capacity, side = adj_tiles.shape[2:4]
    tiles = adj_tiles.reshape(capacity, side, side)
    packed = jnp.concatenate([tile_rows, tile_cols, tile_counts[:, :, None]], axis=2).reshape(2 * capacity + 1)
    row_count = lax.axis_size("row")
    col_count = lax.axis_size("col")
    per_strip = node_rows // side
    stages = build_stages(packed, tiles, col_count * per_strip, row_count * per_strip, per_strip)
    shards, dense, cotangents = gathered_shards(features, stages, out_grad)

    for_sibling = forward_product(dense, shards, 1, row_count, col_count)
    for_sibling, cell = lax.optimization_barrier((for_sibling, dense))
    sums = added(forward_product(cell, shards, 0, row_count, col_count), swapped(for_sibling, "col", 1))
    sums = [sums] + [swapped(sums, "col", partner) for partner in range(2, col_count, 2)]
    activations, message, chunk = middle(sums, weight, cotangents, node_rows * row_count * col_count)
    sibling = swapped(message, "col", 1)
    parts, chunks = scattered_sums(dense, message, sibling, chunk)
    grad_features, grad_weight = finish(parts, chunks)
    return (activations, grad_features, grad_weight)


def solution(mesh):
    placed = (
        P(("row", "col"), None),
        P(),
        P("row", "col", None, None, None),
        P("row", "col", None),
        P("row", "col", None),
        P("row", "col"),
        P(("row", "col"), None),
    )
    return jax.shard_map(
        per_device,
        mesh=mesh,
        in_specs=placed,
        out_specs=(P(("row", "col"), None), P(("row", "col"), None), P()),
        check_vma=False,
    )
```

```python
import functools
import math

import jax
import jax.numpy as jnp
from jax import lax
from jax.experimental import pallas as pl
from jax.experimental.pallas import tpu as pltpu
from jax.sharding import PartitionSpec as P

chunk_tiles = 16
chunk_slots = 8
build_grant = 44
strips_per_step = 8
mib = 1024 * 1024


def scratch_bytes(*shapes):
    return sum(math.prod(shape) * jnp.dtype(kind).itemsize for shape, kind in shapes)


def add_tiles(list_ref, tiles_ref, total, held, sems, begin, end, *, first_block, blocks, steps):
    side = tiles_ref.shape[1]
    capacity = tiles_ref.shape[0]
    count = list_ref[2 * capacity]
    slots = held.shape[0]
    row_blocks = total.shape[0] // side - 1

    def fetch(index):
        slot = lax.rem(index - begin, slots)
        return pltpu.make_async_copy(
            tiles_ref.at[pl.ds(index * chunk_tiles, chunk_tiles)], held.at[slot], sems.at[slot]
        )

    def start(index, carry):
        fetch(index).start()
        return carry

    lax.fori_loop(begin, jnp.minimum(end, begin + slots), start, 0)

    def target(place):
        col = list_ref[capacity + place] - first_block
        live = place < count
        if steps > 1:
            live = live & (col >= 0) & (col < blocks)
            col = jnp.where(live, col, 0)
        row = jnp.where(live, list_ref[place], row_blocks)
        return row, col

    def chunk_step(index, carry):
        fetch(index).wait()
        slot = lax.rem(index - begin, slots)
        for lane in range(0, chunk_tiles, 2):
            spots = [target(index * chunk_tiles + lane + turn) for turn in range(2)]
            at = [
                (pl.ds(pl.multiple_of(row * side, side), side), pl.ds(pl.multiple_of(col * side, side), side))
                for row, col in spots
            ]
            first, second = total[at[0]], total[at[1]]
            tiles = [held[slot, lane + turn].astype(jnp.float32) for turn in range(2)]
            same = (spots[0][0] == spots[1][0]) & (spots[0][1] == spots[1][1])
            total[at[0]] = first + tiles[0]
            total[at[1]] = second + tiles[1] + jnp.where(same, tiles[0], 0.0)

        @pl.when(index + slots < end)
        def _():
            fetch(index + slots).start()

        return carry

    return lambda: lax.fori_loop(begin, end, chunk_step, 0)


def each_row_block(total, side, action):
    def step(block, carry):
        action(pl.ds(pl.multiple_of(block * side, side), side))
        return carry

    lax.fori_loop(0, total.shape[0] // side - 1, step, 0)


def live_chunks(list_ref, tiles_ref):
    return (list_ref[2 * tiles_ref.shape[0]] + chunk_tiles - 1) // chunk_tiles


def build_first_kernel(list_ref, tiles_ref, dense_ref, total, held, sems, *, blocks):
    half = (live_chunks(list_ref, tiles_ref) + 1) // 2
    run = add_tiles(list_ref, tiles_ref, total, held, sems, 0, half, first_block=0, blocks=blocks, steps=1)

    def clear(down):
        total[down, :] = jnp.zeros((down.size, total.shape[1]), jnp.float32)

    def rounded(down):
        dense_ref[down, :] = total[down, :].astype(jnp.bfloat16)

    each_row_block(total, tiles_ref.shape[1], clear)
    run()
    each_row_block(total, tiles_ref.shape[1], rounded)


def build_rest_kernel(list_ref, tiles_ref, half_ref, dense_ref, total, held, sems, *, blocks):
    chunks = live_chunks(list_ref, tiles_ref)
    run = add_tiles(
        list_ref, tiles_ref, total, held, sems, (chunks + 1) // 2, chunks, first_block=0, blocks=blocks, steps=1
    )

    def widened(down):
        total[down, :] = half_ref[down, :].astype(jnp.float32)

    def rounded(down):
        dense_ref[down, :] = total[down, :].astype(jnp.bfloat16)

    each_row_block(total, tiles_ref.shape[1], widened)
    run()
    each_row_block(total, tiles_ref.shape[1], rounded)


def build_whole_kernel(list_ref, tiles_ref, dense_ref, total, held, sems, *, blocks, steps):
    chunks = live_chunks(list_ref, tiles_ref)
    first_block = pl.program_id(0) * blocks
    run = add_tiles(
        list_ref, tiles_ref, total, held, sems, 0, chunks, first_block=first_block, blocks=blocks, steps=steps
    )

    def clear(down):
        total[down, :] = jnp.zeros((down.size, total.shape[1]), jnp.float32)

    def rounded(down):
        dense_ref[down, :] = total[down, :].astype(jnp.bfloat16)

    each_row_block(total, tiles_ref.shape[1], clear)
    run()
    each_row_block(total, tiles_ref.shape[1], rounded)


def build_stages(tiles, row_blocks, col_blocks, per_strip):
    capacity, side, _ = tiles.shape
    blocks = min(strips_per_step * per_strip, col_blocks)
    steps = col_blocks // blocks
    high, wide = row_blocks * side, blocks * side
    total = ((high + side, wide), jnp.float32)
    held = ((min(chunk_slots, capacity // chunk_tiles), chunk_tiles, side, side), jnp.bfloat16)
    cost = pl.CostEstimate(
        flops=capacity * side * side, bytes_accessed=capacity * side * side + high * wide, transcendentals=0
    )
    held_scratch = [pltpu.VMEM(*held), pltpu.SemaphoreType.DMA((held[0][0],))]
    dense_shape = jax.ShapeDtypeStruct((high, col_blocks * side), jnp.bfloat16)
    whole = pl.BlockSpec(memory_space=pltpu.VMEM)
    apart = pl.BlockSpec(memory_space=pl.ANY)
    listed = pl.BlockSpec(memory_space=pltpu.SMEM)
    if steps > 1:
        block = ((high, wide), jnp.bfloat16)
        return [
            lambda packed: pl.pallas_call(
                functools.partial(build_whole_kernel, blocks=blocks, steps=steps),
                out_shape=dense_shape,
                grid_spec=pltpu.PrefetchScalarGridSpec(
                    num_scalar_prefetch=1,
                    grid=(steps,),
                    in_specs=[apart],
                    out_specs=pl.BlockSpec((high, wide), lambda i, *_: (0, i)),
                    scratch_shapes=[pltpu.VMEM(*total)] + held_scratch,
                ),
                compiler_params=pltpu.CompilerParams(
                    vmem_limit_bytes=scratch_bytes(total, held, block, block) + 4 * mib
                ),
                cost_estimate=cost,
                name="build_whole",
            )(packed, tiles)
        ]
    params = pltpu.CompilerParams(vmem_limit_bytes=build_grant * mib)
    scratch = [pltpu.VMEM(*total)] + held_scratch
    return [
        lambda packed: (packed, pl.pallas_call(
            functools.partial(build_first_kernel, blocks=blocks),
            out_shape=dense_shape,
            in_specs=[listed, apart],
            out_specs=whole,
            scratch_shapes=scratch,
            compiler_params=params,
            cost_estimate=cost,
            name="build_first",
        )(packed, tiles)),
        lambda state: pl.pallas_call(
            functools.partial(build_rest_kernel, blocks=blocks),
            out_shape=dense_shape,
            in_specs=[listed, apart, whole],
            out_specs=whole,
            scratch_shapes=scratch,
            compiler_params=params,
            cost_estimate=cost,
            name="build_rest",
        )(state[0], tiles, state[1]),
    ]


def ring_place(row, count):
    return jnp.where(lax.rem(row, 2) == 0, row // 2, count - 1 - row // 2)


def ring_row(place, count):
    place = lax.rem(place + 2 * count, count)
    return jnp.where(place < count // 2, 2 * place, 2 * (count - 1 - place) + 1)


def forward_kernel(dense_ref, *refs, pieces, sibling, row_count):
    piece_refs, out_ref = refs[: len(pieces)], refs[len(pieces)]
    count = lax.axis_size("col")
    rows = dense_ref.shape[0] // count
    block = dense_ref.shape[1] // row_count
    place = ring_place(lax.axis_index("row"), row_count)
    col = lax.axis_index("col") ^ sibling
    operands = []
    for piece, ref in zip(pieces, piece_refs):
        for offset, first, start, high in piece:
            along = pl.ds(pl.multiple_of(ring_row(place + offset, row_count) * block + first, 128), high)
            operands.append((along, ref, pl.ds(start, high)))
    for index in range(count // 2):
        down = pl.ds(pl.multiple_of((col ^ (2 * index)) * rows, rows), rows)
        total = None
        for along, ref, part in operands:
            product = jnp.dot(dense_ref[down, along], ref[part, :], preferred_element_type=jnp.float32)
            total = product if total is None else total + product
        out_ref[pl.ds(index * rows, rows), :] = total.astype(jnp.bfloat16)


def forward_product(dense, shards, sibling, row_count, col_count):
    pieces = tuple(piece for piece, _ in shards)
    arrays = [array for _, array in shards]
    high, deep = dense.shape
    width = arrays[0].shape[1]
    half = high // 2
    cell = ((high, deep), jnp.bfloat16)
    depth = ((deep, width), jnp.bfloat16)
    out = ((high, width), jnp.float32)
    return pl.pallas_call(
        functools.partial(forward_kernel, pieces=pieces, sibling=sibling, row_count=row_count),
        out_shape=jax.ShapeDtypeStruct((half, width), jnp.bfloat16),
        in_specs=[pl.BlockSpec(memory_space=pltpu.VMEM)] * (1 + len(arrays)),
        out_specs=pl.BlockSpec(memory_space=pltpu.VMEM),
        compiler_params=pltpu.CompilerParams(vmem_limit_bytes=scratch_bytes(cell, depth, out) + 6 * mib),
        cost_estimate=pl.CostEstimate(
            flops=2 * half * deep * width,
            bytes_accessed=2 * (half * deep + deep * width + half * width),
            transcendentals=0,
        ),
        name="forward_product",
    )(dense, *arrays)


def middle_kernel(*refs, blocks, scale):
    sums, refs = refs[:blocks], refs[blocks:]
    weight_ref, refs = refs[0], refs[1:]
    cotangent_refs, (act_ref, message_ref, chunk_ref, product) = refs[:blocks], refs[blocks:]
    weight = weight_ref[...]
    rows, width = act_ref.shape
    over_nodes = (((0,), (0,)), ((), ()))
    terms = None
    for index in range(blocks):
        aggregate = sums[0][pl.ds(index * rows, rows), :].astype(jnp.float32)
        for other in range(1, blocks):
            aggregate += sums[other][pl.ds((index ^ other) * rows, rows), :].astype(jnp.float32)
        high = aggregate.astype(jnp.bfloat16)
        low = (aggregate - high.astype(jnp.float32)).astype(jnp.bfloat16)
        pre = jnp.dot(high, weight, preferred_element_type=jnp.float32)
        pre += jnp.dot(low, weight, preferred_element_type=jnp.float32)
        sig = jax.nn.sigmoid(pre)
        cotangent = cotangent_refs[index][...].astype(jnp.float32)
        grad = (cotangent * sig * (1.0 + pre * (1.0 - sig))).astype(jnp.bfloat16)
        message_ref[pl.ds(index * width, width), :] = lax.dot_general(
            weight, grad, (((1,), (1,)), ((), ())), preferred_element_type=jnp.float32
        ).astype(jnp.bfloat16)
        if index == 0:
            act_ref[...] = (pre * sig).astype(jnp.bfloat16)
        part = lax.dot_general(high, grad, over_nodes, preferred_element_type=jnp.float32)
        part += lax.dot_general(low, grad, over_nodes, preferred_element_type=jnp.float32)
        terms = part if terms is None else terms + part
    product[...] = terms * scale
    col = lax.axis_index("col")
    size = chunk_ref.shape[0]
    chunk_ref[...] = product[pl.ds(pl.multiple_of(col * size, size), size), :]
    sent = product[pl.ds(pl.multiple_of((col ^ 1) * size, size), size), :]
    high = sent.astype(jnp.bfloat16)
    low = (sent - high.astype(jnp.float32)).astype(jnp.bfloat16)
    message_ref[pl.ds(blocks * width, size), :] = high
    message_ref[pl.ds(blocks * width + size, size), :] = low


def middle(sums, weight, cotangents, total_nodes):
    rows, width = cotangents[0].shape
    blocks = len(cotangents)
    size = width // (2 * blocks)
    return pl.pallas_call(
        functools.partial(middle_kernel, blocks=blocks, scale=1.0 / math.sqrt(total_nodes)),
        out_shape=[
            jax.ShapeDtypeStruct((rows, width), jnp.bfloat16),
            jax.ShapeDtypeStruct((blocks * width + 2 * size, rows), jnp.bfloat16),
            jax.ShapeDtypeStruct((size, width), jnp.float32),
        ],
        in_specs=[pl.BlockSpec(memory_space=pltpu.VMEM)] * (2 * blocks + 1),
        out_specs=[pl.BlockSpec(memory_space=pltpu.VMEM)] * 3,
        scratch_shapes=[pltpu.VMEM((width, width), jnp.float32)],
        compiler_params=pltpu.CompilerParams(vmem_limit_bytes=12 * mib),
        cost_estimate=pl.CostEstimate(
            flops=10 * blocks * rows * width * width,
            bytes_accessed=2 * (blocks * blocks + 2 * blocks + 4) * rows * width,
            transcendentals=blocks * rows * width,
        ),
        name="middle",
    )(*sums, weight, *cotangents)


def backward_kernel(dense_ref, own_ref, sibling_ref, chunk_ref, *refs, outputs, row_count):
    out_refs, (depth, sems) = refs[:-2], refs[-2:]
    count = lax.axis_size("col")
    width, rows = depth.shape[0], own_ref.shape[1]
    wide = dense_ref.shape[1] // row_count
    col = lax.axis_index("col")
    copies = []
    for index in range(count):
        block = pl.ds(index // 2 * width, width)
        along = pl.ds(pl.multiple_of((col ^ index) * rows, rows), rows)
        source = sibling_ref if index % 2 else own_ref
        copy = pltpu.make_async_copy(source.at[block], depth.at[:, along], sems.at[index])
        copy.start()
        copies.append(copy)
    size = chunk_ref.shape[0]
    from_sibling = count // 2 * width
    high, low = (sibling_ref[pl.ds(from_sibling + turn * size, size), :].astype(jnp.float32) for turn in range(2))
    terms = (chunk_ref[...] + (high + low)).astype(jnp.bfloat16)
    for copy in copies:
        copy.wait()
    place = ring_place(lax.axis_index("row"), row_count)
    for (offset, tail), out_ref in zip(outputs, out_refs):
        if tail != "terms alone":
            along = pl.ds(pl.multiple_of(ring_row(place + offset, row_count) * wide, wide), wide)
            part = jnp.dot(depth[...], dense_ref[:, along], preferred_element_type=jnp.float32)
            out_ref[pl.ds(0, width), :] = part.astype(jnp.bfloat16)
        if tail == "terms alone":
            out_ref[...] = terms
        elif tail == "terms":
            out_ref[pl.ds(width, size), :] = terms
        elif tail == "zeros":
            out_ref[pl.ds(width, size), :] = jnp.zeros_like(terms)


def backward_product(dense, own, sibling, chunk, outputs, row_count, col_count):
    high, deep = dense.shape
    size, width = chunk.shape
    wide = deep // row_count
    heights = {"": width, "terms alone": size, "terms": width + size, "zeros": width + size}
    cell = ((high, deep), jnp.bfloat16)
    depth = ((width, high), jnp.bfloat16)
    out = ((len(outputs), width + size, wide), jnp.float32)
    return pl.pallas_call(
        functools.partial(backward_kernel, outputs=outputs, row_count=row_count),
        out_shape=[jax.ShapeDtypeStruct((heights[tail], wide), jnp.bfloat16) for _, tail in outputs],
        in_specs=[pl.BlockSpec(memory_space=pltpu.VMEM)] * 4,
        out_specs=[pl.BlockSpec(memory_space=pltpu.VMEM)] * len(outputs),
        scratch_shapes=[pltpu.VMEM(*depth), pltpu.SemaphoreType.DMA((col_count,))],
        compiler_params=pltpu.CompilerParams(vmem_limit_bytes=scratch_bytes(cell, depth, out) + 6 * mib),
        cost_estimate=pl.CostEstimate(
            flops=2 * high * wide * width, bytes_accessed=2 * wide * len(outputs) * width, transcendentals=0
        ),
        name="backward_product",
    )(dense, own, sibling, chunk)


def terms_kernel(*refs, offsets, first_rows):
    term_refs, out_ref, places = refs[:-2], refs[-2], refs[-1]
    row_count, size, _ = places.shape
    place = ring_place(lax.axis_index("row"), row_count)
    for offset, first, ref in zip(offsets, first_rows, term_refs):
        places[ring_row(place + offset, row_count)] = ref[pl.ds(first, size), :].astype(jnp.float32)
    total = places[0]
    for index in range(1, row_count):
        total += places[index]
    out_ref[...] = total


def summed_terms(terms, size):
    offsets = tuple(offset for offset, _, _ in terms)
    first_rows = tuple(first for _, first, _ in terms)
    arrays = [array for _, _, array in terms]
    width = arrays[0].shape[1]
    return pl.pallas_call(
        functools.partial(terms_kernel, offsets=offsets, first_rows=first_rows),
        out_shape=jax.ShapeDtypeStruct((size, width), jnp.float32),
        in_specs=[pl.BlockSpec(memory_space=pltpu.VMEM)] * len(arrays),
        out_specs=pl.BlockSpec(memory_space=pltpu.VMEM),
        scratch_shapes=[pltpu.VMEM((len(arrays), size, width), jnp.float32)],
        compiler_params=pltpu.CompilerParams(
            vmem_limit_bytes=scratch_bytes(*((array.shape, array.dtype) for array in arrays)) + 8 * mib
        ),
        cost_estimate=pl.CostEstimate(
            flops=len(arrays) * size * width, bytes_accessed=2 * len(arrays) * size * width, transcendentals=0
        ),
        name="summed_terms",
    )(*arrays)


def finish_kernel(*refs, parts):
    part_refs, chunk_refs, (features_ref, weight_ref) = refs[:parts], refs[parts:-2], refs[-2:]
    width = features_ref.shape[1]
    total = part_refs[0][pl.ds(0, width), :].astype(jnp.float32)
    for part_ref in part_refs[1:]:
        total += part_ref[pl.ds(0, width), :].astype(jnp.float32)
    features_ref[...] = total.astype(jnp.bfloat16).T
    rows = chunk_refs[0].shape[0]
    col = lax.axis_index("col")
    for partner, chunk_ref in enumerate(chunk_refs):
        weight_ref[pl.ds(pl.multiple_of((col ^ partner) * rows, rows), rows), :] = chunk_ref[...]


def finish(parts, chunks):
    width, rows = parts[0].shape
    return pl.pallas_call(
        functools.partial(finish_kernel, parts=len(parts)),
        out_shape=[
            jax.ShapeDtypeStruct((rows, width), jnp.bfloat16),
            jax.ShapeDtypeStruct((width, width), jnp.float32),
        ],
        in_specs=[pl.BlockSpec(memory_space=pltpu.VMEM)] * (len(parts) + len(chunks)),
        out_specs=[pl.BlockSpec(memory_space=pltpu.VMEM)] * 2,
        compiler_params=pltpu.CompilerParams(vmem_limit_bytes=8 * mib),
        cost_estimate=pl.CostEstimate(
            flops=len(parts) * rows * width, bytes_accessed=2 * (len(parts) + 5) * rows * width, transcendentals=0
        ),
        name="finish",
    )(*parts, *chunks)


def around(value, step):
    count = lax.axis_size("row")
    order = list(range(0, count, 2)) + list(range(count - 1, 0, -2))
    return lax.ppermute(value, "row", [(order[i], order[(i + step) % count]) for i in range(count)])


def swapped(value, axis, partner):
    return lax.ppermute(value, axis, [(i, i ^ partner) for i in range(lax.axis_size(axis))])


def gathered_shards(own, packed, stages, cotangent):
    reach = lax.axis_size("row") // 2
    rows = own.shape[0]
    shards = [(((0, 0, 0, rows),), own)]
    up = down = own
    dense = packed
    others = [swapped(cotangent, "col", partner) for partner in range(2, lax.axis_size("col"), 2)]
    for step in range(1, reach + 1):
        up = around(up, 1)
        if step < reach:
            down = around(down, -1)
        if step == 1:
            up, down, dense, others = lax.optimization_barrier((up, down, dense, others))
        elif step in (2, reach):
            dense = stages.pop(0)(dense) if stages else dense
        if 1 < step < reach:
            up, down, dense = lax.optimization_barrier((up, down, dense))
        shards.append((((-step, 0, 0, rows),), up))
        if step < reach:
            shards.append((((step, 0, 0, rows),), down))
    return shards, dense, [cotangent] + others


def added(first, second):
    return (first.astype(jnp.float32) + second[: first.shape[0]].astype(jnp.float32)).astype(jnp.bfloat16)


def scattered_sums(dense, own, sibling, chunk):
    row_count, col_count = lax.axis_size("row"), lax.axis_size("col")
    size, width = chunk.shape
    reach = row_count // 2
    first = ((reach, "terms"), (1 - reach, "terms"), (0, "terms alone"))
    above, below, terms = backward_product(dense, own, sibling, chunk, first, row_count, col_count)
    above, below, terms, cell = lax.optimization_barrier((above, below, terms, dense))
    up, down = around(above, 1), around(below, -1)
    all_terms = [(0, 0, terms)]

    ups = tuple((offset, "zeros" if offset > 1 else "") for offset in range(reach - 1, 0, -1))
    downs = tuple((-offset, "zeros") for offset in range(reach - 2, 0, -1))
    strips = backward_product(cell, own, sibling, chunk, ups + downs + ((0, ""),), row_count, col_count)
    ups, downs, mine = strips[: reach - 1], strips[reach - 1 : -1], strips[-1]
    for step in range(1, reach):
        all_terms += [(-step, width, up), (step, width, down)]
        relayed = around(down[width:], -2) if step == reach - 2 else None
        up = around(added(ups[step - 1], up), 1)
        if step < reach - 1:
            down = around(added(downs[step - 1], down), -1)
        if relayed is not None:
            up, down, relayed = lax.optimization_barrier((up, down, relayed))
            all_terms.append((reach, 0, relayed))
    chunk = summed_terms(all_terms, size)
    chunks = [chunk] + [swapped(chunk, "col", partner) for partner in range(1, col_count)]
    return [mine, up, down], chunks


def per_device(features, weight, adj_tiles, tile_rows, tile_cols, tile_counts, out_grad):
    node_rows, width = features.shape
    capacity, side = adj_tiles.shape[2:4]
    tiles = adj_tiles.reshape(capacity, side, side)
    packed = jnp.concatenate([tile_rows, tile_cols, tile_counts[:, :, None]], axis=2).reshape(2 * capacity + 1)
    row_count = lax.axis_size("row")
    col_count = lax.axis_size("col")
    per_strip = node_rows // side
    stages = build_stages(tiles, col_count * per_strip, row_count * per_strip, per_strip)
    shards, dense, cotangents = gathered_shards(features, packed, stages, out_grad)

    for_sibling = forward_product(dense, shards, 1, row_count, col_count)
    for_sibling, cell = lax.optimization_barrier((for_sibling, dense))
    sums = added(forward_product(cell, shards, 0, row_count, col_count), swapped(for_sibling, "col", 1))
    sums = [sums] + [swapped(sums, "col", partner) for partner in range(2, col_count, 2)]
    activations, message, chunk = middle(sums, weight, cotangents, node_rows * row_count * col_count)
    sibling = swapped(message, "col", 1)
    parts, chunks = scattered_sums(dense, message, sibling, chunk)
    grad_features, grad_weight = finish(parts, chunks)
    return (activations, grad_features, grad_weight)


def solution(mesh):
    placed = (
        P(("row", "col"), None),
        P(),
        P("row", "col", None, None, None),
        P("row", "col", None),
        P("row", "col", None),
        P("row", "col"),
        P(("row", "col"), None),
    )
    return jax.shard_map(
        per_device,
        mesh=mesh,
        in_specs=placed,
        out_specs=(P(("row", "col"), None), P(("row", "col"), None), P()),
        check_vma=False,
    )
```

```python
import functools
import math

import jax
import jax.numpy as jnp
from jax import lax
from jax.experimental import pallas as pl
from jax.experimental.pallas import tpu as pltpu
from jax.sharding import PartitionSpec as P

chunk_tiles = 16
chunk_slots = 8
build_grant = 44
strips_per_step = 8
mib = 1024 * 1024


def scratch_bytes(*shapes):
    return sum(math.prod(shape) * jnp.dtype(kind).itemsize for shape, kind in shapes)


def add_tiles(list_ref, tiles_ref, total, held, sems, begin, end, *, first_block, blocks, steps):
    side = tiles_ref.shape[1]
    capacity = tiles_ref.shape[0]
    count = list_ref[2 * capacity]
    slots = held.shape[0]
    row_blocks = total.shape[0] // side - 1

    def fetch(index):
        slot = lax.rem(index - begin, slots)
        return pltpu.make_async_copy(
            tiles_ref.at[pl.ds(index * chunk_tiles, chunk_tiles)], held.at[slot], sems.at[slot]
        )

    def start(index, carry):
        fetch(index).start()
        return carry

    lax.fori_loop(begin, jnp.minimum(end, begin + slots), start, 0)

    def target(place):
        col = list_ref[capacity + place] - first_block
        live = place < count
        if steps > 1:
            live = live & (col >= 0) & (col < blocks)
            col = jnp.where(live, col, 0)
        row = jnp.where(live, list_ref[place], row_blocks)
        return row, col

    def chunk_step(index, carry):
        fetch(index).wait()
        slot = lax.rem(index - begin, slots)
        for lane in range(0, chunk_tiles, 2):
            spots = [target(index * chunk_tiles + lane + turn) for turn in range(2)]
            at = [
                (pl.ds(pl.multiple_of(row * side, side), side), pl.ds(pl.multiple_of(col * side, side), side))
                for row, col in spots
            ]
            first, second = total[at[0]], total[at[1]]
            tiles = [held[slot, lane + turn].astype(jnp.float32) for turn in range(2)]
            same = (spots[0][0] == spots[1][0]) & (spots[0][1] == spots[1][1])
            total[at[0]] = first + tiles[0]
            total[at[1]] = second + tiles[1] + jnp.where(same, tiles[0], 0.0)

        @pl.when(index + slots < end)
        def _():
            fetch(index + slots).start()

        return carry

    return lambda: lax.fori_loop(begin, end, chunk_step, 0)


def each_row_block(total, side, action):
    def step(block, carry):
        action(pl.ds(pl.multiple_of(block * side, side), side))
        return carry

    lax.fori_loop(0, total.shape[0] // side - 1, step, 0)


def live_chunks(list_ref, tiles_ref):
    return (list_ref[2 * tiles_ref.shape[0]] + chunk_tiles - 1) // chunk_tiles


def build_first_kernel(list_ref, tiles_ref, dense_ref, total, held, sems, *, blocks):
    half = (live_chunks(list_ref, tiles_ref) + 1) // 2
    run = add_tiles(list_ref, tiles_ref, total, held, sems, 0, half, first_block=0, blocks=blocks, steps=1)

    def clear(down):
        total[down, :] = jnp.zeros((down.size, total.shape[1]), jnp.float32)

    def rounded(down):
        dense_ref[down, :] = total[down, :].astype(jnp.bfloat16)

    each_row_block(total, tiles_ref.shape[1], clear)
    run()
    each_row_block(total, tiles_ref.shape[1], rounded)


def build_rest_kernel(list_ref, tiles_ref, half_ref, dense_ref, total, held, sems, *, blocks):
    chunks = live_chunks(list_ref, tiles_ref)
    run = add_tiles(
        list_ref, tiles_ref, total, held, sems, (chunks + 1) // 2, chunks, first_block=0, blocks=blocks, steps=1
    )

    def widened(down):
        total[down, :] = half_ref[down, :].astype(jnp.float32)

    def rounded(down):
        dense_ref[down, :] = total[down, :].astype(jnp.bfloat16)

    each_row_block(total, tiles_ref.shape[1], widened)
    run()
    each_row_block(total, tiles_ref.shape[1], rounded)


def build_whole_kernel(list_ref, tiles_ref, dense_ref, total, held, sems, *, blocks, steps):
    chunks = live_chunks(list_ref, tiles_ref)
    first_block = pl.program_id(0) * blocks
    run = add_tiles(
        list_ref, tiles_ref, total, held, sems, 0, chunks, first_block=first_block, blocks=blocks, steps=steps
    )

    def clear(down):
        total[down, :] = jnp.zeros((down.size, total.shape[1]), jnp.float32)

    def rounded(down):
        dense_ref[down, :] = total[down, :].astype(jnp.bfloat16)

    each_row_block(total, tiles_ref.shape[1], clear)
    run()
    each_row_block(total, tiles_ref.shape[1], rounded)


def build_stages(tiles, row_blocks, col_blocks, per_strip):
    capacity, side, _ = tiles.shape
    blocks = min(strips_per_step * per_strip, col_blocks)
    steps = col_blocks // blocks
    high, wide = row_blocks * side, blocks * side
    total = ((high + side, wide), jnp.float32)
    held = ((min(chunk_slots, capacity // chunk_tiles), chunk_tiles, side, side), jnp.bfloat16)
    cost = pl.CostEstimate(
        flops=capacity * side * side, bytes_accessed=capacity * side * side + high * wide, transcendentals=0
    )
    held_scratch = [pltpu.VMEM(*held), pltpu.SemaphoreType.DMA((held[0][0],))]
    dense_shape = jax.ShapeDtypeStruct((high, col_blocks * side), jnp.bfloat16)
    whole = pl.BlockSpec(memory_space=pltpu.VMEM)
    apart = pl.BlockSpec(memory_space=pl.ANY)
    listed = pl.BlockSpec(memory_space=pltpu.SMEM)
    if steps > 1:
        block = ((high, wide), jnp.bfloat16)
        return [
            lambda packed: pl.pallas_call(
                functools.partial(build_whole_kernel, blocks=blocks, steps=steps),
                out_shape=dense_shape,
                grid_spec=pltpu.PrefetchScalarGridSpec(
                    num_scalar_prefetch=1,
                    grid=(steps,),
                    in_specs=[apart],
                    out_specs=pl.BlockSpec((high, wide), lambda i, *_: (0, i)),
                    scratch_shapes=[pltpu.VMEM(*total)] + held_scratch,
                ),
                compiler_params=pltpu.CompilerParams(
                    vmem_limit_bytes=scratch_bytes(total, held, block, block) + 4 * mib
                ),
                cost_estimate=cost,
                name="build_whole",
            )(packed, tiles)
        ]
    params = pltpu.CompilerParams(vmem_limit_bytes=build_grant * mib)
    scratch = [pltpu.VMEM(*total)] + held_scratch
    return [
        lambda packed: (packed, pl.pallas_call(
            functools.partial(build_first_kernel, blocks=blocks),
            out_shape=dense_shape,
            in_specs=[listed, apart],
            out_specs=whole,
            scratch_shapes=scratch,
            compiler_params=params,
            cost_estimate=cost,
            name="build_first",
        )(packed, tiles)),
        lambda state: pl.pallas_call(
            functools.partial(build_rest_kernel, blocks=blocks),
            out_shape=dense_shape,
            in_specs=[listed, apart, whole],
            out_specs=whole,
            scratch_shapes=scratch,
            compiler_params=params,
            cost_estimate=cost,
            name="build_rest",
        )(state[0], tiles, state[1]),
    ]


def ring_place(row, count):
    return jnp.where(lax.rem(row, 2) == 0, row // 2, count - 1 - row // 2)


def ring_row(place, count):
    place = lax.rem(place + 2 * count, count)
    return jnp.where(place < count // 2, 2 * place, 2 * (count - 1 - place) + 1)


def forward_kernel(dense_ref, *refs, pieces, sibling, row_count):
    piece_refs, out_ref = refs[: len(pieces)], refs[len(pieces)]
    count = lax.axis_size("col")
    rows = dense_ref.shape[0] // count
    block = dense_ref.shape[1] // row_count
    place = ring_place(lax.axis_index("row"), row_count)
    col = lax.axis_index("col") ^ sibling
    operands = []
    for piece, ref in zip(pieces, piece_refs):
        for offset, first, start, high in piece:
            along = pl.ds(pl.multiple_of(ring_row(place + offset, row_count) * block + first, 128), high)
            operands.append((along, ref, pl.ds(start, high)))
    for index in range(count // 2):
        down = pl.ds(pl.multiple_of((col ^ (2 * index)) * rows, rows), rows)
        total = None
        for along, ref, part in operands:
            product = jnp.dot(dense_ref[down, along], ref[part, :], preferred_element_type=jnp.float32)
            total = product if total is None else total + product
        out_ref[pl.ds(index * rows, rows), :] = total.astype(jnp.bfloat16)


def forward_product(dense, shards, sibling, row_count, col_count):
    pieces = tuple(piece for piece, _ in shards)
    arrays = [array for _, array in shards]
    high, deep = dense.shape
    width = arrays[0].shape[1]
    half = high // 2
    cell = ((high, deep), jnp.bfloat16)
    depth = ((deep, width), jnp.bfloat16)
    out = ((high, width), jnp.float32)
    return pl.pallas_call(
        functools.partial(forward_kernel, pieces=pieces, sibling=sibling, row_count=row_count),
        out_shape=jax.ShapeDtypeStruct((half, width), jnp.bfloat16),
        in_specs=[pl.BlockSpec(memory_space=pltpu.VMEM)] * (1 + len(arrays)),
        out_specs=pl.BlockSpec(memory_space=pltpu.VMEM),
        compiler_params=pltpu.CompilerParams(vmem_limit_bytes=scratch_bytes(cell, depth, out) + 6 * mib),
        cost_estimate=pl.CostEstimate(
            flops=2 * half * deep * width,
            bytes_accessed=2 * (half * deep + deep * width + half * width),
            transcendentals=0,
        ),
        name="forward_product",
    )(dense, *arrays)


def partners_sum(values):
    while len(values) > 1:
        values = [values[i] + values[i + 1] for i in range(0, len(values), 2)]
    return values[0]


def middle_kernel(*refs, blocks, scale):
    sums, refs = refs[:blocks], refs[blocks:]
    weight_ref, refs = refs[0], refs[1:]
    cotangent_refs, (act_ref, message_ref, chunk_ref, product) = refs[:blocks], refs[blocks:]
    weight = weight_ref[...]
    rows, width = act_ref.shape
    over_nodes = (((0,), (0,)), ((), ()))
    terms = []
    for index in range(blocks):
        aggregate = partners_sum(
            [sums[other][pl.ds((index ^ other) * rows, rows), :].astype(jnp.float32) for other in range(blocks)]
        )
        high = aggregate.astype(jnp.bfloat16)
        low = (aggregate - high.astype(jnp.float32)).astype(jnp.bfloat16)
        pre = jnp.dot(high, weight, preferred_element_type=jnp.float32)
        pre += jnp.dot(low, weight, preferred_element_type=jnp.float32)
        sig = jax.nn.sigmoid(pre)
        cotangent = cotangent_refs[index][...].astype(jnp.float32)
        grad = (cotangent * sig * (1.0 + pre * (1.0 - sig))).astype(jnp.bfloat16)
        message_ref[pl.ds(index * width, width), :] = lax.dot_general(
            weight, grad, (((1,), (1,)), ((), ())), preferred_element_type=jnp.float32
        ).astype(jnp.bfloat16)
        if index == 0:
            act_ref[...] = (pre * sig).astype(jnp.bfloat16)
        part = lax.dot_general(high, grad, over_nodes, preferred_element_type=jnp.float32)
        part += lax.dot_general(low, grad, over_nodes, preferred_element_type=jnp.float32)
        terms.append(part)
    product[...] = partners_sum(terms) * scale
    col = lax.axis_index("col")
    size = chunk_ref.shape[0]
    core = col & 1
    chunk_ref[...] = product[pl.ds(pl.multiple_of(core * size, size), size), :]
    sent = product[pl.ds(pl.multiple_of((core ^ 1) * size, size), size), :]
    high = sent.astype(jnp.bfloat16)
    low = (sent - high.astype(jnp.float32)).astype(jnp.bfloat16)
    message_ref[pl.ds(blocks * width, size), :] = high
    message_ref[pl.ds(blocks * width + size, size), :] = low


def middle(sums, weight, cotangents, total_nodes):
    rows, width = cotangents[0].shape
    blocks = len(cotangents)
    size = width // 2
    return pl.pallas_call(
        functools.partial(middle_kernel, blocks=blocks, scale=1.0 / math.sqrt(total_nodes)),
        out_shape=[
            jax.ShapeDtypeStruct((rows, width), jnp.bfloat16),
            jax.ShapeDtypeStruct((blocks * width + 2 * size, rows), jnp.bfloat16),
            jax.ShapeDtypeStruct((size, width), jnp.float32),
        ],
        in_specs=[pl.BlockSpec(memory_space=pltpu.VMEM)] * (2 * blocks + 1),
        out_specs=[pl.BlockSpec(memory_space=pltpu.VMEM)] * 3,
        scratch_shapes=[pltpu.VMEM((width, width), jnp.float32)],
        compiler_params=pltpu.CompilerParams(vmem_limit_bytes=12 * mib),
        cost_estimate=pl.CostEstimate(
            flops=10 * blocks * rows * width * width,
            bytes_accessed=2 * (blocks * blocks + 2 * blocks + 4) * rows * width,
            transcendentals=blocks * rows * width,
        ),
        name="middle",
    )(*sums, weight, *cotangents)


def backward_kernel(dense_ref, own_ref, sibling_ref, chunk_ref, *refs, outputs, row_count):
    out_refs, (depth, sems) = refs[:-2], refs[-2:]
    count = lax.axis_size("col")
    width, rows = depth.shape[0], own_ref.shape[1]
    wide = dense_ref.shape[1] // row_count
    col = lax.axis_index("col")
    copies = []
    for index in range(count):
        block = pl.ds(index // 2 * width, width)
        along = pl.ds(pl.multiple_of((col ^ index) * rows, rows), rows)
        source = sibling_ref if index % 2 else own_ref
        copy = pltpu.make_async_copy(source.at[block], depth.at[:, along], sems.at[index])
        copy.start()
        copies.append(copy)
    size = chunk_ref.shape[0]
    from_sibling = count // 2 * width
    high, low = (sibling_ref[pl.ds(from_sibling + turn * size, size), :].astype(jnp.float32) for turn in range(2))
    terms = (chunk_ref[...] + (high + low)).astype(jnp.bfloat16)
    for copy in copies:
        copy.wait()
    place = ring_place(lax.axis_index("row"), row_count)
    for (offset, tail), out_ref in zip(outputs, out_refs):
        if tail != "terms alone":
            along = pl.ds(pl.multiple_of(ring_row(place + offset, row_count) * wide, wide), wide)
            part = jnp.dot(depth[...], dense_ref[:, along], preferred_element_type=jnp.float32)
            out_ref[pl.ds(0, width), :] = part.astype(jnp.bfloat16)
        if tail == "terms alone":
            out_ref[...] = terms
        elif tail == "terms":
            out_ref[pl.ds(width, size), :] = terms
        elif tail == "zeros":
            out_ref[pl.ds(width, size), :] = jnp.zeros_like(terms)


def backward_product(dense, own, sibling, chunk, outputs, row_count, col_count):
    high, deep = dense.shape
    size, width = chunk.shape
    wide = deep // row_count
    heights = {"": width, "terms alone": size, "terms": width + size, "zeros": width + size}
    cell = ((high, deep), jnp.bfloat16)
    depth = ((width, high), jnp.bfloat16)
    out = ((len(outputs), width + size, wide), jnp.float32)
    return pl.pallas_call(
        functools.partial(backward_kernel, outputs=outputs, row_count=row_count),
        out_shape=[jax.ShapeDtypeStruct((heights[tail], wide), jnp.bfloat16) for _, tail in outputs],
        in_specs=[pl.BlockSpec(memory_space=pltpu.VMEM)] * 4,
        out_specs=[pl.BlockSpec(memory_space=pltpu.VMEM)] * len(outputs),
        scratch_shapes=[pltpu.VMEM(*depth), pltpu.SemaphoreType.DMA((col_count,))],
        compiler_params=pltpu.CompilerParams(vmem_limit_bytes=scratch_bytes(cell, depth, out) + 6 * mib),
        cost_estimate=pl.CostEstimate(
            flops=2 * high * wide * width, bytes_accessed=2 * wide * len(outputs) * width, transcendentals=0
        ),
        name="backward_product",
    )(dense, own, sibling, chunk)


def terms_kernel(*refs, offsets, first_rows):
    term_refs, out_ref, places = refs[:-2], refs[-2], refs[-1]
    row_count, size, _ = places.shape
    place = ring_place(lax.axis_index("row"), row_count)
    for offset, first, ref in zip(offsets, first_rows, term_refs):
        places[ring_row(place + offset, row_count)] = ref[pl.ds(first, size), :].astype(jnp.float32)
    total = places[0]
    for index in range(1, row_count):
        total += places[index]
    out_ref[...] = total


def summed_terms(terms, size):
    offsets = tuple(offset for offset, _, _ in terms)
    first_rows = tuple(first for _, first, _ in terms)
    arrays = [array for _, _, array in terms]
    width = arrays[0].shape[1]
    return pl.pallas_call(
        functools.partial(terms_kernel, offsets=offsets, first_rows=first_rows),
        out_shape=jax.ShapeDtypeStruct((size, width), jnp.float32),
        in_specs=[pl.BlockSpec(memory_space=pltpu.VMEM)] * len(arrays),
        out_specs=pl.BlockSpec(memory_space=pltpu.VMEM),
        scratch_shapes=[pltpu.VMEM((len(arrays), size, width), jnp.float32)],
        compiler_params=pltpu.CompilerParams(
            vmem_limit_bytes=scratch_bytes(*((array.shape, array.dtype) for array in arrays)) + 8 * mib
        ),
        cost_estimate=pl.CostEstimate(
            flops=len(arrays) * size * width, bytes_accessed=2 * len(arrays) * size * width, transcendentals=0
        ),
        name="summed_terms",
    )(*arrays)


def finish_kernel(*refs):
    *part_refs, features_ref = refs
    width = features_ref.shape[1]
    total = part_refs[0][pl.ds(0, width), :].astype(jnp.float32)
    for part_ref in part_refs[1:]:
        total += part_ref[pl.ds(0, width), :].astype(jnp.float32)
    features_ref[...] = total.astype(jnp.bfloat16).T


def finish(parts):
    width, rows = parts[0].shape
    return pl.pallas_call(
        finish_kernel,
        out_shape=jax.ShapeDtypeStruct((rows, width), jnp.bfloat16),
        in_specs=[pl.BlockSpec(memory_space=pltpu.VMEM)] * len(parts),
        out_specs=pl.BlockSpec(memory_space=pltpu.VMEM),
        compiler_params=pltpu.CompilerParams(vmem_limit_bytes=8 * mib),
        cost_estimate=pl.CostEstimate(
            flops=len(parts) * rows * width, bytes_accessed=2 * (len(parts) + 1) * rows * width, transcendentals=0
        ),
        name="finish",
    )(*parts)


def joined_kernel(own_ref, sibling_ref, weight_ref):
    rows = own_ref.shape[0]
    core = lax.axis_index("col") & 1
    for turn, ref in enumerate((own_ref, sibling_ref)):
        weight_ref[pl.ds(pl.multiple_of((core ^ turn) * rows, rows), rows), :] = ref[...]


def joined(own, sibling):
    rows, width = own.shape
    return pl.pallas_call(
        joined_kernel,
        out_shape=jax.ShapeDtypeStruct((2 * rows, width), jnp.float32),
        in_specs=[pl.BlockSpec(memory_space=pltpu.VMEM)] * 2,
        out_specs=pl.BlockSpec(memory_space=pltpu.VMEM),
        compiler_params=pltpu.CompilerParams(vmem_limit_bytes=8 * mib),
        cost_estimate=pl.CostEstimate(flops=0, bytes_accessed=16 * rows * width, transcendentals=0),
        name="joined",
    )(own, sibling)


def around(value, step):
    count = lax.axis_size("row")
    order = list(range(0, count, 2)) + list(range(count - 1, 0, -2))
    return lax.ppermute(value, "row", [(order[i], order[(i + step) % count]) for i in range(count)])


def swapped(value, axis, partner):
    return lax.ppermute(value, axis, [(i, i ^ partner) for i in range(lax.axis_size(axis))])


def gathered_shards(own, packed, stages, cotangent):
    reach = lax.axis_size("row") // 2
    rows = own.shape[0]
    ups, downs = [own], [own]
    for step in range(reach):
        ups.append(around(ups[-1], 1))
    dense = packed
    others = [swapped(cotangent, "col", partner) for partner in range(2, lax.axis_size("col"), 2)]
    for step in range(1, reach):
        down = around(downs[-1], -1)
        if step == 1:
            down, dense, others = lax.optimization_barrier((down, dense, others))
        elif step == 2:
            dense = stages.pop(0)(dense)
            down, dense = lax.optimization_barrier((down, dense))
        elif step == reach - 1 and stages:
            down, dense = lax.optimization_barrier((down, dense))
        downs.append(down)
    if stages:
        dense = stages.pop(0)(dense)
    shards = [(((0, 0, 0, rows),), own)]
    shards += [(((-step, 0, 0, rows),), ups[step]) for step in range(1, reach + 1)]
    shards += [(((step, 0, 0, rows),), downs[step]) for step in range(1, reach)]
    return shards, dense, [cotangent] + others


def added(first, second):
    return (first.astype(jnp.float32) + second[: first.shape[0]].astype(jnp.float32)).astype(jnp.bfloat16)


def scattered_sums(dense, own, sibling, chunk):
    row_count, col_count = lax.axis_size("row"), lax.axis_size("col")
    size, width = chunk.shape
    reach = row_count // 2
    first = ((reach, "terms"), (1 - reach, "terms"), (0, "terms alone"))
    above, below, terms = backward_product(dense, own, sibling, chunk, first, row_count, col_count)
    above, below, terms, cell = lax.optimization_barrier((above, below, terms, dense))
    up, down = around(above, 1), around(below, -1)
    all_terms = [(0, 0, terms)]

    ups = tuple((offset, "zeros") for offset in range(reach - 1, 0, -1))
    downs = tuple((-offset, "zeros") for offset in range(reach - 2, 0, -1))
    strips = backward_product(cell, own, sibling, chunk, ups + downs + ((0, ""),), row_count, col_count)
    ups, downs, mine = strips[: reach - 1], strips[reach - 1 : -1], strips[-1]
    for step in range(1, reach):
        all_terms += [(-step, width, up), (step, width, down)]
        up = around(added(ups[step - 1], up), 1)
        if step < reach - 1:
            down = around(added(downs[step - 1], down), -1)
    all_terms.append((reach, width, up))
    return [mine, up, down], summed_terms(all_terms, size)


def per_device(features, weight, adj_tiles, tile_rows, tile_cols, tile_counts, out_grad):
    node_rows, width = features.shape
    capacity, side = adj_tiles.shape[2:4]
    tiles = adj_tiles.reshape(capacity, side, side)
    packed = jnp.concatenate([tile_rows, tile_cols, tile_counts[:, :, None]], axis=2).reshape(2 * capacity + 1)
    row_count = lax.axis_size("row")
    col_count = lax.axis_size("col")
    per_strip = node_rows // side
    stages = build_stages(tiles, col_count * per_strip, row_count * per_strip, per_strip)
    shards, dense, cotangents = gathered_shards(features, packed, stages, out_grad)

    for_sibling = forward_product(dense, shards, 1, row_count, col_count)
    for_sibling, cell = lax.optimization_barrier((for_sibling, dense))
    sums = added(forward_product(cell, shards, 0, row_count, col_count), swapped(for_sibling, "col", 1))
    sums = [sums] + [swapped(sums, "col", partner) for partner in range(2, col_count, 2)]
    activations, message, chunk = middle(sums, weight, cotangents, node_rows * row_count * col_count)
    sibling = swapped(message, "col", 1)
    parts, half = scattered_sums(dense, message, sibling, chunk)
    grad_weight = joined(half, swapped(half, "col", 1))
    return (activations, finish(parts), grad_weight)


def solution(mesh):
    placed = (
        P(("row", "col"), None),
        P(),
        P("row", "col", None, None, None),
        P("row", "col", None),
        P("row", "col", None),
        P("row", "col"),
        P(("row", "col"), None),
    )
    return jax.shard_map(
        per_device,
        mesh=mesh,
        in_specs=placed,
        out_specs=(P(("row", "col"), None), P(("row", "col"), None), P()),
        check_vma=False,
    )
```

```python
import functools
import math

import jax
import jax.numpy as jnp
from jax import lax
from jax.experimental import pallas as pl
from jax.experimental.pallas import tpu as pltpu
from jax.sharding import PartitionSpec as P

chunk_tiles = 16
chunk_slots = 8
build_grant = 44
strips_per_step = 8
mib = 1024 * 1024


def scratch_bytes(*shapes):
    return sum(math.prod(shape) * jnp.dtype(kind).itemsize for shape, kind in shapes)


def add_tiles(list_ref, tiles_ref, total, held, sems, begin, end, *, first_block, blocks, steps):
    side = tiles_ref.shape[1]
    capacity = tiles_ref.shape[0]
    count = list_ref[2 * capacity]
    slots = held.shape[0]
    row_blocks = total.shape[0] // side - 1

    def fetch(index):
        slot = lax.rem(index - begin, slots)
        return pltpu.make_async_copy(
            tiles_ref.at[pl.ds(index * chunk_tiles, chunk_tiles)], held.at[slot], sems.at[slot]
        )

    def start(index, carry):
        fetch(index).start()
        return carry

    lax.fori_loop(begin, jnp.minimum(end, begin + slots), start, 0)

    def target(place):
        col = list_ref[capacity + place] - first_block
        live = place < count
        if steps > 1:
            live = live & (col >= 0) & (col < blocks)
            col = jnp.where(live, col, 0)
        row = jnp.where(live, list_ref[place], row_blocks)
        return row, col

    def chunk_step(index, carry):
        fetch(index).wait()
        slot = lax.rem(index - begin, slots)
        for lane in range(0, chunk_tiles, 2):
            spots = [target(index * chunk_tiles + lane + turn) for turn in range(2)]
            at = [
                (pl.ds(pl.multiple_of(row * side, side), side), pl.ds(pl.multiple_of(col * side, side), side))
                for row, col in spots
            ]
            first, second = total[at[0]], total[at[1]]
            tiles = [held[slot, lane + turn].astype(jnp.float32) for turn in range(2)]
            same = (spots[0][0] == spots[1][0]) & (spots[0][1] == spots[1][1])
            total[at[0]] = first + tiles[0]
            total[at[1]] = second + tiles[1] + jnp.where(same, tiles[0], 0.0)

        @pl.when(index + slots < end)
        def _():
            fetch(index + slots).start()

        return carry

    return lambda: lax.fori_loop(begin, end, chunk_step, 0)


def each_row_block(total, side, action):
    def step(block, carry):
        action(pl.ds(pl.multiple_of(block * side, side), side))
        return carry

    lax.fori_loop(0, total.shape[0] // side - 1, step, 0)


def live_chunks(list_ref, tiles_ref):
    return (list_ref[2 * tiles_ref.shape[0]] + chunk_tiles - 1) // chunk_tiles


def first_chunks(list_ref, tiles_ref):
    return (live_chunks(list_ref, tiles_ref) * 3 + 7) // 8


def build_first_kernel(list_ref, tiles_ref, dense_ref, total, held, sems, *, blocks):
    part = first_chunks(list_ref, tiles_ref)
    run = add_tiles(list_ref, tiles_ref, total, held, sems, 0, part, first_block=0, blocks=blocks, steps=1)

    def clear(down):
        total[down, :] = jnp.zeros((down.size, total.shape[1]), jnp.float32)

    def rounded(down):
        dense_ref[down, :] = total[down, :].astype(jnp.bfloat16)

    each_row_block(total, tiles_ref.shape[1], clear)
    run()
    each_row_block(total, tiles_ref.shape[1], rounded)


def build_rest_kernel(list_ref, tiles_ref, half_ref, dense_ref, total, held, sems, *, blocks):
    chunks = live_chunks(list_ref, tiles_ref)
    run = add_tiles(
        list_ref, tiles_ref, total, held, sems, first_chunks(list_ref, tiles_ref), chunks,
        first_block=0, blocks=blocks, steps=1,
    )

    def widened(down):
        total[down, :] = half_ref[down, :].astype(jnp.float32)

    def rounded(down):
        dense_ref[down, :] = total[down, :].astype(jnp.bfloat16)

    each_row_block(total, tiles_ref.shape[1], widened)
    run()
    each_row_block(total, tiles_ref.shape[1], rounded)


def build_whole_kernel(list_ref, tiles_ref, dense_ref, total, held, sems, *, blocks, steps):
    chunks = live_chunks(list_ref, tiles_ref)
    first_block = pl.program_id(0) * blocks
    run = add_tiles(
        list_ref, tiles_ref, total, held, sems, 0, chunks, first_block=first_block, blocks=blocks, steps=steps
    )

    def clear(down):
        total[down, :] = jnp.zeros((down.size, total.shape[1]), jnp.float32)

    def rounded(down):
        dense_ref[down, :] = total[down, :].astype(jnp.bfloat16)

    each_row_block(total, tiles_ref.shape[1], clear)
    run()
    each_row_block(total, tiles_ref.shape[1], rounded)


def build_stages(tiles, row_blocks, col_blocks, per_strip):
    capacity, side, _ = tiles.shape
    blocks = min(strips_per_step * per_strip, col_blocks)
    steps = col_blocks // blocks
    high, wide = row_blocks * side, blocks * side
    total = ((high + side, wide), jnp.float32)
    held = ((min(chunk_slots, capacity // chunk_tiles), chunk_tiles, side, side), jnp.bfloat16)
    cost = pl.CostEstimate(
        flops=capacity * side * side, bytes_accessed=capacity * side * side + high * wide, transcendentals=0
    )
    held_scratch = [pltpu.VMEM(*held), pltpu.SemaphoreType.DMA((held[0][0],))]
    dense_shape = jax.ShapeDtypeStruct((high, col_blocks * side), jnp.bfloat16)
    whole = pl.BlockSpec(memory_space=pltpu.VMEM)
    apart = pl.BlockSpec(memory_space=pl.ANY)
    listed = pl.BlockSpec(memory_space=pltpu.SMEM)
    if steps > 1:
        block = ((high, wide), jnp.bfloat16)
        return [
            lambda packed: pl.pallas_call(
                functools.partial(build_whole_kernel, blocks=blocks, steps=steps),
                out_shape=dense_shape,
                grid_spec=pltpu.PrefetchScalarGridSpec(
                    num_scalar_prefetch=1,
                    grid=(steps,),
                    in_specs=[apart],
                    out_specs=pl.BlockSpec((high, wide), lambda i, *_: (0, i)),
                    scratch_shapes=[pltpu.VMEM(*total)] + held_scratch,
                ),
                compiler_params=pltpu.CompilerParams(
                    vmem_limit_bytes=scratch_bytes(total, held, block, block) + 4 * mib
                ),
                cost_estimate=cost,
                name="build_whole",
            )(packed, tiles)
        ]
    params = pltpu.CompilerParams(vmem_limit_bytes=build_grant * mib)
    scratch = [pltpu.VMEM(*total)] + held_scratch
    return [
        lambda packed: (packed, pl.pallas_call(
            functools.partial(build_first_kernel, blocks=blocks),
            out_shape=dense_shape,
            in_specs=[listed, apart],
            out_specs=whole,
            scratch_shapes=scratch,
            compiler_params=params,
            cost_estimate=cost,
            name="build_first",
        )(packed, tiles)),
        lambda state: pl.pallas_call(
            functools.partial(build_rest_kernel, blocks=blocks),
            out_shape=dense_shape,
            in_specs=[listed, apart, whole],
            out_specs=whole,
            scratch_shapes=scratch,
            compiler_params=params,
            cost_estimate=cost,
            name="build_rest",
        )(state[0], tiles, state[1]),
    ]


def ring_place(row, count):
    return jnp.where(lax.rem(row, 2) == 0, row // 2, count - 1 - row // 2)


def ring_row(place, count):
    place = lax.rem(place + 2 * count, count)
    return jnp.where(place < count // 2, 2 * place, 2 * (count - 1 - place) + 1)


def forward_kernel(dense_ref, *refs, pieces, sibling, row_count):
    piece_refs, out_ref = refs[: len(pieces)], refs[len(pieces)]
    count = lax.axis_size("col")
    rows = dense_ref.shape[0] // count
    block = dense_ref.shape[1] // row_count
    place = ring_place(lax.axis_index("row"), row_count)
    col = lax.axis_index("col") ^ sibling
    operands = []
    for piece, ref in zip(pieces, piece_refs):
        for offset, first, start, high in piece:
            along = pl.ds(pl.multiple_of(ring_row(place + offset, row_count) * block + first, 128), high)
            operands.append((along, ref, pl.ds(start, high)))
    for index in range(count // 2):
        down = pl.ds(pl.multiple_of((col ^ (2 * index)) * rows, rows), rows)
        total = None
        for along, ref, part in operands:
            product = jnp.dot(dense_ref[down, along], ref[part, :], preferred_element_type=jnp.float32)
            total = product if total is None else total + product
        out_ref[pl.ds(index * rows, rows), :] = total.astype(jnp.bfloat16)


def forward_product(dense, shards, sibling, row_count, col_count):
    pieces = tuple(piece for piece, _ in shards)
    arrays = [array for _, array in shards]
    high, deep = dense.shape
    width = arrays[0].shape[1]
    half = high // 2
    cell = ((high, deep), jnp.bfloat16)
    depth = ((deep, width), jnp.bfloat16)
    out = ((high, width), jnp.float32)
    return pl.pallas_call(
        functools.partial(forward_kernel, pieces=pieces, sibling=sibling, row_count=row_count),
        out_shape=jax.ShapeDtypeStruct((half, width), jnp.bfloat16),
        in_specs=[pl.BlockSpec(memory_space=pltpu.VMEM)] * (1 + len(arrays)),
        out_specs=pl.BlockSpec(memory_space=pltpu.VMEM),
        compiler_params=pltpu.CompilerParams(vmem_limit_bytes=scratch_bytes(cell, depth, out) + 6 * mib),
        cost_estimate=pl.CostEstimate(
            flops=2 * half * deep * width,
            bytes_accessed=2 * (half * deep + deep * width + half * width),
            transcendentals=0,
        ),
        name="forward_product",
    )(dense, *arrays)


def partners_sum(values):
    while len(values) > 1:
        values = [values[i] + values[i + 1] for i in range(0, len(values), 2)]
    return values[0]


def middle_kernel(*refs, blocks, scale):
    sums, refs = refs[:blocks], refs[blocks:]
    weight_ref, refs = refs[0], refs[1:]
    cotangent_refs, (act_ref, message_ref, chunk_ref, product) = refs[:blocks], refs[blocks:]
    weight = weight_ref[...]
    rows, width = act_ref.shape
    over_nodes = (((0,), (0,)), ((), ()))
    terms = []
    for index in range(blocks):
        aggregate = partners_sum(
            [sums[other][pl.ds((index ^ other) * rows, rows), :].astype(jnp.float32) for other in range(blocks)]
        )
        high = aggregate.astype(jnp.bfloat16)
        low = (aggregate - high.astype(jnp.float32)).astype(jnp.bfloat16)
        pre = jnp.dot(high, weight, preferred_element_type=jnp.float32)
        pre += jnp.dot(low, weight, preferred_element_type=jnp.float32)
        sig = jax.nn.sigmoid(pre)
        cotangent = cotangent_refs[index][...].astype(jnp.float32)
        grad = (cotangent * sig * (1.0 + pre * (1.0 - sig))).astype(jnp.bfloat16)
        message_ref[pl.ds(index * width, width), :] = lax.dot_general(
            weight, grad, (((1,), (1,)), ((), ())), preferred_element_type=jnp.float32
        ).astype(jnp.bfloat16)
        if index == 0:
            act_ref[...] = (pre * sig).astype(jnp.bfloat16)
        part = lax.dot_general(high, grad, over_nodes, preferred_element_type=jnp.float32)
        part += lax.dot_general(low, grad, over_nodes, preferred_element_type=jnp.float32)
        terms.append(part)
    product[...] = partners_sum(terms) * scale
    col = lax.axis_index("col")
    size = chunk_ref.shape[0]
    core = col & 1
    chunk_ref[...] = product[pl.ds(pl.multiple_of(core * size, size), size), :]
    sent = product[pl.ds(pl.multiple_of((core ^ 1) * size, size), size), :]
    high = sent.astype(jnp.bfloat16)
    low = (sent - high.astype(jnp.float32)).astype(jnp.bfloat16)
    message_ref[pl.ds(blocks * width, size), :] = high
    message_ref[pl.ds(blocks * width + size, size), :] = low


def middle(sums, weight, cotangents, total_nodes):
    rows, width = cotangents[0].shape
    blocks = len(cotangents)
    size = width // 2
    return pl.pallas_call(
        functools.partial(middle_kernel, blocks=blocks, scale=1.0 / math.sqrt(total_nodes)),
        out_shape=[
            jax.ShapeDtypeStruct((rows, width), jnp.bfloat16),
            jax.ShapeDtypeStruct((blocks * width + 2 * size, rows), jnp.bfloat16),
            jax.ShapeDtypeStruct((size, width), jnp.float32),
        ],
        in_specs=[pl.BlockSpec(memory_space=pltpu.VMEM)] * (2 * blocks + 1),
        out_specs=[pl.BlockSpec(memory_space=pltpu.VMEM)] * 3,
        scratch_shapes=[pltpu.VMEM((width, width), jnp.float32)],
        compiler_params=pltpu.CompilerParams(vmem_limit_bytes=12 * mib),
        cost_estimate=pl.CostEstimate(
            flops=10 * blocks * rows * width * width,
            bytes_accessed=2 * (blocks * blocks + 2 * blocks + 4) * rows * width,
            transcendentals=blocks * rows * width,
        ),
        name="middle",
    )(*sums, weight, *cotangents)


def backward_kernel(dense_ref, own_ref, sibling_ref, chunk_ref, *refs, outputs, row_count):
    out_refs, (depth, sems) = refs[:-2], refs[-2:]
    count = lax.axis_size("col")
    width, rows = depth.shape[0], own_ref.shape[1]
    wide = dense_ref.shape[1] // row_count
    col = lax.axis_index("col")
    copies = []
    for index in range(count):
        block = pl.ds(index // 2 * width, width)
        along = pl.ds(pl.multiple_of((col ^ index) * rows, rows), rows)
        source = sibling_ref if index % 2 else own_ref
        copy = pltpu.make_async_copy(source.at[block], depth.at[:, along], sems.at[index])
        copy.start()
        copies.append(copy)
    size = chunk_ref.shape[0]
    from_sibling = count // 2 * width
    high, low = (sibling_ref[pl.ds(from_sibling + turn * size, size), :].astype(jnp.float32) for turn in range(2))
    terms = (chunk_ref[...] + (high + low)).astype(jnp.bfloat16)
    for copy in copies:
        copy.wait()
    place = ring_place(lax.axis_index("row"), row_count)
    for (offset, tail), out_ref in zip(outputs, out_refs):
        if tail != "terms alone":
            along = pl.ds(pl.multiple_of(ring_row(place + offset, row_count) * wide, wide), wide)
            part = jnp.dot(depth[...], dense_ref[:, along], preferred_element_type=jnp.float32)
            out_ref[pl.ds(0, width), :] = part.astype(jnp.bfloat16)
        if tail == "terms alone":
            out_ref[...] = terms
        elif tail == "terms":
            out_ref[pl.ds(width, size), :] = terms
        elif tail == "zeros":
            out_ref[pl.ds(width, size), :] = jnp.zeros_like(terms)


def backward_product(dense, own, sibling, chunk, outputs, row_count, col_count):
    high, deep = dense.shape
    size, width = chunk.shape
    wide = deep // row_count
    heights = {"": width, "terms alone": size, "terms": width + size, "zeros": width + size}
    cell = ((high, deep), jnp.bfloat16)
    depth = ((width, high), jnp.bfloat16)
    out = ((len(outputs), width + size, wide), jnp.float32)
    return pl.pallas_call(
        functools.partial(backward_kernel, outputs=outputs, row_count=row_count),
        out_shape=[jax.ShapeDtypeStruct((heights[tail], wide), jnp.bfloat16) for _, tail in outputs],
        in_specs=[pl.BlockSpec(memory_space=pltpu.VMEM)] * 4,
        out_specs=[pl.BlockSpec(memory_space=pltpu.VMEM)] * len(outputs),
        scratch_shapes=[pltpu.VMEM(*depth), pltpu.SemaphoreType.DMA((col_count,))],
        compiler_params=pltpu.CompilerParams(vmem_limit_bytes=scratch_bytes(cell, depth, out) + 6 * mib),
        cost_estimate=pl.CostEstimate(
            flops=2 * high * wide * width, bytes_accessed=2 * wide * len(outputs) * width, transcendentals=0
        ),
        name="backward_product",
    )(dense, own, sibling, chunk)


def terms_kernel(*refs, offsets, first_rows):
    term_refs, out_ref, places = refs[:-2], refs[-2], refs[-1]
    row_count, size, _ = places.shape
    place = ring_place(lax.axis_index("row"), row_count)
    for offset, first, ref in zip(offsets, first_rows, term_refs):
        places[ring_row(place + offset, row_count)] = ref[pl.ds(first, size), :].astype(jnp.float32)
    total = places[0]
    for index in range(1, row_count):
        total += places[index]
    out_ref[...] = total


def summed_terms(terms, size):
    offsets = tuple(offset for offset, _, _ in terms)
    first_rows = tuple(first for _, first, _ in terms)
    arrays = [array for _, _, array in terms]
    width = arrays[0].shape[1]
    return pl.pallas_call(
        functools.partial(terms_kernel, offsets=offsets, first_rows=first_rows),
        out_shape=jax.ShapeDtypeStruct((size, width), jnp.float32),
        in_specs=[pl.BlockSpec(memory_space=pltpu.VMEM)] * len(arrays),
        out_specs=pl.BlockSpec(memory_space=pltpu.VMEM),
        scratch_shapes=[pltpu.VMEM((len(arrays), size, width), jnp.float32)],
        compiler_params=pltpu.CompilerParams(
            vmem_limit_bytes=scratch_bytes(*((array.shape, array.dtype) for array in arrays)) + 8 * mib
        ),
        cost_estimate=pl.CostEstimate(
            flops=len(arrays) * size * width, bytes_accessed=2 * len(arrays) * size * width, transcendentals=0
        ),
        name="summed_terms",
    )(*arrays)


def finish_kernel(*refs):
    *part_refs, features_ref = refs
    width = features_ref.shape[1]
    total = part_refs[0][pl.ds(0, width), :].astype(jnp.float32)
    for part_ref in part_refs[1:]:
        total += part_ref[pl.ds(0, width), :].astype(jnp.float32)
    features_ref[...] = total.astype(jnp.bfloat16).T


def finish(parts):
    width, rows = parts[0].shape
    return pl.pallas_call(
        finish_kernel,
        out_shape=jax.ShapeDtypeStruct((rows, width), jnp.bfloat16),
        in_specs=[pl.BlockSpec(memory_space=pltpu.VMEM)] * len(parts),
        out_specs=pl.BlockSpec(memory_space=pltpu.VMEM),
        compiler_params=pltpu.CompilerParams(vmem_limit_bytes=8 * mib),
        cost_estimate=pl.CostEstimate(
            flops=len(parts) * rows * width, bytes_accessed=2 * (len(parts) + 1) * rows * width, transcendentals=0
        ),
        name="finish",
    )(*parts)


def joined_kernel(own_ref, sibling_ref, weight_ref):
    rows = own_ref.shape[0]
    core = lax.axis_index("col") & 1
    for turn, ref in enumerate((own_ref, sibling_ref)):
        weight_ref[pl.ds(pl.multiple_of((core ^ turn) * rows, rows), rows), :] = ref[...]


def joined(own, sibling):
    rows, width = own.shape
    return pl.pallas_call(
        joined_kernel,
        out_shape=jax.ShapeDtypeStruct((2 * rows, width), jnp.float32),
        in_specs=[pl.BlockSpec(memory_space=pltpu.VMEM)] * 2,
        out_specs=pl.BlockSpec(memory_space=pltpu.VMEM),
        compiler_params=pltpu.CompilerParams(vmem_limit_bytes=8 * mib),
        cost_estimate=pl.CostEstimate(flops=0, bytes_accessed=16 * rows * width, transcendentals=0),
        name="joined",
    )(own, sibling)


def around(value, step):
    count = lax.axis_size("row")
    order = list(range(0, count, 2)) + list(range(count - 1, 0, -2))
    return lax.ppermute(value, "row", [(order[i], order[(i + step) % count]) for i in range(count)])


def swapped(value, axis, partner):
    return lax.ppermute(value, axis, [(i, i ^ partner) for i in range(lax.axis_size(axis))])


def gathered_shards(own, packed, stages, cotangent):
    reach = lax.axis_size("row") // 2
    rows = own.shape[0]
    ups, downs, dense = [own], [own], packed
    others = []
    for step in range(1, reach + 1):
        up = around(ups[-1], 1)
        if step == reach - 1:
            up, dense, others = lax.optimization_barrier((up, dense, others))
        ups.append(up)
        if step == reach:
            break
        down = around(downs[-1], -1)
        if step == 1:
            down, dense = lax.optimization_barrier((down, dense))
        elif step == 2:
            dense = stages.pop(0)(dense)
            down, dense, cotangent = lax.optimization_barrier((down, dense, cotangent))
            others = [swapped(cotangent, "col", partner) for partner in range(2, lax.axis_size("col"), 2)]
        downs.append(down)
    if stages:
        dense = stages.pop(0)(dense)
    shards = [(((0, 0, 0, rows),), own)]
    shards += [(((-step, 0, 0, rows),), ups[step]) for step in range(1, reach + 1)]
    shards += [(((step, 0, 0, rows),), downs[step]) for step in range(1, reach)]
    return shards, dense, [cotangent] + others


def added(first, second):
    return (first.astype(jnp.float32) + second[: first.shape[0]].astype(jnp.float32)).astype(jnp.bfloat16)


def scattered_sums(dense, own, sibling, chunk):
    row_count, col_count = lax.axis_size("row"), lax.axis_size("col")
    size, width = chunk.shape
    reach = row_count // 2
    first = ((reach, "terms"), (1 - reach, "terms"), (0, "terms alone"))
    above, below, terms = backward_product(dense, own, sibling, chunk, first, row_count, col_count)
    above, below, terms, cell = lax.optimization_barrier((above, below, terms, dense))
    up, down = around(above, 1), around(below, -1)
    all_terms = [(0, 0, terms)]

    ups = tuple((offset, "zeros") for offset in range(reach - 1, 0, -1))
    downs = tuple((-offset, "zeros") for offset in range(reach - 2, 0, -1))
    strips = backward_product(cell, own, sibling, chunk, ups + downs + ((0, ""),), row_count, col_count)
    ups, downs, mine = strips[: reach - 1], strips[reach - 1 : -1], strips[-1]
    for step in range(1, reach):
        all_terms += [(-step, width, up), (step, width, down)]
        up = around(added(ups[step - 1], up), 1)
        if step < reach - 1:
            down = around(added(downs[step - 1], down), -1)
    all_terms.append((reach, width, up))
    return [mine, up, down], summed_terms(all_terms, size)


def per_device(features, weight, adj_tiles, tile_rows, tile_cols, tile_counts, out_grad):
    node_rows, width = features.shape
    capacity, side = adj_tiles.shape[2:4]
    tiles = adj_tiles.reshape(capacity, side, side)
    packed = jnp.concatenate([tile_rows, tile_cols, tile_counts[:, :, None]], axis=2).reshape(2 * capacity + 1)
    row_count = lax.axis_size("row")
    col_count = lax.axis_size("col")
    per_strip = node_rows // side
    stages = build_stages(tiles, col_count * per_strip, row_count * per_strip, per_strip)
    shards, dense, cotangents = gathered_shards(features, packed, stages, out_grad)

    for_sibling = forward_product(dense, shards, 1, row_count, col_count)
    for_sibling, cell = lax.optimization_barrier((for_sibling, dense))
    sums = added(forward_product(cell, shards, 0, row_count, col_count), swapped(for_sibling, "col", 1))
    sums = [sums] + [swapped(sums, "col", partner) for partner in range(2, col_count, 2)]
    activations, message, chunk = middle(sums, weight, cotangents, node_rows * row_count * col_count)
    sibling = swapped(message, "col", 1)
    parts, half = scattered_sums(dense, message, sibling, chunk)
    grad_weight = joined(half, swapped(half, "col", 1))
    return (activations, finish(parts), grad_weight)


def solution(mesh):
    placed = (
        P(("row", "col"), None),
        P(),
        P("row", "col", None, None, None),
        P("row", "col", None),
        P("row", "col", None),
        P("row", "col"),
        P(("row", "col"), None),
    )
    return jax.shard_map(
        per_device,
        mesh=mesh,
        in_specs=placed,
        out_specs=(P(("row", "col"), None), P(("row", "col"), None), P()),
        check_vma=False,
    )
```

```python
import functools
import math

import jax
import jax.numpy as jnp
from jax import lax
from jax.experimental import pallas as pl
from jax.experimental.pallas import tpu as pltpu
from jax.sharding import PartitionSpec as P

chunk_tiles = 16
chunk_slots = 8
build_grant = 44
strips_per_step = 8
mib = 1024 * 1024


def scratch_bytes(*shapes):
    return sum(math.prod(shape) * jnp.dtype(kind).itemsize for shape, kind in shapes)


def add_tiles(list_ref, tiles_ref, total, held, sems, begin, end, *, first_block, blocks, steps):
    side = tiles_ref.shape[1]
    capacity = tiles_ref.shape[0]
    count = list_ref[2 * capacity]
    slots = held.shape[0]
    row_blocks = total.shape[0] // side - 1

    def fetch(index):
        slot = lax.rem(index - begin, slots)
        return pltpu.make_async_copy(
            tiles_ref.at[pl.ds(index * chunk_tiles, chunk_tiles)], held.at[slot], sems.at[slot]
        )

    def start(index, carry):
        fetch(index).start()
        return carry

    lax.fori_loop(begin, jnp.minimum(end, begin + slots), start, 0)

    def target(place):
        col = list_ref[capacity + place] - first_block
        live = place < count
        if steps > 1:
            live = live & (col >= 0) & (col < blocks)
            col = jnp.where(live, col, 0)
        row = jnp.where(live, list_ref[place], row_blocks)
        return row, col

    def chunk_step(index, carry):
        fetch(index).wait()
        slot = lax.rem(index - begin, slots)
        for lane in range(0, chunk_tiles, 2):
            spots = [target(index * chunk_tiles + lane + turn) for turn in range(2)]
            at = [
                (pl.ds(pl.multiple_of(row * side, side), side), pl.ds(pl.multiple_of(col * side, side), side))
                for row, col in spots
            ]
            first, second = total[at[0]], total[at[1]]
            tiles = [held[slot, lane + turn].astype(jnp.float32) for turn in range(2)]
            same = (spots[0][0] == spots[1][0]) & (spots[0][1] == spots[1][1])
            total[at[0]] = first + tiles[0]
            total[at[1]] = second + tiles[1] + jnp.where(same, tiles[0], 0.0)

        @pl.when(index + slots < end)
        def _():
            fetch(index + slots).start()

        return carry

    return lambda: lax.fori_loop(begin, end, chunk_step, 0)


def each_row_block(total, side, action):
    def step(block, carry):
        action(pl.ds(pl.multiple_of(block * side, side), side))
        return carry

    lax.fori_loop(0, total.shape[0] // side - 1, step, 0)


def live_chunks(list_ref, tiles_ref):
    return (list_ref[2 * tiles_ref.shape[0]] + chunk_tiles - 1) // chunk_tiles


def first_chunks(list_ref, tiles_ref):
    return (live_chunks(list_ref, tiles_ref) * 3 + 7) // 8


def build_first_kernel(list_ref, tiles_ref, dense_ref, total, held, sems, *, blocks):
    part = first_chunks(list_ref, tiles_ref)
    run = add_tiles(list_ref, tiles_ref, total, held, sems, 0, part, first_block=0, blocks=blocks, steps=1)

    def clear(down):
        total[down, :] = jnp.zeros((down.size, total.shape[1]), jnp.float32)

    def rounded(down):
        dense_ref[down, :] = total[down, :].astype(jnp.bfloat16)

    each_row_block(total, tiles_ref.shape[1], clear)
    run()
    each_row_block(total, tiles_ref.shape[1], rounded)


def build_rest_kernel(list_ref, tiles_ref, half_ref, dense_ref, total, held, sems, *, blocks):
    chunks = live_chunks(list_ref, tiles_ref)
    run = add_tiles(
        list_ref, tiles_ref, total, held, sems, first_chunks(list_ref, tiles_ref), chunks,
        first_block=0, blocks=blocks, steps=1,
    )

    def widened(down):
        total[down, :] = half_ref[down, :].astype(jnp.float32)

    def rounded(down):
        dense_ref[down, :] = total[down, :].astype(jnp.bfloat16)

    each_row_block(total, tiles_ref.shape[1], widened)
    run()
    each_row_block(total, tiles_ref.shape[1], rounded)


def build_whole_kernel(list_ref, tiles_ref, dense_ref, total, held, sems, *, blocks, steps):
    chunks = live_chunks(list_ref, tiles_ref)
    first_block = pl.program_id(0) * blocks
    run = add_tiles(
        list_ref, tiles_ref, total, held, sems, 0, chunks, first_block=first_block, blocks=blocks, steps=steps
    )

    def clear(down):
        total[down, :] = jnp.zeros((down.size, total.shape[1]), jnp.float32)

    def rounded(down):
        dense_ref[down, :] = total[down, :].astype(jnp.bfloat16)

    each_row_block(total, tiles_ref.shape[1], clear)
    run()
    each_row_block(total, tiles_ref.shape[1], rounded)


def build_stages(tiles, row_blocks, col_blocks, per_strip):
    capacity, side, _ = tiles.shape
    blocks = min(strips_per_step * per_strip, col_blocks)
    steps = col_blocks // blocks
    high, wide = row_blocks * side, blocks * side
    total = ((high + side, wide), jnp.float32)
    held = ((min(chunk_slots, capacity // chunk_tiles), chunk_tiles, side, side), jnp.bfloat16)
    cost = pl.CostEstimate(
        flops=capacity * side * side, bytes_accessed=capacity * side * side + high * wide, transcendentals=0
    )
    held_scratch = [pltpu.VMEM(*held), pltpu.SemaphoreType.DMA((held[0][0],))]
    dense_shape = jax.ShapeDtypeStruct((high, col_blocks * side), jnp.bfloat16)
    whole = pl.BlockSpec(memory_space=pltpu.VMEM)
    apart = pl.BlockSpec(memory_space=pl.ANY)
    listed = pl.BlockSpec(memory_space=pltpu.SMEM)
    if steps > 1:
        block = ((high, wide), jnp.bfloat16)
        return [
            lambda packed: pl.pallas_call(
                functools.partial(build_whole_kernel, blocks=blocks, steps=steps),
                out_shape=dense_shape,
                grid_spec=pltpu.PrefetchScalarGridSpec(
                    num_scalar_prefetch=1,
                    grid=(steps,),
                    in_specs=[apart],
                    out_specs=pl.BlockSpec((high, wide), lambda i, *_: (0, i)),
                    scratch_shapes=[pltpu.VMEM(*total)] + held_scratch,
                ),
                compiler_params=pltpu.CompilerParams(
                    vmem_limit_bytes=scratch_bytes(total, held, block, block) + 4 * mib
                ),
                cost_estimate=cost,
                name="build_whole",
            )(packed, tiles)
        ]
    params = pltpu.CompilerParams(vmem_limit_bytes=build_grant * mib)
    scratch = [pltpu.VMEM(*total)] + held_scratch
    return [
        lambda packed: (packed, pl.pallas_call(
            functools.partial(build_first_kernel, blocks=blocks),
            out_shape=dense_shape,
            in_specs=[listed, apart],
            out_specs=whole,
            scratch_shapes=scratch,
            compiler_params=params,
            cost_estimate=cost,
            name="build_first",
        )(packed, tiles)),
        lambda state: pl.pallas_call(
            functools.partial(build_rest_kernel, blocks=blocks),
            out_shape=dense_shape,
            in_specs=[listed, apart, whole],
            out_specs=whole,
            scratch_shapes=scratch,
            compiler_params=params,
            cost_estimate=cost,
            name="build_rest",
        )(state[0], tiles, state[1]),
    ]


def ring_order(count, core):
    order = list(range(0, count, 2)) + list(range(count - 1, 0, -2))
    return order if core == 0 else order[:1] + order[:0:-1]


def turned(place, count):
    return jnp.where(lax.axis_index("col") & 1 == 1, lax.rem(count - place, count), place)


def ring_place(count):
    row = lax.axis_index("row")
    return turned(jnp.where(lax.rem(row, 2) == 0, row // 2, count - 1 - row // 2), count)


def ring_row(place, count):
    place = turned(lax.rem(place + 2 * count, count), count)
    return jnp.where(place < count // 2, 2 * place, 2 * (count - 1 - place) + 1)


def forward_kernel(dense_ref, *refs, pieces, sibling, row_count):
    piece_refs, out_ref = refs[: len(pieces)], refs[len(pieces)]
    count = lax.axis_size("col")
    rows = dense_ref.shape[0] // count
    block = dense_ref.shape[1] // row_count
    place = ring_place(row_count)
    col = lax.axis_index("col") ^ sibling
    operands = []
    for piece, ref in zip(pieces, piece_refs):
        for offset, first, start, high in piece:
            along = pl.ds(pl.multiple_of(ring_row(place + offset, row_count) * block + first, 128), high)
            operands.append((along, ref, pl.ds(start, high)))
    for index in range(count // 2):
        down = pl.ds(pl.multiple_of((col ^ (2 * index)) * rows, rows), rows)
        total = None
        for along, ref, part in operands:
            product = jnp.dot(dense_ref[down, along], ref[part, :], preferred_element_type=jnp.float32)
            total = product if total is None else total + product
        out_ref[pl.ds(index * rows, rows), :] = total.astype(jnp.bfloat16)


def forward_product(dense, shards, sibling, row_count, col_count):
    pieces = tuple(piece for piece, _ in shards)
    arrays = [array for _, array in shards]
    high, deep = dense.shape
    width = arrays[0].shape[1]
    half = high // 2
    cell = ((high, deep), jnp.bfloat16)
    depth = ((deep, width), jnp.bfloat16)
    out = ((high, width), jnp.float32)
    return pl.pallas_call(
        functools.partial(forward_kernel, pieces=pieces, sibling=sibling, row_count=row_count),
        out_shape=jax.ShapeDtypeStruct((half, width), jnp.bfloat16),
        in_specs=[pl.BlockSpec(memory_space=pltpu.VMEM)] * (1 + len(arrays)),
        out_specs=pl.BlockSpec(memory_space=pltpu.VMEM),
        compiler_params=pltpu.CompilerParams(vmem_limit_bytes=scratch_bytes(cell, depth, out) + 6 * mib),
        cost_estimate=pl.CostEstimate(
            flops=2 * half * deep * width,
            bytes_accessed=2 * (half * deep + deep * width + half * width),
            transcendentals=0,
        ),
        name="forward_product",
    )(dense, *arrays)


def partners_sum(values):
    while len(values) > 1:
        values = [values[i] + values[i + 1] for i in range(0, len(values), 2)]
    return values[0]


def middle_kernel(*refs, blocks, scale):
    sums, refs = refs[:blocks], refs[blocks:]
    weight_ref, refs = refs[0], refs[1:]
    cotangent_refs, (act_ref, message_ref, chunk_ref, product) = refs[:blocks], refs[blocks:]
    weight = weight_ref[...]
    rows, width = act_ref.shape
    over_nodes = (((0,), (0,)), ((), ()))
    terms = []
    for index in range(blocks):
        aggregate = partners_sum(
            [sums[other][pl.ds((index ^ other) * rows, rows), :].astype(jnp.float32) for other in range(blocks)]
        )
        high = aggregate.astype(jnp.bfloat16)
        low = (aggregate - high.astype(jnp.float32)).astype(jnp.bfloat16)
        pre = jnp.dot(high, weight, preferred_element_type=jnp.float32)
        pre += jnp.dot(low, weight, preferred_element_type=jnp.float32)
        sig = jax.nn.sigmoid(pre)
        cotangent = cotangent_refs[index][...].astype(jnp.float32)
        grad = (cotangent * sig * (1.0 + pre * (1.0 - sig))).astype(jnp.bfloat16)
        message_ref[pl.ds(index * width, width), :] = lax.dot_general(
            weight, grad, (((1,), (1,)), ((), ())), preferred_element_type=jnp.float32
        ).astype(jnp.bfloat16)
        if index == 0:
            act_ref[...] = (pre * sig).astype(jnp.bfloat16)
        part = lax.dot_general(high, grad, over_nodes, preferred_element_type=jnp.float32)
        part += lax.dot_general(low, grad, over_nodes, preferred_element_type=jnp.float32)
        terms.append(part)
    product[...] = partners_sum(terms) * scale
    col = lax.axis_index("col")
    size = chunk_ref.shape[0]
    core = col & 1
    chunk_ref[...] = product[pl.ds(pl.multiple_of(core * size, size), size), :]
    sent = product[pl.ds(pl.multiple_of((core ^ 1) * size, size), size), :]
    high = sent.astype(jnp.bfloat16)
    low = (sent - high.astype(jnp.float32)).astype(jnp.bfloat16)
    message_ref[pl.ds(blocks * width, size), :] = high
    message_ref[pl.ds(blocks * width + size, size), :] = low


def middle(sums, weight, cotangents, total_nodes):
    rows, width = cotangents[0].shape
    blocks = len(cotangents)
    size = width // 2
    return pl.pallas_call(
        functools.partial(middle_kernel, blocks=blocks, scale=1.0 / math.sqrt(total_nodes)),
        out_shape=[
            jax.ShapeDtypeStruct((rows, width), jnp.bfloat16),
            jax.ShapeDtypeStruct((blocks * width + 2 * size, rows), jnp.bfloat16),
            jax.ShapeDtypeStruct((size, width), jnp.float32),
        ],
        in_specs=[pl.BlockSpec(memory_space=pltpu.VMEM)] * (2 * blocks + 1),
        out_specs=[pl.BlockSpec(memory_space=pltpu.VMEM)] * 3,
        scratch_shapes=[pltpu.VMEM((width, width), jnp.float32)],
        compiler_params=pltpu.CompilerParams(vmem_limit_bytes=12 * mib),
        cost_estimate=pl.CostEstimate(
            flops=10 * blocks * rows * width * width,
            bytes_accessed=2 * (blocks * blocks + 2 * blocks + 4) * rows * width,
            transcendentals=blocks * rows * width,
        ),
        name="middle",
    )(*sums, weight, *cotangents)


def backward_kernel(dense_ref, own_ref, sibling_ref, chunk_ref, *refs, outputs, row_count):
    out_refs, (depth, sems) = refs[:-2], refs[-2:]
    count = lax.axis_size("col")
    width, rows = depth.shape[0], own_ref.shape[1]
    wide = dense_ref.shape[1] // row_count
    col = lax.axis_index("col")
    copies = []
    for index in range(count):
        block = pl.ds(index // 2 * width, width)
        along = pl.ds(pl.multiple_of((col ^ index) * rows, rows), rows)
        source = sibling_ref if index % 2 else own_ref
        copy = pltpu.make_async_copy(source.at[block], depth.at[:, along], sems.at[index])
        copy.start()
        copies.append(copy)
    size = chunk_ref.shape[0]
    from_sibling = count // 2 * width
    high, low = (sibling_ref[pl.ds(from_sibling + turn * size, size), :].astype(jnp.float32) for turn in range(2))
    terms = (chunk_ref[...] + (high + low)).astype(jnp.bfloat16)
    for copy in copies:
        copy.wait()
    place = ring_place(row_count)
    for (offset, tail), out_ref in zip(outputs, out_refs):
        if tail != "terms alone":
            along = pl.ds(pl.multiple_of(ring_row(place + offset, row_count) * wide, wide), wide)
            part = jnp.dot(depth[...], dense_ref[:, along], preferred_element_type=jnp.float32)
            out_ref[pl.ds(0, width), :] = part.astype(jnp.bfloat16)
        if tail == "terms alone":
            out_ref[...] = terms
        elif tail == "terms":
            out_ref[pl.ds(width, size), :] = terms
        elif tail == "zeros":
            out_ref[pl.ds(width, size), :] = jnp.zeros_like(terms)


def backward_product(dense, own, sibling, chunk, outputs, row_count, col_count):
    high, deep = dense.shape
    size, width = chunk.shape
    wide = deep // row_count
    heights = {"": width, "terms alone": size, "terms": width + size, "zeros": width + size}
    cell = ((high, deep), jnp.bfloat16)
    depth = ((width, high), jnp.bfloat16)
    out = ((len(outputs), width + size, wide), jnp.float32)
    return pl.pallas_call(
        functools.partial(backward_kernel, outputs=outputs, row_count=row_count),
        out_shape=[jax.ShapeDtypeStruct((heights[tail], wide), jnp.bfloat16) for _, tail in outputs],
        in_specs=[pl.BlockSpec(memory_space=pltpu.VMEM)] * 4,
        out_specs=[pl.BlockSpec(memory_space=pltpu.VMEM)] * len(outputs),
        scratch_shapes=[pltpu.VMEM(*depth), pltpu.SemaphoreType.DMA((col_count,))],
        compiler_params=pltpu.CompilerParams(vmem_limit_bytes=scratch_bytes(cell, depth, out) + 6 * mib),
        cost_estimate=pl.CostEstimate(
            flops=2 * high * wide * width, bytes_accessed=2 * wide * len(outputs) * width, transcendentals=0
        ),
        name="backward_product",
    )(dense, own, sibling, chunk)


def terms_kernel(*refs, offsets, first_rows):
    term_refs, out_ref, places = refs[:-2], refs[-2], refs[-1]
    row_count, size, _ = places.shape
    place = ring_place(row_count)
    for offset, first, ref in zip(offsets, first_rows, term_refs):
        places[ring_row(place + offset, row_count)] = ref[pl.ds(first, size), :].astype(jnp.float32)
    total = places[0]
    for index in range(1, row_count):
        total += places[index]
    out_ref[...] = total


def summed_terms(terms, size):
    offsets = tuple(offset for offset, _, _ in terms)
    first_rows = tuple(first for _, first, _ in terms)
    arrays = [array for _, _, array in terms]
    width = arrays[0].shape[1]
    return pl.pallas_call(
        functools.partial(terms_kernel, offsets=offsets, first_rows=first_rows),
        out_shape=jax.ShapeDtypeStruct((size, width), jnp.float32),
        in_specs=[pl.BlockSpec(memory_space=pltpu.VMEM)] * len(arrays),
        out_specs=pl.BlockSpec(memory_space=pltpu.VMEM),
        scratch_shapes=[pltpu.VMEM((len(arrays), size, width), jnp.float32)],
        compiler_params=pltpu.CompilerParams(
            vmem_limit_bytes=scratch_bytes(*((array.shape, array.dtype) for array in arrays)) + 8 * mib
        ),
        cost_estimate=pl.CostEstimate(
            flops=len(arrays) * size * width, bytes_accessed=2 * len(arrays) * size * width, transcendentals=0
        ),
        name="summed_terms",
    )(*arrays)


def finish_kernel(*refs):
    *part_refs, features_ref = refs
    width = features_ref.shape[1]
    total = part_refs[0][pl.ds(0, width), :].astype(jnp.float32)
    for part_ref in part_refs[1:]:
        total += part_ref[pl.ds(0, width), :].astype(jnp.float32)
    features_ref[...] = total.astype(jnp.bfloat16).T


def finish(parts):
    width, rows = parts[0].shape
    return pl.pallas_call(
        finish_kernel,
        out_shape=jax.ShapeDtypeStruct((rows, width), jnp.bfloat16),
        in_specs=[pl.BlockSpec(memory_space=pltpu.VMEM)] * len(parts),
        out_specs=pl.BlockSpec(memory_space=pltpu.VMEM),
        compiler_params=pltpu.CompilerParams(vmem_limit_bytes=8 * mib),
        cost_estimate=pl.CostEstimate(
            flops=len(parts) * rows * width, bytes_accessed=2 * (len(parts) + 1) * rows * width, transcendentals=0
        ),
        name="finish",
    )(*parts)


def joined_kernel(own_ref, sibling_ref, weight_ref):
    rows = own_ref.shape[0]
    core = lax.axis_index("col") & 1
    for turn, ref in enumerate((own_ref, sibling_ref)):
        weight_ref[pl.ds(pl.multiple_of((core ^ turn) * rows, rows), rows), :] = ref[...]


def joined(own, sibling):
    rows, width = own.shape
    return pl.pallas_call(
        joined_kernel,
        out_shape=jax.ShapeDtypeStruct((2 * rows, width), jnp.float32),
        in_specs=[pl.BlockSpec(memory_space=pltpu.VMEM)] * 2,
        out_specs=pl.BlockSpec(memory_space=pltpu.VMEM),
        compiler_params=pltpu.CompilerParams(vmem_limit_bytes=8 * mib),
        cost_estimate=pl.CostEstimate(flops=0, bytes_accessed=16 * rows * width, transcendentals=0),
        name="joined",
    )(own, sibling)


def around(value, step):
    row_count, col_count = lax.axis_size("row"), lax.axis_size("col")
    pairs = []
    for col in range(col_count):
        order = ring_order(row_count, col % 2)
        for place, row in enumerate(order):
            pairs.append((row * col_count + col, order[(place + step) % row_count] * col_count + col))
    return lax.ppermute(value, ("row", "col"), pairs)


def swapped(value, axis, partner):
    return lax.ppermute(value, axis, [(i, i ^ partner) for i in range(lax.axis_size(axis))])


def gathered_shards(own, packed, stages, cotangent):
    reach = lax.axis_size("row") // 2
    rows = own.shape[0]
    ups, downs, dense = [own], [own], packed
    others = []
    for step in range(1, reach + 1):
        up = around(ups[-1], 1)
        if step == reach - 1:
            up, dense, others = lax.optimization_barrier((up, dense, others))
        ups.append(up)
        if step == reach:
            break
        down = around(downs[-1], -1)
        if step == 1:
            down, dense = lax.optimization_barrier((down, dense))
        elif step == 2:
            dense = stages.pop(0)(dense)
            down, dense, cotangent = lax.optimization_barrier((down, dense, cotangent))
            others = [swapped(cotangent, "col", partner) for partner in range(2, lax.axis_size("col"), 2)]
        downs.append(down)
    if stages:
        dense = stages.pop(0)(dense)
    shards = [(((0, 0, 0, rows),), own)]
    shards += [(((-step, 0, 0, rows),), ups[step]) for step in range(1, reach + 1)]
    shards += [(((step, 0, 0, rows),), downs[step]) for step in range(1, reach)]
    return shards, dense, [cotangent] + others


def added(first, second):
    return (first.astype(jnp.float32) + second[: first.shape[0]].astype(jnp.float32)).astype(jnp.bfloat16)


def scattered_sums(dense, own, sibling, chunk):
    row_count, col_count = lax.axis_size("row"), lax.axis_size("col")
    size, width = chunk.shape
    reach = row_count // 2
    first = ((reach, "terms"), (1 - reach, "terms"), (0, "terms alone"))
    above, below, terms = backward_product(dense, own, sibling, chunk, first, row_count, col_count)
    above, below, terms, cell = lax.optimization_barrier((above, below, terms, dense))
    up, down = around(above, 1), around(below, -1)
    all_terms = [(0, 0, terms)]

    ups = tuple((offset, "zeros") for offset in range(reach - 1, 0, -1))
    downs = tuple((-offset, "zeros") for offset in range(reach - 2, 0, -1))
    strips = backward_product(cell, own, sibling, chunk, ups + downs + ((0, ""),), row_count, col_count)
    ups, downs, mine = strips[: reach - 1], strips[reach - 1 : -1], strips[-1]
    for step in range(1, reach):
        all_terms += [(-step, width, up), (step, width, down)]
        up = around(added(ups[step - 1], up), 1)
        if step < reach - 1:
            down = around(added(downs[step - 1], down), -1)
    all_terms.append((reach, width, up))
    return [mine, up, down], summed_terms(all_terms, size)


def per_device(features, weight, adj_tiles, tile_rows, tile_cols, tile_counts, out_grad):
    node_rows, width = features.shape
    capacity, side = adj_tiles.shape[2:4]
    tiles = adj_tiles.reshape(capacity, side, side)
    packed = jnp.concatenate([tile_rows, tile_cols, tile_counts[:, :, None]], axis=2).reshape(2 * capacity + 1)
    row_count = lax.axis_size("row")
    col_count = lax.axis_size("col")
    per_strip = node_rows // side
    stages = build_stages(tiles, col_count * per_strip, row_count * per_strip, per_strip)
    shards, dense, cotangents = gathered_shards(features, packed, stages, out_grad)

    for_sibling = forward_product(dense, shards, 1, row_count, col_count)
    for_sibling, cell = lax.optimization_barrier((for_sibling, dense))
    sums = added(forward_product(cell, shards, 0, row_count, col_count), swapped(for_sibling, "col", 1))
    sums = [sums] + [swapped(sums, "col", partner) for partner in range(2, col_count, 2)]
    activations, message, chunk = middle(sums, weight, cotangents, node_rows * row_count * col_count)
    sibling = swapped(message, "col", 1)
    parts, half = scattered_sums(dense, message, sibling, chunk)
    grad_weight = joined(half, swapped(half, "col", 1))
    return (activations, finish(parts), grad_weight)


def solution(mesh):
    placed = (
        P(("row", "col"), None),
        P(),
        P("row", "col", None, None, None),
        P("row", "col", None),
        P("row", "col", None),
        P("row", "col"),
        P(("row", "col"), None),
    )
    return jax.shard_map(
        per_device,
        mesh=mesh,
        in_specs=placed,
        out_specs=(P(("row", "col"), None), P(("row", "col"), None), P()),
        check_vma=False,
    )
```

```python
import functools
import math

import jax
import jax.numpy as jnp
from jax import lax
from jax.experimental import pallas as pl
from jax.experimental.pallas import tpu as pltpu
from jax.sharding import PartitionSpec as P

chunk_tiles = 16
chunk_slots = 8
build_grant = 44
strips_per_step = 8
mib = 1024 * 1024


def scratch_bytes(*shapes):
    return sum(math.prod(shape) * jnp.dtype(kind).itemsize for shape, kind in shapes)


def add_tiles(list_ref, tiles_ref, total, held, sems, begin, end, *, first_block, blocks, steps):
    side = tiles_ref.shape[1]
    capacity = tiles_ref.shape[0]
    count = list_ref[2 * capacity]
    slots = held.shape[0]
    row_blocks = total.shape[0] // side - 1

    def fetch(index):
        slot = lax.rem(index - begin, slots)
        return pltpu.make_async_copy(
            tiles_ref.at[pl.ds(index * chunk_tiles, chunk_tiles)], held.at[slot], sems.at[slot]
        )

    def start(index, carry):
        fetch(index).start()
        return carry

    lax.fori_loop(begin, jnp.minimum(end, begin + slots), start, 0)

    def target(place):
        col = list_ref[capacity + place] - first_block
        live = place < count
        if steps > 1:
            live = live & (col >= 0) & (col < blocks)
            col = jnp.where(live, col, 0)
        row = jnp.where(live, list_ref[place], row_blocks)
        return row, col

    def chunk_step(index, carry):
        fetch(index).wait()
        slot = lax.rem(index - begin, slots)
        for lane in range(0, chunk_tiles, 2):
            spots = [target(index * chunk_tiles + lane + turn) for turn in range(2)]
            at = [
                (pl.ds(pl.multiple_of(row * side, side), side), pl.ds(pl.multiple_of(col * side, side), side))
                for row, col in spots
            ]
            first, second = total[at[0]], total[at[1]]
            tiles = [held[slot, lane + turn].astype(jnp.float32) for turn in range(2)]
            same = (spots[0][0] == spots[1][0]) & (spots[0][1] == spots[1][1])
            total[at[0]] = first + tiles[0]
            total[at[1]] = second + tiles[1] + jnp.where(same, tiles[0], 0.0)

        @pl.when(index + slots < end)
        def _():
            fetch(index + slots).start()

        return carry

    return lambda: lax.fori_loop(begin, end, chunk_step, 0)


def each_row_block(total, side, action):
    def step(block, carry):
        action(pl.ds(pl.multiple_of(block * side, side), side))
        return carry

    lax.fori_loop(0, total.shape[0] // side - 1, step, 0)


def live_chunks(list_ref, tiles_ref):
    return (list_ref[2 * tiles_ref.shape[0]] + chunk_tiles - 1) // chunk_tiles


def first_chunks(list_ref, tiles_ref):
    return (live_chunks(list_ref, tiles_ref) * 3 + 7) // 8


def build_first_kernel(list_ref, tiles_ref, dense_ref, total, held, sems, *, blocks):
    part = first_chunks(list_ref, tiles_ref)
    run = add_tiles(list_ref, tiles_ref, total, held, sems, 0, part, first_block=0, blocks=blocks, steps=1)

    def clear(down):
        total[down, :] = jnp.zeros((down.size, total.shape[1]), jnp.float32)

    def rounded(down):
        dense_ref[down, :] = total[down, :].astype(jnp.bfloat16)

    each_row_block(total, tiles_ref.shape[1], clear)
    run()
    each_row_block(total, tiles_ref.shape[1], rounded)


def build_rest_kernel(list_ref, tiles_ref, half_ref, dense_ref, total, held, sems, *, blocks):
    chunks = live_chunks(list_ref, tiles_ref)
    run = add_tiles(
        list_ref, tiles_ref, total, held, sems, first_chunks(list_ref, tiles_ref), chunks,
        first_block=0, blocks=blocks, steps=1,
    )

    def widened(down):
        total[down, :] = half_ref[down, :].astype(jnp.float32)

    def rounded(down):
        dense_ref[down, :] = total[down, :].astype(jnp.bfloat16)

    each_row_block(total, tiles_ref.shape[1], widened)
    run()
    each_row_block(total, tiles_ref.shape[1], rounded)


def build_whole_kernel(list_ref, tiles_ref, dense_ref, total, held, sems, *, blocks, steps):
    chunks = live_chunks(list_ref, tiles_ref)
    first_block = pl.program_id(0) * blocks
    run = add_tiles(
        list_ref, tiles_ref, total, held, sems, 0, chunks, first_block=first_block, blocks=blocks, steps=steps
    )

    def clear(down):
        total[down, :] = jnp.zeros((down.size, total.shape[1]), jnp.float32)

    def rounded(down):
        dense_ref[down, :] = total[down, :].astype(jnp.bfloat16)

    each_row_block(total, tiles_ref.shape[1], clear)
    run()
    each_row_block(total, tiles_ref.shape[1], rounded)


def build_stages(tiles, row_blocks, col_blocks, per_strip):
    capacity, side, _ = tiles.shape
    blocks = min(strips_per_step * per_strip, col_blocks)
    steps = col_blocks // blocks
    high, wide = row_blocks * side, blocks * side
    total = ((high + side, wide), jnp.float32)
    held = ((min(chunk_slots, capacity // chunk_tiles), chunk_tiles, side, side), jnp.bfloat16)
    cost = pl.CostEstimate(
        flops=capacity * side * side, bytes_accessed=capacity * side * side + high * wide, transcendentals=0
    )
    held_scratch = [pltpu.VMEM(*held), pltpu.SemaphoreType.DMA((held[0][0],))]
    dense_shape = jax.ShapeDtypeStruct((high, col_blocks * side), jnp.bfloat16)
    whole = pl.BlockSpec(memory_space=pltpu.VMEM)
    apart = pl.BlockSpec(memory_space=pl.ANY)
    listed = pl.BlockSpec(memory_space=pltpu.SMEM)
    if steps > 1:
        block = ((high, wide), jnp.bfloat16)
        return [
            lambda packed: pl.pallas_call(
                functools.partial(build_whole_kernel, blocks=blocks, steps=steps),
                out_shape=dense_shape,
                grid_spec=pltpu.PrefetchScalarGridSpec(
                    num_scalar_prefetch=1,
                    grid=(steps,),
                    in_specs=[apart],
                    out_specs=pl.BlockSpec((high, wide), lambda i, *_: (0, i)),
                    scratch_shapes=[pltpu.VMEM(*total)] + held_scratch,
                ),
                compiler_params=pltpu.CompilerParams(
                    vmem_limit_bytes=scratch_bytes(total, held, block, block) + 4 * mib
                ),
                cost_estimate=cost,
                name="build_whole",
            )(packed, tiles)
        ]
    params = pltpu.CompilerParams(vmem_limit_bytes=build_grant * mib)
    scratch = [pltpu.VMEM(*total)] + held_scratch
    return [
        lambda packed: (packed, pl.pallas_call(
            functools.partial(build_first_kernel, blocks=blocks),
            out_shape=dense_shape,
            in_specs=[listed, apart],
            out_specs=whole,
            scratch_shapes=scratch,
            compiler_params=params,
            cost_estimate=cost,
            name="build_first",
        )(packed, tiles)),
        lambda state: pl.pallas_call(
            functools.partial(build_rest_kernel, blocks=blocks),
            out_shape=dense_shape,
            in_specs=[listed, apart, whole],
            out_specs=whole,
            scratch_shapes=scratch,
            compiler_params=params,
            cost_estimate=cost,
            name="build_rest",
        )(state[0], tiles, state[1]),
    ]


def ring_place(row, count):
    return jnp.where(lax.rem(row, 2) == 0, row // 2, count - 1 - row // 2)


def ring_row(place, count):
    place = lax.rem(place + 2 * count, count)
    return jnp.where(place < count // 2, 2 * place, 2 * (count - 1 - place) + 1)


def forward_kernel(dense_ref, *refs, pieces, sibling, row_count):
    piece_refs, out_ref = refs[: len(pieces)], refs[len(pieces)]
    count = lax.axis_size("col")
    rows = dense_ref.shape[0] // count
    block = dense_ref.shape[1] // row_count
    place = ring_place(lax.axis_index("row"), row_count)
    col = lax.axis_index("col") ^ sibling
    operands = []
    for piece, ref in zip(pieces, piece_refs):
        for offset, first, start, high in piece:
            along = pl.ds(pl.multiple_of(ring_row(place + offset, row_count) * block + first, 128), high)
            operands.append((along, ref, pl.ds(start, high)))
    for index in range(count // 2):
        down = pl.ds(pl.multiple_of((col ^ (2 * index)) * rows, rows), rows)
        total = None
        for along, ref, part in operands:
            product = jnp.dot(dense_ref[down, along], ref[part, :], preferred_element_type=jnp.float32)
            total = product if total is None else total + product
        out_ref[pl.ds(index * rows, rows), :] = total.astype(jnp.bfloat16)


def forward_product(dense, shards, sibling, row_count, col_count):
    pieces = tuple(piece for piece, _ in shards)
    arrays = [array for _, array in shards]
    high, deep = dense.shape
    width = arrays[0].shape[1]
    half = high // 2
    cell = ((high, deep), jnp.bfloat16)
    depth = ((deep, width), jnp.bfloat16)
    out = ((high, width), jnp.float32)
    return pl.pallas_call(
        functools.partial(forward_kernel, pieces=pieces, sibling=sibling, row_count=row_count),
        out_shape=jax.ShapeDtypeStruct((half, width), jnp.bfloat16),
        in_specs=[pl.BlockSpec(memory_space=pltpu.VMEM)] * (1 + len(arrays)),
        out_specs=pl.BlockSpec(memory_space=pltpu.VMEM),
        compiler_params=pltpu.CompilerParams(vmem_limit_bytes=scratch_bytes(cell, depth, out) + 6 * mib),
        cost_estimate=pl.CostEstimate(
            flops=2 * half * deep * width,
            bytes_accessed=2 * (half * deep + deep * width + half * width),
            transcendentals=0,
        ),
        name="forward_product",
    )(dense, *arrays)


def partners_sum(values):
    while len(values) > 1:
        values = [values[i] + values[i + 1] for i in range(0, len(values), 2)]
    return values[0]


def middle_kernel(*refs, blocks, scale):
    sums, refs = refs[:blocks], refs[blocks:]
    weight_ref, refs = refs[0], refs[1:]
    cotangent_refs, (act_ref, message_ref, chunk_ref, product) = refs[:blocks], refs[blocks:]
    weight = weight_ref[...]
    rows, width = act_ref.shape
    over_nodes = (((0,), (0,)), ((), ()))
    terms = []
    for index in range(blocks):
        aggregate = partners_sum(
            [sums[other][pl.ds((index ^ other) * rows, rows), :].astype(jnp.float32) for other in range(blocks)]
        )
        high = aggregate.astype(jnp.bfloat16)
        low = (aggregate - high.astype(jnp.float32)).astype(jnp.bfloat16)
        pre = jnp.dot(high, weight, preferred_element_type=jnp.float32)
        pre += jnp.dot(low, weight, preferred_element_type=jnp.float32)
        sig = jax.nn.sigmoid(pre)
        cotangent = cotangent_refs[index][...].astype(jnp.float32)
        grad = (cotangent * sig * (1.0 + pre * (1.0 - sig))).astype(jnp.bfloat16)
        message_ref[pl.ds(index * width, width), :] = lax.dot_general(
            weight, grad, (((1,), (1,)), ((), ())), preferred_element_type=jnp.float32
        ).astype(jnp.bfloat16)
        if index == 0:
            act_ref[...] = (pre * sig).astype(jnp.bfloat16)
        part = lax.dot_general(high, grad, over_nodes, preferred_element_type=jnp.float32)
        part += lax.dot_general(low, grad, over_nodes, preferred_element_type=jnp.float32)
        terms.append(part)
    product[...] = partners_sum(terms) * scale
    col = lax.axis_index("col")
    size = chunk_ref.shape[0]
    core = col & 1
    chunk_ref[...] = product[pl.ds(pl.multiple_of(core * size, size), size), :]
    sent = product[pl.ds(pl.multiple_of((core ^ 1) * size, size), size), :]
    high = sent.astype(jnp.bfloat16)
    low = (sent - high.astype(jnp.float32)).astype(jnp.bfloat16)
    message_ref[pl.ds(blocks * width, size), :] = high
    message_ref[pl.ds(blocks * width + size, size), :] = low


def middle(sums, weight, cotangents, total_nodes):
    rows, width = cotangents[0].shape
    blocks = len(cotangents)
    size = width // 2
    return pl.pallas_call(
        functools.partial(middle_kernel, blocks=blocks, scale=1.0 / math.sqrt(total_nodes)),
        out_shape=[
            jax.ShapeDtypeStruct((rows, width), jnp.bfloat16),
            jax.ShapeDtypeStruct((blocks * width + 2 * size, rows), jnp.bfloat16),
            jax.ShapeDtypeStruct((size, width), jnp.float32),
        ],
        in_specs=[pl.BlockSpec(memory_space=pltpu.VMEM)] * (2 * blocks + 1),
        out_specs=[pl.BlockSpec(memory_space=pltpu.VMEM)] * 3,
        scratch_shapes=[pltpu.VMEM((width, width), jnp.float32)],
        compiler_params=pltpu.CompilerParams(vmem_limit_bytes=12 * mib),
        cost_estimate=pl.CostEstimate(
            flops=10 * blocks * rows * width * width,
            bytes_accessed=2 * (blocks * blocks + 2 * blocks + 4) * rows * width,
            transcendentals=blocks * rows * width,
        ),
        name="middle",
    )(*sums, weight, *cotangents)


def backward_kernel(dense_ref, own_ref, sibling_ref, chunk_ref, *refs, outputs, row_count):
    out_refs, (depth, sems) = refs[:-2], refs[-2:]
    count = lax.axis_size("col")
    width, rows = depth.shape[0], own_ref.shape[1]
    wide = dense_ref.shape[1] // row_count
    col = lax.axis_index("col")
    copies = []
    for index in range(count):
        block = pl.ds(index // 2 * width, width)
        along = pl.ds(pl.multiple_of((col ^ index) * rows, rows), rows)
        source = sibling_ref if index % 2 else own_ref
        copy = pltpu.make_async_copy(source.at[block], depth.at[:, along], sems.at[index])
        copy.start()
        copies.append(copy)
    size = chunk_ref.shape[0]
    from_sibling = count // 2 * width
    high, low = (sibling_ref[pl.ds(from_sibling + turn * size, size), :].astype(jnp.float32) for turn in range(2))
    terms = (chunk_ref[...] + (high + low)).astype(jnp.bfloat16)
    for copy in copies:
        copy.wait()
    place = ring_place(lax.axis_index("row"), row_count)
    strips = {}
    for (offset, layout), out_ref in zip(outputs, out_refs):
        start = 0
        for kind, first, high in layout:
            if kind == "strip" and offset not in strips:
                along = pl.ds(pl.multiple_of(ring_row(place + offset, row_count) * wide, wide), wide)
                part = jnp.dot(depth[...], dense_ref[:, along], preferred_element_type=jnp.float32)
                strips[offset] = part.astype(jnp.bfloat16)
            source = {"strip": strips.get(offset), "terms": terms, "zeros": jnp.zeros_like(terms)}[kind]
            out_ref[start : start + high, :] = source[first : first + high, :]
            start += high


def backward_product(dense, own, sibling, chunk, outputs, row_count, col_count):
    high, deep = dense.shape
    size, width = chunk.shape
    wide = deep // row_count
    cell = ((high, deep), jnp.bfloat16)
    depth = ((width, high), jnp.bfloat16)
    out = ((len(outputs), width + size, wide), jnp.float32)
    return pl.pallas_call(
        functools.partial(backward_kernel, outputs=outputs, row_count=row_count),
        out_shape=[
            jax.ShapeDtypeStruct((sum(high for _, _, high in layout), wide), jnp.bfloat16) for _, layout in outputs
        ],
        in_specs=[pl.BlockSpec(memory_space=pltpu.VMEM)] * 4,
        out_specs=[pl.BlockSpec(memory_space=pltpu.VMEM)] * len(outputs),
        scratch_shapes=[pltpu.VMEM(*depth), pltpu.SemaphoreType.DMA((col_count,))],
        compiler_params=pltpu.CompilerParams(vmem_limit_bytes=scratch_bytes(cell, depth, out) + 6 * mib),
        cost_estimate=pl.CostEstimate(
            flops=2 * high * wide * width, bytes_accessed=2 * wide * len(outputs) * width, transcendentals=0
        ),
        name="backward_product",
    )(dense, own, sibling, chunk)


def terms_kernel(*refs, pieces):
    term_refs, out_ref, places = refs[:-2], refs[-2], refs[-1]
    row_count = places.shape[0]
    place = ring_place(lax.axis_index("row"), row_count)
    for (offset, first, high, at), ref in zip(pieces, term_refs):
        places[ring_row(place + offset, row_count), pl.ds(at, high), :] = ref[pl.ds(first, high), :].astype(jnp.float32)
    total = places[0]
    for index in range(1, row_count):
        total += places[index]
    out_ref[...] = total


def summed_terms(terms, size, row_count):
    pieces = tuple(piece for *piece, _ in terms)
    arrays = [array for *_, array in terms]
    width = arrays[0].shape[1]
    return pl.pallas_call(
        functools.partial(terms_kernel, pieces=pieces),
        out_shape=jax.ShapeDtypeStruct((size, width), jnp.float32),
        in_specs=[pl.BlockSpec(memory_space=pltpu.VMEM)] * len(arrays),
        out_specs=pl.BlockSpec(memory_space=pltpu.VMEM),
        scratch_shapes=[pltpu.VMEM((row_count, size, width), jnp.float32)],
        compiler_params=pltpu.CompilerParams(
            vmem_limit_bytes=scratch_bytes(*((array.shape, array.dtype) for array in arrays))
            + scratch_bytes(((row_count, size, width), jnp.float32))
            + 6 * mib
        ),
        cost_estimate=pl.CostEstimate(
            flops=row_count * size * width, bytes_accessed=2 * row_count * size * width, transcendentals=0
        ),
        name="summed_terms",
    )(*arrays)


def finish_kernel(*refs, firsts):
    *part_refs, features_ref = refs
    width = features_ref.shape[1]
    total = jnp.zeros(features_ref.shape[::-1], jnp.float32)
    for first, part_ref in zip(firsts, part_refs):
        total += part_ref[pl.ds(first, width), :].astype(jnp.float32)
    features_ref[...] = total.astype(jnp.bfloat16).T


def finish(parts):
    firsts = tuple(first for first, _ in parts)
    parts = [array for _, array in parts]
    width, rows = parts[0].shape
    return pl.pallas_call(
        functools.partial(finish_kernel, firsts=firsts),
        out_shape=jax.ShapeDtypeStruct((rows, width), jnp.bfloat16),
        in_specs=[pl.BlockSpec(memory_space=pltpu.VMEM)] * len(parts),
        out_specs=pl.BlockSpec(memory_space=pltpu.VMEM),
        compiler_params=pltpu.CompilerParams(vmem_limit_bytes=8 * mib),
        cost_estimate=pl.CostEstimate(
            flops=len(parts) * rows * width, bytes_accessed=2 * (len(parts) + 1) * rows * width, transcendentals=0
        ),
        name="finish",
    )(*parts)


def joined_kernel(own_ref, sibling_ref, weight_ref):
    rows = own_ref.shape[0]
    core = lax.axis_index("col") & 1
    for turn, ref in enumerate((own_ref, sibling_ref)):
        weight_ref[pl.ds(pl.multiple_of((core ^ turn) * rows, rows), rows), :] = ref[...]


def joined(own, sibling):
    rows, width = own.shape
    return pl.pallas_call(
        joined_kernel,
        out_shape=jax.ShapeDtypeStruct((2 * rows, width), jnp.float32),
        in_specs=[pl.BlockSpec(memory_space=pltpu.VMEM)] * 2,
        out_specs=pl.BlockSpec(memory_space=pltpu.VMEM),
        compiler_params=pltpu.CompilerParams(vmem_limit_bytes=8 * mib),
        cost_estimate=pl.CostEstimate(flops=0, bytes_accessed=16 * rows * width, transcendentals=0),
        name="joined",
    )(own, sibling)


def around(value, step):
    count = lax.axis_size("row")
    order = list(range(0, count, 2)) + list(range(count - 1, 0, -2))
    return lax.ppermute(value, "row", [(order[i], order[(i + step) % count]) for i in range(count)])


def swapped(value, axis, partner):
    return lax.ppermute(value, axis, [(i, i ^ partner) for i in range(lax.axis_size(axis))])


def gathered_shards(own, packed, stages, cotangent):
    reach = lax.axis_size("row") // 2
    rows = own.shape[0]
    ups, downs, dense = [own], [own], packed
    others = []
    for step in range(1, reach + 1):
        up = around(ups[-1], 1)
        if step == reach - 1:
            up, dense, others = lax.optimization_barrier((up, dense, others))
        ups.append(up)
        if step == reach:
            break
        down = around(downs[-1], -1)
        if step == 1:
            down, dense = lax.optimization_barrier((down, dense))
        elif step == 2:
            dense = stages.pop(0)(dense)
            down, dense, cotangent = lax.optimization_barrier((down, dense, cotangent))
            others = [swapped(cotangent, "col", partner) for partner in range(2, lax.axis_size("col"), 2)]
        downs.append(down)
    if stages:
        dense = stages.pop(0)(dense)
    shards = [(((0, 0, 0, rows),), own)]
    shards += [(((-step, 0, 0, rows),), ups[step]) for step in range(1, reach + 1)]
    shards += [(((step, 0, 0, rows),), downs[step]) for step in range(1, reach)]
    return shards, dense, [cotangent] + others


def added(first, second, at=0):
    spare = first.shape[0] - at - second.shape[0]
    second = jnp.pad(second.astype(jnp.float32), ((at, spare), (0, 0)))
    return (first.astype(jnp.float32) + second).astype(jnp.bfloat16)


def scattered_sums(dense, own, sibling, chunk):
    row_count, col_count = lax.axis_size("row"), lax.axis_size("col")
    size, width = chunk.shape
    half, half_size = width // 2, size // 2
    reach = row_count // 2
    strip, terms, zeros = ("strip", 0, width), ("terms", 0, size), ("zeros", 0, size)
    first = (
        (reach, (terms, ("strip", 0, half))),
        (reach, (("strip", half, half), terms)),
        (0, (terms,)),
    )
    above, below, terms = backward_product(dense, own, sibling, chunk, first, row_count, col_count)
    above, below, terms, cell = lax.optimization_barrier((above, below, terms, dense))
    up, down = around(above, 1), around(below, -1)
    all_terms = [(0, 0, size, 0, terms)]

    few_zeros = ("zeros", 0, half_size)
    ups = tuple((offset, (zeros if offset > 1 else few_zeros, strip)) for offset in range(reach - 1, 0, -1))
    downs = tuple((-offset, (strip, zeros if offset > 1 else few_zeros)) for offset in range(reach - 1, 0, -1))
    strips = backward_product(cell, own, sibling, chunk, ups + downs + ((0, (strip,)),), row_count, col_count)
    ups, downs, mine = strips[: reach - 1], strips[reach - 1 : -1], strips[-1]
    for step in range(1, reach):
        all_terms += [(-step, 0, size, 0, up), (step, down.shape[0] - size, size, 0, down)]
        if step == reach - 1:
            up, down = up[half_size:], down[: width + half_size]
        up = around(added(ups[step - 1], up), 1)
        down = around(added(downs[step - 1], down, half if step == 1 else 0), -1)
    all_terms += [(reach, 0, half_size, half_size, up), (reach, width, half_size, 0, down)]
    return [(0, mine), (half_size, up), (0, down)], summed_terms(all_terms, size, row_count)


def per_device(features, weight, adj_tiles, tile_rows, tile_cols, tile_counts, out_grad):
    node_rows, width = features.shape
    capacity, side = adj_tiles.shape[2:4]
    tiles = adj_tiles.reshape(capacity, side, side)
    packed = jnp.concatenate([tile_rows, tile_cols, tile_counts[:, :, None]], axis=2).reshape(2 * capacity + 1)
    row_count = lax.axis_size("row")
    col_count = lax.axis_size("col")
    per_strip = node_rows // side
    stages = build_stages(tiles, col_count * per_strip, row_count * per_strip, per_strip)
    shards, dense, cotangents = gathered_shards(features, packed, stages, out_grad)

    for_sibling = forward_product(dense, shards, 1, row_count, col_count)
    for_sibling, cell = lax.optimization_barrier((for_sibling, dense))
    sums = added(forward_product(cell, shards, 0, row_count, col_count), swapped(for_sibling, "col", 1))
    sums = [sums] + [swapped(sums, "col", partner) for partner in range(2, col_count, 2)]
    activations, message, chunk = middle(sums, weight, cotangents, node_rows * row_count * col_count)
    sibling = swapped(message, "col", 1)
    parts, half = scattered_sums(dense, message, sibling, chunk)
    grad_weight = joined(half, swapped(half, "col", 1))
    return (activations, finish(parts), grad_weight)


def solution(mesh):
    placed = (
        P(("row", "col"), None),
        P(),
        P("row", "col", None, None, None),
        P("row", "col", None),
        P("row", "col", None),
        P("row", "col"),
        P(("row", "col"), None),
    )
    return jax.shard_map(
        per_device,
        mesh=mesh,
        in_specs=placed,
        out_specs=(P(("row", "col"), None), P(("row", "col"), None), P()),
        check_vma=False,
    )
```

```python
import functools
import math

import jax
import jax.numpy as jnp
from jax import lax
from jax.experimental import pallas as pl
from jax.experimental.pallas import tpu as pltpu
from jax.sharding import PartitionSpec as P

chunk_tiles = 16
chunk_slots = 8
build_grant = 44
strips_per_step = 8
mib = 1024 * 1024


def scratch_bytes(*shapes):
    return sum(math.prod(shape) * jnp.dtype(kind).itemsize for shape, kind in shapes)


def add_tiles(list_ref, tiles_ref, total, held, sems, begin, end, *, first_block, blocks, steps):
    side = tiles_ref.shape[1]
    capacity = tiles_ref.shape[0]
    count = list_ref[2 * capacity]
    slots = held.shape[0]
    row_blocks = total.shape[0] // side - 1

    def fetch(index):
        slot = lax.rem(index - begin, slots)
        return pltpu.make_async_copy(
            tiles_ref.at[pl.ds(index * chunk_tiles, chunk_tiles)], held.at[slot], sems.at[slot]
        )

    def start(index, carry):
        fetch(index).start()
        return carry

    lax.fori_loop(begin, jnp.minimum(end, begin + slots), start, 0)

    def target(place):
        col = list_ref[capacity + place] - first_block
        live = place < count
        if steps > 1:
            live = live & (col >= 0) & (col < blocks)
            col = jnp.where(live, col, 0)
        row = jnp.where(live, list_ref[place], row_blocks)
        return row, col

    def chunk_step(index, carry):
        fetch(index).wait()
        slot = lax.rem(index - begin, slots)
        spots = [target(index * chunk_tiles + lane) for lane in range(chunk_tiles)]
        at = [
            (pl.ds(pl.multiple_of(row * side, side), side), pl.ds(pl.multiple_of(col * side, side), side))
            for row, col in spots
        ]
        current = total[at[0]]
        for lane in range(chunk_tiles):
            last = lane == chunk_tiles - 1
            following = None if last else total[at[lane + 1]]
            current = current + held[slot, lane].astype(jnp.float32)
            total[at[lane]] = current
            if not last:
                same = (spots[lane][0] == spots[lane + 1][0]) & (spots[lane][1] == spots[lane + 1][1])
                current = jnp.where(same, current, following)

        @pl.when(index + slots < end)
        def _():
            fetch(index + slots).start()

        return carry

    return lambda: lax.fori_loop(begin, end, chunk_step, 0)


def each_row_block(total, side, action):
    def step(block, carry):
        action(pl.ds(pl.multiple_of(block * side, side), side))
        return carry

    lax.fori_loop(0, total.shape[0] // side - 1, step, 0)


def live_chunks(list_ref, tiles_ref):
    return (list_ref[2 * tiles_ref.shape[0]] + chunk_tiles - 1) // chunk_tiles


def first_chunks(list_ref, tiles_ref):
    return (live_chunks(list_ref, tiles_ref) * 3 + 7) // 8


def build_first_kernel(list_ref, tiles_ref, dense_ref, total, held, sems, *, blocks):
    part = first_chunks(list_ref, tiles_ref)
    run = add_tiles(list_ref, tiles_ref, total, held, sems, 0, part, first_block=0, blocks=blocks, steps=1)

    def clear(down):
        total[down, :] = jnp.zeros((down.size, total.shape[1]), jnp.float32)

    def rounded(down):
        dense_ref[down, :] = total[down, :].astype(jnp.bfloat16)

    each_row_block(total, tiles_ref.shape[1], clear)
    run()
    each_row_block(total, tiles_ref.shape[1], rounded)


def build_rest_kernel(list_ref, tiles_ref, half_ref, dense_ref, total, held, sems, *, blocks):
    chunks = live_chunks(list_ref, tiles_ref)
    run = add_tiles(
        list_ref, tiles_ref, total, held, sems, first_chunks(list_ref, tiles_ref), chunks,
        first_block=0, blocks=blocks, steps=1,
    )

    def widened(down):
        total[down, :] = half_ref[down, :].astype(jnp.float32)

    def rounded(down):
        dense_ref[down, :] = total[down, :].astype(jnp.bfloat16)

    each_row_block(total, tiles_ref.shape[1], widened)
    run()
    each_row_block(total, tiles_ref.shape[1], rounded)


def build_whole_kernel(list_ref, tiles_ref, dense_ref, total, held, sems, *, blocks, steps):
    chunks = live_chunks(list_ref, tiles_ref)
    first_block = pl.program_id(0) * blocks
    run = add_tiles(
        list_ref, tiles_ref, total, held, sems, 0, chunks, first_block=first_block, blocks=blocks, steps=steps
    )

    def clear(down):
        total[down, :] = jnp.zeros((down.size, total.shape[1]), jnp.float32)

    def rounded(down):
        dense_ref[down, :] = total[down, :].astype(jnp.bfloat16)

    each_row_block(total, tiles_ref.shape[1], clear)
    run()
    each_row_block(total, tiles_ref.shape[1], rounded)


def build_stages(tiles, row_blocks, col_blocks, per_strip):
    capacity, side, _ = tiles.shape
    blocks = min(strips_per_step * per_strip, col_blocks)
    steps = col_blocks // blocks
    high, wide = row_blocks * side, blocks * side
    total = ((high + side, wide), jnp.float32)
    held = ((min(chunk_slots, capacity // chunk_tiles), chunk_tiles, side, side), jnp.bfloat16)
    cost = pl.CostEstimate(
        flops=capacity * side * side, bytes_accessed=capacity * side * side + high * wide, transcendentals=0
    )
    held_scratch = [pltpu.VMEM(*held), pltpu.SemaphoreType.DMA((held[0][0],))]
    dense_shape = jax.ShapeDtypeStruct((high, col_blocks * side), jnp.bfloat16)
    whole = pl.BlockSpec(memory_space=pltpu.VMEM)
    apart = pl.BlockSpec(memory_space=pl.ANY)
    listed = pl.BlockSpec(memory_space=pltpu.SMEM)
    if steps > 1:
        block = ((high, wide), jnp.bfloat16)
        return [
            lambda packed: pl.pallas_call(
                functools.partial(build_whole_kernel, blocks=blocks, steps=steps),
                out_shape=dense_shape,
                grid_spec=pltpu.PrefetchScalarGridSpec(
                    num_scalar_prefetch=1,
                    grid=(steps,),
                    in_specs=[apart],
                    out_specs=pl.BlockSpec((high, wide), lambda i, *_: (0, i)),
                    scratch_shapes=[pltpu.VMEM(*total)] + held_scratch,
                ),
                compiler_params=pltpu.CompilerParams(
                    vmem_limit_bytes=scratch_bytes(total, held, block, block) + 4 * mib
                ),
                cost_estimate=cost,
                name="build_whole",
            )(packed, tiles)
        ]
    params = pltpu.CompilerParams(vmem_limit_bytes=build_grant * mib)
    scratch = [pltpu.VMEM(*total)] + held_scratch
    return [
        lambda packed: (packed, pl.pallas_call(
            functools.partial(build_first_kernel, blocks=blocks),
            out_shape=dense_shape,
            in_specs=[listed, apart],
            out_specs=whole,
            scratch_shapes=scratch,
            compiler_params=params,
            cost_estimate=cost,
            name="build_first",
        )(packed, tiles)),
        lambda state: pl.pallas_call(
            functools.partial(build_rest_kernel, blocks=blocks),
            out_shape=dense_shape,
            in_specs=[listed, apart, whole],
            out_specs=whole,
            scratch_shapes=scratch,
            compiler_params=params,
            cost_estimate=cost,
            name="build_rest",
        )(state[0], tiles, state[1]),
    ]


def ring_place(row, count):
    return jnp.where(lax.rem(row, 2) == 0, row // 2, count - 1 - row // 2)


def ring_row(place, count):
    place = lax.rem(place + 2 * count, count)
    return jnp.where(place < count // 2, 2 * place, 2 * (count - 1 - place) + 1)


def forward_kernel(dense_ref, *refs, pieces, sibling, row_count):
    piece_refs, out_ref = refs[: len(pieces)], refs[len(pieces)]
    count = lax.axis_size("col")
    rows = dense_ref.shape[0] // count
    block = dense_ref.shape[1] // row_count
    place = ring_place(lax.axis_index("row"), row_count)
    col = lax.axis_index("col") ^ sibling
    operands = []
    for piece, ref in zip(pieces, piece_refs):
        for offset, first, start, high in piece:
            along = pl.ds(pl.multiple_of(ring_row(place + offset, row_count) * block + first, 128), high)
            operands.append((along, ref, pl.ds(start, high)))
    for index in range(count // 2):
        down = pl.ds(pl.multiple_of((col ^ (2 * index)) * rows, rows), rows)
        total = None
        for along, ref, part in operands:
            product = jnp.dot(dense_ref[down, along], ref[part, :], preferred_element_type=jnp.float32)
            total = product if total is None else total + product
        out_ref[pl.ds(index * rows, rows), :] = total.astype(jnp.bfloat16)


def forward_product(dense, shards, sibling, row_count, col_count):
    pieces = tuple(piece for piece, _ in shards)
    arrays = [array for _, array in shards]
    high, deep = dense.shape
    width = arrays[0].shape[1]
    half = high // 2
    cell = ((high, deep), jnp.bfloat16)
    depth = ((deep, width), jnp.bfloat16)
    out = ((high, width), jnp.float32)
    return pl.pallas_call(
        functools.partial(forward_kernel, pieces=pieces, sibling=sibling, row_count=row_count),
        out_shape=jax.ShapeDtypeStruct((half, width), jnp.bfloat16),
        in_specs=[pl.BlockSpec(memory_space=pltpu.VMEM)] * (1 + len(arrays)),
        out_specs=pl.BlockSpec(memory_space=pltpu.VMEM),
        compiler_params=pltpu.CompilerParams(vmem_limit_bytes=scratch_bytes(cell, depth, out) + 6 * mib),
        cost_estimate=pl.CostEstimate(
            flops=2 * half * deep * width,
            bytes_accessed=2 * (half * deep + deep * width + half * width),
            transcendentals=0,
        ),
        name="forward_product",
    )(dense, *arrays)


def partners_sum(values):
    while len(values) > 1:
        values = [values[i] + values[i + 1] for i in range(0, len(values), 2)]
    return values[0]


def middle_kernel(*refs, blocks, scale):
    sums, refs = refs[:blocks], refs[blocks:]
    weight_ref, refs = refs[0], refs[1:]
    cotangent_refs, (act_ref, message_ref, chunk_ref, product) = refs[:blocks], refs[blocks:]
    weight = weight_ref[...]
    rows, width = act_ref.shape
    over_nodes = (((0,), (0,)), ((), ()))
    terms = []
    for index in range(blocks):
        aggregate = partners_sum(
            [sums[other][pl.ds((index ^ other) * rows, rows), :].astype(jnp.float32) for other in range(blocks)]
        )
        high = aggregate.astype(jnp.bfloat16)
        low = (aggregate - high.astype(jnp.float32)).astype(jnp.bfloat16)
        pre = jnp.dot(high, weight, preferred_element_type=jnp.float32)
        pre += jnp.dot(low, weight, preferred_element_type=jnp.float32)
        sig = jax.nn.sigmoid(pre)
        cotangent = cotangent_refs[index][...].astype(jnp.float32)
        grad = (cotangent * sig * (1.0 + pre * (1.0 - sig))).astype(jnp.bfloat16)
        message_ref[pl.ds(index * width, width), :] = lax.dot_general(
            weight, grad, (((1,), (1,)), ((), ())), preferred_element_type=jnp.float32
        ).astype(jnp.bfloat16)
        if index == 0:
            act_ref[...] = (pre * sig).astype(jnp.bfloat16)
        part = lax.dot_general(high, grad, over_nodes, preferred_element_type=jnp.float32)
        part += lax.dot_general(low, grad, over_nodes, preferred_element_type=jnp.float32)
        terms.append(part)
    product[...] = partners_sum(terms) * scale
    col = lax.axis_index("col")
    size = chunk_ref.shape[0]
    core = col & 1
    chunk_ref[...] = product[pl.ds(pl.multiple_of(core * size, size), size), :]
    sent = product[pl.ds(pl.multiple_of((core ^ 1) * size, size), size), :]
    high = sent.astype(jnp.bfloat16)
    low = (sent - high.astype(jnp.float32)).astype(jnp.bfloat16)
    message_ref[pl.ds(blocks * width, size), :] = high
    message_ref[pl.ds(blocks * width + size, size), :] = low


def middle(sums, weight, cotangents, total_nodes):
    rows, width = cotangents[0].shape
    blocks = len(cotangents)
    size = width // 2
    return pl.pallas_call(
        functools.partial(middle_kernel, blocks=blocks, scale=1.0 / math.sqrt(total_nodes)),
        out_shape=[
            jax.ShapeDtypeStruct((rows, width), jnp.bfloat16),
            jax.ShapeDtypeStruct((blocks * width + 2 * size, rows), jnp.bfloat16),
            jax.ShapeDtypeStruct((size, width), jnp.float32),
        ],
        in_specs=[pl.BlockSpec(memory_space=pltpu.VMEM)] * (2 * blocks + 1),
        out_specs=[pl.BlockSpec(memory_space=pltpu.VMEM)] * 3,
        scratch_shapes=[pltpu.VMEM((width, width), jnp.float32)],
        compiler_params=pltpu.CompilerParams(vmem_limit_bytes=12 * mib),
        cost_estimate=pl.CostEstimate(
            flops=10 * blocks * rows * width * width,
            bytes_accessed=2 * (blocks * blocks + 2 * blocks + 4) * rows * width,
            transcendentals=blocks * rows * width,
        ),
        name="middle",
    )(*sums, weight, *cotangents)


def backward_kernel(dense_ref, own_ref, sibling_ref, chunk_ref, *refs, outputs, row_count):
    out_refs, (depth, sems) = refs[:-2], refs[-2:]
    count = lax.axis_size("col")
    width, rows = depth.shape[0], own_ref.shape[1]
    wide = dense_ref.shape[1] // row_count
    col = lax.axis_index("col")
    copies = []
    for index in range(count):
        block = pl.ds(index // 2 * width, width)
        along = pl.ds(pl.multiple_of((col ^ index) * rows, rows), rows)
        source = sibling_ref if index % 2 else own_ref
        copy = pltpu.make_async_copy(source.at[block], depth.at[:, along], sems.at[index])
        copy.start()
        copies.append(copy)
    size = chunk_ref.shape[0]
    from_sibling = count // 2 * width
    high, low = (sibling_ref[pl.ds(from_sibling + turn * size, size), :].astype(jnp.float32) for turn in range(2))
    terms = (chunk_ref[...] + (high + low)).astype(jnp.bfloat16)
    for copy in copies:
        copy.wait()
    place = ring_place(lax.axis_index("row"), row_count)
    strips = {}
    for (offset, layout), out_ref in zip(outputs, out_refs):
        start = 0
        for kind, first, high in layout:
            if kind == "strip" and offset not in strips:
                along = pl.ds(pl.multiple_of(ring_row(place + offset, row_count) * wide, wide), wide)
                part = jnp.dot(depth[...], dense_ref[:, along], preferred_element_type=jnp.float32)
                strips[offset] = part.astype(jnp.bfloat16)
            source = {"strip": strips.get(offset), "terms": terms, "zeros": jnp.zeros_like(terms)}[kind]
            out_ref[start : start + high, :] = source[first : first + high, :]
            start += high


def backward_product(dense, own, sibling, chunk, outputs, row_count, col_count):
    high, deep = dense.shape
    size, width = chunk.shape
    wide = deep // row_count
    cell = ((high, deep), jnp.bfloat16)
    depth = ((width, high), jnp.bfloat16)
    out = ((len(outputs), width + size, wide), jnp.float32)
    return pl.pallas_call(
        functools.partial(backward_kernel, outputs=outputs, row_count=row_count),
        out_shape=[
            jax.ShapeDtypeStruct((sum(high for _, _, high in layout), wide), jnp.bfloat16) for _, layout in outputs
        ],
        in_specs=[pl.BlockSpec(memory_space=pltpu.VMEM)] * 4,
        out_specs=[pl.BlockSpec(memory_space=pltpu.VMEM)] * len(outputs),
        scratch_shapes=[pltpu.VMEM(*depth), pltpu.SemaphoreType.DMA((col_count,))],
        compiler_params=pltpu.CompilerParams(vmem_limit_bytes=scratch_bytes(cell, depth, out) + 6 * mib),
        cost_estimate=pl.CostEstimate(
            flops=2 * high * wide * width, bytes_accessed=2 * wide * len(outputs) * width, transcendentals=0
        ),
        name="backward_product",
    )(dense, own, sibling, chunk)


def terms_kernel(*refs, pieces):
    term_refs, out_ref, places = refs[:-2], refs[-2], refs[-1]
    row_count = places.shape[0]
    place = ring_place(lax.axis_index("row"), row_count)
    for (offset, first, high, at), ref in zip(pieces, term_refs):
        places[ring_row(place + offset, row_count), pl.ds(at, high), :] = ref[pl.ds(first, high), :].astype(jnp.float32)
    total = places[0]
    for index in range(1, row_count):
        total += places[index]
    out_ref[...] = total


def summed_terms(terms, size, row_count):
    pieces = tuple(piece for *piece, _ in terms)
    arrays = [array for *_, array in terms]
    width = arrays[0].shape[1]
    return pl.pallas_call(
        functools.partial(terms_kernel, pieces=pieces),
        out_shape=jax.ShapeDtypeStruct((size, width), jnp.float32),
        in_specs=[pl.BlockSpec(memory_space=pltpu.VMEM)] * len(arrays),
        out_specs=pl.BlockSpec(memory_space=pltpu.VMEM),
        scratch_shapes=[pltpu.VMEM((row_count, size, width), jnp.float32)],
        compiler_params=pltpu.CompilerParams(
            vmem_limit_bytes=scratch_bytes(*((array.shape, array.dtype) for array in arrays))
            + scratch_bytes(((row_count, size, width), jnp.float32))
            + 6 * mib
        ),
        cost_estimate=pl.CostEstimate(
            flops=row_count * size * width, bytes_accessed=2 * row_count * size * width, transcendentals=0
        ),
        name="summed_terms",
    )(*arrays)


def finish_kernel(*refs, firsts):
    *part_refs, features_ref = refs
    width = features_ref.shape[1]
    total = jnp.zeros(features_ref.shape[::-1], jnp.float32)
    for first, part_ref in zip(firsts, part_refs):
        total += part_ref[pl.ds(first, width), :].astype(jnp.float32)
    features_ref[...] = total.astype(jnp.bfloat16).T


def finish(parts):
    firsts = tuple(first for first, _ in parts)
    parts = [array for _, array in parts]
    width, rows = parts[0].shape
    return pl.pallas_call(
        functools.partial(finish_kernel, firsts=firsts),
        out_shape=jax.ShapeDtypeStruct((rows, width), jnp.bfloat16),
        in_specs=[pl.BlockSpec(memory_space=pltpu.VMEM)] * len(parts),
        out_specs=pl.BlockSpec(memory_space=pltpu.VMEM),
        compiler_params=pltpu.CompilerParams(vmem_limit_bytes=8 * mib),
        cost_estimate=pl.CostEstimate(
            flops=len(parts) * rows * width, bytes_accessed=2 * (len(parts) + 1) * rows * width, transcendentals=0
        ),
        name="finish",
    )(*parts)


def joined_kernel(own_ref, sibling_ref, weight_ref):
    rows = own_ref.shape[0]
    core = lax.axis_index("col") & 1
    for turn, ref in enumerate((own_ref, sibling_ref)):
        weight_ref[pl.ds(pl.multiple_of((core ^ turn) * rows, rows), rows), :] = ref[...]


def joined(own, sibling):
    rows, width = own.shape
    return pl.pallas_call(
        joined_kernel,
        out_shape=jax.ShapeDtypeStruct((2 * rows, width), jnp.float32),
        in_specs=[pl.BlockSpec(memory_space=pltpu.VMEM)] * 2,
        out_specs=pl.BlockSpec(memory_space=pltpu.VMEM),
        compiler_params=pltpu.CompilerParams(vmem_limit_bytes=8 * mib),
        cost_estimate=pl.CostEstimate(flops=0, bytes_accessed=16 * rows * width, transcendentals=0),
        name="joined",
    )(own, sibling)


def around(value, step):
    count = lax.axis_size("row")
    order = list(range(0, count, 2)) + list(range(count - 1, 0, -2))
    return lax.ppermute(value, "row", [(order[i], order[(i + step) % count]) for i in range(count)])


def swapped(value, axis, partner):
    return lax.ppermute(value, axis, [(i, i ^ partner) for i in range(lax.axis_size(axis))])


def gathered_shards(own, packed, stages, cotangent):
    reach = lax.axis_size("row") // 2
    rows = own.shape[0]
    ups, downs, dense = [own], [own], packed
    others = []
    for step in range(1, reach + 1):
        up = around(ups[-1], 1)
        if step == reach - 1:
            up, dense, others = lax.optimization_barrier((up, dense, others))
        ups.append(up)
        if step == reach:
            break
        down = around(downs[-1], -1)
        if step == 1:
            down, dense = lax.optimization_barrier((down, dense))
        elif step == 2:
            dense = stages.pop(0)(dense)
            down, dense, cotangent = lax.optimization_barrier((down, dense, cotangent))
            others = [swapped(cotangent, "col", partner) for partner in range(2, lax.axis_size("col"), 2)]
        downs.append(down)
    if stages:
        dense = stages.pop(0)(dense)
    shards = [(((0, 0, 0, rows),), own)]
    shards += [(((-step, 0, 0, rows),), ups[step]) for step in range(1, reach + 1)]
    shards += [(((step, 0, 0, rows),), downs[step]) for step in range(1, reach)]
    return shards, dense, [cotangent] + others


def added(first, second, at=0):
    spare = first.shape[0] - at - second.shape[0]
    second = jnp.pad(second.astype(jnp.float32), ((at, spare), (0, 0)))
    return (first.astype(jnp.float32) + second).astype(jnp.bfloat16)


def scattered_sums(dense, own, sibling, chunk):
    row_count, col_count = lax.axis_size("row"), lax.axis_size("col")
    size, width = chunk.shape
    half = width // 2
    reach = row_count // 2
    strip, terms, zeros = ("strip", 0, width), ("terms", 0, size), ("zeros", 0, size)
    first = (
        (reach, (terms, ("strip", 0, half))),
        (reach, (("strip", half, half), terms)),
        (0, (terms,)),
    )
    above, below, terms = backward_product(dense, own, sibling, chunk, first, row_count, col_count)
    above, below, terms, cell = lax.optimization_barrier((above, below, terms, dense))
    up, down = around(above, 1), around(below, -1)
    all_terms = [(0, 0, size, 0, terms)]

    ups = tuple((offset, (zeros, strip) if offset > 1 else (strip,)) for offset in range(reach - 1, 0, -1))
    downs = tuple((-offset, (strip, zeros)) for offset in range(reach - 1, 0, -1))
    strips = backward_product(cell, own, sibling, chunk, ups + downs + ((0, (strip,)),), row_count, col_count)
    ups, downs, mine = strips[: reach - 1], strips[reach - 1 : -1], strips[-1]
    for step in range(1, reach):
        all_terms += [(-step, 0, size, 0, up), (step, down.shape[0] - size, size, 0, down)]
        if step == reach - 1:
            up = up[size:]
        up = around(added(ups[step - 1], up), 1)
        down = around(added(downs[step - 1], down, half if step == 1 else 0), -1)
    all_terms.append((reach, width, size, 0, down))
    return [(0, mine), (0, up), (0, down)], summed_terms(all_terms, size, row_count)


def per_device(features, weight, adj_tiles, tile_rows, tile_cols, tile_counts, out_grad):
    node_rows, width = features.shape
    capacity, side = adj_tiles.shape[2:4]
    tiles = adj_tiles.reshape(capacity, side, side)
    packed = jnp.concatenate([tile_rows, tile_cols, tile_counts[:, :, None]], axis=2).reshape(2 * capacity + 1)
    row_count = lax.axis_size("row")
    col_count = lax.axis_size("col")
    per_strip = node_rows // side
    stages = build_stages(tiles, col_count * per_strip, row_count * per_strip, per_strip)
    shards, dense, cotangents = gathered_shards(features, packed, stages, out_grad)

    for_sibling = forward_product(dense, shards, 1, row_count, col_count)
    for_sibling, cell = lax.optimization_barrier((for_sibling, dense))
    sums = added(forward_product(cell, shards, 0, row_count, col_count), swapped(for_sibling, "col", 1))
    sums = [sums] + [swapped(sums, "col", partner) for partner in range(2, col_count, 2)]
    activations, message, chunk = middle(sums, weight, cotangents, node_rows * row_count * col_count)
    sibling = swapped(message, "col", 1)
    parts, half = scattered_sums(dense, message, sibling, chunk)
    grad_weight = joined(half, swapped(half, "col", 1))
    return (activations, finish(parts), grad_weight)


def solution(mesh):
    placed = (
        P(("row", "col"), None),
        P(),
        P("row", "col", None, None, None),
        P("row", "col", None),
        P("row", "col", None),
        P("row", "col"),
        P(("row", "col"), None),
    )
    return jax.shard_map(
        per_device,
        mesh=mesh,
        in_specs=placed,
        out_specs=(P(("row", "col"), None), P(("row", "col"), None), P()),
        check_vma=False,
    )
```

```python
import functools
import math

import jax
import jax.numpy as jnp
from jax import lax
from jax.experimental import pallas as pl
from jax.experimental.pallas import tpu as pltpu
from jax.sharding import PartitionSpec as P

chunk_tiles = 16
chunk_slots = 16
build_grant = 44
strips_per_step = 8
mib = 1024 * 1024


def scratch_bytes(*shapes):
    return sum(math.prod(shape) * jnp.dtype(kind).itemsize for shape, kind in shapes)


def add_tiles(list_ref, tiles_ref, total, held, sems, begin, end, *, first_block, blocks, steps):
    side = tiles_ref.shape[1]
    capacity = tiles_ref.shape[0]
    count = list_ref[2 * capacity]
    slots = held.shape[0]
    row_blocks = total.shape[0] // side - 1

    def fetch(index):
        slot = lax.rem(index - begin, slots)
        return pltpu.make_async_copy(
            tiles_ref.at[pl.ds(index * chunk_tiles, chunk_tiles)], held.at[slot], sems.at[slot]
        )

    def start(index, carry):
        fetch(index).start()
        return carry

    lax.fori_loop(begin, jnp.minimum(end, begin + slots), start, 0)

    def target(place):
        col = list_ref[capacity + place] - first_block
        live = place < count
        if steps > 1:
            live = live & (col >= 0) & (col < blocks)
            col = jnp.where(live, col, 0)
        row = jnp.where(live, list_ref[place], row_blocks)
        return row, col

    def chunk_step(index, carry):
        fetch(index).wait()
        slot = lax.rem(index - begin, slots)
        spots = [target(index * chunk_tiles + lane) for lane in range(chunk_tiles)]
        at = [
            (pl.ds(pl.multiple_of(row * side, side), side), pl.ds(pl.multiple_of(col * side, side), side))
            for row, col in spots
        ]
        current = total[at[0]]
        for lane in range(chunk_tiles):
            last = lane == chunk_tiles - 1
            following = None if last else total[at[lane + 1]]
            current = current + held[slot, lane].astype(jnp.float32)
            total[at[lane]] = current
            if not last:
                same = (spots[lane][0] == spots[lane + 1][0]) & (spots[lane][1] == spots[lane + 1][1])
                current = jnp.where(same, current, following)

        @pl.when(index + slots < end)
        def _():
            fetch(index + slots).start()

        return carry

    return lambda: lax.fori_loop(begin, end, chunk_step, 0)


def each_row_block(total, side, action):
    def step(block, carry):
        action(pl.ds(pl.multiple_of(block * side, side), side))
        return carry

    lax.fori_loop(0, total.shape[0] // side - 1, step, 0)


def live_chunks(list_ref, tiles_ref):
    return (list_ref[2 * tiles_ref.shape[0]] + chunk_tiles - 1) // chunk_tiles


def first_chunks(list_ref, tiles_ref):
    return (live_chunks(list_ref, tiles_ref) * 7 + 15) // 16


def build_first_kernel(list_ref, tiles_ref, dense_ref, total, held, sems, *, blocks):
    part = first_chunks(list_ref, tiles_ref)
    run = add_tiles(list_ref, tiles_ref, total, held, sems, 0, part, first_block=0, blocks=blocks, steps=1)

    def clear(down):
        total[down, :] = jnp.zeros((down.size, total.shape[1]), jnp.float32)

    def rounded(down):
        dense_ref[down, :] = total[down, :].astype(jnp.bfloat16)

    each_row_block(total, tiles_ref.shape[1], clear)
    run()
    each_row_block(total, tiles_ref.shape[1], rounded)


def build_rest_kernel(list_ref, tiles_ref, half_ref, dense_ref, total, held, sems, *, blocks):
    chunks = live_chunks(list_ref, tiles_ref)
    run = add_tiles(
        list_ref, tiles_ref, total, held, sems, first_chunks(list_ref, tiles_ref), chunks,
        first_block=0, blocks=blocks, steps=1,
    )

    def widened(down):
        total[down, :] = half_ref[down, :].astype(jnp.float32)

    def rounded(down):
        dense_ref[down, :] = total[down, :].astype(jnp.bfloat16)

    each_row_block(total, tiles_ref.shape[1], widened)
    run()
    each_row_block(total, tiles_ref.shape[1], rounded)


def build_whole_kernel(list_ref, tiles_ref, dense_ref, total, held, sems, *, blocks, steps):
    chunks = live_chunks(list_ref, tiles_ref)
    first_block = pl.program_id(0) * blocks
    run = add_tiles(
        list_ref, tiles_ref, total, held, sems, 0, chunks, first_block=first_block, blocks=blocks, steps=steps
    )

    def clear(down):
        total[down, :] = jnp.zeros((down.size, total.shape[1]), jnp.float32)

    def rounded(down):
        dense_ref[down, :] = total[down, :].astype(jnp.bfloat16)

    each_row_block(total, tiles_ref.shape[1], clear)
    run()
    each_row_block(total, tiles_ref.shape[1], rounded)


def build_stages(tiles, row_blocks, col_blocks, per_strip):
    capacity, side, _ = tiles.shape
    blocks = min(strips_per_step * per_strip, col_blocks)
    steps = col_blocks // blocks
    high, wide = row_blocks * side, blocks * side
    total = ((high + side, wide), jnp.float32)
    held = ((min(chunk_slots, capacity // chunk_tiles), chunk_tiles, side, side), jnp.bfloat16)
    cost = pl.CostEstimate(
        flops=capacity * side * side, bytes_accessed=capacity * side * side + high * wide, transcendentals=0
    )
    held_scratch = [pltpu.VMEM(*held), pltpu.SemaphoreType.DMA((held[0][0],))]
    dense_shape = jax.ShapeDtypeStruct((high, col_blocks * side), jnp.bfloat16)
    whole = pl.BlockSpec(memory_space=pltpu.VMEM)
    apart = pl.BlockSpec(memory_space=pl.ANY)
    listed = pl.BlockSpec(memory_space=pltpu.SMEM)
    if steps > 1:
        block = ((high, wide), jnp.bfloat16)
        return [
            lambda packed: pl.pallas_call(
                functools.partial(build_whole_kernel, blocks=blocks, steps=steps),
                out_shape=dense_shape,
                grid_spec=pltpu.PrefetchScalarGridSpec(
                    num_scalar_prefetch=1,
                    grid=(steps,),
                    in_specs=[apart],
                    out_specs=pl.BlockSpec((high, wide), lambda i, *_: (0, i)),
                    scratch_shapes=[pltpu.VMEM(*total)] + held_scratch,
                ),
                compiler_params=pltpu.CompilerParams(
                    vmem_limit_bytes=scratch_bytes(total, held, block, block) + 4 * mib
                ),
                cost_estimate=cost,
                name="build_whole",
            )(packed, tiles)
        ]
    params = pltpu.CompilerParams(vmem_limit_bytes=build_grant * mib)
    scratch = [pltpu.VMEM(*total)] + held_scratch
    return [
        lambda packed: (packed, pl.pallas_call(
            functools.partial(build_first_kernel, blocks=blocks),
            out_shape=dense_shape,
            in_specs=[listed, apart],
            out_specs=whole,
            scratch_shapes=scratch,
            compiler_params=params,
            cost_estimate=cost,
            name="build_first",
        )(packed, tiles)),
        lambda state: pl.pallas_call(
            functools.partial(build_rest_kernel, blocks=blocks),
            out_shape=dense_shape,
            in_specs=[listed, apart, whole],
            out_specs=whole,
            scratch_shapes=scratch,
            compiler_params=params,
            cost_estimate=cost,
            name="build_rest",
        )(state[0], tiles, state[1]),
    ]


def ring_place(row, count):
    return jnp.where(lax.rem(row, 2) == 0, row // 2, count - 1 - row // 2)


def ring_row(place, count):
    place = lax.rem(place + 2 * count, count)
    return jnp.where(place < count // 2, 2 * place, 2 * (count - 1 - place) + 1)


def forward_kernel(dense_ref, *refs, pieces, sibling, row_count):
    piece_refs, out_ref = refs[: len(pieces)], refs[len(pieces)]
    count = lax.axis_size("col")
    rows = dense_ref.shape[0] // count
    block = dense_ref.shape[1] // row_count
    place = ring_place(lax.axis_index("row"), row_count)
    col = lax.axis_index("col") ^ sibling
    operands = []
    for piece, ref in zip(pieces, piece_refs):
        for offset, first, start, high in piece:
            along = pl.ds(pl.multiple_of(ring_row(place + offset, row_count) * block + first, 128), high)
            operands.append((along, ref, pl.ds(start, high)))
    for index in range(count // 2):
        down = pl.ds(pl.multiple_of((col ^ (2 * index)) * rows, rows), rows)
        total = None
        for along, ref, part in operands:
            product = jnp.dot(dense_ref[down, along], ref[part, :], preferred_element_type=jnp.float32)
            total = product if total is None else total + product
        out_ref[pl.ds(index * rows, rows), :] = total.astype(jnp.bfloat16)


def forward_product(dense, shards, sibling, row_count, col_count):
    pieces = tuple(piece for piece, _ in shards)
    arrays = [array for _, array in shards]
    high, deep = dense.shape
    width = arrays[0].shape[1]
    half = high // 2
    cell = ((high, deep), jnp.bfloat16)
    depth = ((deep, width), jnp.bfloat16)
    out = ((high, width), jnp.float32)
    return pl.pallas_call(
        functools.partial(forward_kernel, pieces=pieces, sibling=sibling, row_count=row_count),
        out_shape=jax.ShapeDtypeStruct((half, width), jnp.bfloat16),
        in_specs=[pl.BlockSpec(memory_space=pltpu.VMEM)] * (1 + len(arrays)),
        out_specs=pl.BlockSpec(memory_space=pltpu.VMEM),
        compiler_params=pltpu.CompilerParams(vmem_limit_bytes=scratch_bytes(cell, depth, out) + 6 * mib),
        cost_estimate=pl.CostEstimate(
            flops=2 * half * deep * width,
            bytes_accessed=2 * (half * deep + deep * width + half * width),
            transcendentals=0,
        ),
        name="forward_product",
    )(dense, *arrays)


def partners_sum(values):
    while len(values) > 1:
        values = [values[i] + values[i + 1] for i in range(0, len(values), 2)]
    return values[0]


def middle_kernel(*refs, blocks, scale):
    sums, refs = refs[:blocks], refs[blocks:]
    weight_ref, refs = refs[0], refs[1:]
    cotangent_refs, (act_ref, message_ref, chunk_ref, product) = refs[:blocks], refs[blocks:]
    weight = weight_ref[...]
    rows, width = act_ref.shape
    over_nodes = (((0,), (0,)), ((), ()))
    terms = []
    for index in range(blocks):
        aggregate = partners_sum(
            [sums[other][pl.ds((index ^ other) * rows, rows), :].astype(jnp.float32) for other in range(blocks)]
        )
        high = aggregate.astype(jnp.bfloat16)
        low = (aggregate - high.astype(jnp.float32)).astype(jnp.bfloat16)
        pre = jnp.dot(high, weight, preferred_element_type=jnp.float32)
        pre += jnp.dot(low, weight, preferred_element_type=jnp.float32)
        sig = jax.nn.sigmoid(pre)
        cotangent = cotangent_refs[index][...].astype(jnp.float32)
        grad = (cotangent * sig * (1.0 + pre * (1.0 - sig))).astype(jnp.bfloat16)
        message_ref[pl.ds(index * width, width), :] = lax.dot_general(
            weight, grad, (((1,), (1,)), ((), ())), preferred_element_type=jnp.float32
        ).astype(jnp.bfloat16)
        if index == 0:
            act_ref[...] = (pre * sig).astype(jnp.bfloat16)
        part = lax.dot_general(high, grad, over_nodes, preferred_element_type=jnp.float32)
        part += lax.dot_general(low, grad, over_nodes, preferred_element_type=jnp.float32)
        terms.append(part)
    product[...] = partners_sum(terms) * scale
    col = lax.axis_index("col")
    size = chunk_ref.shape[0]
    core = col & 1
    chunk_ref[...] = product[pl.ds(pl.multiple_of(core * size, size), size), :]
    sent = product[pl.ds(pl.multiple_of((core ^ 1) * size, size), size), :]
    high = sent.astype(jnp.bfloat16)
    low = (sent - high.astype(jnp.float32)).astype(jnp.bfloat16)
    message_ref[pl.ds(blocks * width, size), :] = high
    message_ref[pl.ds(blocks * width + size, size), :] = low


def middle(sums, weight, cotangents, total_nodes):
    rows, width = cotangents[0].shape
    blocks = len(cotangents)
    size = width // 2
    return pl.pallas_call(
        functools.partial(middle_kernel, blocks=blocks, scale=1.0 / math.sqrt(total_nodes)),
        out_shape=[
            jax.ShapeDtypeStruct((rows, width), jnp.bfloat16),
            jax.ShapeDtypeStruct((blocks * width + 2 * size, rows), jnp.bfloat16),
            jax.ShapeDtypeStruct((size, width), jnp.float32),
        ],
        in_specs=[pl.BlockSpec(memory_space=pltpu.VMEM)] * (2 * blocks + 1),
        out_specs=[pl.BlockSpec(memory_space=pltpu.VMEM)] * 3,
        scratch_shapes=[pltpu.VMEM((width, width), jnp.float32)],
        compiler_params=pltpu.CompilerParams(vmem_limit_bytes=12 * mib),
        cost_estimate=pl.CostEstimate(
            flops=10 * blocks * rows * width * width,
            bytes_accessed=2 * (blocks * blocks + 2 * blocks + 4) * rows * width,
            transcendentals=blocks * rows * width,
        ),
        name="middle",
    )(*sums, weight, *cotangents)


def backward_kernel(dense_ref, own_ref, sibling_ref, chunk_ref, *refs, outputs, row_count):
    out_refs, (depth, sems) = refs[:-2], refs[-2:]
    count = lax.axis_size("col")
    width, rows = depth.shape[0], own_ref.shape[1]
    wide = dense_ref.shape[1] // row_count
    col = lax.axis_index("col")
    copies = []
    for index in range(count):
        block = pl.ds(index // 2 * width, width)
        along = pl.ds(pl.multiple_of((col ^ index) * rows, rows), rows)
        source = sibling_ref if index % 2 else own_ref
        copy = pltpu.make_async_copy(source.at[block], depth.at[:, along], sems.at[index])
        copy.start()
        copies.append(copy)
    size = chunk_ref.shape[0]
    from_sibling = count // 2 * width
    high, low = (sibling_ref[pl.ds(from_sibling + turn * size, size), :].astype(jnp.float32) for turn in range(2))
    terms = (chunk_ref[...] + (high + low)).astype(jnp.bfloat16)
    for copy in copies:
        copy.wait()
    place = ring_place(lax.axis_index("row"), row_count)
    strips = {}
    for (offset, layout), out_ref in zip(outputs, out_refs):
        start = 0
        for kind, first, high in layout:
            if kind == "strip" and offset not in strips:
                along = pl.ds(pl.multiple_of(ring_row(place + offset, row_count) * wide, wide), wide)
                part = jnp.dot(depth[...], dense_ref[:, along], preferred_element_type=jnp.float32)
                strips[offset] = part.astype(jnp.bfloat16)
            source = {"strip": strips.get(offset), "terms": terms, "zeros": jnp.zeros_like(terms)}[kind]
            out_ref[start : start + high, :] = source[first : first + high, :]
            start += high


def backward_product(dense, own, sibling, chunk, outputs, row_count, col_count):
    high, deep = dense.shape
    size, width = chunk.shape
    wide = deep // row_count
    cell = ((high, deep), jnp.bfloat16)
    depth = ((width, high), jnp.bfloat16)
    out = ((len(outputs), width + size, wide), jnp.float32)
    return pl.pallas_call(
        functools.partial(backward_kernel, outputs=outputs, row_count=row_count),
        out_shape=[
            jax.ShapeDtypeStruct((sum(high for _, _, high in layout), wide), jnp.bfloat16) for _, layout in outputs
        ],
        in_specs=[pl.BlockSpec(memory_space=pltpu.VMEM)] * 4,
        out_specs=[pl.BlockSpec(memory_space=pltpu.VMEM)] * len(outputs),
        scratch_shapes=[pltpu.VMEM(*depth), pltpu.SemaphoreType.DMA((col_count,))],
        compiler_params=pltpu.CompilerParams(vmem_limit_bytes=scratch_bytes(cell, depth, out) + 6 * mib),
        cost_estimate=pl.CostEstimate(
            flops=2 * high * wide * width, bytes_accessed=2 * wide * len(outputs) * width, transcendentals=0
        ),
        name="backward_product",
    )(dense, own, sibling, chunk)


def terms_kernel(*refs, pieces):
    term_refs, out_ref, places = refs[:-2], refs[-2], refs[-1]
    row_count = places.shape[0]
    place = ring_place(lax.axis_index("row"), row_count)
    for (offset, first, high, at), ref in zip(pieces, term_refs):
        places[ring_row(place + offset, row_count), pl.ds(at, high), :] = ref[pl.ds(first, high), :].astype(jnp.float32)
    total = places[0]
    for index in range(1, row_count):
        total += places[index]
    out_ref[...] = total


def summed_terms(terms, size, row_count):
    pieces = tuple(piece for *piece, _ in terms)
    arrays = [array for *_, array in terms]
    width = arrays[0].shape[1]
    return pl.pallas_call(
        functools.partial(terms_kernel, pieces=pieces),
        out_shape=jax.ShapeDtypeStruct((size, width), jnp.float32),
        in_specs=[pl.BlockSpec(memory_space=pltpu.VMEM)] * len(arrays),
        out_specs=pl.BlockSpec(memory_space=pltpu.VMEM),
        scratch_shapes=[pltpu.VMEM((row_count, size, width), jnp.float32)],
        compiler_params=pltpu.CompilerParams(
            vmem_limit_bytes=scratch_bytes(*((array.shape, array.dtype) for array in arrays))
            + scratch_bytes(((row_count, size, width), jnp.float32))
            + 6 * mib
        ),
        cost_estimate=pl.CostEstimate(
            flops=row_count * size * width, bytes_accessed=2 * row_count * size * width, transcendentals=0
        ),
        name="summed_terms",
    )(*arrays)


def finish_kernel(*refs, firsts):
    *part_refs, features_ref = refs
    width = features_ref.shape[1]
    total = jnp.zeros(features_ref.shape[::-1], jnp.float32)
    for first, part_ref in zip(firsts, part_refs):
        total += part_ref[pl.ds(first, width), :].astype(jnp.float32)
    features_ref[...] = total.astype(jnp.bfloat16).T


def finish(parts):
    firsts = tuple(first for first, _ in parts)
    parts = [array for _, array in parts]
    width, rows = parts[0].shape
    return pl.pallas_call(
        functools.partial(finish_kernel, firsts=firsts),
        out_shape=jax.ShapeDtypeStruct((rows, width), jnp.bfloat16),
        in_specs=[pl.BlockSpec(memory_space=pltpu.VMEM)] * len(parts),
        out_specs=pl.BlockSpec(memory_space=pltpu.VMEM),
        compiler_params=pltpu.CompilerParams(vmem_limit_bytes=8 * mib),
        cost_estimate=pl.CostEstimate(
            flops=len(parts) * rows * width, bytes_accessed=2 * (len(parts) + 1) * rows * width, transcendentals=0
        ),
        name="finish",
    )(*parts)


def joined_kernel(own_ref, sibling_ref, weight_ref):
    rows = own_ref.shape[0]
    core = lax.axis_index("col") & 1
    for turn, ref in enumerate((own_ref, sibling_ref)):
        weight_ref[pl.ds(pl.multiple_of((core ^ turn) * rows, rows), rows), :] = ref[...]


def joined(own, sibling):
    rows, width = own.shape
    return pl.pallas_call(
        joined_kernel,
        out_shape=jax.ShapeDtypeStruct((2 * rows, width), jnp.float32),
        in_specs=[pl.BlockSpec(memory_space=pltpu.VMEM)] * 2,
        out_specs=pl.BlockSpec(memory_space=pltpu.VMEM),
        compiler_params=pltpu.CompilerParams(vmem_limit_bytes=8 * mib),
        cost_estimate=pl.CostEstimate(flops=0, bytes_accessed=16 * rows * width, transcendentals=0),
        name="joined",
    )(own, sibling)


def around(value, step):
    count = lax.axis_size("row")
    order = list(range(0, count, 2)) + list(range(count - 1, 0, -2))
    return lax.ppermute(value, "row", [(order[i], order[(i + step) % count]) for i in range(count)])


def swapped(value, axis, partner):
    return lax.ppermute(value, axis, [(i, i ^ partner) for i in range(lax.axis_size(axis))])


def gathered_shards(own, packed, stages, cotangent):
    reach = lax.axis_size("row") // 2
    rows = own.shape[0]
    ups, downs, dense = [own], [own], packed
    others = []
    for step in range(1, reach + 1):
        up = around(ups[-1], 1)
        if step == reach - 1:
            up, dense, others = lax.optimization_barrier((up, dense, others))
        ups.append(up)
        if step == reach:
            break
        down = around(downs[-1], -1)
        if step == 1:
            down, dense = lax.optimization_barrier((down, dense))
        elif step == 2:
            dense = stages.pop(0)(dense)
            down, dense, cotangent = lax.optimization_barrier((down, dense, cotangent))
            others = [swapped(cotangent, "col", partner) for partner in range(2, lax.axis_size("col"), 2)]
        downs.append(down)
    if stages:
        dense = stages.pop(0)(dense)
    shards = [(((0, 0, 0, rows),), own)]
    shards += [(((-step, 0, 0, rows),), ups[step]) for step in range(1, reach + 1)]
    shards += [(((step, 0, 0, rows),), downs[step]) for step in range(1, reach)]
    return shards, dense, [cotangent] + others


def added(first, second, at=0):
    spare = first.shape[0] - at - second.shape[0]
    second = jnp.pad(second.astype(jnp.float32), ((at, spare), (0, 0)))
    return (first.astype(jnp.float32) + second).astype(jnp.bfloat16)


def scattered_sums(dense, own, sibling, chunk):
    row_count, col_count = lax.axis_size("row"), lax.axis_size("col")
    size, width = chunk.shape
    half = width // 2
    reach = row_count // 2
    strip, terms, zeros = ("strip", 0, width), ("terms", 0, size), ("zeros", 0, size)
    first = (
        (reach, (terms, ("strip", 0, half))),
        (reach, (("strip", half, half), terms)),
        (0, (terms,)),
    )
    above, below, terms = backward_product(dense, own, sibling, chunk, first, row_count, col_count)
    above, below, terms, cell = lax.optimization_barrier((above, below, terms, dense))
    up, down = around(above, 1), around(below, -1)
    all_terms = [(0, 0, size, 0, terms)]

    ups = tuple((offset, (zeros, strip) if offset > 1 else (strip,)) for offset in range(reach - 1, 0, -1))
    downs = tuple((-offset, (strip, zeros)) for offset in range(reach - 1, 0, -1))
    strips = backward_product(cell, own, sibling, chunk, ups + downs + ((0, (strip,)),), row_count, col_count)
    ups, downs, mine = strips[: reach - 1], strips[reach - 1 : -1], strips[-1]
    for step in range(1, reach):
        all_terms += [(-step, 0, size, 0, up), (step, down.shape[0] - size, size, 0, down)]
        if step == reach - 1:
            up = up[size:]
        up = around(added(ups[step - 1], up), 1)
        down = around(added(downs[step - 1], down, half if step == 1 else 0), -1)
    all_terms.append((reach, width, size, 0, down))
    return [(0, mine), (0, up), (0, down)], summed_terms(all_terms, size, row_count)


def per_device(features, weight, adj_tiles, tile_rows, tile_cols, tile_counts, out_grad):
    node_rows, width = features.shape
    capacity, side = adj_tiles.shape[2:4]
    tiles = adj_tiles.reshape(capacity, side, side)
    packed = jnp.concatenate([tile_rows, tile_cols, tile_counts[:, :, None]], axis=2).reshape(2 * capacity + 1)
    row_count = lax.axis_size("row")
    col_count = lax.axis_size("col")
    per_strip = node_rows // side
    stages = build_stages(tiles, col_count * per_strip, row_count * per_strip, per_strip)
    shards, dense, cotangents = gathered_shards(features, packed, stages, out_grad)

    for_sibling = forward_product(dense, shards, 1, row_count, col_count)
    for_sibling, cell = lax.optimization_barrier((for_sibling, dense))
    sums = added(forward_product(cell, shards, 0, row_count, col_count), swapped(for_sibling, "col", 1))
    sums = [sums] + [swapped(sums, "col", partner) for partner in range(2, col_count, 2)]
    activations, message, chunk = middle(sums, weight, cotangents, node_rows * row_count * col_count)
    sibling = swapped(message, "col", 1)
    parts, half = scattered_sums(dense, message, sibling, chunk)
    grad_weight = joined(half, swapped(half, "col", 1))
    return (activations, finish(parts), grad_weight)


def solution(mesh):
    placed = (
        P(("row", "col"), None),
        P(),
        P("row", "col", None, None, None),
        P("row", "col", None),
        P("row", "col", None),
        P("row", "col"),
        P(("row", "col"), None),
    )
    return jax.shard_map(
        per_device,
        mesh=mesh,
        in_specs=placed,
        out_specs=(P(("row", "col"), None), P(("row", "col"), None), P()),
        check_vma=False,
    )
```

```python
import functools
import math

import jax
import jax.numpy as jnp
from jax import lax
from jax.experimental import pallas as pl
from jax.experimental.pallas import tpu as pltpu
from jax.sharding import PartitionSpec as P

chunk_tiles = 16
chunk_slots = 16
build_grant = 44
build_cuts = (5, 10, 16)
strips_per_step = 8
mib = 1024 * 1024


def scratch_bytes(*shapes):
    return sum(math.prod(shape) * jnp.dtype(kind).itemsize for shape, kind in shapes)


def add_tiles(list_ref, tiles_ref, total, held, sems, begin, end, *, first_block, blocks, steps):
    side = tiles_ref.shape[1]
    capacity = tiles_ref.shape[0]
    count = list_ref[2 * capacity]
    slots = held.shape[0]
    row_blocks = total.shape[0] // side - 1

    def fetch(index):
        slot = lax.rem(index - begin, slots)
        return pltpu.make_async_copy(
            tiles_ref.at[pl.ds(index * chunk_tiles, chunk_tiles)], held.at[slot], sems.at[slot]
        )

    def start(index, carry):
        fetch(index).start()
        return carry

    lax.fori_loop(begin, jnp.minimum(end, begin + slots), start, 0)

    def target(place):
        col = list_ref[capacity + place] - first_block
        live = place < count
        if steps > 1:
            live = live & (col >= 0) & (col < blocks)
            col = jnp.where(live, col, 0)
        row = jnp.where(live, list_ref[place], row_blocks)
        return row, col

    def chunk_step(index, carry):
        fetch(index).wait()
        slot = lax.rem(index - begin, slots)
        spots = [target(index * chunk_tiles + lane) for lane in range(chunk_tiles)]
        at = [
            (pl.ds(pl.multiple_of(row * side, side), side), pl.ds(pl.multiple_of(col * side, side), side))
            for row, col in spots
        ]
        current = total[at[0]]
        for lane in range(chunk_tiles):
            last = lane == chunk_tiles - 1
            following = None if last else total[at[lane + 1]]
            current = current + held[slot, lane].astype(jnp.float32)
            total[at[lane]] = current
            if not last:
                same = (spots[lane][0] == spots[lane + 1][0]) & (spots[lane][1] == spots[lane + 1][1])
                current = jnp.where(same, current, following)

        @pl.when(index + slots < end)
        def _():
            fetch(index + slots).start()

        return carry

    return lambda: lax.fori_loop(begin, end, chunk_step, 0)


def each_row_block(total, side, action):
    def step(block, carry):
        action(pl.ds(pl.multiple_of(block * side, side), side))
        return carry

    lax.fori_loop(0, total.shape[0] // side - 1, step, 0)


def live_chunks(list_ref, tiles_ref):
    return (list_ref[2 * tiles_ref.shape[0]] + chunk_tiles - 1) // chunk_tiles


def cut_chunks(list_ref, tiles_ref, cut):
    return (live_chunks(list_ref, tiles_ref) * cut + 15) // 16


def build_first_kernel(list_ref, tiles_ref, dense_ref, total, held, sems, *, blocks, cuts):
    part = cut_chunks(list_ref, tiles_ref, cuts[1])
    run = add_tiles(list_ref, tiles_ref, total, held, sems, 0, part, first_block=0, blocks=blocks, steps=1)

    def clear(down):
        total[down, :] = jnp.zeros((down.size, total.shape[1]), jnp.float32)

    def rounded(down):
        dense_ref[down, :] = total[down, :].astype(jnp.bfloat16)

    each_row_block(total, tiles_ref.shape[1], clear)
    run()
    each_row_block(total, tiles_ref.shape[1], rounded)


def build_more_kernel(list_ref, tiles_ref, half_ref, dense_ref, total, held, sems, *, blocks, cuts):
    begin, end = (cut_chunks(list_ref, tiles_ref, cut) for cut in cuts)
    run = add_tiles(
        list_ref, tiles_ref, total, held, sems, begin, end, first_block=0, blocks=blocks, steps=1
    )

    def widened(down):
        total[down, :] = half_ref[down, :].astype(jnp.float32)

    def rounded(down):
        dense_ref[down, :] = total[down, :].astype(jnp.bfloat16)

    each_row_block(total, tiles_ref.shape[1], widened)
    run()
    each_row_block(total, tiles_ref.shape[1], rounded)


def build_whole_kernel(list_ref, tiles_ref, dense_ref, total, held, sems, *, blocks, steps):
    chunks = live_chunks(list_ref, tiles_ref)
    first_block = pl.program_id(0) * blocks
    run = add_tiles(
        list_ref, tiles_ref, total, held, sems, 0, chunks, first_block=first_block, blocks=blocks, steps=steps
    )

    def clear(down):
        total[down, :] = jnp.zeros((down.size, total.shape[1]), jnp.float32)

    def rounded(down):
        dense_ref[down, :] = total[down, :].astype(jnp.bfloat16)

    each_row_block(total, tiles_ref.shape[1], clear)
    run()
    each_row_block(total, tiles_ref.shape[1], rounded)


def build_stages(tiles, row_blocks, col_blocks, per_strip):
    capacity, side, _ = tiles.shape
    blocks = min(strips_per_step * per_strip, col_blocks)
    steps = col_blocks // blocks
    high, wide = row_blocks * side, blocks * side
    total = ((high + side, wide), jnp.float32)
    held = ((min(chunk_slots, capacity // chunk_tiles), chunk_tiles, side, side), jnp.bfloat16)
    cost = pl.CostEstimate(
        flops=capacity * side * side, bytes_accessed=capacity * side * side + high * wide, transcendentals=0
    )
    held_scratch = [pltpu.VMEM(*held), pltpu.SemaphoreType.DMA((held[0][0],))]
    dense_shape = jax.ShapeDtypeStruct((high, col_blocks * side), jnp.bfloat16)
    whole = pl.BlockSpec(memory_space=pltpu.VMEM)
    apart = pl.BlockSpec(memory_space=pl.ANY)
    listed = pl.BlockSpec(memory_space=pltpu.SMEM)
    if steps > 1:
        block = ((high, wide), jnp.bfloat16)
        return [
            lambda packed: pl.pallas_call(
                functools.partial(build_whole_kernel, blocks=blocks, steps=steps),
                out_shape=dense_shape,
                grid_spec=pltpu.PrefetchScalarGridSpec(
                    num_scalar_prefetch=1,
                    grid=(steps,),
                    in_specs=[apart],
                    out_specs=pl.BlockSpec((high, wide), lambda i, *_: (0, i)),
                    scratch_shapes=[pltpu.VMEM(*total)] + held_scratch,
                ),
                compiler_params=pltpu.CompilerParams(
                    vmem_limit_bytes=scratch_bytes(total, held, block, block) + 4 * mib
                ),
                cost_estimate=cost,
                name="build_whole",
            )(packed, tiles)
        ]
    params = pltpu.CompilerParams(vmem_limit_bytes=build_grant * mib)
    scratch = [pltpu.VMEM(*total)] + held_scratch

    def first(packed):
        half = pl.pallas_call(
            functools.partial(build_first_kernel, blocks=blocks, cuts=(0, build_cuts[0])),
            out_shape=dense_shape,
            in_specs=[listed, apart],
            out_specs=whole,
            scratch_shapes=scratch,
            compiler_params=params,
            cost_estimate=cost,
            name="build_first",
        )(packed, tiles)
        return packed, half

    def more(state, begin, end):
        packed, half = state
        dense = pl.pallas_call(
            functools.partial(build_more_kernel, blocks=blocks, cuts=(begin, end)),
            out_shape=dense_shape,
            in_specs=[listed, apart, whole],
            out_specs=whole,
            scratch_shapes=scratch,
            compiler_params=params,
            cost_estimate=cost,
            name="build_more",
        )(packed, tiles, half)
        return (packed, dense) if end < 16 else dense

    return [first] + [functools.partial(more, begin=begin, end=end) for begin, end in zip(build_cuts, build_cuts[1:])]


def ring_place(row, count):
    return jnp.where(lax.rem(row, 2) == 0, row // 2, count - 1 - row // 2)


def ring_row(place, count):
    place = lax.rem(place + 2 * count, count)
    return jnp.where(place < count // 2, 2 * place, 2 * (count - 1 - place) + 1)


def forward_kernel(dense_ref, *refs, pieces, sibling, row_count):
    piece_refs, out_ref = refs[: len(pieces)], refs[len(pieces)]
    count = lax.axis_size("col")
    rows = dense_ref.shape[0] // count
    block = dense_ref.shape[1] // row_count
    place = ring_place(lax.axis_index("row"), row_count)
    col = lax.axis_index("col") ^ sibling
    operands = []
    for piece, ref in zip(pieces, piece_refs):
        for offset, first, start, high in piece:
            along = pl.ds(pl.multiple_of(ring_row(place + offset, row_count) * block + first, 128), high)
            operands.append((along, ref, pl.ds(start, high)))
    for index in range(count // 2):
        down = pl.ds(pl.multiple_of((col ^ (2 * index)) * rows, rows), rows)
        total = None
        for along, ref, part in operands:
            product = jnp.dot(dense_ref[down, along], ref[part, :], preferred_element_type=jnp.float32)
            total = product if total is None else total + product
        out_ref[pl.ds(index * rows, rows), :] = total.astype(jnp.bfloat16)


def forward_product(dense, shards, sibling, row_count, col_count):
    pieces = tuple(piece for piece, _ in shards)
    arrays = [array for _, array in shards]
    high, deep = dense.shape
    width = arrays[0].shape[1]
    half = high // 2
    cell = ((high, deep), jnp.bfloat16)
    depth = ((deep, width), jnp.bfloat16)
    out = ((high, width), jnp.float32)
    return pl.pallas_call(
        functools.partial(forward_kernel, pieces=pieces, sibling=sibling, row_count=row_count),
        out_shape=jax.ShapeDtypeStruct((half, width), jnp.bfloat16),
        in_specs=[pl.BlockSpec(memory_space=pltpu.VMEM)] * (1 + len(arrays)),
        out_specs=pl.BlockSpec(memory_space=pltpu.VMEM),
        compiler_params=pltpu.CompilerParams(vmem_limit_bytes=scratch_bytes(cell, depth, out) + 6 * mib),
        cost_estimate=pl.CostEstimate(
            flops=2 * half * deep * width,
            bytes_accessed=2 * (half * deep + deep * width + half * width),
            transcendentals=0,
        ),
        name="forward_product",
    )(dense, *arrays)


def partners_sum(values):
    while len(values) > 1:
        values = [values[i] + values[i + 1] for i in range(0, len(values), 2)]
    return values[0]


def middle_kernel(*refs, blocks, scale):
    sums, refs = refs[:blocks], refs[blocks:]
    weight_ref, refs = refs[0], refs[1:]
    cotangent_refs, (act_ref, message_ref, chunk_ref, product) = refs[:blocks], refs[blocks:]
    weight = weight_ref[...]
    rows, width = act_ref.shape
    over_nodes = (((0,), (0,)), ((), ()))
    terms = []
    for index in range(blocks):
        aggregate = partners_sum(
            [sums[other][pl.ds((index ^ other) * rows, rows), :].astype(jnp.float32) for other in range(blocks)]
        )
        high = aggregate.astype(jnp.bfloat16)
        low = (aggregate - high.astype(jnp.float32)).astype(jnp.bfloat16)
        pre = jnp.dot(high, weight, preferred_element_type=jnp.float32)
        pre += jnp.dot(low, weight, preferred_element_type=jnp.float32)
        sig = jax.nn.sigmoid(pre)
        cotangent = cotangent_refs[index][...].astype(jnp.float32)
        grad = (cotangent * sig * (1.0 + pre * (1.0 - sig))).astype(jnp.bfloat16)
        message_ref[pl.ds(index * width, width), :] = lax.dot_general(
            weight, grad, (((1,), (1,)), ((), ())), preferred_element_type=jnp.float32
        ).astype(jnp.bfloat16)
        if index == 0:
            act_ref[...] = (pre * sig).astype(jnp.bfloat16)
        part = lax.dot_general(high, grad, over_nodes, preferred_element_type=jnp.float32)
        part += lax.dot_general(low, grad, over_nodes, preferred_element_type=jnp.float32)
        terms.append(part)
    product[...] = partners_sum(terms) * scale
    col = lax.axis_index("col")
    size = chunk_ref.shape[0]
    core = col & 1
    chunk_ref[...] = product[pl.ds(pl.multiple_of(core * size, size), size), :]
    sent = product[pl.ds(pl.multiple_of((core ^ 1) * size, size), size), :]
    high = sent.astype(jnp.bfloat16)
    low = (sent - high.astype(jnp.float32)).astype(jnp.bfloat16)
    message_ref[pl.ds(blocks * width, size), :] = high
    message_ref[pl.ds(blocks * width + size, size), :] = low


def middle(sums, weight, cotangents, total_nodes):
    rows, width = cotangents[0].shape
    blocks = len(cotangents)
    size = width // 2
    return pl.pallas_call(
        functools.partial(middle_kernel, blocks=blocks, scale=1.0 / math.sqrt(total_nodes)),
        out_shape=[
            jax.ShapeDtypeStruct((rows, width), jnp.bfloat16),
            jax.ShapeDtypeStruct((blocks * width + 2 * size, rows), jnp.bfloat16),
            jax.ShapeDtypeStruct((size, width), jnp.float32),
        ],
        in_specs=[pl.BlockSpec(memory_space=pltpu.VMEM)] * (2 * blocks + 1),
        out_specs=[pl.BlockSpec(memory_space=pltpu.VMEM)] * 3,
        scratch_shapes=[pltpu.VMEM((width, width), jnp.float32)],
        compiler_params=pltpu.CompilerParams(vmem_limit_bytes=12 * mib),
        cost_estimate=pl.CostEstimate(
            flops=10 * blocks * rows * width * width,
            bytes_accessed=2 * (blocks * blocks + 2 * blocks + 4) * rows * width,
            transcendentals=blocks * rows * width,
        ),
        name="middle",
    )(*sums, weight, *cotangents)


def backward_kernel(dense_ref, own_ref, sibling_ref, chunk_ref, *refs, outputs, row_count):
    out_refs, (depth, sems) = refs[:-2], refs[-2:]
    count = lax.axis_size("col")
    width, rows = depth.shape[0], own_ref.shape[1]
    wide = dense_ref.shape[1] // row_count
    col = lax.axis_index("col")
    copies = []
    for index in range(count):
        block = pl.ds(index // 2 * width, width)
        along = pl.ds(pl.multiple_of((col ^ index) * rows, rows), rows)
        source = sibling_ref if index % 2 else own_ref
        copy = pltpu.make_async_copy(source.at[block], depth.at[:, along], sems.at[index])
        copy.start()
        copies.append(copy)
    size = chunk_ref.shape[0]
    from_sibling = count // 2 * width
    high, low = (sibling_ref[pl.ds(from_sibling + turn * size, size), :].astype(jnp.float32) for turn in range(2))
    terms = (chunk_ref[...] + (high + low)).astype(jnp.bfloat16)
    for copy in copies:
        copy.wait()
    place = ring_place(lax.axis_index("row"), row_count)
    strips = {}
    for (offset, layout), out_ref in zip(outputs, out_refs):
        start = 0
        for kind, first, high in layout:
            if kind == "strip" and offset not in strips:
                along = pl.ds(pl.multiple_of(ring_row(place + offset, row_count) * wide, wide), wide)
                part = jnp.dot(depth[...], dense_ref[:, along], preferred_element_type=jnp.float32)
                strips[offset] = part.astype(jnp.bfloat16)
            source = {"strip": strips.get(offset), "terms": terms, "zeros": jnp.zeros_like(terms)}[kind]
            out_ref[start : start + high, :] = source[first : first + high, :]
            start += high


def backward_product(dense, own, sibling, chunk, outputs, row_count, col_count):
    high, deep = dense.shape
    size, width = chunk.shape
    wide = deep // row_count
    cell = ((high, deep), jnp.bfloat16)
    depth = ((width, high), jnp.bfloat16)
    out = ((len(outputs), width + size, wide), jnp.float32)
    return pl.pallas_call(
        functools.partial(backward_kernel, outputs=outputs, row_count=row_count),
        out_shape=[
            jax.ShapeDtypeStruct((sum(high for _, _, high in layout), wide), jnp.bfloat16) for _, layout in outputs
        ],
        in_specs=[pl.BlockSpec(memory_space=pltpu.VMEM)] * 4,
        out_specs=[pl.BlockSpec(memory_space=pltpu.VMEM)] * len(outputs),
        scratch_shapes=[pltpu.VMEM(*depth), pltpu.SemaphoreType.DMA((col_count,))],
        compiler_params=pltpu.CompilerParams(vmem_limit_bytes=scratch_bytes(cell, depth, out) + 6 * mib),
        cost_estimate=pl.CostEstimate(
            flops=2 * high * wide * width, bytes_accessed=2 * wide * len(outputs) * width, transcendentals=0
        ),
        name="backward_product",
    )(dense, own, sibling, chunk)


def terms_kernel(*refs, pieces):
    term_refs, out_ref, places = refs[:-2], refs[-2], refs[-1]
    row_count = places.shape[0]
    place = ring_place(lax.axis_index("row"), row_count)
    for (offset, first, high, at), ref in zip(pieces, term_refs):
        places[ring_row(place + offset, row_count), pl.ds(at, high), :] = ref[pl.ds(first, high), :].astype(jnp.float32)
    total = places[0]
    for index in range(1, row_count):
        total += places[index]
    out_ref[...] = total


def summed_terms(terms, size, row_count):
    pieces = tuple(piece for *piece, _ in terms)
    arrays = [array for *_, array in terms]
    width = arrays[0].shape[1]
    return pl.pallas_call(
        functools.partial(terms_kernel, pieces=pieces),
        out_shape=jax.ShapeDtypeStruct((size, width), jnp.float32),
        in_specs=[pl.BlockSpec(memory_space=pltpu.VMEM)] * len(arrays),
        out_specs=pl.BlockSpec(memory_space=pltpu.VMEM),
        scratch_shapes=[pltpu.VMEM((row_count, size, width), jnp.float32)],
        compiler_params=pltpu.CompilerParams(
            vmem_limit_bytes=scratch_bytes(*((array.shape, array.dtype) for array in arrays))
            + scratch_bytes(((row_count, size, width), jnp.float32))
            + 6 * mib
        ),
        cost_estimate=pl.CostEstimate(
            flops=row_count * size * width, bytes_accessed=2 * row_count * size * width, transcendentals=0
        ),
        name="summed_terms",
    )(*arrays)


def finish_kernel(*refs, firsts):
    *part_refs, features_ref = refs
    width = features_ref.shape[1]
    total = jnp.zeros(features_ref.shape[::-1], jnp.float32)
    for first, part_ref in zip(firsts, part_refs):
        total += part_ref[pl.ds(first, width), :].astype(jnp.float32)
    features_ref[...] = total.astype(jnp.bfloat16).T


def finish(parts):
    firsts = tuple(first for first, _ in parts)
    parts = [array for _, array in parts]
    width, rows = parts[0].shape
    return pl.pallas_call(
        functools.partial(finish_kernel, firsts=firsts),
        out_shape=jax.ShapeDtypeStruct((rows, width), jnp.bfloat16),
        in_specs=[pl.BlockSpec(memory_space=pltpu.VMEM)] * len(parts),
        out_specs=pl.BlockSpec(memory_space=pltpu.VMEM),
        compiler_params=pltpu.CompilerParams(vmem_limit_bytes=8 * mib),
        cost_estimate=pl.CostEstimate(
            flops=len(parts) * rows * width, bytes_accessed=2 * (len(parts) + 1) * rows * width, transcendentals=0
        ),
        name="finish",
    )(*parts)


def joined_kernel(own_ref, sibling_ref, weight_ref):
    rows = own_ref.shape[0]
    core = lax.axis_index("col") & 1
    for turn, ref in enumerate((own_ref, sibling_ref)):
        weight_ref[pl.ds(pl.multiple_of((core ^ turn) * rows, rows), rows), :] = ref[...]


def joined(own, sibling):
    rows, width = own.shape
    return pl.pallas_call(
        joined_kernel,
        out_shape=jax.ShapeDtypeStruct((2 * rows, width), jnp.float32),
        in_specs=[pl.BlockSpec(memory_space=pltpu.VMEM)] * 2,
        out_specs=pl.BlockSpec(memory_space=pltpu.VMEM),
        compiler_params=pltpu.CompilerParams(vmem_limit_bytes=8 * mib),
        cost_estimate=pl.CostEstimate(flops=0, bytes_accessed=16 * rows * width, transcendentals=0),
        name="joined",
    )(own, sibling)


def around(value, step):
    count = lax.axis_size("row")
    order = list(range(0, count, 2)) + list(range(count - 1, 0, -2))
    return lax.ppermute(value, "row", [(order[i], order[(i + step) % count]) for i in range(count)])


def swapped(value, axis, partner):
    return lax.ppermute(value, axis, [(i, i ^ partner) for i in range(lax.axis_size(axis))])


def gathered_shards(own, packed, stages, cotangent):
    reach = lax.axis_size("row") // 2
    rows = own.shape[0]
    ups, downs, dense = [own], [own], packed
    others = []
    for step in range(1, reach + 1):
        up = around(ups[-1], 1)
        if step == reach - 1:
            if len(stages) > 1:
                dense = stages.pop(0)(dense)
            up, dense, others = lax.optimization_barrier((up, dense, others))
        ups.append(up)
        if step == reach:
            break
        down = around(downs[-1], -1)
        if step == 1:
            down, dense = lax.optimization_barrier((down, dense))
        elif step == 2:
            dense = stages.pop(0)(dense)
            down, dense, cotangent = lax.optimization_barrier((down, dense, cotangent))
            others = [swapped(cotangent, "col", partner) for partner in range(2, lax.axis_size("col"), 2)]
        downs.append(down)
    if stages:
        dense = stages.pop(0)(dense)
    shards = [(((0, 0, 0, rows),), own)]
    shards += [(((-step, 0, 0, rows),), ups[step]) for step in range(1, reach + 1)]
    shards += [(((step, 0, 0, rows),), downs[step]) for step in range(1, reach)]
    return shards, dense, [cotangent] + others


def added(first, second, at=0):
    spare = first.shape[0] - at - second.shape[0]
    second = jnp.pad(second.astype(jnp.float32), ((at, spare), (0, 0)))
    return (first.astype(jnp.float32) + second).astype(jnp.bfloat16)


def scattered_sums(dense, own, sibling, chunk):
    row_count, col_count = lax.axis_size("row"), lax.axis_size("col")
    size, width = chunk.shape
    half = width // 2
    reach = row_count // 2
    strip, terms, zeros = ("strip", 0, width), ("terms", 0, size), ("zeros", 0, size)
    first = (
        (reach, (terms, ("strip", 0, half))),
        (reach, (("strip", half, half), terms)),
        (0, (terms,)),
    )
    above, below, terms = backward_product(dense, own, sibling, chunk, first, row_count, col_count)
    above, below, terms, cell = lax.optimization_barrier((above, below, terms, dense))
    up, down = around(above, 1), around(below, -1)
    all_terms = [(0, 0, size, 0, terms)]

    ups = tuple((offset, (zeros, strip) if offset > 1 else (strip,)) for offset in range(reach - 1, 0, -1))
    downs = tuple((-offset, (strip, zeros)) for offset in range(reach - 1, 0, -1))
    strips = backward_product(cell, own, sibling, chunk, ups + downs + ((0, (strip,)),), row_count, col_count)
    ups, downs, mine = strips[: reach - 1], strips[reach - 1 : -1], strips[-1]
    for step in range(1, reach):
        all_terms += [(-step, 0, size, 0, up), (step, down.shape[0] - size, size, 0, down)]
        if step == reach - 1:
            up = up[size:]
        up = around(added(ups[step - 1], up), 1)
        down = around(added(downs[step - 1], down, half if step == 1 else 0), -1)
    all_terms.append((reach, width, size, 0, down))
    return [(0, mine), (0, up), (0, down)], summed_terms(all_terms, size, row_count)


def per_device(features, weight, adj_tiles, tile_rows, tile_cols, tile_counts, out_grad):
    node_rows, width = features.shape
    capacity, side = adj_tiles.shape[2:4]
    tiles = adj_tiles.reshape(capacity, side, side)
    packed = jnp.concatenate([tile_rows, tile_cols, tile_counts[:, :, None]], axis=2).reshape(2 * capacity + 1)
    row_count = lax.axis_size("row")
    col_count = lax.axis_size("col")
    per_strip = node_rows // side
    stages = build_stages(tiles, col_count * per_strip, row_count * per_strip, per_strip)
    shards, dense, cotangents = gathered_shards(features, packed, stages, out_grad)

    for_sibling = forward_product(dense, shards, 1, row_count, col_count)
    for_sibling, cell = lax.optimization_barrier((for_sibling, dense))
    sums = added(forward_product(cell, shards, 0, row_count, col_count), swapped(for_sibling, "col", 1))
    sums = [sums] + [swapped(sums, "col", partner) for partner in range(2, col_count, 2)]
    activations, message, chunk = middle(sums, weight, cotangents, node_rows * row_count * col_count)
    sibling = swapped(message, "col", 1)
    parts, half = scattered_sums(dense, message, sibling, chunk)
    grad_weight = joined(half, swapped(half, "col", 1))
    return (activations, finish(parts), grad_weight)


def solution(mesh):
    placed = (
        P(("row", "col"), None),
        P(),
        P("row", "col", None, None, None),
        P("row", "col", None),
        P("row", "col", None),
        P("row", "col"),
        P(("row", "col"), None),
    )
    return jax.shard_map(
        per_device,
        mesh=mesh,
        in_specs=placed,
        out_specs=(P(("row", "col"), None), P(("row", "col"), None), P()),
        check_vma=False,
    )
```

```python
import functools
import math

import jax
import jax.numpy as jnp
from jax import lax
from jax.experimental import pallas as pl
from jax.experimental.pallas import tpu as pltpu
from jax.sharding import PartitionSpec as P

chunk_tiles = 16
chunk_slots = 16
build_grant = 44
strips_per_step = 8
mib = 1024 * 1024


def scratch_bytes(*shapes):
    return sum(math.prod(shape) * jnp.dtype(kind).itemsize for shape, kind in shapes)


def add_tiles(list_ref, tiles_ref, total, held, sems, begin, end, *, first_block, blocks, steps):
    side = tiles_ref.shape[1]
    capacity = tiles_ref.shape[0]
    count = list_ref[2 * capacity]
    slots = held.shape[0]
    row_blocks = total.shape[0] // side - 1

    def fetch(index):
        slot = lax.rem(index - begin, slots)
        return pltpu.make_async_copy(
            tiles_ref.at[pl.ds(index * chunk_tiles, chunk_tiles)], held.at[slot], sems.at[slot]
        )

    def start(index, carry):
        fetch(index).start()
        return carry

    lax.fori_loop(begin, jnp.minimum(end, begin + slots), start, 0)

    def target(place):
        col = list_ref[capacity + place] - first_block
        live = place < count
        if steps > 1:
            live = live & (col >= 0) & (col < blocks)
            col = jnp.where(live, col, 0)
        row = jnp.where(live, list_ref[place], row_blocks)
        return row, col

    down, along = (lax.broadcasted_iota(jnp.int32, (side, side), axis) for axis in range(2))
    unit = (down == along).astype(jnp.float32).astype(jnp.bfloat16)

    def chunk_step(index, carry):
        fetch(index).wait()
        slot = lax.rem(index - begin, slots)
        spots = [target(index * chunk_tiles + lane) for lane in range(chunk_tiles)]
        at = [
            (pl.ds(pl.multiple_of(row * side, side), side), pl.ds(pl.multiple_of(col * side, side), side))
            for row, col in spots
        ]
        current = total[at[0]]
        for lane in range(chunk_tiles):
            last = lane == chunk_tiles - 1
            following = None if last else total[at[lane + 1]]
            current = current + jnp.dot(held[slot, lane], unit, preferred_element_type=jnp.float32)
            total[at[lane]] = current
            if not last:
                same = (spots[lane][0] == spots[lane + 1][0]) & (spots[lane][1] == spots[lane + 1][1])
                current = jnp.where(same, current, following)

        @pl.when(index + slots < end)
        def _():
            fetch(index + slots).start()

        return carry

    return lambda: lax.fori_loop(begin, end, chunk_step, 0)


def each_row_block(total, side, action):
    def step(block, carry):
        action(pl.ds(pl.multiple_of(block * side, side), side))
        return carry

    lax.fori_loop(0, total.shape[0] // side - 1, step, 0)


def live_chunks(list_ref, tiles_ref):
    return (list_ref[2 * tiles_ref.shape[0]] + chunk_tiles - 1) // chunk_tiles


def first_chunks(list_ref, tiles_ref):
    return (live_chunks(list_ref, tiles_ref) * 7 + 15) // 16


def build_first_kernel(list_ref, tiles_ref, dense_ref, total, held, sems, *, blocks):
    part = first_chunks(list_ref, tiles_ref)
    run = add_tiles(list_ref, tiles_ref, total, held, sems, 0, part, first_block=0, blocks=blocks, steps=1)

    def clear(down):
        total[down, :] = jnp.zeros((down.size, total.shape[1]), jnp.float32)

    def rounded(down):
        dense_ref[down, :] = total[down, :].astype(jnp.bfloat16)

    each_row_block(total, tiles_ref.shape[1], clear)
    run()
    each_row_block(total, tiles_ref.shape[1], rounded)


def build_rest_kernel(list_ref, tiles_ref, half_ref, dense_ref, total, held, sems, *, blocks):
    chunks = live_chunks(list_ref, tiles_ref)
    run = add_tiles(
        list_ref, tiles_ref, total, held, sems, first_chunks(list_ref, tiles_ref), chunks,
        first_block=0, blocks=blocks, steps=1,
    )

    def widened(down):
        total[down, :] = half_ref[down, :].astype(jnp.float32)

    def rounded(down):
        dense_ref[down, :] = total[down, :].astype(jnp.bfloat16)

    each_row_block(total, tiles_ref.shape[1], widened)
    run()
    each_row_block(total, tiles_ref.shape[1], rounded)


def build_whole_kernel(list_ref, tiles_ref, dense_ref, total, held, sems, *, blocks, steps):
    chunks = live_chunks(list_ref, tiles_ref)
    first_block = pl.program_id(0) * blocks
    run = add_tiles(
        list_ref, tiles_ref, total, held, sems, 0, chunks, first_block=first_block, blocks=blocks, steps=steps
    )

    def clear(down):
        total[down, :] = jnp.zeros((down.size, total.shape[1]), jnp.float32)

    def rounded(down):
        dense_ref[down, :] = total[down, :].astype(jnp.bfloat16)

    each_row_block(total, tiles_ref.shape[1], clear)
    run()
    each_row_block(total, tiles_ref.shape[1], rounded)


def build_stages(tiles, row_blocks, col_blocks, per_strip):
    capacity, side, _ = tiles.shape
    blocks = min(strips_per_step * per_strip, col_blocks)
    steps = col_blocks // blocks
    high, wide = row_blocks * side, blocks * side
    total = ((high + side, wide), jnp.float32)
    held = ((min(chunk_slots, capacity // chunk_tiles), chunk_tiles, side, side), jnp.bfloat16)
    cost = pl.CostEstimate(
        flops=capacity * side * side, bytes_accessed=capacity * side * side + high * wide, transcendentals=0
    )
    held_scratch = [pltpu.VMEM(*held), pltpu.SemaphoreType.DMA((held[0][0],))]
    dense_shape = jax.ShapeDtypeStruct((high, col_blocks * side), jnp.bfloat16)
    whole = pl.BlockSpec(memory_space=pltpu.VMEM)
    apart = pl.BlockSpec(memory_space=pl.ANY)
    listed = pl.BlockSpec(memory_space=pltpu.SMEM)
    if steps > 1:
        block = ((high, wide), jnp.bfloat16)
        return [
            lambda packed: pl.pallas_call(
                functools.partial(build_whole_kernel, blocks=blocks, steps=steps),
                out_shape=dense_shape,
                grid_spec=pltpu.PrefetchScalarGridSpec(
                    num_scalar_prefetch=1,
                    grid=(steps,),
                    in_specs=[apart],
                    out_specs=pl.BlockSpec((high, wide), lambda i, *_: (0, i)),
                    scratch_shapes=[pltpu.VMEM(*total)] + held_scratch,
                ),
                compiler_params=pltpu.CompilerParams(
                    vmem_limit_bytes=scratch_bytes(total, held, block, block) + 4 * mib
                ),
                cost_estimate=cost,
                name="build_whole",
            )(packed, tiles)
        ]
    params = pltpu.CompilerParams(vmem_limit_bytes=build_grant * mib)
    scratch = [pltpu.VMEM(*total)] + held_scratch
    return [
        lambda packed: (packed, pl.pallas_call(
            functools.partial(build_first_kernel, blocks=blocks),
            out_shape=dense_shape,
            in_specs=[listed, apart],
            out_specs=whole,
            scratch_shapes=scratch,
            compiler_params=params,
            cost_estimate=cost,
            name="build_first",
        )(packed, tiles)),
        lambda state: pl.pallas_call(
            functools.partial(build_rest_kernel, blocks=blocks),
            out_shape=dense_shape,
            in_specs=[listed, apart, whole],
            out_specs=whole,
            scratch_shapes=scratch,
            compiler_params=params,
            cost_estimate=cost,
            name="build_rest",
        )(state[0], tiles, state[1]),
    ]


def ring_place(row, count):
    return jnp.where(lax.rem(row, 2) == 0, row // 2, count - 1 - row // 2)


def ring_row(place, count):
    place = lax.rem(place + 2 * count, count)
    return jnp.where(place < count // 2, 2 * place, 2 * (count - 1 - place) + 1)


def forward_kernel(dense_ref, *refs, pieces, sibling, row_count):
    piece_refs, out_ref = refs[: len(pieces)], refs[len(pieces)]
    count = lax.axis_size("col")
    rows = dense_ref.shape[0] // count
    block = dense_ref.shape[1] // row_count
    place = ring_place(lax.axis_index("row"), row_count)
    col = lax.axis_index("col") ^ sibling
    operands = []
    for piece, ref in zip(pieces, piece_refs):
        for offset, first, start, high in piece:
            along = pl.ds(pl.multiple_of(ring_row(place + offset, row_count) * block + first, 128), high)
            operands.append((along, ref, pl.ds(start, high)))
    for index in range(count // 2):
        down = pl.ds(pl.multiple_of((col ^ (2 * index)) * rows, rows), rows)
        total = None
        for along, ref, part in operands:
            product = jnp.dot(dense_ref[down, along], ref[part, :], preferred_element_type=jnp.float32)
            total = product if total is None else total + product
        out_ref[pl.ds(index * rows, rows), :] = total.astype(jnp.bfloat16)


def forward_product(dense, shards, sibling, row_count, col_count):
    pieces = tuple(piece for piece, _ in shards)
    arrays = [array for _, array in shards]
    high, deep = dense.shape
    width = arrays[0].shape[1]
    half = high // 2
    cell = ((high, deep), jnp.bfloat16)
    depth = ((deep, width), jnp.bfloat16)
    out = ((high, width), jnp.float32)
    return pl.pallas_call(
        functools.partial(forward_kernel, pieces=pieces, sibling=sibling, row_count=row_count),
        out_shape=jax.ShapeDtypeStruct((half, width), jnp.bfloat16),
        in_specs=[pl.BlockSpec(memory_space=pltpu.VMEM)] * (1 + len(arrays)),
        out_specs=pl.BlockSpec(memory_space=pltpu.VMEM),
        compiler_params=pltpu.CompilerParams(vmem_limit_bytes=scratch_bytes(cell, depth, out) + 6 * mib),
        cost_estimate=pl.CostEstimate(
            flops=2 * half * deep * width,
            bytes_accessed=2 * (half * deep + deep * width + half * width),
            transcendentals=0,
        ),
        name="forward_product",
    )(dense, *arrays)


def partners_sum(values):
    while len(values) > 1:
        values = [values[i] + values[i + 1] for i in range(0, len(values), 2)]
    return values[0]


def middle_kernel(*refs, blocks, scale):
    sums, refs = refs[:blocks], refs[blocks:]
    weight_ref, refs = refs[0], refs[1:]
    cotangent_refs, (act_ref, message_ref, chunk_ref, product) = refs[:blocks], refs[blocks:]
    weight = weight_ref[...]
    rows, width = act_ref.shape
    over_nodes = (((0,), (0,)), ((), ()))
    terms = []
    for index in range(blocks):
        aggregate = partners_sum(
            [sums[other][pl.ds((index ^ other) * rows, rows), :].astype(jnp.float32) for other in range(blocks)]
        )
        high = aggregate.astype(jnp.bfloat16)
        low = (aggregate - high.astype(jnp.float32)).astype(jnp.bfloat16)
        pre = jnp.dot(high, weight, preferred_element_type=jnp.float32)
        pre += jnp.dot(low, weight, preferred_element_type=jnp.float32)
        sig = jax.nn.sigmoid(pre)
        cotangent = cotangent_refs[index][...].astype(jnp.float32)
        grad = (cotangent * sig * (1.0 + pre * (1.0 - sig))).astype(jnp.bfloat16)
        message_ref[pl.ds(index * width, width), :] = lax.dot_general(
            weight, grad, (((1,), (1,)), ((), ())), preferred_element_type=jnp.float32
        ).astype(jnp.bfloat16)
        if index == 0:
            act_ref[...] = (pre * sig).astype(jnp.bfloat16)
        part = lax.dot_general(high, grad, over_nodes, preferred_element_type=jnp.float32)
        part += lax.dot_general(low, grad, over_nodes, preferred_element_type=jnp.float32)
        terms.append(part)
    product[...] = partners_sum(terms) * scale
    col = lax.axis_index("col")
    size = chunk_ref.shape[0]
    core = col & 1
    chunk_ref[...] = product[pl.ds(pl.multiple_of(core * size, size), size), :]
    sent = product[pl.ds(pl.multiple_of((core ^ 1) * size, size), size), :]
    high = sent.astype(jnp.bfloat16)
    low = (sent - high.astype(jnp.float32)).astype(jnp.bfloat16)
    message_ref[pl.ds(blocks * width, size), :] = high
    message_ref[pl.ds(blocks * width + size, size), :] = low


def middle(sums, weight, cotangents, total_nodes):
    rows, width = cotangents[0].shape
    blocks = len(cotangents)
    size = width // 2
    return pl.pallas_call(
        functools.partial(middle_kernel, blocks=blocks, scale=1.0 / math.sqrt(total_nodes)),
        out_shape=[
            jax.ShapeDtypeStruct((rows, width), jnp.bfloat16),
            jax.ShapeDtypeStruct((blocks * width + 2 * size, rows), jnp.bfloat16),
            jax.ShapeDtypeStruct((size, width), jnp.float32),
        ],
        in_specs=[pl.BlockSpec(memory_space=pltpu.VMEM)] * (2 * blocks + 1),
        out_specs=[pl.BlockSpec(memory_space=pltpu.VMEM)] * 3,
        scratch_shapes=[pltpu.VMEM((width, width), jnp.float32)],
        compiler_params=pltpu.CompilerParams(vmem_limit_bytes=12 * mib),
        cost_estimate=pl.CostEstimate(
            flops=10 * blocks * rows * width * width,
            bytes_accessed=2 * (blocks * blocks + 2 * blocks + 4) * rows * width,
            transcendentals=blocks * rows * width,
        ),
        name="middle",
    )(*sums, weight, *cotangents)


def backward_kernel(dense_ref, own_ref, sibling_ref, chunk_ref, *refs, outputs, row_count):
    out_refs, (depth, sems) = refs[:-2], refs[-2:]
    count = lax.axis_size("col")
    width, rows = depth.shape[0], own_ref.shape[1]
    wide = dense_ref.shape[1] // row_count
    col = lax.axis_index("col")
    copies = []
    for index in range(count):
        block = pl.ds(index // 2 * width, width)
        along = pl.ds(pl.multiple_of((col ^ index) * rows, rows), rows)
        source = sibling_ref if index % 2 else own_ref
        copy = pltpu.make_async_copy(source.at[block], depth.at[:, along], sems.at[index])
        copy.start()
        copies.append(copy)
    size = chunk_ref.shape[0]
    from_sibling = count // 2 * width
    high, low = (sibling_ref[pl.ds(from_sibling + turn * size, size), :].astype(jnp.float32) for turn in range(2))
    terms = (chunk_ref[...] + (high + low)).astype(jnp.bfloat16)
    for copy in copies:
        copy.wait()
    place = ring_place(lax.axis_index("row"), row_count)
    strips = {}
    for (offset, layout), out_ref in zip(outputs, out_refs):
        start = 0
        for kind, first, high in layout:
            if kind == "strip" and offset not in strips:
                along = pl.ds(pl.multiple_of(ring_row(place + offset, row_count) * wide, wide), wide)
                part = jnp.dot(depth[...], dense_ref[:, along], preferred_element_type=jnp.float32)
                strips[offset] = part.astype(jnp.bfloat16)
            source = {"strip": strips.get(offset), "terms": terms, "zeros": jnp.zeros_like(terms)}[kind]
            out_ref[start : start + high, :] = source[first : first + high, :]
            start += high


def backward_product(dense, own, sibling, chunk, outputs, row_count, col_count):
    high, deep = dense.shape
    size, width = chunk.shape
    wide = deep // row_count
    cell = ((high, deep), jnp.bfloat16)
    depth = ((width, high), jnp.bfloat16)
    out = ((len(outputs), width + size, wide), jnp.float32)
    return pl.pallas_call(
        functools.partial(backward_kernel, outputs=outputs, row_count=row_count),
        out_shape=[
            jax.ShapeDtypeStruct((sum(high for _, _, high in layout), wide), jnp.bfloat16) for _, layout in outputs
        ],
        in_specs=[pl.BlockSpec(memory_space=pltpu.VMEM)] * 4,
        out_specs=[pl.BlockSpec(memory_space=pltpu.VMEM)] * len(outputs),
        scratch_shapes=[pltpu.VMEM(*depth), pltpu.SemaphoreType.DMA((col_count,))],
        compiler_params=pltpu.CompilerParams(vmem_limit_bytes=scratch_bytes(cell, depth, out) + 6 * mib),
        cost_estimate=pl.CostEstimate(
            flops=2 * high * wide * width, bytes_accessed=2 * wide * len(outputs) * width, transcendentals=0
        ),
        name="backward_product",
    )(dense, own, sibling, chunk)


def terms_kernel(*refs, pieces):
    term_refs, out_ref, places = refs[:-2], refs[-2], refs[-1]
    row_count = places.shape[0]
    place = ring_place(lax.axis_index("row"), row_count)
    for (offset, first, high, at), ref in zip(pieces, term_refs):
        places[ring_row(place + offset, row_count), pl.ds(at, high), :] = ref[pl.ds(first, high), :].astype(jnp.float32)
    total = places[0]
    for index in range(1, row_count):
        total += places[index]
    out_ref[...] = total


def summed_terms(terms, size, row_count):
    pieces = tuple(piece for *piece, _ in terms)
    arrays = [array for *_, array in terms]
    width = arrays[0].shape[1]
    return pl.pallas_call(
        functools.partial(terms_kernel, pieces=pieces),
        out_shape=jax.ShapeDtypeStruct((size, width), jnp.float32),
        in_specs=[pl.BlockSpec(memory_space=pltpu.VMEM)] * len(arrays),
        out_specs=pl.BlockSpec(memory_space=pltpu.VMEM),
        scratch_shapes=[pltpu.VMEM((row_count, size, width), jnp.float32)],
        compiler_params=pltpu.CompilerParams(
            vmem_limit_bytes=scratch_bytes(*((array.shape, array.dtype) for array in arrays))
            + scratch_bytes(((row_count, size, width), jnp.float32))
            + 6 * mib
        ),
        cost_estimate=pl.CostEstimate(
            flops=row_count * size * width, bytes_accessed=2 * row_count * size * width, transcendentals=0
        ),
        name="summed_terms",
    )(*arrays)


def finish_kernel(*refs, firsts):
    *part_refs, features_ref = refs
    width = features_ref.shape[1]
    total = jnp.zeros(features_ref.shape[::-1], jnp.float32)
    for first, part_ref in zip(firsts, part_refs):
        total += part_ref[pl.ds(first, width), :].astype(jnp.float32)
    features_ref[...] = total.astype(jnp.bfloat16).T


def finish(parts):
    firsts = tuple(first for first, _ in parts)
    parts = [array for _, array in parts]
    width, rows = parts[0].shape
    return pl.pallas_call(
        functools.partial(finish_kernel, firsts=firsts),
        out_shape=jax.ShapeDtypeStruct((rows, width), jnp.bfloat16),
        in_specs=[pl.BlockSpec(memory_space=pltpu.VMEM)] * len(parts),
        out_specs=pl.BlockSpec(memory_space=pltpu.VMEM),
        compiler_params=pltpu.CompilerParams(vmem_limit_bytes=8 * mib),
        cost_estimate=pl.CostEstimate(
            flops=len(parts) * rows * width, bytes_accessed=2 * (len(parts) + 1) * rows * width, transcendentals=0
        ),
        name="finish",
    )(*parts)


def joined_kernel(own_ref, sibling_ref, weight_ref):
    rows = own_ref.shape[0]
    core = lax.axis_index("col") & 1
    for turn, ref in enumerate((own_ref, sibling_ref)):
        weight_ref[pl.ds(pl.multiple_of((core ^ turn) * rows, rows), rows), :] = ref[...]


def joined(own, sibling):
    rows, width = own.shape
    return pl.pallas_call(
        joined_kernel,
        out_shape=jax.ShapeDtypeStruct((2 * rows, width), jnp.float32),
        in_specs=[pl.BlockSpec(memory_space=pltpu.VMEM)] * 2,
        out_specs=pl.BlockSpec(memory_space=pltpu.VMEM),
        compiler_params=pltpu.CompilerParams(vmem_limit_bytes=8 * mib),
        cost_estimate=pl.CostEstimate(flops=0, bytes_accessed=16 * rows * width, transcendentals=0),
        name="joined",
    )(own, sibling)


def around(value, step):
    count = lax.axis_size("row")
    order = list(range(0, count, 2)) + list(range(count - 1, 0, -2))
    return lax.ppermute(value, "row", [(order[i], order[(i + step) % count]) for i in range(count)])


def swapped(value, axis, partner):
    return lax.ppermute(value, axis, [(i, i ^ partner) for i in range(lax.axis_size(axis))])


def gathered_shards(own, packed, stages, cotangent):
    reach = lax.axis_size("row") // 2
    rows = own.shape[0]
    ups, downs, dense = [own], [own], packed
    others = []
    for step in range(1, reach + 1):
        up = around(ups[-1], 1)
        if step == reach - 1:
            up, dense, others = lax.optimization_barrier((up, dense, others))
        ups.append(up)
        if step == reach:
            break
        down = around(downs[-1], -1)
        if step == 1:
            down, dense = lax.optimization_barrier((down, dense))
        elif step == 2:
            dense = stages.pop(0)(dense)
            down, dense, cotangent = lax.optimization_barrier((down, dense, cotangent))
            others = [swapped(cotangent, "col", partner) for partner in range(2, lax.axis_size("col"), 2)]
        downs.append(down)
    if stages:
        dense = stages.pop(0)(dense)
    shards = [(((0, 0, 0, rows),), own)]
    shards += [(((-step, 0, 0, rows),), ups[step]) for step in range(1, reach + 1)]
    shards += [(((step, 0, 0, rows),), downs[step]) for step in range(1, reach)]
    return shards, dense, [cotangent] + others


def added(first, second, at=0):
    spare = first.shape[0] - at - second.shape[0]
    second = jnp.pad(second.astype(jnp.float32), ((at, spare), (0, 0)))
    return (first.astype(jnp.float32) + second).astype(jnp.bfloat16)


def scattered_sums(dense, own, sibling, chunk):
    row_count, col_count = lax.axis_size("row"), lax.axis_size("col")
    size, width = chunk.shape
    half = width // 2
    reach = row_count // 2
    strip, terms, zeros = ("strip", 0, width), ("terms", 0, size), ("zeros", 0, size)
    first = (
        (reach, (terms, ("strip", 0, half))),
        (reach, (("strip", half, half), terms)),
        (0, (terms,)),
    )
    above, below, terms = backward_product(dense, own, sibling, chunk, first, row_count, col_count)
    above, below, terms, cell = lax.optimization_barrier((above, below, terms, dense))
    up, down = around(above, 1), around(below, -1)
    all_terms = [(0, 0, size, 0, terms)]

    ups = tuple((offset, (zeros, strip) if offset > 1 else (strip,)) for offset in range(reach - 1, 0, -1))
    downs = tuple((-offset, (strip, zeros)) for offset in range(reach - 1, 0, -1))
    strips = backward_product(cell, own, sibling, chunk, ups + downs + ((0, (strip,)),), row_count, col_count)
    ups, downs, mine = strips[: reach - 1], strips[reach - 1 : -1], strips[-1]
    for step in range(1, reach):
        all_terms += [(-step, 0, size, 0, up), (step, down.shape[0] - size, size, 0, down)]
        if step == reach - 1:
            up = up[size:]
        up = around(added(ups[step - 1], up), 1)
        down = around(added(downs[step - 1], down, half if step == 1 else 0), -1)
    all_terms.append((reach, width, size, 0, down))
    return [(0, mine), (0, up), (0, down)], summed_terms(all_terms, size, row_count)


def per_device(features, weight, adj_tiles, tile_rows, tile_cols, tile_counts, out_grad):
    node_rows, width = features.shape
    capacity, side = adj_tiles.shape[2:4]
    tiles = adj_tiles.reshape(capacity, side, side)
    packed = jnp.concatenate([tile_rows, tile_cols, tile_counts[:, :, None]], axis=2).reshape(2 * capacity + 1)
    row_count = lax.axis_size("row")
    col_count = lax.axis_size("col")
    per_strip = node_rows // side
    stages = build_stages(tiles, col_count * per_strip, row_count * per_strip, per_strip)
    shards, dense, cotangents = gathered_shards(features, packed, stages, out_grad)

    for_sibling = forward_product(dense, shards, 1, row_count, col_count)
    for_sibling, cell = lax.optimization_barrier((for_sibling, dense))
    sums = added(forward_product(cell, shards, 0, row_count, col_count), swapped(for_sibling, "col", 1))
    sums = [sums] + [swapped(sums, "col", partner) for partner in range(2, col_count, 2)]
    activations, message, chunk = middle(sums, weight, cotangents, node_rows * row_count * col_count)
    sibling = swapped(message, "col", 1)
    parts, half = scattered_sums(dense, message, sibling, chunk)
    grad_weight = joined(half, swapped(half, "col", 1))
    return (activations, finish(parts), grad_weight)


def solution(mesh):
    placed = (
        P(("row", "col"), None),
        P(),
        P("row", "col", None, None, None),
        P("row", "col", None),
        P("row", "col", None),
        P("row", "col"),
        P(("row", "col"), None),
    )
    return jax.shard_map(
        per_device,
        mesh=mesh,
        in_specs=placed,
        out_specs=(P(("row", "col"), None), P(("row", "col"), None), P()),
        check_vma=False,
    )
```

```python
import functools
import math

import jax
import jax.numpy as jnp
from jax import lax
from jax.experimental import pallas as pl
from jax.experimental.pallas import tpu as pltpu
from jax.sharding import PartitionSpec as P

chunk_tiles = 16
chunk_slots = 16
build_grant = 44
strips_per_step = 8
mib = 1024 * 1024


def scratch_bytes(*shapes):
    return sum(math.prod(shape) * jnp.dtype(kind).itemsize for shape, kind in shapes)


def add_tiles(list_ref, tiles_ref, total, held, sems, begin, end, *, first_block, blocks, steps):
    side = tiles_ref.shape[1]
    capacity = tiles_ref.shape[0]
    count = list_ref[2 * capacity]
    slots = held.shape[0]
    row_blocks = total.shape[0] // side - 1

    def fetch(index):
        slot = lax.rem(index - begin, slots)
        return pltpu.make_async_copy(
            tiles_ref.at[pl.ds(index * chunk_tiles, chunk_tiles)], held.at[slot], sems.at[slot]
        )

    def start(index, carry):
        fetch(index).start()
        return carry

    lax.fori_loop(begin, jnp.minimum(end, begin + slots), start, 0)

    def target(place):
        col = list_ref[capacity + place] - first_block
        live = place < count
        if steps > 1:
            live = live & (col >= 0) & (col < blocks)
            col = jnp.where(live, col, 0)
        row = jnp.where(live, list_ref[place], row_blocks)
        return row, col

    def chunk_step(index, carry):
        fetch(index).wait()
        slot = lax.rem(index - begin, slots)
        for lane in range(0, chunk_tiles, 2):
            spots = [target(index * chunk_tiles + lane + turn) for turn in range(2)]
            at = [
                (pl.ds(pl.multiple_of(row * side, side), side), pl.ds(pl.multiple_of(col * side, side), side))
                for row, col in spots
            ]
            first, second = total[at[0]], total[at[1]]
            tiles = [held[slot, lane + turn].astype(jnp.float32) for turn in range(2)]
            same = (spots[0][0] == spots[1][0]) & (spots[0][1] == spots[1][1])
            total[at[0]] = first + tiles[0]
            total[at[1]] = second + tiles[1] + jnp.where(same, tiles[0], 0.0)

        @pl.when(index + slots < end)
        def _():
            fetch(index + slots).start()

        return carry

    return lambda: lax.fori_loop(begin, end, chunk_step, 0)


def each_row_block(total, side, action):
    def step(block, carry):
        action(pl.ds(pl.multiple_of(block * side, side), side))
        return carry

    lax.fori_loop(0, total.shape[0] // side - 1, step, 0)


def live_chunks(list_ref, tiles_ref):
    return (list_ref[2 * tiles_ref.shape[0]] + chunk_tiles - 1) // chunk_tiles


def first_chunks(list_ref, tiles_ref):
    return (live_chunks(list_ref, tiles_ref) * 7 + 15) // 16


def build_first_kernel(list_ref, tiles_ref, dense_ref, total, held, sems, *, blocks):
    part = first_chunks(list_ref, tiles_ref)
    run = add_tiles(list_ref, tiles_ref, total, held, sems, 0, part, first_block=0, blocks=blocks, steps=1)

    def clear(down):
        total[down, :] = jnp.zeros((down.size, total.shape[1]), jnp.float32)

    def rounded(down):
        dense_ref[down, :] = total[down, :].astype(jnp.bfloat16)

    each_row_block(total, tiles_ref.shape[1], clear)
    run()
    each_row_block(total, tiles_ref.shape[1], rounded)


def build_rest_kernel(list_ref, tiles_ref, half_ref, dense_ref, total, held, sems, *, blocks):
    chunks = live_chunks(list_ref, tiles_ref)
    run = add_tiles(
        list_ref, tiles_ref, total, held, sems, first_chunks(list_ref, tiles_ref), chunks,
        first_block=0, blocks=blocks, steps=1,
    )

    def widened(down):
        total[down, :] = half_ref[down, :].astype(jnp.float32)

    def rounded(down):
        dense_ref[down, :] = total[down, :].astype(jnp.bfloat16)

    each_row_block(total, tiles_ref.shape[1], widened)
    run()
    each_row_block(total, tiles_ref.shape[1], rounded)


def build_whole_kernel(list_ref, tiles_ref, dense_ref, total, held, sems, *, blocks, steps):
    chunks = live_chunks(list_ref, tiles_ref)
    first_block = pl.program_id(0) * blocks
    run = add_tiles(
        list_ref, tiles_ref, total, held, sems, 0, chunks, first_block=first_block, blocks=blocks, steps=steps
    )

    def clear(down):
        total[down, :] = jnp.zeros((down.size, total.shape[1]), jnp.float32)

    def rounded(down):
        dense_ref[down, :] = total[down, :].astype(jnp.bfloat16)

    each_row_block(total, tiles_ref.shape[1], clear)
    run()
    each_row_block(total, tiles_ref.shape[1], rounded)


def build_stages(tiles, row_blocks, col_blocks, per_strip):
    capacity, side, _ = tiles.shape
    blocks = min(strips_per_step * per_strip, col_blocks)
    steps = col_blocks // blocks
    high, wide = row_blocks * side, blocks * side
    total = ((high + side, wide), jnp.float32)
    held = ((min(chunk_slots, capacity // chunk_tiles), chunk_tiles, side, side), jnp.bfloat16)
    cost = pl.CostEstimate(
        flops=capacity * side * side, bytes_accessed=capacity * side * side + high * wide, transcendentals=0
    )
    held_scratch = [pltpu.VMEM(*held), pltpu.SemaphoreType.DMA((held[0][0],))]
    dense_shape = jax.ShapeDtypeStruct((high, col_blocks * side), jnp.bfloat16)
    whole = pl.BlockSpec(memory_space=pltpu.VMEM)
    apart = pl.BlockSpec(memory_space=pl.ANY)
    listed = pl.BlockSpec(memory_space=pltpu.SMEM)
    if steps > 1:
        block = ((high, wide), jnp.bfloat16)
        return [
            lambda packed: pl.pallas_call(
                functools.partial(build_whole_kernel, blocks=blocks, steps=steps),
                out_shape=dense_shape,
                grid_spec=pltpu.PrefetchScalarGridSpec(
                    num_scalar_prefetch=1,
                    grid=(steps,),
                    in_specs=[apart],
                    out_specs=pl.BlockSpec((high, wide), lambda i, *_: (0, i)),
                    scratch_shapes=[pltpu.VMEM(*total)] + held_scratch,
                ),
                compiler_params=pltpu.CompilerParams(
                    vmem_limit_bytes=scratch_bytes(total, held, block, block) + 4 * mib
                ),
                cost_estimate=cost,
                name="build_whole",
            )(packed, tiles)
        ]
    params = pltpu.CompilerParams(vmem_limit_bytes=build_grant * mib)
    scratch = [pltpu.VMEM(*total)] + held_scratch
    return [
        lambda packed: (packed, pl.pallas_call(
            functools.partial(build_first_kernel, blocks=blocks),
            out_shape=dense_shape,
            in_specs=[listed, apart],
            out_specs=whole,
            scratch_shapes=scratch,
            compiler_params=params,
            cost_estimate=cost,
            name="build_first",
        )(packed, tiles)),
        lambda state: pl.pallas_call(
            functools.partial(build_rest_kernel, blocks=blocks),
            out_shape=dense_shape,
            in_specs=[listed, apart, whole],
            out_specs=whole,
            scratch_shapes=scratch,
            compiler_params=params,
            cost_estimate=cost,
            name="build_rest",
        )(state[0], tiles, state[1]),
    ]


def ring_place(row, count):
    return jnp.where(lax.rem(row, 2) == 0, row // 2, count - 1 - row // 2)


def ring_row(place, count):
    place = lax.rem(place + 2 * count, count)
    return jnp.where(place < count // 2, 2 * place, 2 * (count - 1 - place) + 1)


def forward_kernel(dense_ref, *refs, pieces, sibling, row_count):
    piece_refs, out_ref = refs[: len(pieces)], refs[len(pieces)]
    count = lax.axis_size("col")
    rows = dense_ref.shape[0] // count
    block = dense_ref.shape[1] // row_count
    place = ring_place(lax.axis_index("row"), row_count)
    col = lax.axis_index("col") ^ sibling
    operands = []
    for piece, ref in zip(pieces, piece_refs):
        for offset, first, start, high in piece:
            along = pl.ds(pl.multiple_of(ring_row(place + offset, row_count) * block + first, 128), high)
            operands.append((along, ref, pl.ds(start, high)))
    for index in range(count // 2):
        down = pl.ds(pl.multiple_of((col ^ (2 * index)) * rows, rows), rows)
        total = None
        for along, ref, part in operands:
            product = jnp.dot(dense_ref[down, along], ref[part, :], preferred_element_type=jnp.float32)
            total = product if total is None else total + product
        out_ref[pl.ds(index * rows, rows), :] = total.astype(jnp.bfloat16)


def forward_product(dense, shards, sibling, row_count, col_count):
    pieces = tuple(piece for piece, _ in shards)
    arrays = [array for _, array in shards]
    high, deep = dense.shape
    width = arrays[0].shape[1]
    half = high // 2
    cell = ((high, deep), jnp.bfloat16)
    depth = ((deep, width), jnp.bfloat16)
    out = ((high, width), jnp.float32)
    return pl.pallas_call(
        functools.partial(forward_kernel, pieces=pieces, sibling=sibling, row_count=row_count),
        out_shape=jax.ShapeDtypeStruct((half, width), jnp.bfloat16),
        in_specs=[pl.BlockSpec(memory_space=pltpu.VMEM)] * (1 + len(arrays)),
        out_specs=pl.BlockSpec(memory_space=pltpu.VMEM),
        compiler_params=pltpu.CompilerParams(vmem_limit_bytes=scratch_bytes(cell, depth, out) + 6 * mib),
        cost_estimate=pl.CostEstimate(
            flops=2 * half * deep * width,
            bytes_accessed=2 * (half * deep + deep * width + half * width),
            transcendentals=0,
        ),
        name="forward_product",
    )(dense, *arrays)


def partners_sum(values):
    while len(values) > 1:
        values = [values[i] + values[i + 1] for i in range(0, len(values), 2)]
    return values[0]


def middle_kernel(*refs, blocks, scale):
    sums, refs = refs[:blocks], refs[blocks:]
    weight_ref, refs = refs[0], refs[1:]
    cotangent_refs, (act_ref, message_ref, chunk_ref, product) = refs[:blocks], refs[blocks:]
    weight = weight_ref[...]
    rows, width = act_ref.shape
    over_nodes = (((0,), (0,)), ((), ()))
    terms = []
    for index in range(blocks):
        aggregate = partners_sum(
            [sums[other][pl.ds((index ^ other) * rows, rows), :].astype(jnp.float32) for other in range(blocks)]
        )
        high = aggregate.astype(jnp.bfloat16)
        low = (aggregate - high.astype(jnp.float32)).astype(jnp.bfloat16)
        pre = jnp.dot(high, weight, preferred_element_type=jnp.float32)
        pre += jnp.dot(low, weight, preferred_element_type=jnp.float32)
        sig = jax.nn.sigmoid(pre)
        cotangent = cotangent_refs[index][...].astype(jnp.float32)
        grad = (cotangent * sig * (1.0 + pre * (1.0 - sig))).astype(jnp.bfloat16)
        message_ref[pl.ds(index * width, width), :] = lax.dot_general(
            weight, grad, (((1,), (1,)), ((), ())), preferred_element_type=jnp.float32
        ).astype(jnp.bfloat16)
        if index == 0:
            act_ref[...] = (pre * sig).astype(jnp.bfloat16)
        part = lax.dot_general(high, grad, over_nodes, preferred_element_type=jnp.float32)
        part += lax.dot_general(low, grad, over_nodes, preferred_element_type=jnp.float32)
        terms.append(part)
    product[...] = partners_sum(terms) * scale
    col = lax.axis_index("col")
    size = chunk_ref.shape[0]
    core = col & 1
    chunk_ref[...] = product[pl.ds(pl.multiple_of(core * size, size), size), :]
    sent = product[pl.ds(pl.multiple_of((core ^ 1) * size, size), size), :]
    high = sent.astype(jnp.bfloat16)
    low = (sent - high.astype(jnp.float32)).astype(jnp.bfloat16)
    message_ref[pl.ds(blocks * width, size), :] = high
    message_ref[pl.ds(blocks * width + size, size), :] = low


def middle(sums, weight, cotangents, total_nodes):
    rows, width = cotangents[0].shape
    blocks = len(cotangents)
    size = width // 2
    return pl.pallas_call(
        functools.partial(middle_kernel, blocks=blocks, scale=1.0 / math.sqrt(total_nodes)),
        out_shape=[
            jax.ShapeDtypeStruct((rows, width), jnp.bfloat16),
            jax.ShapeDtypeStruct((blocks * width + 2 * size, rows), jnp.bfloat16),
            jax.ShapeDtypeStruct((size, width), jnp.float32),
        ],
        in_specs=[pl.BlockSpec(memory_space=pltpu.VMEM)] * (2 * blocks + 1),
        out_specs=[pl.BlockSpec(memory_space=pltpu.VMEM)] * 3,
        scratch_shapes=[pltpu.VMEM((width, width), jnp.float32)],
        compiler_params=pltpu.CompilerParams(vmem_limit_bytes=12 * mib),
        cost_estimate=pl.CostEstimate(
            flops=10 * blocks * rows * width * width,
            bytes_accessed=2 * (blocks * blocks + 2 * blocks + 4) * rows * width,
            transcendentals=blocks * rows * width,
        ),
        name="middle",
    )(*sums, weight, *cotangents)


def backward_kernel(dense_ref, own_ref, sibling_ref, chunk_ref, *refs, outputs, row_count):
    out_refs, (depth, sems) = refs[:-2], refs[-2:]
    count = lax.axis_size("col")
    width, rows = depth.shape[0], own_ref.shape[1]
    wide = dense_ref.shape[1] // row_count
    col = lax.axis_index("col")
    copies = []
    for index in range(count):
        block = pl.ds(index // 2 * width, width)
        along = pl.ds(pl.multiple_of((col ^ index) * rows, rows), rows)
        source = sibling_ref if index % 2 else own_ref
        copy = pltpu.make_async_copy(source.at[block], depth.at[:, along], sems.at[index])
        copy.start()
        copies.append(copy)
    size = chunk_ref.shape[0]
    from_sibling = count // 2 * width
    high, low = (sibling_ref[pl.ds(from_sibling + turn * size, size), :].astype(jnp.float32) for turn in range(2))
    terms = (chunk_ref[...] + (high + low)).astype(jnp.bfloat16)
    for copy in copies:
        copy.wait()
    place = ring_place(lax.axis_index("row"), row_count)
    strips = {}
    for (offset, layout), out_ref in zip(outputs, out_refs):
        start = 0
        for kind, first, high in layout:
            if kind == "strip" and offset not in strips:
                along = pl.ds(pl.multiple_of(ring_row(place + offset, row_count) * wide, wide), wide)
                part = jnp.dot(depth[...], dense_ref[:, along], preferred_element_type=jnp.float32)
                strips[offset] = part.astype(jnp.bfloat16)
            source = {"strip": strips.get(offset), "terms": terms, "zeros": jnp.zeros_like(terms)}[kind]
            out_ref[start : start + high, :] = source[first : first + high, :]
            start += high


def backward_product(dense, own, sibling, chunk, outputs, row_count, col_count):
    high, deep = dense.shape
    size, width = chunk.shape
    wide = deep // row_count
    cell = ((high, deep), jnp.bfloat16)
    depth = ((width, high), jnp.bfloat16)
    out = ((len(outputs), width + size, wide), jnp.float32)
    return pl.pallas_call(
        functools.partial(backward_kernel, outputs=outputs, row_count=row_count),
        out_shape=[
            jax.ShapeDtypeStruct((sum(high for _, _, high in layout), wide), jnp.bfloat16) for _, layout in outputs
        ],
        in_specs=[pl.BlockSpec(memory_space=pltpu.VMEM)] * 4,
        out_specs=[pl.BlockSpec(memory_space=pltpu.VMEM)] * len(outputs),
        scratch_shapes=[pltpu.VMEM(*depth), pltpu.SemaphoreType.DMA((col_count,))],
        compiler_params=pltpu.CompilerParams(vmem_limit_bytes=scratch_bytes(cell, depth, out) + 6 * mib),
        cost_estimate=pl.CostEstimate(
            flops=2 * high * wide * width, bytes_accessed=2 * wide * len(outputs) * width, transcendentals=0
        ),
        name="backward_product",
    )(dense, own, sibling, chunk)


def terms_kernel(*refs, pieces):
    term_refs, out_ref, places = refs[:-2], refs[-2], refs[-1]
    row_count = places.shape[0]
    place = ring_place(lax.axis_index("row"), row_count)
    for (offset, first, high, at), ref in zip(pieces, term_refs):
        places[ring_row(place + offset, row_count), pl.ds(at, high), :] = ref[pl.ds(first, high), :].astype(jnp.float32)
    total = places[0]
    for index in range(1, row_count):
        total += places[index]
    out_ref[...] = total


def summed_terms(terms, size, row_count):
    pieces = tuple(piece for *piece, _ in terms)
    arrays = [array for *_, array in terms]
    width = arrays[0].shape[1]
    return pl.pallas_call(
        functools.partial(terms_kernel, pieces=pieces),
        out_shape=jax.ShapeDtypeStruct((size, width), jnp.float32),
        in_specs=[pl.BlockSpec(memory_space=pltpu.VMEM)] * len(arrays),
        out_specs=pl.BlockSpec(memory_space=pltpu.VMEM),
        scratch_shapes=[pltpu.VMEM((row_count, size, width), jnp.float32)],
        compiler_params=pltpu.CompilerParams(
            vmem_limit_bytes=scratch_bytes(*((array.shape, array.dtype) for array in arrays))
            + scratch_bytes(((row_count, size, width), jnp.float32))
            + 6 * mib
        ),
        cost_estimate=pl.CostEstimate(
            flops=row_count * size * width, bytes_accessed=2 * row_count * size * width, transcendentals=0
        ),
        name="summed_terms",
    )(*arrays)


def finish_kernel(*refs, firsts):
    *part_refs, features_ref = refs
    width = features_ref.shape[1]
    total = jnp.zeros(features_ref.shape[::-1], jnp.float32)
    for first, part_ref in zip(firsts, part_refs):
        total += part_ref[pl.ds(first, width), :].astype(jnp.float32)
    features_ref[...] = total.astype(jnp.bfloat16).T


def finish(parts):
    firsts = tuple(first for first, _ in parts)
    parts = [array for _, array in parts]
    width, rows = parts[0].shape
    return pl.pallas_call(
        functools.partial(finish_kernel, firsts=firsts),
        out_shape=jax.ShapeDtypeStruct((rows, width), jnp.bfloat16),
        in_specs=[pl.BlockSpec(memory_space=pltpu.VMEM)] * len(parts),
        out_specs=pl.BlockSpec(memory_space=pltpu.VMEM),
        compiler_params=pltpu.CompilerParams(vmem_limit_bytes=8 * mib),
        cost_estimate=pl.CostEstimate(
            flops=len(parts) * rows * width, bytes_accessed=2 * (len(parts) + 1) * rows * width, transcendentals=0
        ),
        name="finish",
    )(*parts)


def joined_kernel(own_ref, sibling_ref, weight_ref):
    rows = own_ref.shape[0]
    core = lax.axis_index("col") & 1
    for turn, ref in enumerate((own_ref, sibling_ref)):
        weight_ref[pl.ds(pl.multiple_of((core ^ turn) * rows, rows), rows), :] = ref[...]


def joined(own, sibling):
    rows, width = own.shape
    return pl.pallas_call(
        joined_kernel,
        out_shape=jax.ShapeDtypeStruct((2 * rows, width), jnp.float32),
        in_specs=[pl.BlockSpec(memory_space=pltpu.VMEM)] * 2,
        out_specs=pl.BlockSpec(memory_space=pltpu.VMEM),
        compiler_params=pltpu.CompilerParams(vmem_limit_bytes=8 * mib),
        cost_estimate=pl.CostEstimate(flops=0, bytes_accessed=16 * rows * width, transcendentals=0),
        name="joined",
    )(own, sibling)


def around(value, step):
    count = lax.axis_size("row")
    order = list(range(0, count, 2)) + list(range(count - 1, 0, -2))
    return lax.ppermute(value, "row", [(order[i], order[(i + step) % count]) for i in range(count)])


def swapped(value, axis, partner):
    return lax.ppermute(value, axis, [(i, i ^ partner) for i in range(lax.axis_size(axis))])


def gathered_shards(own, packed, stages, cotangent):
    reach = lax.axis_size("row") // 2
    rows = own.shape[0]
    ups, downs, dense = [own], [own], packed
    others = []
    for step in range(1, reach + 1):
        up = around(ups[-1], 1)
        if step == reach - 1:
            up, dense, others = lax.optimization_barrier((up, dense, others))
        ups.append(up)
        if step == reach:
            break
        down = around(downs[-1], -1)
        if step == 1:
            down, dense = lax.optimization_barrier((down, dense))
        elif step == 2:
            dense = stages.pop(0)(dense)
            down, dense, cotangent = lax.optimization_barrier((down, dense, cotangent))
            others = [swapped(cotangent, "col", partner) for partner in range(2, lax.axis_size("col"), 2)]
        downs.append(down)
    if stages:
        dense = stages.pop(0)(dense)
    shards = [(((0, 0, 0, rows),), own)]
    shards += [(((-step, 0, 0, rows),), ups[step]) for step in range(1, reach + 1)]
    shards += [(((step, 0, 0, rows),), downs[step]) for step in range(1, reach)]
    return shards, dense, [cotangent] + others


def added(first, second, at=0):
    spare = first.shape[0] - at - second.shape[0]
    second = jnp.pad(second.astype(jnp.float32), ((at, spare), (0, 0)))
    return (first.astype(jnp.float32) + second).astype(jnp.bfloat16)


def scattered_sums(dense, own, sibling, chunk):
    row_count, col_count = lax.axis_size("row"), lax.axis_size("col")
    size, width = chunk.shape
    half = width // 2
    reach = row_count // 2
    strip, terms, zeros = ("strip", 0, width), ("terms", 0, size), ("zeros", 0, size)
    first = (
        (reach, (terms, ("strip", 0, half))),
        (reach, (("strip", half, half), terms)),
        (0, (terms,)),
    )
    above, below, terms = backward_product(dense, own, sibling, chunk, first, row_count, col_count)
    above, below, terms, cell = lax.optimization_barrier((above, below, terms, dense))
    up, down = around(above, 1), around(below, -1)
    all_terms = [(0, 0, size, 0, terms)]

    ups = tuple((offset, (zeros, strip) if offset > 1 else (strip,)) for offset in range(reach - 1, 0, -1))
    downs = tuple((-offset, (strip, zeros)) for offset in range(reach - 1, 0, -1))
    strips = backward_product(cell, own, sibling, chunk, ups + downs + ((0, (strip,)),), row_count, col_count)
    ups, downs, mine = strips[: reach - 1], strips[reach - 1 : -1], strips[-1]
    for step in range(1, reach):
        all_terms += [(-step, 0, size, 0, up), (step, down.shape[0] - size, size, 0, down)]
        if step == reach - 1:
            up = up[size:]
        up = around(added(ups[step - 1], up), 1)
        down = around(added(downs[step - 1], down, half if step == 1 else 0), -1)
    all_terms.append((reach, width, size, 0, down))
    return [(0, mine), (0, up), (0, down)], summed_terms(all_terms, size, row_count)


def per_device(features, weight, adj_tiles, tile_rows, tile_cols, tile_counts, out_grad):
    node_rows, width = features.shape
    capacity, side = adj_tiles.shape[2:4]
    tiles = adj_tiles.reshape(capacity, side, side)
    packed = jnp.concatenate([tile_rows, tile_cols, tile_counts[:, :, None]], axis=2).reshape(2 * capacity + 1)
    row_count = lax.axis_size("row")
    col_count = lax.axis_size("col")
    per_strip = node_rows // side
    stages = build_stages(tiles, col_count * per_strip, row_count * per_strip, per_strip)
    shards, dense, cotangents = gathered_shards(features, packed, stages, out_grad)

    for_sibling = forward_product(dense, shards, 1, row_count, col_count)
    for_sibling, cell = lax.optimization_barrier((for_sibling, dense))
    sums = added(forward_product(cell, shards, 0, row_count, col_count), swapped(for_sibling, "col", 1))
    sums = [sums] + [swapped(sums, "col", partner) for partner in range(2, col_count, 2)]
    activations, message, chunk = middle(sums, weight, cotangents, node_rows * row_count * col_count)
    sibling = swapped(message, "col", 1)
    parts, half = scattered_sums(dense, message, sibling, chunk)
    grad_weight = joined(half, swapped(half, "col", 1))
    return (activations, finish(parts), grad_weight)


def solution(mesh):
    placed = (
        P(("row", "col"), None),
        P(),
        P("row", "col", None, None, None),
        P("row", "col", None),
        P("row", "col", None),
        P("row", "col"),
        P(("row", "col"), None),
    )
    return jax.shard_map(
        per_device,
        mesh=mesh,
        in_specs=placed,
        out_specs=(P(("row", "col"), None), P(("row", "col"), None), P()),
        check_vma=False,
    )
```
